128 devices in a mesh: seq: 4 (over z_hi, core), tp: 32 (over x, y, z_lo).
Axes of the slice: x: 4, y: 4, z: 4 (z_hi: 2, z_lo: 2; z = z_hi * 2 + z_lo), core: 2. Of those that a mesh axis runs over, the one named last changes fastest.
Arguments:
- tokens: bfloat16 [2048, 8192], P('seq', 'tp'), may hold values from -6 to 6
- up_weight: bfloat16 [128, 6, 256, 256], P(('seq', 'tp')), may hold values from -0.15625 to 0.15625
- down_weight: bfloat16 [128, 6, 256, 256], P(('seq', 'tp')), may hold values from -0.078125 to 0.078125
- block_mask: int32 [128, 6], P(('seq', 'tp')), may hold values from 0 to 1, as said below
- cotangent: bfloat16 [2048, 8192], P('seq', 'tp'), may hold values from -1.5 to 1.5
Outputs:
- output: bfloat16 [2048, 8192], P('seq', 'tp')
- grad_tokens: bfloat16 [2048, 8192], P('seq', 'tp')
- grad_up: float32 [128, 6, 256, 256], P(('seq', 'tp'))
- grad_down: float32 [128, 6, 256, 256], P(('seq', 'tp'))
The draws below stay inside these ranges and needn't reach their ends.
Inputs may be any that keep to these rules, and one draw needn't show every extreme that they name: `block_mask`: entries are 0 or 1; level 0 is 1 for every hidden group; for every owner index and level, at least one of the 4 hidden groups with that owner index has a 1.
All inputs are finite; a program needn't handle non-finite values.
Results may differ from the reference program's by a relative error of at most 0.0056.
Values may be sent and summed in bfloat16 or wider, within the bound.
A program may use at most 128 MiB of HBM per device.

```python
import jax
import jax.numpy as jnp
import numpy as np
from jax import lax

D = 8192
TOKENS = 2048
LEVELS = 6
DG = 256
HID_GROUPS = 128
HG = 256
N_SEQ = 4
N_TP = 32


def draw_block_mask(key, part):
    key = jax.random.fold_in(key, 11)
    coins = jax.random.randint(key, (HID_GROUPS, LEVELS), 0, 4)
    group = jnp.arange(HID_GROUPS, dtype=jnp.int32)[:, None]
    level = jnp.arange(LEVELS, dtype=jnp.int32)[None, :]
    seq_index = group // N_TP
    owner = group % N_TP
    forced = seq_index == (owner + level) % N_SEQ
    keep = (level == 0) | forced | (coins < 3)
    return jnp.where(keep, 1, 0).astype(jnp.int32)


def shard_levels(key, extent, pieces, smallest, top_value):
    factor_of, own = 1.0, jax.random.fold_in(key, 6)
    for position, shards_of in pieces:
        heights = jnp.exp(jax.random.uniform(jax.random.fold_in(own, position), (shards_of,), jnp.float32, smallest / len(pieces), top_value / len(pieces)))
        factor_of = factor_of * jnp.repeat(heights, extent[position] // shards_of).reshape([-1 if axis == position else 1 for axis in range(len(extent))])
    return factor_of


def scatter_about(key, extent, deviation, limit, shards=(), kind=jnp.bfloat16):
    entries = jax.random.normal(key, extent, jnp.float32) * deviation
    if len(shards) > 0:
        entries = shard_levels(key, extent, shards, -0.22, 0.18) * entries
    return jnp.clip(entries, min=-limit, max=limit).astype(kind)


def setup_inputs(seed: int = 0) -> dict:
    streams_of = jax.random.split(jax.random.key(seed), 6)
    tokens = scatter_about(streams_of[0], (TOKENS, D), 1.0, 6.0, ((0, 4), (1, 32)))
    up_weight = scatter_about(streams_of[1], (HID_GROUPS, LEVELS, DG, HG), (LEVELS * DG) ** -0.5, 0.15625, ((0, 128),))
    down_weight = scatter_about(streams_of[2], (HID_GROUPS, LEVELS, HG, DG), (LEVELS * N_SEQ * HG) ** -0.5, 0.078125, ((0, 128),))
    block_mask = draw_block_mask(jax.random.fold_in(streams_of[5], 71), 0)
    cotangent = scatter_about(streams_of[4], (TOKENS, D), 0.25, 1.5, ((0, 4), (1, 32)))
    return {"tokens": tokens, "up_weight": up_weight, "down_weight": down_weight, "block_mask": block_mask, "cotangent": cotangent}


def column_table():
    rows = []
    for owner in range(N_TP):
        rows.append([owner ^ (1 << level - 1 if level else 0) for level in range(LEVELS)])
    return jnp.asarray(np.array(rows, dtype=np.int32))

def rounded(value):
    return lax.optimization_barrier(value.astype(jnp.bfloat16)).astype(jnp.float32)

def reference(tokens, up_weight, down_weight, block_mask, cotangent):
    mask_b = block_mask.astype(jnp.bfloat16)
    mask_f = block_mask.astype(jnp.float32).reshape(N_SEQ, N_TP, LEVELS)
    up_masked = (up_weight * mask_b[:, :, None, None]).reshape(N_SEQ, N_TP, LEVELS, DG, HG)
    down_masked = (down_weight * mask_b[:, :, None, None]).reshape(N_SEQ, N_TP, LEVELS, HG, DG)
    x_groups = tokens.reshape(TOKENS, N_TP, DG)
    g_groups = cotangent.reshape(TOKENS, N_TP, DG)
    table = column_table()

    def step(carry, owner):
        out_acc, gin_acc = carry
        cols = table[owner]
        xs = jnp.take(x_groups, cols, axis=1).astype(jnp.float32)
        gs = jnp.take(g_groups, cols, axis=1).astype(jnp.float32)
        w_up = up_masked[:, owner].astype(jnp.float32)
        w_down = down_masked[:, owner].astype(jnp.float32)
        masks = mask_f[:, owner]
        pre = jnp.einsum('tkd,skdh->sth', xs, w_up)
        act = rounded(jax.nn.gelu(pre))
        part = jnp.einsum('sth,skhd->ktd', act, w_down)
        contrib = jnp.concatenate([part[:1], rounded(part[1:])], axis=0)
        out_acc = out_acc.at[cols].add(contrib)
        grad_act = jnp.einsum('tkd,skhd->sth', gs, w_down)
        pull = jax.vjp(jax.nn.gelu, pre)[1]
        grad_pre = rounded(pull(grad_act)[0])
        g_down = jnp.einsum('sth,tkd->skhd', act, gs) * masks[:, :, None, None]
        g_up = jnp.einsum('tkd,sth->skdh', xs, grad_pre) * masks[:, :, None, None]
        gpart = jnp.einsum('sth,skdh->ktd', grad_pre, w_up)
        gcontrib = jnp.concatenate([gpart[:1], rounded(gpart[1:])], axis=0)
        gin_acc = gin_acc.at[cols].add(gcontrib)
        return ((out_acc, gin_acc), (g_up, g_down))
    start = (jnp.zeros((N_TP, TOKENS, DG), jnp.float32), jnp.zeros((N_TP, TOKENS, DG), jnp.float32))
    (out_acc, gin_acc), (g_up, g_down) = lax.scan(step, start, jnp.arange(N_TP, dtype=jnp.int32))
    output = out_acc.transpose(1, 0, 2).reshape(TOKENS, D).astype(jnp.bfloat16)
    grad_tokens = gin_acc.transpose(1, 0, 2).reshape(TOKENS, D).astype(jnp.bfloat16)
    grad_up = g_up.transpose(1, 0, 2, 3, 4).reshape(HID_GROUPS, LEVELS, DG, HG)
    grad_down = g_down.transpose(1, 0, 2, 3, 4).reshape(HID_GROUPS, LEVELS, HG, DG)
    return (output, grad_tokens, grad_up, grad_down)
```

```python
import functools
import math

import jax
import jax.numpy as jnp
from jax import lax
from jax.experimental import pallas as pl
from jax.experimental.pallas import tpu as pltpu
from jax.sharding import PartitionSpec as P

MESH = pl.DeviceIdType.MESH
F32 = jnp.float32
BF16 = jnp.bfloat16
ROWS = 512
PART = 256
PIECES = ROWS // PART
G = 256
LEVELS = 6
WIDE = LEVELS * G
NEAR = {"x": 4, "y": 2}
FAR = {"x": 5, "y": 3}
SCALE = math.sqrt(2.0 / math.pi)
CUBE = 0.044715


def numbering():
    table, count = {}, 0
    for which in range(2):
        for name in ("z1", "z3", "zr"):
            table[name, which] = count
            count += PIECES
        for name in ("near", "far", "term", "sum"):
            for axis in "xy":
                for slot in range(2):
                    table[name, axis, which, slot] = count
                    count += PIECES
        for name in ("out1", "out3", "half"):
            table[name, which] = count
            count += PIECES
        table["weight", which] = count
        count += 1
        table["grad", which] = count
        count += LEVELS
    return table, count


NUMBER, COPIES = numbering()


def flip(index, bit):
    return index + bit - 2 * bit * lax.rem(lax.div(index, bit), 2)


def dot_nt(a, b):
    return lax.dot_general(a, b, (((1,), (1,)), ((), ())), preferred_element_type=F32)


def dot_tn(a, b):
    return lax.dot_general(a, b, (((0,), (0,)), ((), ())), preferred_element_type=F32)


def kernel(
    tok, cot, up, down, mask, out, gtok, gup, gdown,
    held, raw, uall, dall, act, gpre, slope,
    term_send, term_recv, near_term, sum_send, sum_recv, base, z_term,
    half_send, half_recv, z_send, z_recv,
    grad_own, grad_peer, grad_recv, done,
    sends, recvs, local,
):
    shared = (tok, cot)
    seq, tp = lax.axis_index("seq"), lax.axis_index("tp")
    place = {
        "core": (flip(seq, 1), tp),
        "z1": (seq, flip(tp, 1)),
        "z3": (flip(seq, 2), flip(tp, 1)),
        "x1": (seq, flip(tp, 8)),
        "x3": (seq, flip(flip(tp, 8), 16)),
        "y1": (seq, flip(tp, 2)),
        "y3": (seq, flip(flip(tp, 2), 4)),
    }

    def remote(src, dst, number, target):
        return pltpu.make_async_remote_copy(
            src_ref=src,
            dst_ref=dst,
            send_sem=sends.at[number],
            recv_sem=recvs.at[number],
            device_id=place[target],
            device_id_type=MESH,
        )

    def rows(slot, j):
        return pl.ds(slot * ROWS + j * PART, PART)

    def piece(j):
        return pl.ds(j * PART, PART)

    def columns(level):
        return pl.ds(level * G, G)

    def z1(which, j):
        return remote(shared[which].at[piece(j)], held.at[which, rows(0, j), columns(1)], NUMBER["z1", which] + j, "z1")

    def z3(which, j):
        return remote(shared[which].at[piece(j)], held.at[which, rows(1, j), columns(1)], NUMBER["z3", which] + j, "z3")

    def zr(which, j):
        return remote(
            held.at[which, rows(j, j), columns(1)],
            held.at[which, rows(1, j), columns(0)],
            NUMBER["zr", which] + j,
            "z3" if j == 0 else "z1",
        )

    def near(axis, which, slot, j):
        src = shared[which].at[piece(j)] if slot == 0 else held.at[which, rows(1, j), columns(0)]
        return remote(src, held.at[which, rows(slot, j), columns(NEAR[axis])], NUMBER["near", axis, which, slot] + j, axis + "1")

    def far(axis, which, slot, j):
        return remote(
            held.at[which, rows(slot, j), columns(NEAR[axis])],
            held.at[which, rows(slot, j), columns(FAR[axis])],
            NUMBER["far", axis, which, slot] + j,
            axis + "3",
        )

    def term(axis, which, slot, j):
        a = "xy".index(axis)
        return remote(
            term_send.at[which, a, rows(slot, j)],
            term_recv.at[which, a, rows(slot, j)],
            NUMBER["term", axis, which, slot] + j,
            axis + "3",
        )

    def summed(axis, which, slot, j):
        a = "xy".index(axis)
        return remote(
            sum_send.at[which, a, rows(slot, j)],
            sum_recv.at[which, a, rows(slot, j)],
            NUMBER["sum", axis, which, slot] + j,
            axis + "1",
        )

    def half(which, j):
        return remote(half_send.at[which, piece(j)], half_recv.at[which, piece(j)], NUMBER["half", which] + j, "z3" if j == 0 else "z1")

    def out1(which, j):
        return remote(z_send.at[which, rows(0, j)], z_recv.at[which, rows(0, j)], NUMBER["out1", which] + j, "z1")

    def out3(which, j):
        return remote(z_send.at[which, rows(1, j)], z_recv.at[which, rows(1, j)], NUMBER["out3", which] + j, "z3")

    def weight(which):
        if which == 0:
            return remote(uall.at[:, pl.ds(0, G)], uall.at[:, pl.ds(G, G)], NUMBER["weight", 0], "core")
        return remote(dall.at[pl.ds(0, G)], dall.at[pl.ds(G, G)], NUMBER["weight", 1], "core")

    def grad(which, level):
        return remote(grad_peer.at[which, level], grad_recv.at[which, level], NUMBER["grad", which] + level, "core")

    own = [
        pltpu.make_async_copy(shared[which], held.at[which, pl.ds(0, ROWS), columns(0)], local.at[which])
        for which in range(2)
    ]
    loads = [pltpu.make_async_copy(ref, raw.at[which], local.at[2 + which]) for which, ref in enumerate((up, down))]
    for copy in loads + own:
        copy.start()

    barrier = pltpu.get_barrier_semaphore()
    for target in place.values():
        pl.semaphore_signal(barrier, inc=1, device_id=target, device_id_type=MESH)
    pl.semaphore_wait(barrier, len(place))

    def send_own(which):
        for j in range(PIECES):
            z1(which, j).start()
            z3(which, j).start()
            near("x", which, 0, j).start()
            near("y", which, 0, j).start()

    def relay_z(which):
        for j in range(PIECES):
            z1(which, j).wait_recv()
            z3(which, j).wait_recv()
            zr(which, j).start()

    def relay_xy(which, slot):
        for j in range(PIECES):
            for axis in "xy":
                near(axis, which, slot, j).wait_recv()
                far(axis, which, slot, j).start()

    def send_other(which):
        for j in range(PIECES):
            zr(which, j).wait_recv()
            near("x", which, 1, j).start()
            near("y", which, 1, j).start()

    def arrived(which, slot):
        for j in range(PIECES):
            for axis in "xy":
                far(axis, which, slot, j).wait_recv()

    def scale_up(k, carry):
        factor = mask[0, k].astype(F32)
        uall[pl.ds(pl.multiple_of(k * G, G), G), pl.ds(0, G)] = (raw[0, k].astype(F32) * factor).astype(BF16)
        return carry

    def scale_down(k, carry):
        factor = mask[0, k].astype(F32)
        dall[pl.ds(0, G), pl.ds(pl.multiple_of(k * G, G), G)] = (raw[1, k].astype(F32) * factor).astype(BF16)
        return carry

    def terms(which, slot, j, at, left, weights):
        for axis in "xy":
            term_send[which, "xy".index(axis), at] = weights(left, FAR[axis]).astype(BF16)
            term(axis, which, slot, j).start()
        for axis in "xy":
            near_term[which, "xy".index(axis), at] = weights(left, NEAR[axis])
        z_term[which, at] = weights(left, 1)
        base[which, at] = weights(left, 0)

    def by_down(left, level):
        return jnp.dot(left, dall[:, pl.ds(level * G, G)], preferred_element_type=F32)

    def by_up(left, level):
        return dot_nt(left, uall[pl.ds(level * G, G), :])

    def forward(slot):
        def body(j, carry):
            at = pl.ds(pl.multiple_of(slot * ROWS + j * PART, PART), PART)
            pre = jnp.dot(held[0, at, :], uall[...], preferred_element_type=F32)
            square = pre * pre
            tanh = jnp.tanh(SCALE * pre * (1.0 + CUBE * square))
            cdf = 0.5 + 0.5 * tanh
            act[at, :] = (pre * cdf).astype(BF16)
            slope[at, :] = cdf + (0.5 * SCALE) * pre * (1.0 - tanh * tanh) * (1.0 + (3.0 * CUBE) * square)
            terms(0, slot, j, at, act[at, :], by_down)
            return carry

        lax.fori_loop(0, PIECES, body, 0)
        plain(0, slot)

    def backward(slot):
        def body(j, carry):
            at = pl.ds(pl.multiple_of(slot * ROWS + j * PART, PART), PART)
            gact = dot_nt(held[1, at, :], dall[...])
            gpre[at, :] = (gact * slope[at, :]).astype(BF16)
            terms(1, slot, j, at, gpre[at, :], by_up)
            return carry

        lax.fori_loop(0, PIECES, body, 0)
        plain(1, slot)

    def plain(which, slot):
        at = rows(slot, 1 - slot)
        z_send[which, at] = z_term[which, at].astype(BF16)
        (out1 if slot == 0 else out3)(which, 1 - slot).start()

    def join(which, slot):
        for j in range(PIECES):
            for a, axis in enumerate("xy"):
                at = rows(slot, j)
                term(axis, which, slot, j).wait_recv()
                sum_send[which, a, at] = (near_term[which, a, at] + term_recv[which, a, at].astype(F32)).astype(BF16)
                summed(axis, which, slot, j).start()

    def collect(which, slot):
        for j in range(PIECES):
            at = rows(slot, j)
            for axis in "xy":
                summed(axis, which, slot, j).wait_recv()
            total = base[which, at] + sum_recv[which, 0, at].astype(F32) + sum_recv[which, 1, at].astype(F32)
            if slot == 0:
                base[which, at] = total
            else:
                half_send[which, piece(j)] = total.astype(BF16)
                half(which, j).start()

    def pass_on(which):
        for j in range(PIECES):
            at = rows(j, j)
            half(which, j).wait_recv()
            z_send[which, at] = (z_term[which, at] + half_recv[which, piece(j)].astype(F32)).astype(BF16)
            (out1 if j == 0 else out3)(which, j).start()

    def finish(which, result):
        for j in range(PIECES):
            out1(which, j).wait_recv()
            out3(which, j).wait_recv()
            total = base[which, rows(0, j)] + z_recv[which, rows(0, j)].astype(F32) + z_recv[which, rows(1, j)].astype(F32)
            result[piece(j), :] = total.astype(BF16)

    def grads_down():
        def body(k, carry):
            at = pl.ds(pl.multiple_of(k * G, G), G)
            both = dot_tn(act[...], held[1, :, at])
            grad_own[1, k] = both[:G]
            grad_peer[1, k] = both[G:]
            grad(1, k).start()
            return carry

        lax.fori_loop(0, LEVELS, body, 0)

    def grads_up():
        def body(k, carry):
            at = pl.ds(pl.multiple_of(k * G, G), G)
            both = dot_tn(held[0, :, at], gpre[...])
            grad_own[0, k] = both[:, :G]
            grad_peer[0, k] = both[:, G:]
            grad(0, k).start()
            return carry

        lax.fori_loop(0, LEVELS, body, 0)

    def grads_sum(which, result):
        def body(k, carry):
            grad(which, k).wait_recv()
            factor = mask[0, k].astype(F32)
            done[which, k] = (grad_own[which, k] + grad_recv[which, k]) * factor
            pltpu.make_async_copy(done.at[which, k], result.at[k], local.at[4 + which * LEVELS + k]).start()
            return carry

        lax.fori_loop(0, LEVELS, body, 0)

    send_own(0)
    loads[0].wait()
    lax.fori_loop(0, LEVELS, scale_up, 0)
    weight(0).start()
    loads[1].wait()
    lax.fori_loop(0, LEVELS, scale_down, 0)
    weight(1).start()
    for copy in own:
        copy.wait()

    relay_z(0)
    relay_xy(0, 0)
    send_own(1)
    send_other(0)
    relay_z(1)
    relay_xy(1, 0)
    weight(0).wait_recv()
    weight(1).wait_recv()
    arrived(0, 0)
    forward(0)
    relay_xy(0, 1)
    send_other(1)
    arrived(1, 0)
    backward(0)
    arrived(0, 1)
    forward(1)
    relay_xy(1, 1)
    join(0, 0)
    join(1, 0)
    arrived(1, 1)
    backward(1)
    join(0, 1)
    collect(0, 0)
    collect(1, 0)
    grads_down()
    join(1, 1)
    collect(0, 1)
    grads_up()
    collect(1, 1)
    pass_on(0)
    pass_on(1)
    grads_sum(1, gdown)
    grads_sum(0, gup)
    finish(0, out)
    finish(1, gtok)

    for which, result in enumerate((gup, gdown)):
        for k in range(LEVELS):
            pltpu.make_async_copy(done.at[which, k], result.at[k], local.at[4 + which * LEVELS + k]).wait()
    for which in range(2):
        weight(which).wait_send()
        for k in range(LEVELS):
            grad(which, k).wait_send()
        for j in range(PIECES):
            for make in (z1, z3, zr, half, out1, out3):
                make(which, j).wait_send()
            for slot in range(2):
                for axis in "xy":
                    for make in (near, far, term, summed):
                        make(axis, which, slot, j).wait_send()


def shards(tokens, up_weight, down_weight, block_mask, cotangent):
    hbm = pl.BlockSpec(memory_space=pl.ANY)
    vmem = pl.BlockSpec(memory_space=pltpu.VMEM)
    both = 2 * ROWS
    output, grad_tokens, grad_up, grad_down = pl.pallas_call(
        kernel,
        out_shape=(
            jax.ShapeDtypeStruct((ROWS, G), BF16),
            jax.ShapeDtypeStruct((ROWS, G), BF16),
            jax.ShapeDtypeStruct((LEVELS, G, G), F32),
            jax.ShapeDtypeStruct((LEVELS, G, G), F32),
        ),
        in_specs=[hbm, hbm, hbm, hbm, pl.BlockSpec(memory_space=pltpu.SMEM)],
        out_specs=(vmem, vmem, hbm, hbm),
        scratch_shapes=[
            pltpu.VMEM((2, both, WIDE), BF16),
            pltpu.VMEM((2, LEVELS, G, G), BF16),
            pltpu.VMEM((WIDE, 2 * G), BF16),
            pltpu.VMEM((2 * G, WIDE), BF16),
            pltpu.VMEM((both, 2 * G), BF16),
            pltpu.VMEM((both, 2 * G), BF16),
            pltpu.VMEM((both, 2 * G), F32),
            pltpu.VMEM((2, 2, both, G), BF16),
            pltpu.VMEM((2, 2, both, G), BF16),
            pltpu.VMEM((2, 2, both, G), F32),
            pltpu.VMEM((2, 2, both, G), BF16),
            pltpu.VMEM((2, 2, both, G), BF16),
            pltpu.VMEM((2, both, G), F32),
            pltpu.VMEM((2, both, G), F32),
            pltpu.VMEM((2, ROWS, G), BF16),
            pltpu.VMEM((2, ROWS, G), BF16),
            pltpu.VMEM((2, both, G), BF16),
            pltpu.VMEM((2, both, G), BF16),
            pltpu.VMEM((2, LEVELS, G, G), F32),
            pltpu.VMEM((2, LEVELS, G, G), F32),
            pltpu.VMEM((2, LEVELS, G, G), F32),
            pltpu.VMEM((2, LEVELS, G, G), F32),
            pltpu.SemaphoreType.DMA((COPIES,)),
            pltpu.SemaphoreType.DMA((COPIES,)),
            pltpu.SemaphoreType.DMA((4 + 2 * LEVELS,)),
        ],
        compiler_params=pltpu.CompilerParams(
            collective_id=0, has_side_effects=True, vmem_limit_bytes=58 * 1024 * 1024
        ),
    )(tokens, cotangent, up_weight[0], down_weight[0], block_mask)
    return output, grad_tokens, grad_up[None], grad_down[None]


def solution(mesh):
    placed = (
        P("seq", "tp"),
        P(("seq", "tp"), None, None, None),
        P(("seq", "tp"), None, None, None),
        P(("seq", "tp"), None),
        P("seq", "tp"),
    )
    return jax.shard_map(
        shards,
        mesh=mesh,
        in_specs=placed,
        out_specs=(
            P("seq", "tp"),
            P("seq", "tp"),
            P(("seq", "tp"), None, None, None),
            P(("seq", "tp"), None, None, None),
        ),
        check_vma=False,
    )
```

```python
import functools
import math

import jax
import jax.numpy as jnp
from jax import lax
from jax.experimental import pallas as pl
from jax.experimental.pallas import tpu as pltpu
from jax.sharding import PartitionSpec as P

MESH = pl.DeviceIdType.MESH
F32 = jnp.float32
BF16 = jnp.bfloat16
ROWS = 512
PART = 256
PIECES = ROWS // PART
G = 256
LEVELS = 6
WIDE = LEVELS * G
NEAR = {"x": 4, "y": 2}
FAR = {"x": 5, "y": 3}
SCALE = math.sqrt(2.0 / math.pi)
CUBE = 0.044715


def numbering():
    table, count = {}, 0
    for which in range(2):
        for name in ("z1", "z3", "zr"):
            table[name, which] = count
            count += PIECES
        for name in ("near", "far", "term", "sum"):
            for axis in "xy":
                for slot in range(2):
                    table[name, axis, which, slot] = count
                    count += PIECES
        for name in ("out1", "out3", "half"):
            table[name, which] = count
            count += PIECES
        table["weight", which] = count
        count += 1
        table["grad", which] = count
        count += LEVELS
    return table, count


NUMBER, COPIES = numbering()


def flip(index, bit):
    return index + bit - 2 * bit * lax.rem(lax.div(index, bit), 2)


def dot_nt(a, b):
    return lax.dot_general(a, b, (((1,), (1,)), ((), ())), preferred_element_type=F32)


def dot_tn(a, b):
    return lax.dot_general(a, b, (((0,), (0,)), ((), ())), preferred_element_type=F32)


def kernel(
    tok, cot, up, down, mask, out, gtok, gup, gdown,
    held, raw, uall, dall, act, gpre, slope,
    term_send, term_recv, near_term, sum_send, sum_recv, base, z_term,
    half_send, half_recv, z_send, z_recv,
    grad_own, grad_peer, grad_recv,
    sends, recvs, local,
):
    shared = (tok, cot)
    seq, tp = lax.axis_index("seq"), lax.axis_index("tp")
    place = {
        "core": (flip(seq, 1), tp),
        "z1": (seq, flip(tp, 1)),
        "z3": (flip(seq, 2), flip(tp, 1)),
        "x1": (seq, flip(tp, 8)),
        "x3": (seq, flip(flip(tp, 8), 16)),
        "y1": (seq, flip(tp, 2)),
        "y3": (seq, flip(flip(tp, 2), 4)),
    }

    def remote(src, dst, number, target):
        return pltpu.make_async_remote_copy(
            src_ref=src,
            dst_ref=dst,
            send_sem=sends.at[number],
            recv_sem=recvs.at[number],
            device_id=place[target],
            device_id_type=MESH,
        )

    def rows(slot, j):
        start = slot * ROWS + j * PART
        return pl.ds(start if isinstance(j, int) else pl.multiple_of(start, PART), PART)

    def piece(j):
        return pl.ds(j * PART, PART)

    def columns(level):
        return pl.ds(level * G, G)

    def z1(which, j):
        return remote(shared[which].at[piece(j)], held.at[which, rows(0, j), columns(1)], NUMBER["z1", which] + j, "z1")

    def z3(which, j):
        return remote(shared[which].at[piece(j)], held.at[which, rows(1, j), columns(1)], NUMBER["z3", which] + j, "z3")

    def zr(which, j):
        return remote(
            held.at[which, rows(j, j), columns(1)],
            held.at[which, rows(1, j), columns(0)],
            NUMBER["zr", which] + j,
            "z3" if j == 0 else "z1",
        )

    def near(axis, which, slot, j):
        src = shared[which].at[piece(j)] if slot == 0 else held.at[which, rows(1, j), columns(0)]
        return remote(src, held.at[which, rows(slot, j), columns(NEAR[axis])], NUMBER["near", axis, which, slot] + j, axis + "1")

    def far(axis, which, slot, j):
        return remote(
            held.at[which, rows(slot, j), columns(NEAR[axis])],
            held.at[which, rows(slot, j), columns(FAR[axis])],
            NUMBER["far", axis, which, slot] + j,
            axis + "3",
        )

    def term(axis, which, slot, j):
        a = "xy".index(axis)
        return remote(
            term_send.at[which, a, rows(slot, j)],
            term_recv.at[which, a, rows(slot, j)],
            NUMBER["term", axis, which, slot] + j,
            axis + "3",
        )

    def summed(axis, which, slot, j):
        a = "xy".index(axis)
        return remote(
            sum_send.at[which, a, rows(slot, j)],
            sum_recv.at[which, a, rows(slot, j)],
            NUMBER["sum", axis, which, slot] + j,
            axis + "1",
        )

    def half(which, j):
        return remote(half_send.at[which, piece(j)], half_recv.at[which, piece(j)], NUMBER["half", which] + j, "z3" if j == 0 else "z1")

    def out1(which, j):
        return remote(z_send.at[which, rows(0, j)], z_recv.at[which, rows(0, j)], NUMBER["out1", which] + j, "z1")

    def out3(which, j):
        return remote(z_send.at[which, rows(1, j)], z_recv.at[which, rows(1, j)], NUMBER["out3", which] + j, "z3")

    def weight(which):
        if which == 0:
            return remote(uall.at[:, pl.ds(0, G)], uall.at[:, pl.ds(G, G)], NUMBER["weight", 0], "core")
        return remote(dall.at[pl.ds(0, G)], dall.at[pl.ds(G, G)], NUMBER["weight", 1], "core")

    def grad(which, level):
        return remote(grad_peer.at[which, level], grad_recv.at[which, level], NUMBER["grad", which] + level, "core")

    own = [
        pltpu.make_async_copy(shared[which], held.at[which, pl.ds(0, ROWS), columns(0)], local.at[which])
        for which in range(2)
    ]
    loads = [pltpu.make_async_copy(ref, raw.at[which], local.at[2 + which]) for which, ref in enumerate((up, down))]
    for copy in loads + own:
        copy.start()

    barrier = pltpu.get_barrier_semaphore()
    for target in place.values():
        pl.semaphore_signal(barrier, inc=1, device_id=target, device_id_type=MESH)
    pl.semaphore_wait(barrier, len(place))

    def own_z(which, j):
        z1(which, j).start()
        z3(which, j).start()

    def own_xy(which, j):
        near("x", which, 0, j).start()
        near("y", which, 0, j).start()

    def relay_z(which, j):
        (z1 if j == 0 else z3)(which, j).wait_recv()
        zr(which, j).start()

    def relay_xy(which, slot, j):
        for axis in "xy":
            near(axis, which, slot, j).wait_recv()
            far(axis, which, slot, j).start()

    def other(which, j):
        zr(which, j).wait_recv()
        near("x", which, 1, j).start()
        near("y", which, 1, j).start()

    def arrived(which, slot):
        (z1 if slot == 0 else z3)(which, 1 - slot).wait_recv()
        for j in range(PIECES):
            for axis in "xy":
                far(axis, which, slot, j).wait_recv()

    def scale_up(k, carry):
        factor = mask[0, k].astype(F32)
        uall[pl.ds(pl.multiple_of(k * G, G), G), pl.ds(0, G)] = (raw[0, k].astype(F32) * factor).astype(BF16)
        return carry

    def scale_down(k, carry):
        factor = mask[0, k].astype(F32)
        dall[pl.ds(0, G), pl.ds(pl.multiple_of(k * G, G), G)] = (raw[1, k].astype(F32) * factor).astype(BF16)
        return carry

    def terms(which, slot, j, at, left, weights):
        for axis in "xy":
            term_send[which, "xy".index(axis), at] = weights(left, FAR[axis]).astype(BF16)
            term(axis, which, slot, j).start()
        for axis in "xy":
            near_term[which, "xy".index(axis), at] = weights(left, NEAR[axis])
        z_term[which, at] = weights(left, 1)
        base[which, at] = weights(left, 0)

    def by_down(left, level):
        return jnp.dot(left, dall[:, pl.ds(level * G, G)], preferred_element_type=F32)

    def by_up(left, level):
        return dot_nt(left, uall[pl.ds(level * G, G), :])

    def forward(slot, after=lambda j: None):
        def body(j, carry):
            at = pl.ds(pl.multiple_of(slot * ROWS + j * PART, PART), PART)
            pre = jnp.dot(held[0, at, :], uall[...], preferred_element_type=F32)
            square = pre * pre
            tanh = jnp.tanh(SCALE * pre * (1.0 + CUBE * square))
            cdf = 0.5 + 0.5 * tanh
            act[at, :] = (pre * cdf).astype(BF16)
            slope[at, :] = cdf + (0.5 * SCALE) * pre * (1.0 - tanh * tanh) * (1.0 + (3.0 * CUBE) * square)
            terms(0, slot, j, at, act[at, :], by_down)
            after(j)
            return carry

        lax.fori_loop(0, PIECES, body, 0)
        plain(0, slot)

    def backward(slot):
        def body(j, carry):
            at = pl.ds(pl.multiple_of(slot * ROWS + j * PART, PART), PART)
            gact = dot_nt(held[1, at, :], dall[...])
            gpre[at, :] = (gact * slope[at, :]).astype(BF16)
            terms(1, slot, j, at, gpre[at, :], by_up)
            return carry

        lax.fori_loop(0, PIECES, body, 0)
        plain(1, slot)

    def plain(which, slot):
        at = rows(slot, 1 - slot)
        z_send[which, at] = z_term[which, at].astype(BF16)
        (out1 if slot == 0 else out3)(which, 1 - slot).start()

    def join(which, slot):
        for j in range(PIECES):
            for a, axis in enumerate("xy"):
                at = rows(slot, j)
                term(axis, which, slot, j).wait_recv()
                sum_send[which, a, at] = (near_term[which, a, at] + term_recv[which, a, at].astype(F32)).astype(BF16)
                summed(axis, which, slot, j).start()

    def collect(which, slot):
        for j in range(PIECES):
            at = rows(slot, j)
            for axis in "xy":
                summed(axis, which, slot, j).wait_recv()
            total = base[which, at] + sum_recv[which, 0, at].astype(F32) + sum_recv[which, 1, at].astype(F32)
            if slot == 0:
                base[which, at] = total
            else:
                half_send[which, piece(j)] = total.astype(BF16)
                half(which, j).start()

    def pass_on(which):
        for j in range(PIECES):
            at = rows(j, j)
            half(which, j).wait_recv()
            z_send[which, at] = (z_term[which, at] + half_recv[which, piece(j)].astype(F32)).astype(BF16)
            (out1 if j == 0 else out3)(which, j).start()

    def finish(which, result):
        for j in range(PIECES):
            out1(which, j).wait_recv()
            out3(which, j).wait_recv()
            total = base[which, rows(0, j)] + z_recv[which, rows(0, j)].astype(F32) + z_recv[which, rows(1, j)].astype(F32)
            result[piece(j), :] = total.astype(BF16)

    def grads_down():
        def body(k, carry):
            at = pl.ds(pl.multiple_of(k * G, G), G)
            both = dot_tn(act[...], held[1, :, at])
            grad_own[1, k] = both[:G]
            grad_peer[1, k] = both[G:]
            grad(1, k).start()
            return carry

        lax.fori_loop(0, LEVELS, body, 0)

    def grads_up():
        def body(k, carry):
            at = pl.ds(pl.multiple_of(k * G, G), G)
            both = dot_tn(held[0, :, at], gpre[...])
            grad_own[0, k] = both[:, :G]
            grad_peer[0, k] = both[:, G:]
            grad(0, k).start()
            return carry

        lax.fori_loop(0, LEVELS, body, 0)

    def grads_sum(which, result):
        def body(k, carry):
            grad(which, k).wait_recv()
            factor = mask[0, k].astype(F32)
            grad_own[which, k] = (grad_own[which, k] + grad_recv[which, k]) * factor
            pltpu.make_async_copy(grad_own.at[which, k], result.at[k], local.at[4 + which * LEVELS + k]).start()
            return carry

        lax.fori_loop(0, LEVELS, body, 0)

    for j in range(PIECES):
        own_z(0, j)
        own_xy(0, j)
    loads[0].wait()
    lax.fori_loop(0, LEVELS, scale_up, 0)
    weight(0).start()
    loads[1].wait()
    lax.fori_loop(0, LEVELS, scale_down, 0)
    weight(1).start()
    for copy in own:
        copy.wait()

    for j in range(PIECES):
        relay_z(0, j)
        relay_xy(0, 0, j)
        own_xy(1, j)
        own_z(1, j)
    for j in range(PIECES):
        other(0, j)
    for j in range(PIECES):
        relay_z(1, j)
        relay_xy(1, 0, j)
    for j in range(PIECES):
        relay_xy(0, 1, j)
        other(1, j)
    weight(0).wait_recv()
    weight(1).wait_recv()
    arrived(0, 0)
    forward(0, lambda j: relay_xy(1, 1, j))
    arrived(0, 1)
    forward(1)
    join(0, 0)
    arrived(1, 1)
    backward(1)
    join(0, 1)
    arrived(1, 0)
    backward(0)
    collect(0, 0)
    collect(0, 1)
    join(1, 1)
    grads_down()
    pass_on(0)
    collect(1, 1)
    join(1, 0)
    grads_up()
    pass_on(1)
    grads_sum(1, gdown)
    grads_sum(0, gup)
    collect(1, 0)
    finish(0, out)
    finish(1, gtok)

    for which, result in enumerate((gup, gdown)):
        for k in range(LEVELS):
            pltpu.make_async_copy(grad_own.at[which, k], result.at[k], local.at[4 + which * LEVELS + k]).wait()
    for which in range(2):
        weight(which).wait_send()
        for k in range(LEVELS):
            grad(which, k).wait_send()
        for j in range(PIECES):
            for make in (z1, z3, zr, half, out1, out3):
                make(which, j).wait_send()
            for slot in range(2):
                for axis in "xy":
                    for make in (near, far, term, summed):
                        make(axis, which, slot, j).wait_send()


def hand_out(*refs):
    sources, results, sems = refs[:4], refs[4:8], refs[8]
    copies = []
    for src, dst in zip(sources, results):
        if len(src.shape) == 2:
            pairs = [(src, dst)]
        else:
            pairs = [(src.at[pl.ds(k, 2)], dst.at[pl.ds(k, 2)]) for k in range(0, LEVELS, 2)]
        for a, b in pairs:
            copies.append(pltpu.make_async_copy(a, b, sems.at[len(copies)]))
    for copy in copies:
        copy.start()
    for copy in copies:
        copy.wait()


def shards(tokens, up_weight, down_weight, block_mask, cotangent):
    hbm = pl.BlockSpec(memory_space=pl.ANY)
    vmem = pl.BlockSpec(memory_space=pltpu.VMEM)
    fixed = pl.BlockSpec(memory_space=pltpu.HBM)
    both = 2 * ROWS
    result = (
        jax.ShapeDtypeStruct((ROWS, G), BF16),
        jax.ShapeDtypeStruct((ROWS, G), BF16),
        jax.ShapeDtypeStruct((LEVELS, G, G), F32),
        jax.ShapeDtypeStruct((LEVELS, G, G), F32),
    )
    worked = pl.pallas_call(
        kernel,
        out_shape=result,
        in_specs=[fixed, fixed, fixed, fixed, pl.BlockSpec(memory_space=pltpu.SMEM)],
        out_specs=(vmem, vmem, hbm, hbm),
        scratch_shapes=[
            pltpu.VMEM((2, both, WIDE), BF16),
            pltpu.VMEM((2, LEVELS, G, G), BF16),
            pltpu.VMEM((WIDE, 2 * G), BF16),
            pltpu.VMEM((2 * G, WIDE), BF16),
            pltpu.VMEM((both, 2 * G), BF16),
            pltpu.VMEM((both, 2 * G), BF16),
            pltpu.VMEM((both, 2 * G), F32),
            pltpu.VMEM((2, 2, both, G), BF16),
            pltpu.VMEM((2, 2, both, G), BF16),
            pltpu.VMEM((2, 2, both, G), F32),
            pltpu.VMEM((2, 2, both, G), BF16),
            pltpu.VMEM((2, 2, both, G), BF16),
            pltpu.VMEM((2, both, G), F32),
            pltpu.VMEM((2, both, G), F32),
            pltpu.VMEM((2, ROWS, G), BF16),
            pltpu.VMEM((2, ROWS, G), BF16),
            pltpu.VMEM((2, both, G), BF16),
            pltpu.VMEM((2, both, G), BF16),
            pltpu.VMEM((2, LEVELS, G, G), F32),
            pltpu.VMEM((2, LEVELS, G, G), F32),
            pltpu.VMEM((2, LEVELS, G, G), F32),
            pltpu.SemaphoreType.DMA((COPIES,)),
            pltpu.SemaphoreType.DMA((COPIES,)),
            pltpu.SemaphoreType.DMA((4 + 2 * LEVELS,)),
        ],
        compiler_params=pltpu.CompilerParams(
            collective_id=0, has_side_effects=True, vmem_limit_bytes=46 * 1024 * 1024
        ),
    )(tokens, cotangent, up_weight[0], down_weight[0], block_mask)
    output, grad_tokens, grad_up, grad_down = pl.pallas_call(
        hand_out,
        out_shape=result,
        in_specs=[hbm] * 4,
        out_specs=(hbm,) * 4,
        scratch_shapes=[pltpu.SemaphoreType.DMA((8,))],
    )(*worked)
    return output, grad_tokens, grad_up[None], grad_down[None]


def solution(mesh):
    placed = (
        P("seq", "tp"),
        P(("seq", "tp"), None, None, None),
        P(("seq", "tp"), None, None, None),
        P(("seq", "tp"), None),
        P("seq", "tp"),
    )
    return jax.shard_map(
        shards,
        mesh=mesh,
        in_specs=placed,
        out_specs=(
            P("seq", "tp"),
            P("seq", "tp"),
            P(("seq", "tp"), None, None, None),
            P(("seq", "tp"), None, None, None),
        ),
        check_vma=False,
    )
```

```python
import functools
import math

import jax
import jax.numpy as jnp
from jax import lax
from jax.experimental import pallas as pl
from jax.experimental.pallas import tpu as pltpu
from jax.sharding import PartitionSpec as P

MESH = pl.DeviceIdType.MESH
F32 = jnp.float32
BF16 = jnp.bfloat16
ROWS = 512
PART = 256
PIECES = ROWS // PART
G = 256
LEVELS = 6
WIDE = LEVELS * G
NEAR = {"x": 4, "y": 2}
FAR = {"x": 5, "y": 3}
SCALE = math.sqrt(2.0 / math.pi)
CUBE = 0.044715


def numbering():
    table, count = {}, 0
    for which in range(2):
        for name in ("z1", "z3", "zr"):
            table[name, which] = count
            count += PIECES
        for name in ("near", "far", "term", "sum"):
            for axis in "xy":
                for slot in range(2):
                    table[name, axis, which, slot] = count
                    count += PIECES
        for name in ("out1", "out3", "half"):
            table[name, which] = count
            count += PIECES
        table["weight", which] = count
        count += 1
        table["grad", which] = count
        count += LEVELS
    return table, count


NUMBER, COPIES = numbering()


def flip(index, bit):
    return index + bit - 2 * bit * lax.rem(lax.div(index, bit), 2)


def dot_nt(a, b):
    return lax.dot_general(a, b, (((1,), (1,)), ((), ())), preferred_element_type=F32)


def dot_tn(a, b):
    return lax.dot_general(a, b, (((0,), (0,)), ((), ())), preferred_element_type=F32)


def kernel(
    tok, cot, up, down, mask, out, gtok, gup, gdown,
    held, raw, uall, dall, act, gpre, slope,
    term_send, term_recv, near_term, sum_send, sum_recv, base, z_term,
    half_send, half_recv, z_send, z_recv,
    grad_own, grad_peer, grad_recv,
    sends, recvs, local,
):
    shared = (tok, cot)
    seq, tp = lax.axis_index("seq"), lax.axis_index("tp")
    place = {
        "core": (flip(seq, 1), tp),
        "z1": (seq, flip(tp, 1)),
        "z3": (flip(seq, 2), flip(tp, 1)),
        "x1": (seq, flip(tp, 8)),
        "x3": (seq, flip(flip(tp, 8), 16)),
        "y1": (seq, flip(tp, 2)),
        "y3": (seq, flip(flip(tp, 2), 4)),
    }

    def remote(src, dst, number, target):
        return pltpu.make_async_remote_copy(
            src_ref=src,
            dst_ref=dst,
            send_sem=sends.at[number],
            recv_sem=recvs.at[number],
            device_id=place[target],
            device_id_type=MESH,
        )

    def rows(slot, j):
        start = slot * ROWS + j * PART
        return pl.ds(start if isinstance(j, int) else pl.multiple_of(start, PART), PART)

    def piece(j):
        return pl.ds(j * PART, PART)

    def columns(level):
        return pl.ds(level * G, G)

    def z1(which, j):
        return remote(shared[which].at[piece(j)], held.at[which, rows(0, j), columns(1)], NUMBER["z1", which] + j, "z1")

    def z3(which, j):
        return remote(shared[which].at[piece(j)], held.at[which, rows(1, j), columns(1)], NUMBER["z3", which] + j, "z3")

    def zr(which, j):
        return remote(
            held.at[which, rows(j, j), columns(1)],
            held.at[which, rows(1, j), columns(0)],
            NUMBER["zr", which] + j,
            "z3" if j == 0 else "z1",
        )

    def near(axis, which, slot, j):
        src = shared[which].at[piece(j)] if slot == 0 else held.at[which, rows(1, j), columns(0)]
        return remote(src, held.at[which, rows(slot, j), columns(NEAR[axis])], NUMBER["near", axis, which, slot] + j, axis + "1")

    def far(axis, which, slot, j):
        return remote(
            held.at[which, rows(slot, j), columns(NEAR[axis])],
            held.at[which, rows(slot, j), columns(FAR[axis])],
            NUMBER["far", axis, which, slot] + j,
            axis + "3",
        )

    def term(axis, which, slot, j):
        a = "xy".index(axis)
        return remote(
            term_send.at[which, a, rows(slot, j)],
            term_recv.at[which, a, rows(slot, j)],
            NUMBER["term", axis, which, slot] + j,
            axis + "3",
        )

    def summed(axis, which, slot, j):
        a = "xy".index(axis)
        return remote(
            sum_send.at[which, a, rows(slot, j)],
            sum_recv.at[which, a, rows(slot, j)],
            NUMBER["sum", axis, which, slot] + j,
            axis + "1",
        )

    def half(which, j):
        return remote(half_send.at[which, piece(j)], half_recv.at[which, piece(j)], NUMBER["half", which] + j, "z3" if j == 0 else "z1")

    def out1(which, j):
        return remote(z_send.at[which, rows(0, j)], z_recv.at[which, rows(0, j)], NUMBER["out1", which] + j, "z1")

    def out3(which, j):
        return remote(z_send.at[which, rows(1, j)], z_recv.at[which, rows(1, j)], NUMBER["out3", which] + j, "z3")

    def weight(which):
        if which == 0:
            return remote(uall.at[:, pl.ds(0, G)], uall.at[:, pl.ds(G, G)], NUMBER["weight", 0], "core")
        return remote(dall.at[pl.ds(0, G)], dall.at[pl.ds(G, G)], NUMBER["weight", 1], "core")

    def grad(which, level):
        return remote(grad_peer.at[which, level], grad_recv.at[which, level], NUMBER["grad", which] + level, "core")

    own = [
        pltpu.make_async_copy(shared[which], held.at[which, pl.ds(0, ROWS), columns(0)], local.at[which])
        for which in range(2)
    ]
    loads = [pltpu.make_async_copy(ref, raw.at[which], local.at[2 + which]) for which, ref in enumerate((up, down))]
    for copy in loads + own:
        copy.start()

    barrier = pltpu.get_barrier_semaphore()
    for target in place.values():
        pl.semaphore_signal(barrier, inc=1, device_id=target, device_id_type=MESH)
    pl.semaphore_wait(barrier, len(place))

    def own_z(which, j):
        z1(which, j).start()
        z3(which, j).start()

    def own_xy(which, j):
        near("x", which, 0, j).start()
        near("y", which, 0, j).start()

    def relay_z(which, j):
        (z1 if j == 0 else z3)(which, j).wait_recv()
        zr(which, j).start()

    def relay_xy(which, slot, j):
        for axis in "xy":
            near(axis, which, slot, j).wait_recv()
            far(axis, which, slot, j).start()

    def other(which, j):
        zr(which, j).wait_recv()
        near("x", which, 1, j).start()
        near("y", which, 1, j).start()

    def arrived(which, slot):
        (z1 if slot == 0 else z3)(which, 1 - slot).wait_recv()
        for j in range(PIECES):
            for axis in "xy":
                far(axis, which, slot, j).wait_recv()

    def scale_up(k, carry):
        factor = mask[0, k].astype(F32)
        uall[pl.ds(pl.multiple_of(k * G, G), G), pl.ds(0, G)] = (raw[0, k].astype(F32) * factor).astype(BF16)
        return carry

    def scale_down(k, carry):
        factor = mask[0, k].astype(F32)
        dall[pl.ds(0, G), pl.ds(pl.multiple_of(k * G, G), G)] = (raw[1, k].astype(F32) * factor).astype(BF16)
        return carry

    def forward(slot, j):
        at = rows(slot, j)
        pre = jnp.dot(held[0, at, :], uall[...], preferred_element_type=F32)
        square = pre * pre
        tanh = jnp.tanh(SCALE * pre * (1.0 + CUBE * square))
        cdf = 0.5 + 0.5 * tanh
        act[at, :] = (pre * cdf).astype(BF16)
        slope[at, :] = cdf + (0.5 * SCALE) * pre * (1.0 - tanh * tanh) * (1.0 + (3.0 * CUBE) * square)

    def backward(slot, j):
        at = rows(slot, j)
        gact = dot_nt(held[1, at, :], dall[...])
        gpre[at, :] = (gact * slope[at, :]).astype(BF16)

    def by_down(slot, j, level):
        return jnp.dot(act[rows(slot, j), :], dall[:, columns(level)], preferred_element_type=F32)

    def by_up(slot, j, level):
        return dot_nt(gpre[rows(slot, j), :], uall[columns(level), :])

    def terms(which, slot, j, send):
        at = rows(slot, j)
        product = by_up if which else by_down
        for a, axis in enumerate("xy"):
            term_send[which, a, at] = product(slot, j, FAR[axis]).astype(BF16)
            if send:
                term(axis, which, slot, j).start()
        for a, axis in enumerate("xy"):
            near_term[which, a, at] = product(slot, j, NEAR[axis])
        z_term[which, at] = product(slot, j, 1)
        base[which, at] = product(slot, j, 0)

    def send_terms(which, slot):
        for j in range(PIECES):
            for axis in "xy":
                term(axis, which, slot, j).start()

    def tiles(which, slot):
        def body(j, carry):
            (backward if which else forward)(slot, j)
            terms(which, slot, j, True)
            return carry

        lax.fori_loop(0, PIECES, body, 0)
        plain(which, slot)

    def plain(which, slot):
        at = rows(slot, 1 - slot)
        z_send[which, at] = z_term[which, at].astype(BF16)
        (out1 if slot == 0 else out3)(which, 1 - slot).start()

    def join(which, slot):
        for j in range(PIECES):
            for a, axis in enumerate("xy"):
                at = rows(slot, j)
                term(axis, which, slot, j).wait_recv()
                sum_send[which, a, at] = (near_term[which, a, at] + term_recv[which, a, at].astype(F32)).astype(BF16)
                summed(axis, which, slot, j).start()

    def collect(which, slot):
        for j in range(PIECES):
            at = rows(slot, j)
            for axis in "xy":
                summed(axis, which, slot, j).wait_recv()
            total = base[which, at] + sum_recv[which, 0, at].astype(F32) + sum_recv[which, 1, at].astype(F32)
            if slot == 0:
                base[which, at] = total
            else:
                half_send[which, piece(j)] = total.astype(BF16)
                half(which, j).start()

    def pass_on(which):
        for j in range(PIECES):
            at = rows(j, j)
            half(which, j).wait_recv()
            z_send[which, at] = (z_term[which, at] + half_recv[which, piece(j)].astype(F32)).astype(BF16)
            (out1 if j == 0 else out3)(which, j).start()

    def finish(which, result):
        for j in range(PIECES):
            out1(which, j).wait_recv()
            out3(which, j).wait_recv()
            total = base[which, rows(0, j)] + z_recv[which, rows(0, j)].astype(F32) + z_recv[which, rows(1, j)].astype(F32)
            result[piece(j), :] = total.astype(BF16)

    def grads_down(first, last):
        def body(k, carry):
            at = pl.ds(pl.multiple_of(k * G, G), G)
            both = dot_tn(act[...], held[1, :, at])
            grad_own[1, k] = both[:G]
            grad_peer[1, k] = both[G:]
            grad(1, k).start()
            return carry

        lax.fori_loop(first, last, body, 0)

    def grads_up(first, last):
        def body(k, carry):
            at = pl.ds(pl.multiple_of(k * G, G), G)
            both = dot_tn(held[0, :, at], gpre[...])
            grad_own[0, k] = both[:, :G]
            grad_peer[0, k] = both[:, G:]
            grad(0, k).start()
            return carry

        lax.fori_loop(first, last, body, 0)

    def grads_sum(which, result):
        def body(k, carry):
            grad(which, k).wait_recv()
            factor = mask[0, k].astype(F32)
            grad_own[which, k] = (grad_own[which, k] + grad_recv[which, k]) * factor
            pltpu.make_async_copy(grad_own.at[which, k], result.at[k], local.at[4 + which * LEVELS + k]).start()
            return carry

        lax.fori_loop(0, LEVELS, body, 0)

    for j in range(PIECES):
        own_z(0, j)
        own_xy(0, j)
    loads[0].wait()
    lax.fori_loop(0, LEVELS, scale_up, 0)
    weight(0).start()
    loads[1].wait()
    lax.fori_loop(0, LEVELS, scale_down, 0)
    weight(1).start()
    for copy in own:
        copy.wait()

    for j in range(PIECES):
        relay_xy(0, 0, j)
        own_xy(1, j)
        relay_z(0, j)
        own_z(1, j)
    for j in range(PIECES):
        relay_xy(1, 0, j)
        other(0, j)
    for j in range(PIECES):
        relay_z(1, j)
    weight(0).wait_recv()
    weight(1).wait_recv()
    arrived(0, 0)
    forward(0, 0)
    terms(0, 0, 0, False)
    for j in range(PIECES):
        relay_xy(0, 1, j)
        other(1, j)
    forward(0, 1)
    terms(0, 0, 1, False)
    plain(0, 0)
    for j in range(PIECES):
        relay_xy(1, 1, j)

    arrived(0, 1)
    tiles(0, 1)
    arrived(1, 1)
    tiles(1, 1)
    send_terms(0, 0)
    join(0, 1)
    arrived(1, 0)
    tiles(1, 0)
    grads_down(0, LEVELS // 2)
    join(1, 1)
    collect(0, 1)
    grads_down(LEVELS // 2, LEVELS)
    join(0, 0)
    collect(1, 1)
    pass_on(0)
    grads_up(0, LEVELS)
    join(1, 0)
    pass_on(1)
    collect(0, 0)
    grads_sum(1, gdown)
    finish(0, out)
    grads_sum(0, gup)
    collect(1, 0)
    finish(1, gtok)

    for which, result in enumerate((gup, gdown)):
        for k in range(LEVELS):
            pltpu.make_async_copy(grad_own.at[which, k], result.at[k], local.at[4 + which * LEVELS + k]).wait()
    for which in range(2):
        weight(which).wait_send()
        for k in range(LEVELS):
            grad(which, k).wait_send()
        for j in range(PIECES):
            for make in (z1, z3, zr, half, out1, out3):
                make(which, j).wait_send()
            for slot in range(2):
                for axis in "xy":
                    for make in (near, far, term, summed):
                        make(axis, which, slot, j).wait_send()


def hand_out(*refs):
    sources, results, rooms, sems = refs[:4], refs[4:8], refs[8:12], refs[12]
    moves = []
    for src, room, dst in zip(sources, rooms, results):
        if len(src.shape) == 2:
            trio = [(src, room, dst)]
        else:
            trio = [tuple(ref.at[pl.ds(k, 2)] for ref in (src, room, dst)) for k in range(0, LEVELS, 2)]
        for a, b, c in trio:
            n = 2 * len(moves)
            moves.append((pltpu.make_async_copy(a, b, sems.at[n]), pltpu.make_async_copy(b, c, sems.at[n + 1])))
    for first, _ in moves:
        first.start()
    for first, second in moves:
        first.wait()
        second.start()
    for _, second in moves:
        second.wait()


def shards(tokens, up_weight, down_weight, block_mask, cotangent):
    hbm = pl.BlockSpec(memory_space=pl.ANY)
    vmem = pl.BlockSpec(memory_space=pltpu.VMEM)
    both = 2 * ROWS
    result = (
        jax.ShapeDtypeStruct((ROWS, G), BF16),
        jax.ShapeDtypeStruct((ROWS, G), BF16),
        jax.ShapeDtypeStruct((LEVELS, G, G), F32),
        jax.ShapeDtypeStruct((LEVELS, G, G), F32),
    )
    worked = pl.pallas_call(
        kernel,
        out_shape=result,
        in_specs=[hbm, hbm, hbm, hbm, pl.BlockSpec(memory_space=pltpu.SMEM)],
        out_specs=(vmem, vmem, hbm, hbm),
        scratch_shapes=[
            pltpu.VMEM((2, both, WIDE), BF16),
            pltpu.VMEM((2, LEVELS, G, G), BF16),
            pltpu.VMEM((WIDE, 2 * G), BF16),
            pltpu.VMEM((2 * G, WIDE), BF16),
            pltpu.VMEM((both, 2 * G), BF16),
            pltpu.VMEM((both, 2 * G), BF16),
            pltpu.VMEM((both, 2 * G), F32),
            pltpu.VMEM((2, 2, both, G), BF16),
            pltpu.VMEM((2, 2, both, G), BF16),
            pltpu.VMEM((2, 2, both, G), F32),
            pltpu.VMEM((2, 2, both, G), BF16),
            pltpu.VMEM((2, 2, both, G), BF16),
            pltpu.VMEM((2, both, G), F32),
            pltpu.VMEM((2, both, G), F32),
            pltpu.VMEM((2, ROWS, G), BF16),
            pltpu.VMEM((2, ROWS, G), BF16),
            pltpu.VMEM((2, both, G), BF16),
            pltpu.VMEM((2, both, G), BF16),
            pltpu.VMEM((2, LEVELS, G, G), F32),
            pltpu.VMEM((2, LEVELS, G, G), F32),
            pltpu.VMEM((2, LEVELS, G, G), F32),
            pltpu.SemaphoreType.DMA((COPIES,)),
            pltpu.SemaphoreType.DMA((COPIES,)),
            pltpu.SemaphoreType.DMA((4 + 2 * LEVELS,)),
        ],
        compiler_params=pltpu.CompilerParams(
            collective_id=0, has_side_effects=True, vmem_limit_bytes=58 * 1024 * 1024
        ),
    )(tokens, cotangent, up_weight[0], down_weight[0], block_mask)
    output, grad_tokens, grad_up, grad_down = pl.pallas_call(
        hand_out,
        out_shape=result,
        in_specs=[hbm] * 4,
        out_specs=(hbm,) * 4,
        scratch_shapes=[pltpu.VMEM(a.shape, a.dtype) for a in result] + [pltpu.SemaphoreType.DMA((16,))],
        compiler_params=pltpu.CompilerParams(vmem_limit_bytes=58 * 1024 * 1024),
    )(*worked)
    return output, grad_tokens, grad_up[None], grad_down[None]


def solution(mesh):
    placed = (
        P("seq", "tp"),
        P(("seq", "tp"), None, None, None),
        P(("seq", "tp"), None, None, None),
        P(("seq", "tp"), None),
        P("seq", "tp"),
    )
    return jax.shard_map(
        shards,
        mesh=mesh,
        in_specs=placed,
        out_specs=(
            P("seq", "tp"),
            P("seq", "tp"),
            P(("seq", "tp"), None, None, None),
            P(("seq", "tp"), None, None, None),
        ),
        check_vma=False,
    )
```

```python
import functools
import math

import jax
import jax.numpy as jnp
from jax import lax
from jax.experimental import pallas as pl
from jax.experimental.pallas import tpu as pltpu
from jax.sharding import PartitionSpec as P

MESH = pl.DeviceIdType.MESH
F32 = jnp.float32
BF16 = jnp.bfloat16
ROWS = 512
PART = 256
PIECES = ROWS // PART
G = 256
LEVELS = 6
WIDE = LEVELS * G
NEAR = {"x": 4, "y": 2}
FAR = {"x": 5, "y": 3}
SCALE = math.sqrt(2.0 / math.pi)
CUBE = 0.044715


def numbering():
    table, count = {}, 0
    for which in range(2):
        for name in ("z1", "z3", "zr"):
            table[name, which] = count
            count += PIECES
        for name in ("near", "far", "term", "sum"):
            for axis in "xy":
                for slot in range(2):
                    table[name, axis, which, slot] = count
                    count += PIECES
        for name in ("out1", "out3", "half"):
            table[name, which] = count
            count += PIECES
        table["weight", which] = count
        count += 1
        table["grad", which] = count
        count += LEVELS
    return table, count


NUMBER, COPIES = numbering()


def flip(index, bit):
    return index + bit - 2 * bit * lax.rem(lax.div(index, bit), 2)


def dot_nt(a, b):
    return lax.dot_general(a, b, (((1,), (1,)), ((), ())), preferred_element_type=F32)


def kernel(
    tok, cot, up, down, mask, out, gtok, gup, gdown,
    held, held_t, raw, uall, dall, act, act_t, gpre, slope,
    term_send, term_recv, near_term, sum_send, sum_recv, base, z_term,
    half_send, half_recv, z_send, z_recv,
    grad_own, grad_peer, grad_recv,
    sends, recvs, local,
):
    shared = (tok, cot)
    seq, tp = lax.axis_index("seq"), lax.axis_index("tp")
    place = {
        "core": (flip(seq, 1), tp),
        "z1": (seq, flip(tp, 1)),
        "z3": (flip(seq, 2), flip(tp, 1)),
        "x1": (seq, flip(tp, 8)),
        "x3": (seq, flip(flip(tp, 8), 16)),
        "y1": (seq, flip(tp, 2)),
        "y3": (seq, flip(flip(tp, 2), 4)),
    }

    def remote(src, dst, number, target):
        return pltpu.make_async_remote_copy(
            src_ref=src,
            dst_ref=dst,
            send_sem=sends.at[number],
            recv_sem=recvs.at[number],
            device_id=place[target],
            device_id_type=MESH,
        )

    def rows(slot, j):
        start = slot * ROWS + j * PART
        return pl.ds(start if isinstance(j, int) else pl.multiple_of(start, PART), PART)

    def piece(j):
        return pl.ds(j * PART, PART)

    def columns(level):
        return pl.ds(level * G, G)

    def z1(which, j):
        return remote(shared[which].at[piece(j)], held.at[which, rows(0, j), columns(1)], NUMBER["z1", which] + j, "z1")

    def z3(which, j):
        return remote(shared[which].at[piece(j)], held.at[which, rows(1, j), columns(1)], NUMBER["z3", which] + j, "z3")

    def zr(which, j):
        return remote(
            held.at[which, rows(j, j), columns(1)],
            held.at[which, rows(1, j), columns(0)],
            NUMBER["zr", which] + j,
            "z3" if j == 0 else "z1",
        )

    def near(axis, which, slot, j):
        src = shared[which].at[piece(j)] if slot == 0 else held.at[which, rows(1, j), columns(0)]
        return remote(src, held.at[which, rows(slot, j), columns(NEAR[axis])], NUMBER["near", axis, which, slot] + j, axis + "1")

    def far(axis, which, slot, j):
        return remote(
            held.at[which, rows(slot, j), columns(NEAR[axis])],
            held.at[which, rows(slot, j), columns(FAR[axis])],
            NUMBER["far", axis, which, slot] + j,
            axis + "3",
        )

    def term(axis, which, slot, j):
        a = "xy".index(axis)
        return remote(
            term_send.at[which, a, rows(slot, j)],
            term_recv.at[which, a, rows(slot, j)],
            NUMBER["term", axis, which, slot] + j,
            axis + "3",
        )

    def summed(axis, which, slot, j):
        a = "xy".index(axis)
        return remote(
            sum_send.at[which, a, rows(slot, j)],
            sum_recv.at[which, a, rows(slot, j)],
            NUMBER["sum", axis, which, slot] + j,
            axis + "1",
        )

    def half(which, j):
        return remote(half_send.at[which, piece(j)], half_recv.at[which, piece(j)], NUMBER["half", which] + j, "z3" if j == 0 else "z1")

    def out1(which, j):
        return remote(z_send.at[which, rows(0, j)], z_recv.at[which, rows(0, j)], NUMBER["out1", which] + j, "z1")

    def out3(which, j):
        return remote(z_send.at[which, rows(1, j)], z_recv.at[which, rows(1, j)], NUMBER["out3", which] + j, "z3")

    def weight(which):
        if which == 0:
            return remote(uall.at[:, pl.ds(0, G)], uall.at[:, pl.ds(G, G)], NUMBER["weight", 0], "core")
        return remote(dall.at[pl.ds(0, G)], dall.at[pl.ds(G, G)], NUMBER["weight", 1], "core")

    def grad(which, level):
        return remote(grad_peer.at[which, level], grad_recv.at[which, level], NUMBER["grad", which] + level, "core")

    own = [
        pltpu.make_async_copy(shared[which], held.at[which, pl.ds(0, ROWS), columns(0)], local.at[which])
        for which in range(2)
    ]
    loads = [pltpu.make_async_copy(ref, raw.at[which], local.at[2 + which]) for which, ref in enumerate((up, down))]
    for copy in loads + own:
        copy.start()

    barrier = pltpu.get_barrier_semaphore()
    for target in place.values():
        pl.semaphore_signal(barrier, inc=1, device_id=target, device_id_type=MESH)
    pl.semaphore_wait(barrier, len(place))

    def own_z(which, j):
        z1(which, j).start()
        z3(which, j).start()

    def own_xy(which, j):
        near("x", which, 0, j).start()
        near("y", which, 0, j).start()

    def relay_z(which, j):
        (z1 if j == 0 else z3)(which, j).wait_recv()
        zr(which, j).start()

    def relay_xy(which, slot, j):
        for axis in "xy":
            near(axis, which, slot, j).wait_recv()
            far(axis, which, slot, j).start()

    def other(which, j):
        zr(which, j).wait_recv()
        near("x", which, 1, j).start()
        near("y", which, 1, j).start()

    def arrived(which, slot):
        (z1 if slot == 0 else z3)(which, 1 - slot).wait_recv()
        for j in range(PIECES):
            for axis in "xy":
                far(axis, which, slot, j).wait_recv()

    def scale_up(k, carry):
        factor = mask[0, k].astype(F32)
        uall[pl.ds(pl.multiple_of(k * G, G), G), pl.ds(0, G)] = (raw[0, k].astype(F32) * factor).astype(BF16)
        return carry

    def scale_down(k, carry):
        factor = mask[0, k].astype(F32)
        dall[pl.ds(0, G), pl.ds(pl.multiple_of(k * G, G), G)] = (raw[1, k].astype(F32) * factor).astype(BF16)
        return carry

    def forward(slot, j):
        at = rows(slot, j)
        pre = jnp.dot(held[0, at, :], uall[...], preferred_element_type=F32)
        square = pre * pre
        tanh = jnp.tanh(SCALE * pre * (1.0 + CUBE * square))
        cdf = 0.5 + 0.5 * tanh
        act[at, :] = (pre * cdf).astype(BF16)
        slope[at, :] = cdf + (0.5 * SCALE) * pre * (1.0 - tanh * tanh) * (1.0 + (3.0 * CUBE) * square)

    def backward(slot, j):
        at = rows(slot, j)
        gact = dot_nt(held[1, at, :], dall[...])
        gpre[at, :] = (gact * slope[at, :]).astype(BF16)

    def turn_act(slot, j):
        act_t[:, rows(slot, j)] = act[rows(slot, j), :].T

    def turn_held(slot):
        def body(k, carry):
            at = pl.ds(pl.multiple_of(k * G, G), G)
            held_t[at, pl.ds(slot * ROWS, ROWS)] = held[0, pl.ds(slot * ROWS, ROWS), at].T
            return carry

        lax.fori_loop(0, LEVELS, body, 0)

    def by_down(slot, j, level):
        return jnp.dot(act[rows(slot, j), :], dall[:, columns(level)], preferred_element_type=F32)

    def by_up(slot, j, level):
        return dot_nt(gpre[rows(slot, j), :], uall[columns(level), :])

    def terms(which, slot, j, send):
        at = rows(slot, j)
        product = by_up if which else by_down
        for a, axis in enumerate("xy"):
            term_send[which, a, at] = product(slot, j, FAR[axis]).astype(BF16)
            if send:
                term(axis, which, slot, j).start()
        for a, axis in enumerate("xy"):
            near_term[which, a, at] = product(slot, j, NEAR[axis])
        z_term[which, at] = product(slot, j, 1)
        base[which, at] = product(slot, j, 0)

    def send_terms(which, slot):
        for j in range(PIECES):
            for axis in "xy":
                term(axis, which, slot, j).start()

    def tiles(which, slot):
        def body(j, carry):
            (backward if which else forward)(slot, j)
            terms(which, slot, j, True)
            if which == 0:
                turn_act(slot, j)
            return carry

        lax.fori_loop(0, PIECES, body, 0)
        plain(which, slot)

    def plain(which, slot):
        at = rows(slot, 1 - slot)
        z_send[which, at] = z_term[which, at].astype(BF16)
        (out1 if slot == 0 else out3)(which, 1 - slot).start()

    def join(which, slot):
        for j in range(PIECES):
            for a, axis in enumerate("xy"):
                at = rows(slot, j)
                term(axis, which, slot, j).wait_recv()
                sum_send[which, a, at] = (near_term[which, a, at] + term_recv[which, a, at].astype(F32)).astype(BF16)
                summed(axis, which, slot, j).start()

    def collect(which, slot):
        for j in range(PIECES):
            at = rows(slot, j)
            for axis in "xy":
                summed(axis, which, slot, j).wait_recv()
            total = base[which, at] + sum_recv[which, 0, at].astype(F32) + sum_recv[which, 1, at].astype(F32)
            if slot == 0:
                base[which, at] = total
            else:
                half_send[which, piece(j)] = total.astype(BF16)
                half(which, j).start()

    def pass_on(which):
        for j in range(PIECES):
            at = rows(j, j)
            half(which, j).wait_recv()
            z_send[which, at] = (z_term[which, at] + half_recv[which, piece(j)].astype(F32)).astype(BF16)
            (out1 if j == 0 else out3)(which, j).start()

    def finish(which, result):
        for j in range(PIECES):
            out1(which, j).wait_recv()
            out3(which, j).wait_recv()
            total = base[which, rows(0, j)] + z_recv[which, rows(0, j)].astype(F32) + z_recv[which, rows(1, j)].astype(F32)
            result[piece(j), :] = total.astype(BF16)

    def grads_down(first, last):
        def body(k, carry):
            at = pl.ds(pl.multiple_of(k * G, G), G)
            both = jnp.dot(act_t[...], held[1, :, at], preferred_element_type=F32)
            grad_own[1, k] = both[:G]
            grad_peer[1, k] = both[G:]
            grad(1, k).start()
            return carry

        lax.fori_loop(first, last, body, 0)

    def grads_up(first, last):
        def body(k, carry):
            at = pl.ds(pl.multiple_of(k * G, G), G)
            both = jnp.dot(held_t[at, :], gpre[...], preferred_element_type=F32)
            grad_own[0, k] = both[:, :G]
            grad_peer[0, k] = both[:, G:]
            grad(0, k).start()
            return carry

        lax.fori_loop(first, last, body, 0)

    def grads_sum(which, result):
        def body(k, carry):
            grad(which, k).wait_recv()
            factor = mask[0, k].astype(F32)
            grad_own[which, k] = (grad_own[which, k] + grad_recv[which, k]) * factor
            pltpu.make_async_copy(grad_own.at[which, k], result.at[k], local.at[4 + which * LEVELS + k]).start()
            return carry

        lax.fori_loop(0, LEVELS, body, 0)

    for j in range(PIECES):
        own_z(0, j)
        own_xy(0, j)
    loads[0].wait()
    lax.fori_loop(0, LEVELS, scale_up, 0)
    weight(0).start()
    loads[1].wait()
    lax.fori_loop(0, LEVELS, scale_down, 0)
    weight(1).start()
    for copy in own:
        copy.wait()

    for j in range(PIECES):
        relay_xy(0, 0, j)
        own_xy(1, j)
        relay_z(0, j)
        own_z(1, j)
    for j in range(PIECES):
        relay_xy(1, 0, j)
        other(0, j)
    for j in range(PIECES):
        relay_z(1, j)
    weight(0).wait_recv()
    weight(1).wait_recv()
    arrived(0, 0)
    forward(0, 0)
    terms(0, 0, 0, False)
    turn_act(0, 0)
    for j in range(PIECES):
        relay_xy(0, 1, j)
        other(1, j)
    forward(0, 1)
    terms(0, 0, 1, False)
    plain(0, 0)
    turn_act(0, 1)
    for j in range(PIECES):
        relay_xy(1, 1, j)
    turn_held(0)

    arrived(0, 1)
    tiles(0, 1)
    arrived(1, 1)
    tiles(1, 1)
    send_terms(0, 0)
    join(0, 1)
    arrived(1, 0)
    tiles(1, 0)
    turn_held(1)
    grads_down(0, LEVELS // 2)
    join(1, 1)
    collect(0, 1)
    grads_down(LEVELS // 2, LEVELS)
    join(0, 0)
    collect(1, 1)
    pass_on(0)
    grads_up(0, LEVELS)
    join(1, 0)
    pass_on(1)
    collect(0, 0)
    grads_sum(1, gdown)
    finish(0, out)
    grads_sum(0, gup)
    collect(1, 0)
    finish(1, gtok)

    for which, result in enumerate((gup, gdown)):
        for k in range(LEVELS):
            pltpu.make_async_copy(grad_own.at[which, k], result.at[k], local.at[4 + which * LEVELS + k]).wait()
    for which in range(2):
        weight(which).wait_send()
        for k in range(LEVELS):
            grad(which, k).wait_send()
        for j in range(PIECES):
            for make in (z1, z3, zr, half, out1, out3):
                make(which, j).wait_send()
            for slot in range(2):
                for axis in "xy":
                    for make in (near, far, term, summed):
                        make(axis, which, slot, j).wait_send()


def hand_out(*refs):
    sources, results, sems = refs[:4], refs[4:8], refs[8]
    copies = []
    for src, dst in zip(sources, results):
        if len(src.shape) == 2:
            pairs = [(src, dst)]
        else:
            pairs = [(src.at[pl.ds(k, 2)], dst.at[pl.ds(k, 2)]) for k in range(0, LEVELS, 2)]
        for a, b in pairs:
            copies.append(pltpu.make_async_copy(a, b, sems.at[len(copies)]))
    for copy in copies:
        copy.start()
    for copy in copies:
        copy.wait()


def shards(tokens, up_weight, down_weight, block_mask, cotangent):
    anywhere = pl.BlockSpec(memory_space=pl.ANY)
    vmem = pl.BlockSpec(memory_space=pltpu.VMEM)
    both = 2 * ROWS
    result = (
        jax.ShapeDtypeStruct((ROWS, G), BF16),
        jax.ShapeDtypeStruct((ROWS, G), BF16),
        jax.ShapeDtypeStruct((LEVELS, G, G), F32),
        jax.ShapeDtypeStruct((LEVELS, G, G), F32),
    )
    operands = [pltpu.with_memory_space_constraint(a, pltpu.HBM) for a in (tokens, cotangent, up_weight[0], down_weight[0])]
    worked = pl.pallas_call(
        kernel,
        out_shape=tuple(pltpu.VMEM(a.shape, a.dtype) for a in result),
        in_specs=[anywhere, anywhere, anywhere, anywhere, pl.BlockSpec(memory_space=pltpu.SMEM)],
        out_specs=(vmem, vmem, anywhere, anywhere),
        scratch_shapes=[
            pltpu.VMEM((2, both, WIDE), BF16),
            pltpu.VMEM((WIDE, both), BF16),
            pltpu.VMEM((2, LEVELS, G, G), BF16),
            pltpu.VMEM((WIDE, 2 * G), BF16),
            pltpu.VMEM((2 * G, WIDE), BF16),
            pltpu.VMEM((both, 2 * G), BF16),
            pltpu.VMEM((2 * G, both), BF16),
            pltpu.VMEM((both, 2 * G), BF16),
            pltpu.VMEM((both, 2 * G), F32),
            pltpu.VMEM((2, 2, both, G), BF16),
            pltpu.VMEM((2, 2, both, G), BF16),
            pltpu.VMEM((2, 2, both, G), F32),
            pltpu.VMEM((2, 2, both, G), BF16),
            pltpu.VMEM((2, 2, both, G), BF16),
            pltpu.VMEM((2, both, G), F32),
            pltpu.VMEM((2, both, G), F32),
            pltpu.VMEM((2, ROWS, G), BF16),
            pltpu.VMEM((2, ROWS, G), BF16),
            pltpu.VMEM((2, both, G), BF16),
            pltpu.VMEM((2, both, G), BF16),
            pltpu.VMEM((2, LEVELS, G, G), F32),
            pltpu.VMEM((2, LEVELS, G, G), F32),
            pltpu.VMEM((2, LEVELS, G, G), F32),
            pltpu.SemaphoreType.DMA((COPIES,)),
            pltpu.SemaphoreType.DMA((COPIES,)),
            pltpu.SemaphoreType.DMA((4 + 2 * LEVELS,)),
        ],
        compiler_params=pltpu.CompilerParams(
            collective_id=0, has_side_effects=True, vmem_limit_bytes=58 * 1024 * 1024
        ),
    )(*operands, block_mask)
    worked = [pltpu.with_memory_space_constraint(a, pltpu.VMEM) for a in worked]
    output, grad_tokens, grad_up, grad_down = pl.pallas_call(
        hand_out,
        out_shape=result,
        in_specs=[anywhere] * 4,
        out_specs=(anywhere,) * 4,
        scratch_shapes=[pltpu.SemaphoreType.DMA((8,))],
        compiler_params=pltpu.CompilerParams(vmem_limit_bytes=1024 * 1024),
    )(*worked)
    return output, grad_tokens, grad_up[None], grad_down[None]


def solution(mesh):
    placed = (
        P("seq", "tp"),
        P(("seq", "tp"), None, None, None),
        P(("seq", "tp"), None, None, None),
        P(("seq", "tp"), None),
        P("seq", "tp"),
    )
    return jax.shard_map(
        shards,
        mesh=mesh,
        in_specs=placed,
        out_specs=(
            P("seq", "tp"),
            P("seq", "tp"),
            P(("seq", "tp"), None, None, None),
            P(("seq", "tp"), None, None, None),
        ),
        check_vma=False,
    )
```

```python
import functools
import math

import jax
import jax.numpy as jnp
from jax import lax
from jax.experimental import pallas as pl
from jax.experimental.pallas import tpu as pltpu
from jax.sharding import PartitionSpec as P

MESH = pl.DeviceIdType.MESH
F32 = jnp.float32
BF16 = jnp.bfloat16
ROWS = 512
PART = 256
PIECES = ROWS // PART
G = 256
LEVELS = 6
WIDE = LEVELS * G
NEAR = {"x": 4, "y": 2}
FAR = {"x": 5, "y": 3}
SCALE = math.sqrt(2.0 / math.pi)
CUBE = 0.044715


def numbering():
    table, count = {}, 0
    for which in range(2):
        for name in ("z1", "z3", "zr"):
            table[name, which] = count
            count += PIECES
        for name in ("near", "far", "term", "sum"):
            for axis in "xy":
                for slot in range(2):
                    table[name, axis, which, slot] = count
                    count += PIECES
        for name in ("out1", "out3", "half"):
            table[name, which] = count
            count += PIECES
        table["weight", which] = count
        count += 1
        table["grad", which] = count
        count += LEVELS
    return table, count


NUMBER, COPIES = numbering()


def flip(index, bit):
    return index + bit - 2 * bit * lax.rem(lax.div(index, bit), 2)


def kernel(
    tok, cot, up, down, mask, out, gtok, gup, gdown,
    held, held_t, raw, uall, dall, uall_t, dall_t, act, act_t, gpre, slope,
    term_send, term_recv, near_term, sum_send, sum_recv, base, z_term,
    half_send, half_recv, z_send, z_recv,
    grad_own, grad_peer, grad_recv,
    sends, recvs, local,
):
    shared = (tok, cot)
    seq, tp = lax.axis_index("seq"), lax.axis_index("tp")
    place = {
        "core": (flip(seq, 1), tp),
        "z1": (seq, flip(tp, 1)),
        "z3": (flip(seq, 2), flip(tp, 1)),
        "x1": (seq, flip(tp, 8)),
        "x3": (seq, flip(flip(tp, 8), 16)),
        "y1": (seq, flip(tp, 2)),
        "y3": (seq, flip(flip(tp, 2), 4)),
    }

    def remote(src, dst, number, target):
        return pltpu.make_async_remote_copy(
            src_ref=src,
            dst_ref=dst,
            send_sem=sends.at[number],
            recv_sem=recvs.at[number],
            device_id=place[target],
            device_id_type=MESH,
        )

    def rows(slot, j):
        start = slot * ROWS + j * PART
        return pl.ds(start if isinstance(j, int) else pl.multiple_of(start, PART), PART)

    def piece(j):
        return pl.ds(j * PART, PART)

    def columns(level):
        return pl.ds(level * G, G)

    def z1(which, j):
        return remote(shared[which].at[piece(j)], held.at[which, rows(0, j), columns(1)], NUMBER["z1", which] + j, "z1")

    def z3(which, j):
        return remote(shared[which].at[piece(j)], held.at[which, rows(1, j), columns(1)], NUMBER["z3", which] + j, "z3")

    def zr(which, j):
        return remote(
            held.at[which, rows(j, j), columns(1)],
            held.at[which, rows(1, j), columns(0)],
            NUMBER["zr", which] + j,
            "z3" if j == 0 else "z1",
        )

    def near(axis, which, slot, j):
        src = shared[which].at[piece(j)] if slot == 0 else held.at[which, rows(1, j), columns(0)]
        return remote(src, held.at[which, rows(slot, j), columns(NEAR[axis])], NUMBER["near", axis, which, slot] + j, axis + "1")

    def far(axis, which, slot, j):
        return remote(
            held.at[which, rows(slot, j), columns(NEAR[axis])],
            held.at[which, rows(slot, j), columns(FAR[axis])],
            NUMBER["far", axis, which, slot] + j,
            axis + "3",
        )

    def term(axis, which, slot, j):
        a = "xy".index(axis)
        return remote(
            term_send.at[which, a, rows(slot, j)],
            term_recv.at[which, a, rows(slot, j)],
            NUMBER["term", axis, which, slot] + j,
            axis + "3",
        )

    def summed(axis, which, slot, j):
        a = "xy".index(axis)
        return remote(
            sum_send.at[which, a, rows(slot, j)],
            sum_recv.at[which, a, rows(slot, j)],
            NUMBER["sum", axis, which, slot] + j,
            axis + "1",
        )

    def half(which, j):
        return remote(half_send.at[which, piece(j)], half_recv.at[which, piece(j)], NUMBER["half", which] + j, "z3" if j == 0 else "z1")

    def out1(which, j):
        return remote(z_send.at[which, rows(0, j)], z_recv.at[which, rows(0, j)], NUMBER["out1", which] + j, "z1")

    def out3(which, j):
        return remote(z_send.at[which, rows(1, j)], z_recv.at[which, rows(1, j)], NUMBER["out3", which] + j, "z3")

    def weight(which):
        if which == 0:
            return remote(uall.at[:, pl.ds(0, G)], uall.at[:, pl.ds(G, G)], NUMBER["weight", 0], "core")
        return remote(dall.at[pl.ds(0, G)], dall.at[pl.ds(G, G)], NUMBER["weight", 1], "core")

    def grad(which, level):
        return remote(grad_peer.at[which, level], grad_recv.at[which, level], NUMBER["grad", which] + level, "core")

    own = [
        pltpu.make_async_copy(shared[which], held.at[which, pl.ds(0, ROWS), columns(0)], local.at[which])
        for which in range(2)
    ]
    loads = [pltpu.make_async_copy(ref, raw.at[which], local.at[2 + which]) for which, ref in enumerate((up, down))]
    for copy in loads + own:
        copy.start()

    barrier = pltpu.get_barrier_semaphore()
    for target in place.values():
        pl.semaphore_signal(barrier, inc=1, device_id=target, device_id_type=MESH)
    pl.semaphore_wait(barrier, len(place))

    def own_z(which, j):
        z1(which, j).start()
        z3(which, j).start()

    def own_xy(which, j):
        near("x", which, 0, j).start()
        near("y", which, 0, j).start()

    def relay_z(which, j):
        (z1 if j == 0 else z3)(which, j).wait_recv()
        zr(which, j).start()

    def relay_xy(which, slot, j):
        for axis in "xy":
            near(axis, which, slot, j).wait_recv()
            far(axis, which, slot, j).start()

    def other(which, j):
        zr(which, j).wait_recv()
        near("x", which, 1, j).start()
        near("y", which, 1, j).start()

    def arrived(which, slot):
        (z1 if slot == 0 else z3)(which, 1 - slot).wait_recv()
        for j in range(PIECES):
            for axis in "xy":
                far(axis, which, slot, j).wait_recv()

    def scale_up(k, carry):
        factor = mask[0, k].astype(F32)
        uall[pl.ds(pl.multiple_of(k * G, G), G), pl.ds(0, G)] = (raw[0, k].astype(F32) * factor).astype(BF16)
        return carry

    def scale_down(k, carry):
        factor = mask[0, k].astype(F32)
        dall[pl.ds(0, G), pl.ds(pl.multiple_of(k * G, G), G)] = (raw[1, k].astype(F32) * factor).astype(BF16)
        return carry

    def forward(slot, j):
        at = rows(slot, j)
        pre = jnp.dot(held[0, at, :], uall[...], preferred_element_type=F32)
        square = pre * pre
        tanh = jnp.tanh(SCALE * pre * (1.0 + CUBE * square))
        cdf = 0.5 + 0.5 * tanh
        act[at, :] = (pre * cdf).astype(BF16)
        slope[at, :] = cdf + (0.5 * SCALE) * pre * (1.0 - tanh * tanh) * (1.0 + (3.0 * CUBE) * square)

    def backward(slot, j):
        at = rows(slot, j)
        gact = jnp.dot(held[1, at, :], dall_t[...], preferred_element_type=F32)
        gpre[at, :] = (gact * slope[at, :]).astype(BF16)

    def turn_act(slot, j):
        act_t[:, rows(slot, j)] = act[rows(slot, j), :].T

    def turn_weights():
        def body(k, carry):
            at = pl.ds(pl.multiple_of(k * G, G), G)
            dall_t[at, :] = dall[:, at].T
            uall_t[:, at] = uall[at, :].T
            return carry

        lax.fori_loop(0, LEVELS, body, 0)

    def turn_held(slot):
        def body(k, carry):
            at = pl.ds(pl.multiple_of(k * G, G), G)
            held_t[at, pl.ds(slot * ROWS, ROWS)] = held[0, pl.ds(slot * ROWS, ROWS), at].T
            return carry

        lax.fori_loop(0, LEVELS, body, 0)

    def by_down(slot, j, level):
        return jnp.dot(act[rows(slot, j), :], dall[:, columns(level)], preferred_element_type=F32)

    def by_up(slot, j, level):
        return jnp.dot(gpre[rows(slot, j), :], uall_t[:, columns(level)], preferred_element_type=F32)

    def terms(which, slot, j, send):
        at = rows(slot, j)
        product = by_up if which else by_down
        for a, axis in enumerate("xy"):
            term_send[which, a, at] = product(slot, j, FAR[axis]).astype(BF16)
            if send:
                term(axis, which, slot, j).start()
        for a, axis in enumerate("xy"):
            near_term[which, a, at] = product(slot, j, NEAR[axis])
        z_term[which, at] = product(slot, j, 1)
        base[which, at] = product(slot, j, 0)

    def send_terms(which, slot):
        for j in range(PIECES):
            for axis in "xy":
                term(axis, which, slot, j).start()

    def tiles(which, slot):
        def body(j, carry):
            (backward if which else forward)(slot, j)
            terms(which, slot, j, True)
            if which == 0:
                turn_act(slot, j)
            return carry

        lax.fori_loop(0, PIECES, body, 0)
        plain(which, slot)

    def plain(which, slot):
        at = rows(slot, 1 - slot)
        z_send[which, at] = z_term[which, at].astype(BF16)
        (out1 if slot == 0 else out3)(which, 1 - slot).start()

    def join(which, slot):
        for j in range(PIECES):
            for a, axis in enumerate("xy"):
                at = rows(slot, j)
                term(axis, which, slot, j).wait_recv()
                sum_send[which, a, at] = (near_term[which, a, at] + term_recv[which, a, at].astype(F32)).astype(BF16)
                summed(axis, which, slot, j).start()

    def collect(which, slot):
        for j in range(PIECES):
            at = rows(slot, j)
            for axis in "xy":
                summed(axis, which, slot, j).wait_recv()
            total = base[which, at] + sum_recv[which, 0, at].astype(F32) + sum_recv[which, 1, at].astype(F32)
            if slot == 0:
                base[which, at] = total
            else:
                half_send[which, piece(j)] = total.astype(BF16)
                half(which, j).start()

    def pass_on(which):
        for j in range(PIECES):
            at = rows(j, j)
            half(which, j).wait_recv()
            z_send[which, at] = (z_term[which, at] + half_recv[which, piece(j)].astype(F32)).astype(BF16)
            (out1 if j == 0 else out3)(which, j).start()

    def finish(which, result):
        for j in range(PIECES):
            out1(which, j).wait_recv()
            out3(which, j).wait_recv()
            total = base[which, rows(0, j)] + z_recv[which, rows(0, j)].astype(F32) + z_recv[which, rows(1, j)].astype(F32)
            result[piece(j), :] = total.astype(BF16)

    def grads_down(first, last):
        def body(k, carry):
            at = pl.ds(pl.multiple_of(k * G, G), G)
            both = jnp.dot(act_t[...], held[1, :, at], preferred_element_type=F32)
            grad_own[1, k] = both[:G]
            grad_peer[1, k] = both[G:]
            grad(1, k).start()
            return carry

        lax.fori_loop(first, last, body, 0)

    def grads_up(first, last):
        def body(k, carry):
            at = pl.ds(pl.multiple_of(k * G, G), G)
            both = jnp.dot(held_t[at, :], gpre[...], preferred_element_type=F32)
            grad_own[0, k] = both[:, :G]
            grad_peer[0, k] = both[:, G:]
            grad(0, k).start()
            return carry

        lax.fori_loop(first, last, body, 0)

    def grads_sum(which, result):
        def body(k, carry):
            grad(which, k).wait_recv()
            factor = mask[0, k].astype(F32)
            grad_own[which, k] = (grad_own[which, k] + grad_recv[which, k]) * factor
            pltpu.make_async_copy(grad_own.at[which, k], result.at[k], local.at[4 + which * LEVELS + k]).start()
            return carry

        lax.fori_loop(0, LEVELS, body, 0)

    for j in range(PIECES):
        own_z(0, j)
        own_xy(0, j)
    loads[0].wait()
    lax.fori_loop(0, LEVELS, scale_up, 0)
    weight(0).start()
    loads[1].wait()
    lax.fori_loop(0, LEVELS, scale_down, 0)
    weight(1).start()
    for copy in own:
        copy.wait()

    for j in range(PIECES):
        relay_xy(0, 0, j)
        own_xy(1, j)
        relay_z(0, j)
        own_z(1, j)
    for j in range(PIECES):
        relay_xy(1, 0, j)
        other(0, j)
    for j in range(PIECES):
        relay_z(1, j)
    weight(0).wait_recv()
    weight(1).wait_recv()
    arrived(0, 0)
    forward(0, 0)
    terms(0, 0, 0, False)
    turn_act(0, 0)
    for j in range(PIECES):
        relay_xy(0, 1, j)
        other(1, j)
    forward(0, 1)
    terms(0, 0, 1, False)
    plain(0, 0)
    turn_act(0, 1)
    for j in range(PIECES):
        relay_xy(1, 1, j)
    turn_weights()
    turn_held(0)

    arrived(0, 1)
    tiles(0, 1)
    arrived(1, 1)
    tiles(1, 1)
    send_terms(0, 0)
    join(0, 1)
    arrived(1, 0)
    tiles(1, 0)
    turn_held(1)
    grads_down(0, LEVELS // 2)
    join(1, 1)
    collect(0, 1)
    grads_down(LEVELS // 2, LEVELS)
    join(0, 0)
    collect(1, 1)
    pass_on(0)
    grads_up(0, LEVELS)
    join(1, 0)
    pass_on(1)
    collect(0, 0)
    grads_sum(1, gdown)
    finish(0, out)
    grads_sum(0, gup)
    collect(1, 0)
    finish(1, gtok)

    for which, result in enumerate((gup, gdown)):
        for k in range(LEVELS):
            pltpu.make_async_copy(grad_own.at[which, k], result.at[k], local.at[4 + which * LEVELS + k]).wait()
    for which in range(2):
        weight(which).wait_send()
        for k in range(LEVELS):
            grad(which, k).wait_send()
        for j in range(PIECES):
            for make in (z1, z3, zr, half, out1, out3):
                make(which, j).wait_send()
            for slot in range(2):
                for axis in "xy":
                    for make in (near, far, term, summed):
                        make(axis, which, slot, j).wait_send()


def hand_out(*refs):
    sources, results, sems = refs[:4], refs[4:8], refs[8]
    copies = []
    for src, dst in zip(sources, results):
        if len(src.shape) == 2:
            pairs = [(src, dst)]
        else:
            pairs = [(src.at[pl.ds(k, 2)], dst.at[pl.ds(k, 2)]) for k in range(0, LEVELS, 2)]
        for a, b in pairs:
            copies.append(pltpu.make_async_copy(a, b, sems.at[len(copies)]))
    for copy in copies:
        copy.start()
    for copy in copies:
        copy.wait()


def shards(tokens, up_weight, down_weight, block_mask, cotangent):
    anywhere = pl.BlockSpec(memory_space=pl.ANY)
    vmem = pl.BlockSpec(memory_space=pltpu.VMEM)
    both = 2 * ROWS
    result = (
        jax.ShapeDtypeStruct((ROWS, G), BF16),
        jax.ShapeDtypeStruct((ROWS, G), BF16),
        jax.ShapeDtypeStruct((LEVELS, G, G), F32),
        jax.ShapeDtypeStruct((LEVELS, G, G), F32),
    )
    operands = [pltpu.with_memory_space_constraint(a, pltpu.HBM) for a in (tokens, cotangent, up_weight[0], down_weight[0])]
    worked = pl.pallas_call(
        kernel,
        out_shape=tuple(pltpu.VMEM(a.shape, a.dtype) for a in result),
        in_specs=[anywhere, anywhere, anywhere, anywhere, pl.BlockSpec(memory_space=pltpu.SMEM)],
        out_specs=(vmem, vmem, anywhere, anywhere),
        scratch_shapes=[
            pltpu.VMEM((2, both, WIDE), BF16),
            pltpu.VMEM((WIDE, both), BF16),
            pltpu.VMEM((2, LEVELS, G, G), BF16),
            pltpu.VMEM((WIDE, 2 * G), BF16),
            pltpu.VMEM((2 * G, WIDE), BF16),
            pltpu.VMEM((2 * G, WIDE), BF16),
            pltpu.VMEM((WIDE, 2 * G), BF16),
            pltpu.VMEM((both, 2 * G), BF16),
            pltpu.VMEM((2 * G, both), BF16),
            pltpu.VMEM((both, 2 * G), BF16),
            pltpu.VMEM((both, 2 * G), F32),
            pltpu.VMEM((2, 2, both, G), BF16),
            pltpu.VMEM((2, 2, both, G), BF16),
            pltpu.VMEM((2, 2, both, G), F32),
            pltpu.VMEM((2, 2, both, G), BF16),
            pltpu.VMEM((2, 2, both, G), BF16),
            pltpu.VMEM((2, both, G), F32),
            pltpu.VMEM((2, both, G), F32),
            pltpu.VMEM((2, ROWS, G), BF16),
            pltpu.VMEM((2, ROWS, G), BF16),
            pltpu.VMEM((2, both, G), BF16),
            pltpu.VMEM((2, both, G), BF16),
            pltpu.VMEM((2, LEVELS, G, G), F32),
            pltpu.VMEM((2, LEVELS, G, G), F32),
            pltpu.VMEM((2, LEVELS, G, G), F32),
            pltpu.SemaphoreType.DMA((COPIES,)),
            pltpu.SemaphoreType.DMA((COPIES,)),
            pltpu.SemaphoreType.DMA((4 + 2 * LEVELS,)),
        ],
        compiler_params=pltpu.CompilerParams(
            collective_id=0, has_side_effects=True, vmem_limit_bytes=58 * 1024 * 1024
        ),
    )(*operands, block_mask)
    worked = [pltpu.with_memory_space_constraint(a, pltpu.VMEM) for a in worked]
    output, grad_tokens, grad_up, grad_down = pl.pallas_call(
        hand_out,
        out_shape=result,
        in_specs=[anywhere] * 4,
        out_specs=(anywhere,) * 4,
        scratch_shapes=[pltpu.SemaphoreType.DMA((8,))],
        compiler_params=pltpu.CompilerParams(vmem_limit_bytes=1024 * 1024),
    )(*worked)
    return output, grad_tokens, grad_up[None], grad_down[None]


def solution(mesh):
    placed = (
        P("seq", "tp"),
        P(("seq", "tp"), None, None, None),
        P(("seq", "tp"), None, None, None),
        P(("seq", "tp"), None),
        P("seq", "tp"),
    )
    return jax.shard_map(
        shards,
        mesh=mesh,
        in_specs=placed,
        out_specs=(
            P("seq", "tp"),
            P("seq", "tp"),
            P(("seq", "tp"), None, None, None),
            P(("seq", "tp"), None, None, None),
        ),
        check_vma=False,
    )
```

```python
import functools
import math

import jax
import jax.numpy as jnp
from jax import lax
from jax.experimental import pallas as pl
from jax.experimental.pallas import tpu as pltpu
from jax.sharding import PartitionSpec as P

MESH = pl.DeviceIdType.MESH
F32 = jnp.float32
BF16 = jnp.bfloat16
ROWS = 512
PART = 256
PIECES = ROWS // PART
G = 256
LEVELS = 6
WIDE = LEVELS * G
NEAR = {"x": 4, "y": 2}
FAR = {"x": 5, "y": 3}
SCALE = math.sqrt(2.0 / math.pi)
CUBE = 0.044715


def numbering():
    table, count = {}, 0
    for which in range(2):
        for name in ("z1", "z3", "zr"):
            table[name, which] = count
            count += PIECES
        for name in ("near", "far", "term", "sum"):
            for axis in "xy":
                for slot in range(2):
                    table[name, axis, which, slot] = count
                    count += PIECES
        for name in ("out1", "out3", "half"):
            table[name, which] = count
            count += PIECES
        table["weight", which] = count
        count += 1
        table["grad", which] = count
        count += LEVELS
    return table, count


NUMBER, COPIES = numbering()


def flip(index, bit):
    return index + bit - 2 * bit * lax.rem(lax.div(index, bit), 2)


def kernel(
    tok, cot, up, down, mask, out, gtok, gup, gdown,
    held, held_t, raw, uall, dall, uall_t, dall_t, act, act_t, gpre, slope,
    term_send, term_recv, near_term, sum_send, sum_recv, base, z_term,
    half_send, half_recv, z_send, z_recv,
    grad_own, grad_peer, grad_recv,
    sends, recvs, local,
):
    shared = (tok, cot)
    seq, tp = lax.axis_index("seq"), lax.axis_index("tp")
    place = {
        "core": (flip(seq, 1), tp),
        "z1": (seq, flip(tp, 1)),
        "z3": (flip(seq, 2), flip(tp, 1)),
        "x1": (seq, flip(tp, 8)),
        "x3": (seq, flip(flip(tp, 8), 16)),
        "y1": (seq, flip(tp, 2)),
        "y3": (seq, flip(flip(tp, 2), 4)),
    }

    def remote(src, dst, number, target):
        return pltpu.make_async_remote_copy(
            src_ref=src,
            dst_ref=dst,
            send_sem=sends.at[number],
            recv_sem=recvs.at[number],
            device_id=place[target],
            device_id_type=MESH,
        )

    def rows(slot, j):
        start = slot * ROWS + j * PART
        return pl.ds(start if isinstance(j, int) else pl.multiple_of(start, PART), PART)

    def piece(j):
        return pl.ds(j * PART, PART)

    def columns(level):
        return pl.ds(level * G, G)

    def z1(which, j):
        return remote(shared[which].at[piece(j)], held.at[which, 1, rows(0, j)], NUMBER["z1", which] + j, "z1")

    def z3(which, j):
        return remote(shared[which].at[piece(j)], held.at[which, 1, rows(1, j)], NUMBER["z3", which] + j, "z3")

    def zr(which, j):
        return remote(
            held.at[which, 1, rows(j, j)],
            held.at[which, 0, rows(1, j)],
            NUMBER["zr", which] + j,
            "z3" if j == 0 else "z1",
        )

    def near(axis, which, slot, j):
        src = shared[which].at[piece(j)] if slot == 0 else held.at[which, 0, rows(1, j)]
        return remote(src, held.at[which, NEAR[axis], rows(slot, j)], NUMBER["near", axis, which, slot] + j, axis + "1")

    def far(axis, which, slot, j):
        return remote(
            held.at[which, NEAR[axis], rows(slot, j)],
            held.at[which, FAR[axis], rows(slot, j)],
            NUMBER["far", axis, which, slot] + j,
            axis + "3",
        )

    def term(axis, which, slot, j):
        a = "xy".index(axis)
        return remote(
            term_send.at[which, a, rows(slot, j)],
            term_recv.at[which, a, rows(slot, j)],
            NUMBER["term", axis, which, slot] + j,
            axis + "3",
        )

    def summed(axis, which, slot, j):
        a = "xy".index(axis)
        return remote(
            sum_send.at[which, a, rows(slot, j)],
            sum_recv.at[which, a, rows(slot, j)],
            NUMBER["sum", axis, which, slot] + j,
            axis + "1",
        )

    def half(which, j):
        return remote(half_send.at[which, piece(j)], half_recv.at[which, piece(j)], NUMBER["half", which] + j, "z3" if j == 0 else "z1")

    def out1(which, j):
        return remote(z_send.at[which, rows(0, j)], z_recv.at[which, rows(0, j)], NUMBER["out1", which] + j, "z1")

    def out3(which, j):
        return remote(z_send.at[which, rows(1, j)], z_recv.at[which, rows(1, j)], NUMBER["out3", which] + j, "z3")

    def weight(which):
        if which == 0:
            return remote(uall.at[:, pl.ds(0, G)], uall.at[:, pl.ds(G, G)], NUMBER["weight", 0], "core")
        return remote(dall.at[pl.ds(0, G)], dall.at[pl.ds(G, G)], NUMBER["weight", 1], "core")

    def grad(which, level):
        return remote(grad_peer.at[which, level], grad_recv.at[which, level], NUMBER["grad", which] + level, "core")

    own = [
        pltpu.make_async_copy(shared[which], held.at[which, 0, pl.ds(0, ROWS)], local.at[which])
        for which in range(2)
    ]
    loads = [pltpu.make_async_copy(ref, raw.at[which], local.at[2 + which]) for which, ref in enumerate((up, down))]
    for copy in loads + own:
        copy.start()

    barrier = pltpu.get_barrier_semaphore()
    for target in place.values():
        pl.semaphore_signal(barrier, inc=1, device_id=target, device_id_type=MESH)
    pl.semaphore_wait(barrier, len(place))

    def own_z(which, j):
        z1(which, j).start()
        z3(which, j).start()

    def own_xy(which, j):
        near("x", which, 0, j).start()
        near("y", which, 0, j).start()

    def relay_z(which, j):
        (z1 if j == 0 else z3)(which, j).wait_recv()
        zr(which, j).start()

    def relay_xy(which, slot, j):
        for axis in "xy":
            near(axis, which, slot, j).wait_recv()
            far(axis, which, slot, j).start()

    def other(which, j):
        zr(which, j).wait_recv()
        near("x", which, 1, j).start()
        near("y", which, 1, j).start()

    def arrived(which, slot):
        (z1 if slot == 0 else z3)(which, 1 - slot).wait_recv()
        for j in range(PIECES):
            for axis in "xy":
                far(axis, which, slot, j).wait_recv()

    def scale_up(k, carry):
        factor = mask[0, k].astype(F32)
        uall[pl.ds(pl.multiple_of(k * G, G), G), pl.ds(0, G)] = (raw[0, k].astype(F32) * factor).astype(BF16)
        return carry

    def scale_down(k, carry):
        factor = mask[0, k].astype(F32)
        dall[pl.ds(0, G), pl.ds(pl.multiple_of(k * G, G), G)] = (raw[1, k].astype(F32) * factor).astype(BF16)
        return carry

    def wide(which, at):
        return jnp.concatenate([held[which, level, at] for level in range(LEVELS)], axis=1)

    def forward(slot, j):
        at = rows(slot, j)
        pre = jnp.dot(wide(0, at), uall[...], preferred_element_type=F32)
        square = pre * pre
        tanh = jnp.tanh(SCALE * pre * (1.0 + CUBE * square))
        cdf = 0.5 + 0.5 * tanh
        act[at, :] = (pre * cdf).astype(BF16)
        slope[at, :] = cdf + (0.5 * SCALE) * pre * (1.0 - tanh * tanh) * (1.0 + (3.0 * CUBE) * square)

    def backward(slot, j):
        at = rows(slot, j)
        gact = jnp.dot(wide(1, at), dall_t[...], preferred_element_type=F32)
        gpre[at, :] = (gact * slope[at, :]).astype(BF16)

    def turn_act(slot, j):
        act_t[:, rows(slot, j)] = act[rows(slot, j), :].T

    def turn_weights():
        def body(k, carry):
            at = pl.ds(pl.multiple_of(k * G, G), G)
            dall_t[at, :] = dall[:, at].T
            uall_t[:, at] = uall[at, :].T
            return carry

        lax.fori_loop(0, LEVELS, body, 0)

    def turn_held(slot):
        def body(k, carry):
            at = pl.ds(pl.multiple_of(k * G, G), G)
            held_t[at, pl.ds(slot * ROWS, ROWS)] = held[0, k, pl.ds(slot * ROWS, ROWS)].T
            return carry

        lax.fori_loop(0, LEVELS, body, 0)

    def by_down(slot, j, level):
        return jnp.dot(act[rows(slot, j), :], dall[:, columns(level)], preferred_element_type=F32)

    def by_up(slot, j, level):
        return jnp.dot(gpre[rows(slot, j), :], uall_t[:, columns(level)], preferred_element_type=F32)

    def terms(which, slot, j, send):
        at = rows(slot, j)
        product = by_up if which else by_down
        for a, axis in enumerate("xy"):
            term_send[which, a, at] = product(slot, j, FAR[axis]).astype(BF16)
            if send:
                term(axis, which, slot, j).start()
        for a, axis in enumerate("xy"):
            near_term[which, a, at] = product(slot, j, NEAR[axis])
        z_term[which, at] = product(slot, j, 1)
        base[which, at] = product(slot, j, 0)

    def send_terms(which, slot):
        for j in range(PIECES):
            for axis in "xy":
                term(axis, which, slot, j).start()

    def tiles(which, slot):
        def body(j, carry):
            (backward if which else forward)(slot, j)
            terms(which, slot, j, True)
            if which == 0:
                turn_act(slot, j)
            return carry

        lax.fori_loop(0, PIECES, body, 0)
        plain(which, slot)

    def plain(which, slot):
        at = rows(slot, 1 - slot)
        z_send[which, at] = z_term[which, at].astype(BF16)
        (out1 if slot == 0 else out3)(which, 1 - slot).start()

    def join(which, slot):
        for j in range(PIECES):
            for a, axis in enumerate("xy"):
                at = rows(slot, j)
                term(axis, which, slot, j).wait_recv()
                sum_send[which, a, at] = (near_term[which, a, at] + term_recv[which, a, at].astype(F32)).astype(BF16)
                summed(axis, which, slot, j).start()

    def collect(which, slot):
        for j in range(PIECES):
            at = rows(slot, j)
            for axis in "xy":
                summed(axis, which, slot, j).wait_recv()
            total = base[which, at] + sum_recv[which, 0, at].astype(F32) + sum_recv[which, 1, at].astype(F32)
            if slot == 0:
                base[which, at] = total
            else:
                half_send[which, piece(j)] = total.astype(BF16)
                half(which, j).start()

    def pass_on(which):
        for j in range(PIECES):
            at = rows(j, j)
            half(which, j).wait_recv()
            z_send[which, at] = (z_term[which, at] + half_recv[which, piece(j)].astype(F32)).astype(BF16)
            (out1 if j == 0 else out3)(which, j).start()

    def finish(which, result):
        for j in range(PIECES):
            out1(which, j).wait_recv()
            out3(which, j).wait_recv()
            total = base[which, rows(0, j)] + z_recv[which, rows(0, j)].astype(F32) + z_recv[which, rows(1, j)].astype(F32)
            result[piece(j), :] = total.astype(BF16)

    def grads_down(first, last):
        def body(k, carry):
            both = jnp.dot(act_t[...], held[1, k], preferred_element_type=F32)
            grad_own[1, k] = both[:G]
            grad_peer[1, k] = both[G:]
            grad(1, k).start()
            return carry

        lax.fori_loop(first, last, body, 0)

    def grads_up(first, last):
        def body(k, carry):
            at = pl.ds(pl.multiple_of(k * G, G), G)
            both = jnp.dot(held_t[at, :], gpre[...], preferred_element_type=F32)
            grad_own[0, k] = both[:, :G]
            grad_peer[0, k] = both[:, G:]
            grad(0, k).start()
            return carry

        lax.fori_loop(first, last, body, 0)

    def grads_sum(which, result):
        def body(k, carry):
            grad(which, k).wait_recv()
            factor = mask[0, k].astype(F32)
            grad_own[which, k] = (grad_own[which, k] + grad_recv[which, k]) * factor
            pltpu.make_async_copy(grad_own.at[which, k], result.at[k], local.at[4 + which * LEVELS + k]).start()
            return carry

        lax.fori_loop(0, LEVELS, body, 0)

    for j in range(PIECES):
        own_z(0, j)
        own_xy(0, j)
    loads[0].wait()
    lax.fori_loop(0, LEVELS, scale_up, 0)
    weight(0).start()
    loads[1].wait()
    lax.fori_loop(0, LEVELS, scale_down, 0)
    weight(1).start()
    for copy in own:
        copy.wait()

    for j in range(PIECES):
        relay_xy(0, 0, j)
        own_xy(1, j)
        relay_z(0, j)
        own_z(1, j)
    for j in range(PIECES):
        relay_xy(1, 0, j)
        other(0, j)
    for j in range(PIECES):
        relay_z(1, j)
    weight(0).wait_recv()
    weight(1).wait_recv()
    arrived(0, 0)
    forward(0, 0)
    terms(0, 0, 0, False)
    turn_act(0, 0)
    for j in range(PIECES):
        relay_xy(0, 1, j)
        other(1, j)
    forward(0, 1)
    terms(0, 0, 1, False)
    plain(0, 0)
    turn_act(0, 1)
    for j in range(PIECES):
        relay_xy(1, 1, j)
    turn_weights()
    turn_held(0)

    arrived(0, 1)
    tiles(0, 1)
    arrived(1, 1)
    tiles(1, 1)
    send_terms(0, 0)
    join(0, 1)
    arrived(1, 0)
    tiles(1, 0)
    turn_held(1)
    grads_down(0, LEVELS // 2)
    join(1, 1)
    collect(0, 1)
    grads_down(LEVELS // 2, LEVELS)
    join(0, 0)
    collect(1, 1)
    pass_on(0)
    grads_up(0, LEVELS)
    join(1, 0)
    pass_on(1)
    collect(0, 0)
    grads_sum(1, gdown)
    finish(0, out)
    grads_sum(0, gup)
    collect(1, 0)
    finish(1, gtok)

    for which, result in enumerate((gup, gdown)):
        for k in range(LEVELS):
            pltpu.make_async_copy(grad_own.at[which, k], result.at[k], local.at[4 + which * LEVELS + k]).wait()
    for which in range(2):
        weight(which).wait_send()
        for k in range(LEVELS):
            grad(which, k).wait_send()
        for j in range(PIECES):
            for make in (z1, z3, zr, half, out1, out3):
                make(which, j).wait_send()
            for slot in range(2):
                for axis in "xy":
                    for make in (near, far, term, summed):
                        make(axis, which, slot, j).wait_send()


def hand_out(*refs):
    sources, results, sems = refs[:4], refs[4:8], refs[8]
    copies = []
    for src, dst in zip(sources, results):
        if len(src.shape) == 2:
            pairs = [(src, dst)]
        else:
            pairs = [(src.at[pl.ds(k, 2)], dst.at[pl.ds(k, 2)]) for k in range(0, LEVELS, 2)]
        for a, b in pairs:
            copies.append(pltpu.make_async_copy(a, b, sems.at[len(copies)]))
    for copy in copies:
        copy.start()
    for copy in copies:
        copy.wait()


def shards(tokens, up_weight, down_weight, block_mask, cotangent):
    anywhere = pl.BlockSpec(memory_space=pl.ANY)
    vmem = pl.BlockSpec(memory_space=pltpu.VMEM)
    both = 2 * ROWS
    result = (
        jax.ShapeDtypeStruct((ROWS, G), BF16),
        jax.ShapeDtypeStruct((ROWS, G), BF16),
        jax.ShapeDtypeStruct((LEVELS, G, G), F32),
        jax.ShapeDtypeStruct((LEVELS, G, G), F32),
    )
    operands = [pltpu.with_memory_space_constraint(a, pltpu.HBM) for a in (tokens, cotangent, up_weight[0], down_weight[0])]
    worked = pl.pallas_call(
        kernel,
        out_shape=tuple(pltpu.VMEM(a.shape, a.dtype) for a in result),
        in_specs=[anywhere, anywhere, anywhere, anywhere, pl.BlockSpec(memory_space=pltpu.SMEM)],
        out_specs=(vmem, vmem, anywhere, anywhere),
        scratch_shapes=[
            pltpu.VMEM((2, LEVELS, both, G), BF16),
            pltpu.VMEM((WIDE, both), BF16),
            pltpu.VMEM((2, LEVELS, G, G), BF16),
            pltpu.VMEM((WIDE, 2 * G), BF16),
            pltpu.VMEM((2 * G, WIDE), BF16),
            pltpu.VMEM((2 * G, WIDE), BF16),
            pltpu.VMEM((WIDE, 2 * G), BF16),
            pltpu.VMEM((both, 2 * G), BF16),
            pltpu.VMEM((2 * G, both), BF16),
            pltpu.VMEM((both, 2 * G), BF16),
            pltpu.VMEM((both, 2 * G), F32),
            pltpu.VMEM((2, 2, both, G), BF16),
            pltpu.VMEM((2, 2, both, G), BF16),
            pltpu.VMEM((2, 2, both, G), F32),
            pltpu.VMEM((2, 2, both, G), BF16),
            pltpu.VMEM((2, 2, both, G), BF16),
            pltpu.VMEM((2, both, G), F32),
            pltpu.VMEM((2, both, G), F32),
            pltpu.VMEM((2, ROWS, G), BF16),
            pltpu.VMEM((2, ROWS, G), BF16),
            pltpu.VMEM((2, both, G), BF16),
            pltpu.VMEM((2, both, G), BF16),
            pltpu.VMEM((2, LEVELS, G, G), F32),
            pltpu.VMEM((2, LEVELS, G, G), F32),
            pltpu.VMEM((2, LEVELS, G, G), F32),
            pltpu.SemaphoreType.DMA((COPIES,)),
            pltpu.SemaphoreType.DMA((COPIES,)),
            pltpu.SemaphoreType.DMA((4 + 2 * LEVELS,)),
        ],
        compiler_params=pltpu.CompilerParams(
            collective_id=0, has_side_effects=True, vmem_limit_bytes=58 * 1024 * 1024
        ),
    )(*operands, block_mask)
    worked = [pltpu.with_memory_space_constraint(a, pltpu.VMEM) for a in worked]
    output, grad_tokens, grad_up, grad_down = pl.pallas_call(
        hand_out,
        out_shape=result,
        in_specs=[anywhere] * 4,
        out_specs=(anywhere,) * 4,
        scratch_shapes=[pltpu.SemaphoreType.DMA((8,))],
        compiler_params=pltpu.CompilerParams(vmem_limit_bytes=1024 * 1024),
    )(*worked)
    return output, grad_tokens, grad_up[None], grad_down[None]


def solution(mesh):
    placed = (
        P("seq", "tp"),
        P(("seq", "tp"), None, None, None),
        P(("seq", "tp"), None, None, None),
        P(("seq", "tp"), None),
        P("seq", "tp"),
    )
    return jax.shard_map(
        shards,
        mesh=mesh,
        in_specs=placed,
        out_specs=(
            P("seq", "tp"),
            P("seq", "tp"),
            P(("seq", "tp"), None, None, None),
            P(("seq", "tp"), None, None, None),
        ),
        check_vma=False,
    )
```

```python
import functools
import math

import jax
import jax.numpy as jnp
from jax import lax
from jax.experimental import pallas as pl
from jax.experimental.pallas import tpu as pltpu
from jax.sharding import PartitionSpec as P

MESH = pl.DeviceIdType.MESH
F32 = jnp.float32
BF16 = jnp.bfloat16
ROWS = 512
PART = 128
PIECES = ROWS // PART
FIRST = PIECES // 2
TILE = 256
PER_TILE = TILE // PART
THIRDS = 3
G = 256
LEVELS = 6
WIDE = LEVELS * G
NEAR = {"x": 4, "y": 2}
FAR = {"x": 5, "y": 3}
SCALE = math.sqrt(2.0 / math.pi)
CUBE = 0.044715


def numbering():
    keys = []
    for which in range(2):
        keys += [(name, which, j) for name in ("z1", "z3", "zr", "out1", "out3", "half") for j in range(PIECES)]
        keys += [
            (name, axis, which, slot, j)
            for name in ("near", "far", "term", "sum")
            for axis in "xy"
            for slot in range(2)
            for j in range(PIECES)
        ]
        keys += [("weight", which)] + [("grad", which, k) for k in range(LEVELS // THIRDS)]
    keys += [("last", axis, j) for axis in "xy" for j in range(PIECES)]
    return {key: n for n, key in enumerate(keys)}


NUMBER = numbering()
COPIES = len(NUMBER)

ORDER = (
    ("ox", 0, 2), ("oz", 0, 2), ("ox", 0, 3), ("sd",), ("oz", 0, 0), ("oz", 0, 1), ("ox", 1, 2), ("su",),
    ("ox", 0, 0), ("oz", 0, 3), ("oz", 1, 0), ("rx", 0, 0, 2), ("ox", 0, 1), ("rx", 0, 0, 3), ("rz", 0, 1),
    ("rx", 1, 0, 2), ("ox", 1, 3), ("rz", 0, 2), ("rz", 0, 0), ("rz", 0, 3), ("ox", 1, 0), ("oz", 1, 3),
    ("rx", 0, 0, 0), ("F", 0, 1), ("rz", 1, 0), ("ox", 1, 1), ("oz", 1, 1), ("rx", 0, 0, 1), ("rx", 1, 0, 3),
    ("ot", 0, 1), ("tw",), ("ot", 0, 2), ("ot", 0, 0), ("oz", 1, 2), ("rx", 1, 0, 0), ("F", 0, 0), ("rx", 0, 1, 1),
    ("rz", 1, 3), ("TN", 0, 0, 1), ("ot", 1, 0), ("rx", 1, 0, 1), ("ot", 0, 3), ("th", 0), ("J", 0, 0, 2),
    ("rz", 1, 1), ("rx", 0, 1, 0), ("rz", 1, 2), ("B", 0, 1), ("Z", 0, 0, 3), ("rx", 0, 1, 2), ("ta", 0, 0),
    ("ot", 1, 3), ("TF", 0, 0, 0), ("TN", 0, 0, 0), ("Z", 0, 0, 2), ("rx", 0, 1, 3), ("TN", 1, 0, 1),
    ("rx", 1, 1, 0), ("ot", 1, 1), ("ot", 1, 2), ("F", 1, 0), ("TF", 0, 1, 0), ("rx", 1, 1, 3), ("TF", 1, 0, 1),
    ("S", 0, 1, 1), ("S", 0, 0, 0), ("J", 0, 0, 3), ("F", 1, 1), ("ta", 0, 1), ("S", 0, 0, 1), ("S", 0, 1, 0),
    ("TN", 0, 1, 0), ("TF", 0, 0, 1), ("rx", 1, 1, 2), ("Z", 1, 0, 2), ("TF", 0, 1, 1), ("rx", 1, 1, 1),
    ("ta", 1, 1), ("TN", 0, 1, 1), ("B", 0, 0), ("TF", 1, 0, 0), ("J", 0, 1, 1), ("ta", 1, 0), ("J", 0, 1, 0),
    ("S", 0, 1, 3), ("S", 0, 0, 3), ("C", 0, 0, 2), ("Z", 0, 1, 0), ("S", 0, 1, 2), ("B", 1, 1), ("TF", 1, 1, 1),
    ("Z", 1, 0, 3), ("J", 0, 0, 0), ("TN", 1, 1, 1), ("J", 0, 0, 1), ("S", 1, 1, 3), ("B", 1, 0), ("TF", 1, 1, 0),
    ("S", 1, 1, 0), ("S", 1, 1, 1), ("S", 1, 1, 2), ("J", 0, 1, 3), ("C", 0, 1, 0), ("TN", 1, 1, 0), ("Z", 1, 1, 0),
    ("G", 1, 1), ("Z", 1, 1, 1), ("J", 1, 1, 3), ("C", 0, 1, 1), ("th", 1), ("J", 1, 1, 0), ("TN", 1, 0, 0),
    ("S", 1, 0, 3), ("PO", 0, 0), ("S", 1, 0, 0), ("S", 1, 0, 2), ("J", 1, 1, 1), ("C", 0, 1, 3), ("Z", 0, 1, 1),
    ("J", 0, 1, 2), ("G", 0, 0), ("J", 1, 1, 2), ("C", 1, 1, 3), ("S", 0, 0, 2), ("PO", 0, 1), ("RL", 3),
    ("C", 1, 1, 0), ("S", 1, 0, 1), ("G", 1, 0), ("C", 1, 1, 1), ("J", 1, 0, 0), ("C", 0, 1, 2), ("PO", 1, 3),
    ("RL", 0), ("PO", 0, 3), ("J", 1, 0, 3), ("C", 1, 1, 2), ("PO", 1, 0), ("RL", 1), ("G", 0, 1), ("J", 1, 0, 2),
    ("PO", 0, 2), ("RL", 2), ("GS", 1, 0), ("PO", 1, 1), ("J", 1, 0, 1), ("PO", 1, 2), ("C", 0, 0, 1),
    ("C", 1, 0, 3), ("GS", 0, 0), ("GS", 1, 1), ("FIN", 0, 1), ("FIN", 1, 3), ("C", 1, 0, 0), ("C", 0, 0, 3),
    ("FIN", 0, 3), ("C", 0, 0, 0), ("FIN", 0, 0), ("FIN", 0, 2), ("GS", 0, 1), ("FIN", 1, 0), ("C", 1, 0, 2),
    ("FIN", 1, 2), ("C", 1, 0, 1), ("FIN", 1, 1),
)


def flip(index, bit):
    return index + bit - 2 * bit * lax.rem(lax.div(index, bit), 2)


def kernel(
    tok, cot, up, down, mask, out, gtok, gup, gdown,
    held, held_t, raw, uall, dall, uall_t, dall_t, act, act_t, gpre, slope,
    term_send, term_recv, near_term, sum_send, sum_recv, base, z_term,
    half_send, half_recv, last_recv, z_send, z_recv,
    grad_own, grad_peer, grad_recv,
    sends, recvs, local,
):
    shared = (tok, cot)
    seq, tp = lax.axis_index("seq"), lax.axis_index("tp")
    place = {
        "core": (flip(seq, 1), tp),
        "z1": (seq, flip(tp, 1)),
        "z3": (flip(seq, 2), flip(tp, 1)),
        "x1": (seq, flip(tp, 8)),
        "x3": (seq, flip(flip(tp, 8), 16)),
        "y1": (seq, flip(tp, 2)),
        "y3": (seq, flip(flip(tp, 2), 4)),
    }

    def remote(src, dst, number, target):
        return pltpu.make_async_remote_copy(
            src_ref=src,
            dst_ref=dst,
            send_sem=sends.at[number],
            recv_sem=recvs.at[number],
            device_id=place[target],
            device_id_type=MESH,
        )

    def rows(slot, j):
        start = slot * ROWS + j * PART
        return pl.ds(start if isinstance(j, int) else pl.multiple_of(start, PART), PART)

    def piece(j):
        return pl.ds(j * PART, PART)

    def columns(level):
        return pl.ds(level * G, G)

    def transfer(key):
        name, rest = key[0], key[1:]
        number = NUMBER[key]
        if name == "weight":
            if rest[0] == 0:
                return remote(uall.at[:, pl.ds(0, G)], uall.at[:, pl.ds(G, G)], number, "core")
            return remote(dall.at[pl.ds(0, G)], dall.at[pl.ds(G, G)], number, "core")
        if name == "grad":
            at = pl.ds(rest[1] * THIRDS, THIRDS)
            return remote(grad_peer.at[rest[0], at], grad_recv.at[rest[0], at], number, "core")
        if name == "last":
            a, j = "xy".index(rest[0]), rest[1]
            return remote(term_recv.at[0, a, rows(0, j)], last_recv.at[a, piece(j)], number, rest[0] + "3")
        if name in ("near", "far", "term", "sum"):
            axis, which, slot, j = rest
            a, at = "xy".index(axis), rows(slot, j)
            if name == "near":
                src = held.at[which, 0, at] if slot else shared[which].at[piece(j)]
                return remote(src, held.at[which, NEAR[axis], at], number, axis + "1")
            if name == "far":
                return remote(held.at[which, NEAR[axis], at], held.at[which, FAR[axis], at], number, axis + "3")
            if name == "term":
                target = axis + ("1" if (which, slot) == (0, 0) else "3")
                return remote(term_send.at[which, a, at], term_recv.at[which, a, at], number, target)
            return remote(sum_send.at[which, a, at], sum_recv.at[which, a, at], number, axis + "1")
        which, j = rest
        if name == "z1":
            return remote(shared[which].at[piece(j)], held.at[which, 1, rows(0, j)], number, "z1")
        if name == "z3":
            return remote(shared[which].at[piece(j)], held.at[which, 1, rows(1, j)], number, "z3")
        onward = "z3" if j < FIRST else "z1"
        if name == "zr":
            return remote(held.at[which, 1, rows(int(j >= FIRST), j)], held.at[which, 0, rows(1, j)], number, onward)
        if name == "half":
            return remote(half_send.at[which, piece(j)], half_recv.at[which, piece(j)], number, onward)
        slot = int(name == "out3")
        return remote(z_send.at[which, rows(slot, j)], z_recv.at[which, rows(slot, j)], number, "z3" if slot else "z1")

    started, landed, copied = set(), set(), set()

    def send(*keys):
        for key in keys:
            started.add(key)
            transfer(key).start()

    def need(*keys):
        for key in keys:
            if key not in landed:
                landed.add(key)
                transfer(key).wait_recv()

    own = [
        pltpu.make_async_copy(shared[which], held.at[which, 0, pl.ds(0, ROWS)], local.at[which])
        for which in range(2)
    ]
    loads = [pltpu.make_async_copy(ref, raw.at[which], local.at[2 + which]) for which, ref in enumerate((up, down))]
    for copy in loads + own:
        copy.start()

    barrier = pltpu.get_barrier_semaphore()
    for target in place.values():
        pl.semaphore_signal(barrier, inc=1, device_id=target, device_id_type=MESH)
    pl.semaphore_wait(barrier, len(place))

    def scale_up(k, carry):
        factor = mask[0, k].astype(F32)
        uall[pl.ds(pl.multiple_of(k * G, G), G), pl.ds(0, G)] = (raw[0, k].astype(F32) * factor).astype(BF16)
        return carry

    def scale_down(k, carry):
        factor = mask[0, k].astype(F32)
        dall[pl.ds(0, G), pl.ds(pl.multiple_of(k * G, G), G)] = (raw[1, k].astype(F32) * factor).astype(BF16)
        return carry

    def wide(which, at):
        return jnp.concatenate([held[which, level, at] for level in range(LEVELS)], axis=1)

    def tile(slot, t):
        return pl.ds(slot * ROWS + t * TILE, TILE)

    def own_z(which, j):
        send(("z1", which, j), ("z3", which, j))

    def own_xy(which, j):
        send(("near", "x", which, 0, j), ("near", "y", which, 0, j))

    def relay_z(which, j):
        need(("z1" if j < FIRST else "z3", which, j))
        send(("zr", which, j))

    def other(which, j):
        need(("zr", which, j))
        send(("near", "x", which, 1, j), ("near", "y", which, 1, j))

    def relay_xy(which, slot, j):
        for axis in "xy":
            need(("near", axis, which, slot, j))
            send(("far", axis, which, slot, j))

    def mask_up():
        loads[0].wait()
        lax.fori_loop(0, LEVELS, scale_up, 0)
        send(("weight", 0))

    def mask_down():
        loads[1].wait()
        lax.fori_loop(0, LEVELS, scale_down, 0)
        send(("weight", 1))

    def turn_weights():
        need(("weight", 0), ("weight", 1))

        def body(k, carry):
            at = pl.ds(pl.multiple_of(k * G, G), G)
            dall_t[at, :] = dall[:, at].T
            uall_t[:, at] = uall[at, :].T
            return carry

        lax.fori_loop(0, LEVELS, body, 0)

    def turn_held(slot):
        def body(k, carry):
            at = pl.ds(pl.multiple_of(k * G, G), G)
            held_t[at, pl.ds(slot * ROWS, ROWS)] = held[0, k, pl.ds(slot * ROWS, ROWS)].T
            return carry

        lax.fori_loop(0, LEVELS, body, 0)

    def turn_act(slot, t):
        act_t[:, tile(slot, t)] = act[tile(slot, t), :].T

    def inputs(which, slot, t):
        if slot == 0 and ("own", which) not in copied:
            copied.add(("own", which))
            own[which].wait()
        for j in range(t * PER_TILE, (t + 1) * PER_TILE):
            need(("z3" if slot else "z1", which, j))
            for axis in "xy":
                need(("far", axis, which, slot, j))

    def forward(slot, t):
        inputs(0, slot, t)
        need(("weight", 0), ("weight", 1))
        at = tile(slot, t)
        pre = jnp.dot(wide(0, at), uall[...], preferred_element_type=F32)
        square = pre * pre
        tanh = jnp.tanh(SCALE * pre * (1.0 + CUBE * square))
        cdf = 0.5 + 0.5 * tanh
        act[at, :] = (pre * cdf).astype(BF16)
        slope[at, :] = cdf + (0.5 * SCALE) * pre * (1.0 - tanh * tanh) * (1.0 + (3.0 * CUBE) * square)

    def backward(slot, t):
        inputs(1, slot, t)
        at = tile(slot, t)
        gact = jnp.dot(wide(1, at), dall_t[...], preferred_element_type=F32)
        gpre[at, :] = (gact * slope[at, :]).astype(BF16)

    def product(which, slot, t, level):
        if which:
            return jnp.dot(gpre[tile(slot, t), :], uall_t[:, columns(level)], preferred_element_type=F32)
        return jnp.dot(act[tile(slot, t), :], dall[:, columns(level)], preferred_element_type=F32)

    def far_terms(which, slot, t):
        for a, axis in enumerate("xy"):
            term_send[which, a, tile(slot, t)] = product(which, slot, t, FAR[axis]).astype(BF16)

    def near_terms(which, slot, t):
        at = tile(slot, t)
        for a, axis in enumerate("xy"):
            near_term[which, a, at] = product(which, slot, t, NEAR[axis])
        z_term[which, at] = product(which, slot, t, 1)
        base[which, at] = product(which, slot, t, 0)

    def send_term(which, slot, j):
        send(("term", "x", which, slot, j), ("term", "y", which, slot, j))

    def hand_on(j):
        for axis in "xy":
            need(("term", axis, 0, 0, j))
            send(("last", axis, j))

    def join(which, slot, j):
        at = rows(slot, j)
        for a, axis in enumerate("xy"):
            total = near_term[which, a, at]
            if (which, slot) != (0, 0):
                need(("term", axis, which, slot, j))
                total = total + term_recv[which, a, at].astype(F32)
            sum_send[which, a, at] = total.astype(BF16)
            send(("sum", axis, which, slot, j))

    def collect(which, slot, j):
        at = rows(slot, j)
        need(("sum", "x", which, slot, j), ("sum", "y", which, slot, j))
        total = base[which, at] + sum_recv[which, 0, at].astype(F32) + sum_recv[which, 1, at].astype(F32)
        if slot == 0:
            base[which, at] = total
        else:
            half_send[which, piece(j)] = total.astype(BF16)
            send(("half", which, j))

    def plain(which, slot, j):
        z_send[which, rows(slot, j)] = z_term[which, rows(slot, j)].astype(BF16)
        send(("out3" if slot else "out1", which, j))

    def pass_on(which, j):
        slot = int(j >= FIRST)
        at = rows(slot, j)
        need(("half", which, j))
        z_send[which, at] = (z_term[which, at] + half_recv[which, piece(j)].astype(F32)).astype(BF16)
        send(("out3" if slot else "out1", which, j))

    def finish(which, j):
        need(("out1", which, j), ("out3", which, j))
        total = base[which, rows(0, j)] + z_recv[which, rows(0, j)].astype(F32) + z_recv[which, rows(1, j)].astype(F32)
        if which == 0:
            need(("last", "x", j), ("last", "y", j))
            total = total + last_recv[0, piece(j)].astype(F32) + last_recv[1, piece(j)].astype(F32)
        (gtok if which else out)[piece(j), :] = total.astype(BF16)

    def grads(which, third):
        def body(k, carry):
            at = pl.ds(pl.multiple_of(k * G, G), G)
            if which:
                both = jnp.dot(act_t[...], held[1, k], preferred_element_type=F32)
                grad_own[1, k] = both[:G]
                grad_peer[1, k] = both[G:]
            else:
                both = jnp.dot(held_t[at, :], gpre[...], preferred_element_type=F32)
                grad_own[0, k] = both[:, :G]
                grad_peer[0, k] = both[:, G:]
            return carry

        lax.fori_loop(third * THIRDS, (third + 1) * THIRDS, body, 0)
        send(("grad", which, third))

    def write_grad(which, k):
        return pltpu.make_async_copy(grad_own.at[which, k], (gdown if which else gup).at[k], local.at[4 + which * LEVELS + k])

    def grads_sum(which, third):
        need(("grad", which, third))

        def body(k, carry):
            grad_own[which, k] = (grad_own[which, k] + grad_recv[which, k]) * mask[0, k].astype(F32)
            write_grad(which, k).start()
            return carry

        lax.fori_loop(third * THIRDS, (third + 1) * THIRDS, body, 0)

    steps = {
        "oz": own_z, "ox": own_xy, "rz": relay_z, "ot": other, "rx": relay_xy, "su": mask_up, "sd": mask_down,
        "tw": turn_weights, "th": turn_held, "ta": turn_act, "F": forward, "B": backward, "TF": far_terms,
        "TN": near_terms, "S": send_term, "RL": hand_on, "J": join, "C": collect, "Z": plain, "PO": pass_on,
        "FIN": finish, "G": grads, "GS": grads_sum,
    }
    for step in ORDER:
        steps[step[0]](*step[1:])

    assert started == landed == set(NUMBER)
    for which in range(2):
        for k in range(LEVELS):
            write_grad(which, k).wait()
    for key in NUMBER:
        transfer(key).wait_send()


def hand_out(*refs):
    sources, results, sems = refs[:4], refs[4:8], refs[8]
    copies = []
    for src, dst in zip(sources, results):
        if len(src.shape) == 2:
            pairs = [(src, dst)]
        else:
            pairs = [(src.at[pl.ds(k, 2)], dst.at[pl.ds(k, 2)]) for k in range(0, LEVELS, 2)]
        for a, b in pairs:
            copies.append(pltpu.make_async_copy(a, b, sems.at[len(copies)]))
    for copy in copies:
        copy.start()
    for copy in copies:
        copy.wait()


def shards(tokens, up_weight, down_weight, block_mask, cotangent):
    anywhere = pl.BlockSpec(memory_space=pl.ANY)
    vmem = pl.BlockSpec(memory_space=pltpu.VMEM)
    both = 2 * ROWS
    result = (
        jax.ShapeDtypeStruct((ROWS, G), BF16),
        jax.ShapeDtypeStruct((ROWS, G), BF16),
        jax.ShapeDtypeStruct((LEVELS, G, G), F32),
        jax.ShapeDtypeStruct((LEVELS, G, G), F32),
    )
    operands = [pltpu.with_memory_space_constraint(a, pltpu.HBM) for a in (tokens, cotangent, up_weight[0], down_weight[0])]
    worked = pl.pallas_call(
        kernel,
        out_shape=tuple(pltpu.VMEM(a.shape, a.dtype) for a in result),
        in_specs=[anywhere, anywhere, anywhere, anywhere, pl.BlockSpec(memory_space=pltpu.SMEM)],
        out_specs=(vmem, vmem, anywhere, anywhere),
        scratch_shapes=[
            pltpu.VMEM((2, LEVELS, both, G), BF16),
            pltpu.VMEM((WIDE, both), BF16),
            pltpu.VMEM((2, LEVELS, G, G), BF16),
            pltpu.VMEM((WIDE, 2 * G), BF16),
            pltpu.VMEM((2 * G, WIDE), BF16),
            pltpu.VMEM((2 * G, WIDE), BF16),
            pltpu.VMEM((WIDE, 2 * G), BF16),
            pltpu.VMEM((both, 2 * G), BF16),
            pltpu.VMEM((2 * G, both), BF16),
            pltpu.VMEM((both, 2 * G), BF16),
            pltpu.VMEM((both, 2 * G), F32),
            pltpu.VMEM((2, 2, both, G), BF16),
            pltpu.VMEM((2, 2, both, G), BF16),
            pltpu.VMEM((2, 2, both, G), F32),
            pltpu.VMEM((2, 2, both, G), BF16),
            pltpu.VMEM((2, 2, both, G), BF16),
            pltpu.VMEM((2, both, G), F32),
            pltpu.VMEM((2, both, G), F32),
            pltpu.VMEM((2, ROWS, G), BF16),
            pltpu.VMEM((2, ROWS, G), BF16),
            pltpu.VMEM((2, ROWS, G), BF16),
            pltpu.VMEM((2, both, G), BF16),
            pltpu.VMEM((2, both, G), BF16),
            pltpu.VMEM((2, LEVELS, G, G), F32),
            pltpu.VMEM((2, LEVELS, G, G), F32),
            pltpu.VMEM((2, LEVELS, G, G), F32),
            pltpu.SemaphoreType.DMA((COPIES,)),
            pltpu.SemaphoreType.DMA((COPIES,)),
            pltpu.SemaphoreType.DMA((4 + 2 * LEVELS,)),
        ],
        compiler_params=pltpu.CompilerParams(
            collective_id=0, has_side_effects=True, vmem_limit_bytes=58 * 1024 * 1024
        ),
    )(*operands, block_mask)
    worked = [pltpu.with_memory_space_constraint(a, pltpu.VMEM) for a in worked]
    output, grad_tokens, grad_up, grad_down = pl.pallas_call(
        hand_out,
        out_shape=result,
        in_specs=[anywhere] * 4,
        out_specs=(anywhere,) * 4,
        scratch_shapes=[pltpu.SemaphoreType.DMA((8,))],
        compiler_params=pltpu.CompilerParams(vmem_limit_bytes=1024 * 1024),
    )(*worked)
    return output, grad_tokens, grad_up[None], grad_down[None]


def solution(mesh):
    placed = (
        P("seq", "tp"),
        P(("seq", "tp"), None, None, None),
        P(("seq", "tp"), None, None, None),
        P(("seq", "tp"), None),
        P("seq", "tp"),
    )
    return jax.shard_map(
        shards,
        mesh=mesh,
        in_specs=placed,
        out_specs=(
            P("seq", "tp"),
            P("seq", "tp"),
            P(("seq", "tp"), None, None, None),
            P(("seq", "tp"), None, None, None),
        ),
        check_vma=False,
    )
```

```python
import functools
import math

import jax
import jax.numpy as jnp
from jax import lax
from jax.experimental import pallas as pl
from jax.experimental.pallas import tpu as pltpu
from jax.sharding import PartitionSpec as P

MESH = pl.DeviceIdType.MESH
F32 = jnp.float32
BF16 = jnp.bfloat16
ROWS = 512
PART = 128
PIECES = ROWS // PART
FIRST = PIECES // 2
TILE = 256
PER_TILE = TILE // PART
THIRDS = 3
G = 256
LEVELS = 6
WIDE = LEVELS * G
NEAR = {"x": 4, "y": 2}
FAR = {"x": 5, "y": 3}
SCALE = math.sqrt(2.0 / math.pi)
CUBE = 0.044715


def numbering():
    keys = []
    for which in range(2):
        keys += [(name, which, j) for name in ("z1", "z3", "zr", "out1", "out3", "half") for j in range(PIECES)]
        keys += [
            (name, axis, which, slot, j)
            for name in ("near", "far", "term", "sum")
            for axis in "xy"
            for slot in range(2)
            for j in range(PIECES)
        ]
        keys += [("weight", which)] + [("grad", which, k) for k in range(LEVELS // THIRDS)]
    keys += [("last", axis, j) for axis in "xy" for j in range(PIECES)]
    return {key: n for n, key in enumerate(keys)}


def family(key):
    name = key[0]
    if name in ("weight", "grad"):
        return key
    if name in ("near", "far", "term", "sum"):
        return name, key[2], key[3]
    if name == "last":
        return (name,)
    return {"z1": "z", "z3": "z", "zr": "middle", "half": "middle", "out1": "out", "out3": "out"}[name], key[1]


NUMBER = numbering()
COPIES = len(NUMBER)
FAMILIES = {name: n for n, name in enumerate(dict.fromkeys(family(key) for key in NUMBER))}

ORDER = (
    ("ox", 0, 2), ("oz", 0, 2), ("ox", 0, 3), ("sd",), ("oz", 0, 0), ("oz", 0, 1), ("ox", 1, 2), ("su",),
    ("ox", 0, 0), ("oz", 0, 3), ("oz", 1, 0), ("rx", 0, 0, 2), ("ox", 0, 1), ("rx", 0, 0, 3), ("rz", 0, 1),
    ("rx", 1, 0, 2), ("ox", 1, 3), ("rz", 0, 2), ("rz", 0, 0), ("rz", 0, 3), ("ox", 1, 0), ("oz", 1, 3),
    ("rx", 0, 0, 0), ("F", 0, 1), ("rz", 1, 0), ("ox", 1, 1), ("oz", 1, 1), ("rx", 0, 0, 1), ("rx", 1, 0, 3),
    ("ot", 0, 1), ("tw",), ("ot", 0, 2), ("ot", 0, 0), ("oz", 1, 2), ("rx", 1, 0, 0), ("F", 0, 0), ("rx", 0, 1, 1),
    ("rz", 1, 3), ("TN", 0, 0, 1), ("ot", 1, 0), ("rx", 1, 0, 1), ("ot", 0, 3), ("th", 0), ("J", 0, 0, 2),
    ("rz", 1, 1), ("rx", 0, 1, 0), ("rz", 1, 2), ("B", 0, 1), ("Z", 0, 0, 3), ("rx", 0, 1, 2), ("ta", 0, 0),
    ("ot", 1, 3), ("TF", 0, 0, 0), ("TN", 0, 0, 0), ("Z", 0, 0, 2), ("rx", 0, 1, 3), ("TN", 1, 0, 1),
    ("rx", 1, 1, 0), ("ot", 1, 1), ("ot", 1, 2), ("F", 1, 0), ("TF", 0, 1, 0), ("rx", 1, 1, 3), ("W", ("weight", 1)),
    ("TF", 1, 0, 1), ("S", 0, 1, 1), ("S", 0, 0, 0), ("J", 0, 0, 3), ("W", ("weight", 0)), ("F", 1, 1), ("ta", 0, 1),
    ("W", ("z", 0)), ("S", 0, 0, 1), ("S", 0, 1, 0), ("TN", 0, 1, 0), ("W", ("near", 0, 0)), ("TF", 0, 0, 1),
    ("rx", 1, 1, 2), ("Z", 1, 0, 2), ("TF", 0, 1, 1), ("rx", 1, 1, 1), ("ta", 1, 1), ("TN", 0, 1, 1), ("B", 0, 0),
    ("TF", 1, 0, 0), ("J", 0, 1, 1), ("ta", 1, 0), ("J", 0, 1, 0), ("S", 0, 1, 3), ("W", ("near", 1, 0)),
    ("S", 0, 0, 3), ("C", 0, 0, 2), ("W", ("far", 0, 0)), ("Z", 0, 1, 0), ("S", 0, 1, 2), ("B", 1, 1),
    ("TF", 1, 1, 1), ("Z", 1, 0, 3), ("J", 0, 0, 0), ("W", ("z", 1)), ("TN", 1, 1, 1), ("J", 0, 0, 1),
    ("S", 1, 1, 3), ("B", 1, 0), ("TF", 1, 1, 0), ("S", 1, 1, 0), ("S", 1, 1, 1), ("W", ("far", 1, 0)),
    ("S", 1, 1, 2), ("W", ("near", 0, 1)), ("J", 0, 1, 3), ("C", 0, 1, 0), ("TN", 1, 1, 0), ("Z", 1, 1, 0),
    ("G", 1, 1), ("Z", 1, 1, 1), ("J", 1, 1, 3), ("C", 0, 1, 1), ("th", 1), ("J", 1, 1, 0), ("TN", 1, 0, 0),
    ("S", 1, 0, 3), ("PO", 0, 0), ("S", 1, 0, 0), ("W", ("far", 0, 1)), ("S", 1, 0, 2), ("J", 1, 1, 1),
    ("C", 0, 1, 3), ("Z", 0, 1, 1), ("W", ("near", 1, 1)), ("J", 0, 1, 2), ("G", 0, 0), ("J", 1, 1, 2),
    ("C", 1, 1, 3), ("S", 0, 0, 2), ("PO", 0, 1), ("RL", 3), ("C", 1, 1, 0), ("S", 1, 0, 1), ("G", 1, 0),
    ("C", 1, 1, 1), ("J", 1, 0, 0), ("C", 0, 1, 2), ("PO", 1, 3), ("RL", 0), ("PO", 0, 3), ("J", 1, 0, 3),
    ("W", ("far", 1, 1)), ("C", 1, 1, 2), ("PO", 1, 0), ("RL", 1), ("G", 0, 1), ("J", 1, 0, 2), ("PO", 0, 2),
    ("RL", 2), ("GS", 1, 0), ("PO", 1, 1), ("J", 1, 0, 1), ("PO", 1, 2), ("C", 0, 0, 1), ("W", ("term", 0, 1)),
    ("C", 1, 0, 3), ("GS", 0, 0), ("GS", 1, 1), ("FIN", 0, 1), ("FIN", 1, 3), ("C", 1, 0, 0), ("W", ("sum", 0, 0)),
    ("C", 0, 0, 3), ("FIN", 0, 3), ("C", 0, 0, 0), ("FIN", 0, 0), ("FIN", 0, 2), ("GS", 0, 1), ("W", ("term", 1, 1)),
    ("FIN", 1, 0), ("C", 1, 0, 2), ("FIN", 1, 2), ("C", 1, 0, 1), ("FIN", 1, 1),
    ("W", ("middle", 0), ("middle", 1), ("out", 0), ("term", 0, 0), ("out", 1), ("sum", 0, 1), ("grad", 1, 1), ("sum", 1, 1), ("term", 1, 0), ("grad", 0, 0), ("last",), ("grad", 1, 0), ("sum", 1, 0), ("grad", 0, 1)),
)


def flip(index, bit):
    return index + bit - 2 * bit * lax.rem(lax.div(index, bit), 2)


def kernel(
    tok, cot, up, down, mask, out, gtok, gup, gdown,
    held, held_t, raw, uall, dall, uall_t, dall_t, act, act_t, gpre, slope,
    term_send, term_recv, near_term, sum_send, sum_recv, base, z_term,
    half_send, half_recv, last_recv, z_send, z_recv,
    grad_own, grad_peer, grad_recv,
    sends, recvs, local,
):
    shared = (tok, cot)
    seq, tp = lax.axis_index("seq"), lax.axis_index("tp")
    place = {
        "core": (flip(seq, 1), tp),
        "z1": (seq, flip(tp, 1)),
        "z3": (flip(seq, 2), flip(tp, 1)),
        "x1": (seq, flip(tp, 8)),
        "x3": (seq, flip(flip(tp, 8), 16)),
        "y1": (seq, flip(tp, 2)),
        "y3": (seq, flip(flip(tp, 2), 4)),
    }

    def remote(src, dst, key, target):
        return pltpu.make_async_remote_copy(
            src_ref=src,
            dst_ref=dst,
            send_sem=sends.at[FAMILIES[family(key)]],
            recv_sem=recvs.at[NUMBER[key]],
            device_id=place[target],
            device_id_type=MESH,
        )

    def rows(slot, j):
        start = slot * ROWS + j * PART
        return pl.ds(start if isinstance(j, int) else pl.multiple_of(start, PART), PART)

    def piece(j):
        return pl.ds(j * PART, PART)

    def columns(level):
        return pl.ds(level * G, G)

    def transfer(key):
        name, rest = key[0], key[1:]
        if name == "weight":
            if rest[0] == 0:
                return remote(uall.at[:, pl.ds(0, G)], uall.at[:, pl.ds(G, G)], key, "core")
            return remote(dall.at[pl.ds(0, G)], dall.at[pl.ds(G, G)], key, "core")
        if name == "grad":
            at = pl.ds(rest[1] * THIRDS, THIRDS)
            return remote(grad_peer.at[rest[0], at], grad_recv.at[rest[0], at], key, "core")
        if name == "last":
            a, j = "xy".index(rest[0]), rest[1]
            return remote(term_recv.at[0, a, rows(0, j)], last_recv.at[a, piece(j)], key, rest[0] + "3")
        if name in ("near", "far", "term", "sum"):
            axis, which, slot, j = rest
            a, at = "xy".index(axis), rows(slot, j)
            if name == "near":
                src = held.at[which, 0, at] if slot else shared[which].at[piece(j)]
                return remote(src, held.at[which, NEAR[axis], at], key, axis + "1")
            if name == "far":
                return remote(held.at[which, NEAR[axis], at], held.at[which, FAR[axis], at], key, axis + "3")
            if name == "term":
                target = axis + ("1" if (which, slot) == (0, 0) else "3")
                return remote(term_send.at[which, a, at], term_recv.at[which, a, at], key, target)
            return remote(sum_send.at[which, a, at], sum_recv.at[which, a, at], key, axis + "1")
        which, j = rest
        if name == "z1":
            return remote(shared[which].at[piece(j)], held.at[which, 1, rows(0, j)], key, "z1")
        if name == "z3":
            return remote(shared[which].at[piece(j)], held.at[which, 1, rows(1, j)], key, "z3")
        onward = "z3" if j < FIRST else "z1"
        if name == "zr":
            return remote(held.at[which, 1, rows(int(j >= FIRST), j)], held.at[which, 0, rows(1, j)], key, onward)
        if name == "half":
            return remote(half_send.at[which, piece(j)], half_recv.at[which, piece(j)], key, onward)
        slot = int(name == "out3")
        return remote(z_send.at[which, rows(slot, j)], z_recv.at[which, rows(slot, j)], key, "z3" if slot else "z1")

    started, landed, copied, sent = set(), set(), set(), set()

    def send(*keys):
        for key in keys:
            started.add(key)
            transfer(key).start()

    def need(*keys):
        for key in keys:
            if key not in landed:
                landed.add(key)
                transfer(key).wait_recv()

    own = [
        pltpu.make_async_copy(shared[which], held.at[which, 0, pl.ds(0, ROWS)], local.at[which])
        for which in range(2)
    ]
    loads = [pltpu.make_async_copy(ref, raw.at[which], local.at[2 + which]) for which, ref in enumerate((up, down))]
    for copy in loads + own:
        copy.start()

    barrier = pltpu.get_barrier_semaphore()
    for target in place.values():
        pl.semaphore_signal(barrier, inc=1, device_id=target, device_id_type=MESH)
    pl.semaphore_wait(barrier, len(place))

    def scale_up(k, carry):
        factor = mask[0, k].astype(F32)
        uall[pl.ds(pl.multiple_of(k * G, G), G), pl.ds(0, G)] = (raw[0, k].astype(F32) * factor).astype(BF16)
        return carry

    def scale_down(k, carry):
        factor = mask[0, k].astype(F32)
        dall[pl.ds(0, G), pl.ds(pl.multiple_of(k * G, G), G)] = (raw[1, k].astype(F32) * factor).astype(BF16)
        return carry

    def wide(which, at):
        return jnp.concatenate([held[which, level, at] for level in range(LEVELS)], axis=1)

    def tile(slot, t):
        return pl.ds(slot * ROWS + t * TILE, TILE)

    def own_z(which, j):
        send(("z1", which, j), ("z3", which, j))

    def own_xy(which, j):
        send(("near", "x", which, 0, j), ("near", "y", which, 0, j))

    def relay_z(which, j):
        need(("z1" if j < FIRST else "z3", which, j))
        send(("zr", which, j))

    def other(which, j):
        need(("zr", which, j))
        send(("near", "x", which, 1, j), ("near", "y", which, 1, j))

    def relay_xy(which, slot, j):
        for axis in "xy":
            need(("near", axis, which, slot, j))
            send(("far", axis, which, slot, j))

    def mask_up():
        loads[0].wait()
        lax.fori_loop(0, LEVELS, scale_up, 0)
        send(("weight", 0))

    def mask_down():
        loads[1].wait()
        lax.fori_loop(0, LEVELS, scale_down, 0)
        send(("weight", 1))

    def turn_weights():
        need(("weight", 0), ("weight", 1))

        def body(k, carry):
            at = pl.ds(pl.multiple_of(k * G, G), G)
            dall_t[at, :] = dall[:, at].T
            uall_t[:, at] = uall[at, :].T
            return carry

        lax.fori_loop(0, LEVELS, body, 0)

    def turn_held(slot):
        def body(k, carry):
            at = pl.ds(pl.multiple_of(k * G, G), G)
            held_t[at, pl.ds(slot * ROWS, ROWS)] = held[0, k, pl.ds(slot * ROWS, ROWS)].T
            return carry

        lax.fori_loop(0, LEVELS, body, 0)

    def turn_act(slot, t):
        act_t[:, tile(slot, t)] = act[tile(slot, t), :].T

    def inputs(which, slot, t):
        if slot == 0 and ("own", which) not in copied:
            copied.add(("own", which))
            own[which].wait()
        for j in range(t * PER_TILE, (t + 1) * PER_TILE):
            need(("z3" if slot else "z1", which, j))
            for axis in "xy":
                need(("far", axis, which, slot, j))

    def forward(slot, t):
        inputs(0, slot, t)
        need(("weight", 0), ("weight", 1))
        at = tile(slot, t)
        pre = jnp.dot(wide(0, at), uall[...], preferred_element_type=F32)
        square = pre * pre
        tanh = jnp.tanh(SCALE * pre * (1.0 + CUBE * square))
        cdf = 0.5 + 0.5 * tanh
        act[at, :] = (pre * cdf).astype(BF16)
        slope[at, :] = cdf + (0.5 * SCALE) * pre * (1.0 - tanh * tanh) * (1.0 + (3.0 * CUBE) * square)

    def backward(slot, t):
        inputs(1, slot, t)
        at = tile(slot, t)
        gact = jnp.dot(wide(1, at), dall_t[...], preferred_element_type=F32)
        gpre[at, :] = (gact * slope[at, :]).astype(BF16)

    def product(which, slot, t, level):
        if which:
            return jnp.dot(gpre[tile(slot, t), :], uall_t[:, columns(level)], preferred_element_type=F32)
        return jnp.dot(act[tile(slot, t), :], dall[:, columns(level)], preferred_element_type=F32)

    def far_terms(which, slot, t):
        for a, axis in enumerate("xy"):
            term_send[which, a, tile(slot, t)] = product(which, slot, t, FAR[axis]).astype(BF16)

    def near_terms(which, slot, t):
        at = tile(slot, t)
        for a, axis in enumerate("xy"):
            near_term[which, a, at] = product(which, slot, t, NEAR[axis])
        z_term[which, at] = product(which, slot, t, 1)
        base[which, at] = product(which, slot, t, 0)

    def send_term(which, slot, j):
        send(("term", "x", which, slot, j), ("term", "y", which, slot, j))

    def hand_on(j):
        for axis in "xy":
            need(("term", axis, 0, 0, j))
            send(("last", axis, j))

    def join(which, slot, j):
        at = rows(slot, j)
        for a, axis in enumerate("xy"):
            total = near_term[which, a, at]
            if (which, slot) != (0, 0):
                need(("term", axis, which, slot, j))
                total = total + term_recv[which, a, at].astype(F32)
            sum_send[which, a, at] = total.astype(BF16)
            send(("sum", axis, which, slot, j))

    def collect(which, slot, j):
        at = rows(slot, j)
        need(("sum", "x", which, slot, j), ("sum", "y", which, slot, j))
        total = base[which, at] + sum_recv[which, 0, at].astype(F32) + sum_recv[which, 1, at].astype(F32)
        if slot == 0:
            base[which, at] = total
        else:
            half_send[which, piece(j)] = total.astype(BF16)
            send(("half", which, j))

    def plain(which, slot, j):
        z_send[which, rows(slot, j)] = z_term[which, rows(slot, j)].astype(BF16)
        send(("out3" if slot else "out1", which, j))

    def pass_on(which, j):
        slot = int(j >= FIRST)
        at = rows(slot, j)
        need(("half", which, j))
        z_send[which, at] = (z_term[which, at] + half_recv[which, piece(j)].astype(F32)).astype(BF16)
        send(("out3" if slot else "out1", which, j))

    def finish(which, j):
        need(("out1", which, j), ("out3", which, j))
        total = base[which, rows(0, j)] + z_recv[which, rows(0, j)].astype(F32) + z_recv[which, rows(1, j)].astype(F32)
        if which == 0:
            need(("last", "x", j), ("last", "y", j))
            total = total + last_recv[0, piece(j)].astype(F32) + last_recv[1, piece(j)].astype(F32)
        (gtok if which else out)[piece(j), :] = total.astype(BF16)

    def grads(which, third):
        def body(k, carry):
            at = pl.ds(pl.multiple_of(k * G, G), G)
            if which:
                both = jnp.dot(act_t[...], held[1, k], preferred_element_type=F32)
                grad_own[1, k] = both[:G]
                grad_peer[1, k] = both[G:]
            else:
                both = jnp.dot(held_t[at, :], gpre[...], preferred_element_type=F32)
                grad_own[0, k] = both[:, :G]
                grad_peer[0, k] = both[:, G:]
            return carry

        lax.fori_loop(third * THIRDS, (third + 1) * THIRDS, body, 0)
        send(("grad", which, third))

    def write_grad(which, k):
        return pltpu.make_async_copy(grad_own.at[which, k], (gdown if which else gup).at[k], local.at[4 + which * LEVELS + k])

    def grads_sum(which, third):
        need(("grad", which, third))

        def body(k, carry):
            grad_own[which, k] = (grad_own[which, k] + grad_recv[which, k]) * mask[0, k].astype(F32)
            write_grad(which, k).start()
            return carry

        lax.fori_loop(third * THIRDS, (third + 1) * THIRDS, body, 0)

    def finish_sends(*names):
        for name in names:
            sent.add(name)
            if name[0] in ("weight", "grad"):
                transfer(name).wait_send()
            else:
                pltpu.make_async_remote_copy(
                    src_ref=held.at[0, 0],
                    dst_ref=held.at[0, 0],
                    send_sem=sends.at[FAMILIES[name]],
                    recv_sem=recvs.at[0],
                    device_id=place["z1"],
                    device_id_type=MESH,
                ).wait_send()

    steps = {
        "W": finish_sends,
        "oz": own_z, "ox": own_xy, "rz": relay_z, "ot": other, "rx": relay_xy, "su": mask_up, "sd": mask_down,
        "tw": turn_weights, "th": turn_held, "ta": turn_act, "F": forward, "B": backward, "TF": far_terms,
        "TN": near_terms, "S": send_term, "RL": hand_on, "J": join, "C": collect, "Z": plain, "PO": pass_on,
        "FIN": finish, "G": grads, "GS": grads_sum,
    }
    for step in ORDER:
        steps[step[0]](*step[1:])

    assert started == landed == set(NUMBER)
    for which in range(2):
        for k in range(LEVELS):
            write_grad(which, k).wait()
    assert sent == set(FAMILIES)


def hand_out(*refs):
    sources, results, sems = refs[:4], refs[4:8], refs[8]
    copies = []
    for src, dst in zip(sources, results):
        if len(src.shape) == 2:
            pairs = [(src, dst)]
        else:
            pairs = [(src.at[pl.ds(k, 2)], dst.at[pl.ds(k, 2)]) for k in range(0, LEVELS, 2)]
        for a, b in pairs:
            copies.append(pltpu.make_async_copy(a, b, sems.at[len(copies)]))
    for copy in copies:
        copy.start()
    for copy in copies:
        copy.wait()


def shards(tokens, up_weight, down_weight, block_mask, cotangent):
    anywhere = pl.BlockSpec(memory_space=pl.ANY)
    vmem = pl.BlockSpec(memory_space=pltpu.VMEM)
    both = 2 * ROWS
    result = (
        jax.ShapeDtypeStruct((ROWS, G), BF16),
        jax.ShapeDtypeStruct((ROWS, G), BF16),
        jax.ShapeDtypeStruct((LEVELS, G, G), F32),
        jax.ShapeDtypeStruct((LEVELS, G, G), F32),
    )
    operands = [pltpu.with_memory_space_constraint(a, pltpu.HBM) for a in (tokens, cotangent, up_weight[0], down_weight[0])]
    worked = pl.pallas_call(
        kernel,
        out_shape=tuple(pltpu.VMEM(a.shape, a.dtype) for a in result),
        in_specs=[anywhere, anywhere, anywhere, anywhere, pl.BlockSpec(memory_space=pltpu.SMEM)],
        out_specs=(vmem, vmem, anywhere, anywhere),
        scratch_shapes=[
            pltpu.VMEM((2, LEVELS, both, G), BF16),
            pltpu.VMEM((WIDE, both), BF16),
            pltpu.VMEM((2, LEVELS, G, G), BF16),
            pltpu.VMEM((WIDE, 2 * G), BF16),
            pltpu.VMEM((2 * G, WIDE), BF16),
            pltpu.VMEM((2 * G, WIDE), BF16),
            pltpu.VMEM((WIDE, 2 * G), BF16),
            pltpu.VMEM((both, 2 * G), BF16),
            pltpu.VMEM((2 * G, both), BF16),
            pltpu.VMEM((both, 2 * G), BF16),
            pltpu.VMEM((both, 2 * G), F32),
            pltpu.VMEM((2, 2, both, G), BF16),
            pltpu.VMEM((2, 2, both, G), BF16),
            pltpu.VMEM((2, 2, both, G), F32),
            pltpu.VMEM((2, 2, both, G), BF16),
            pltpu.VMEM((2, 2, both, G), BF16),
            pltpu.VMEM((2, both, G), F32),
            pltpu.VMEM((2, both, G), F32),
            pltpu.VMEM((2, ROWS, G), BF16),
            pltpu.VMEM((2, ROWS, G), BF16),
            pltpu.VMEM((2, ROWS, G), BF16),
            pltpu.VMEM((2, both, G), BF16),
            pltpu.VMEM((2, both, G), BF16),
            pltpu.VMEM((2, LEVELS, G, G), F32),
            pltpu.VMEM((2, LEVELS, G, G), F32),
            pltpu.VMEM((2, LEVELS, G, G), F32),
            pltpu.SemaphoreType.DMA((len(FAMILIES),)),
            pltpu.SemaphoreType.DMA((COPIES,)),
            pltpu.SemaphoreType.DMA((4 + 2 * LEVELS,)),
        ],
        compiler_params=pltpu.CompilerParams(
            collective_id=0, has_side_effects=True, vmem_limit_bytes=58 * 1024 * 1024
        ),
    )(*operands, block_mask)
    worked = [pltpu.with_memory_space_constraint(a, pltpu.VMEM) for a in worked]
    output, grad_tokens, grad_up, grad_down = pl.pallas_call(
        hand_out,
        out_shape=result,
        in_specs=[anywhere] * 4,
        out_specs=(anywhere,) * 4,
        scratch_shapes=[pltpu.SemaphoreType.DMA((8,))],
        compiler_params=pltpu.CompilerParams(vmem_limit_bytes=1024 * 1024),
    )(*worked)
    return output, grad_tokens, grad_up[None], grad_down[None]


def solution(mesh):
    placed = (
        P("seq", "tp"),
        P(("seq", "tp"), None, None, None),
        P(("seq", "tp"), None, None, None),
        P(("seq", "tp"), None),
        P("seq", "tp"),
    )
    return jax.shard_map(
        shards,
        mesh=mesh,
        in_specs=placed,
        out_specs=(
            P("seq", "tp"),
            P("seq", "tp"),
            P(("seq", "tp"), None, None, None),
            P(("seq", "tp"), None, None, None),
        ),
        check_vma=False,
    )
```

```python
import functools
import math

import jax
import jax.numpy as jnp
from jax import lax
from jax.experimental import pallas as pl
from jax.experimental.pallas import tpu as pltpu
from jax.sharding import PartitionSpec as P

MESH = pl.DeviceIdType.MESH
F32 = jnp.float32
BF16 = jnp.bfloat16
ROWS = 512
PART = 128
PIECES = ROWS // PART
FIRST = PIECES // 2
TILE = 256
PER_TILE = TILE // PART
THIRDS = 3
G = 256
LEVELS = 6
WIDE = LEVELS * G
NEAR = {"x": 4, "y": 2}
FAR = {"x": 5, "y": 3}
SCALE = math.sqrt(2.0 / math.pi)
CUBE = 0.044715


def numbering():
    keys = []
    for which in range(2):
        keys += [(name, which, j) for name in ("z1", "z3", "zr", "out1", "out3", "half") for j in range(PIECES)]
        keys += [
            (name, axis, which, slot, j)
            for name in ("near", "far", "term", "sum")
            for axis in "xy"
            for slot in range(2)
            for j in range(PIECES)
        ]
        keys += [("weight", which)] + [("grad", which, k) for k in range(LEVELS // THIRDS)]
    keys += [("last", axis, j) for axis in "xy" for j in range(PIECES)]
    return {key: n for n, key in enumerate(keys)}


def family(key):
    name = key[0]
    if name in ("weight", "grad"):
        return key
    if name in ("near", "far", "term", "sum"):
        return name, key[2], key[3]
    if name == "last":
        return (name,)
    return {"z1": "z", "z3": "z", "zr": "middle", "half": "middle", "out1": "out", "out3": "out"}[name], key[1]


NUMBER = numbering()
COPIES = len(NUMBER)
FAMILIES = {name: n for n, name in enumerate(dict.fromkeys(family(key) for key in NUMBER))}

ORDER = (
    ("oz", 0, 1), ("ox", 1, 3), ("ox", 0, 1), ("oz", 0, 3), ("sd",), ("su",), ("ox", 0, 2), ("ox", 0, 0),
    ("oz", 0, 2), ("oz", 0, 0), ("rx", 0, 0, 1), ("ox", 0, 3), ("oz", 1, 2), ("rx", 1, 0, 3), ("ox", 1, 0),
    ("rz", 0, 0), ("ox", 1, 1), ("rz", 0, 3), ("rx", 0, 0, 0), ("rz", 0, 1), ("rz", 1, 2), ("ox", 1, 2),
    ("rx", 0, 0, 2), ("oz", 1, 1), ("oz", 1, 3), ("rx", 0, 0, 3), ("ot", 0, 0), ("rx", 1, 0, 0), ("F", 0, 0),
    ("oz", 1, 0), ("rz", 0, 2), ("ot", 0, 3), ("rx", 1, 0, 2), ("ot", 1, 2), ("ta", 0, 0), ("ot", 0, 1),
    ("rz", 1, 1), ("rx", 0, 1, 0), ("rx", 1, 0, 1), ("TN", 0, 0, 0), ("tw",), ("rz", 1, 0), ("rz", 1, 3),
    ("rx", 0, 1, 3), ("ot", 1, 1), ("F", 0, 1), ("ot", 0, 2), ("rx", 0, 1, 1), ("TF", 0, 0, 1), ("TF", 0, 0, 0),
    ("TN", 0, 0, 1), ("Z", 0, 0, 2), ("rx", 1, 1, 2), ("ot", 1, 0), ("J", 0, 0, 0), ("Z", 0, 0, 3), ("ot", 1, 3),
    ("B", 0, 0), ("rx", 1, 1, 1), ("rx", 0, 1, 2), ("J", 0, 0, 3), ("F", 1, 0), ("TF", 0, 1, 0), ("S", 0, 1, 1),
    ("S", 0, 0, 1), ("J", 0, 0, 2), ("ta", 0, 1), ("S", 0, 1, 0), ("TN", 0, 1, 0), ("B", 0, 1), ("TN", 1, 0, 1),
    ("rx", 1, 1, 0), ("S", 0, 0, 2), ("S", 0, 0, 3), ("ta", 1, 0), ("F", 1, 1), ("TF", 0, 1, 1), ("S", 0, 1, 3),
    ("th", 0), ("ta", 1, 1), ("J", 0, 1, 0), ("rx", 1, 1, 3), ("J", 0, 1, 1), ("TF", 1, 0, 1), ("W", ("weight", 1)),
    ("TN", 0, 1, 1), ("W", ("weight", 0)), ("B", 1, 0), ("S", 0, 1, 2), ("TF", 1, 1, 0), ("S", 1, 1, 0),
    ("W", ("z", 0)), ("TN", 1, 0, 0), ("Z", 0, 1, 0), ("W", ("near", 0, 0)), ("th", 1), ("B", 1, 1), ("J", 0, 1, 3),
    ("TF", 1, 0, 0), ("S", 1, 1, 1), ("Z", 1, 0, 2), ("Z", 1, 0, 3), ("TN", 1, 1, 0), ("Z", 0, 1, 1), ("J", 0, 0, 1),
    ("W", ("near", 1, 0)), ("TF", 1, 1, 1), ("S", 1, 1, 2), ("S", 1, 1, 3), ("J", 0, 1, 2), ("W", ("far", 0, 0)),
    ("C", 0, 1, 1), ("J", 1, 1, 0), ("G", 0, 1), ("C", 0, 1, 0), ("W", ("z", 1)), ("C", 0, 1, 3), ("S", 1, 0, 2),
    ("TN", 1, 1, 1), ("J", 1, 1, 1), ("Z", 1, 1, 1), ("G", 1, 0), ("Z", 1, 1, 0), ("S", 1, 0, 0), ("PO", 0, 1),
    ("W", ("far", 1, 0)), ("J", 1, 1, 2), ("J", 1, 1, 3), ("C", 0, 1, 2), ("S", 1, 0, 3), ("PO", 0, 0),
    ("S", 1, 0, 1), ("C", 0, 0, 1), ("PO", 0, 3), ("W", ("near", 0, 1)), ("GS", 0, 1), ("G", 1, 1), ("J", 1, 0, 2),
    ("C", 1, 1, 1), ("C", 0, 0, 3), ("RL", 1), ("GS", 1, 0), ("S", 0, 0, 0), ("C", 1, 1, 2), ("RL", 3),
    ("W", ("near", 1, 1)), ("C", 1, 1, 0), ("RL", 2), ("PO", 0, 2), ("W", ("far", 0, 1)), ("C", 1, 1, 3),
    ("J", 1, 0, 3), ("G", 0, 0), ("PO", 1, 1), ("J", 1, 0, 0), ("PO", 1, 2), ("RL", 0), ("C", 1, 0, 2),
    ("C", 0, 0, 2), ("PO", 1, 0), ("J", 1, 0, 1), ("PO", 1, 3), ("GS", 1, 1), ("C", 1, 0, 3), ("FIN", 0, 2),
    ("FIN", 0, 1), ("FIN", 1, 2), ("C", 0, 0, 0), ("FIN", 0, 3), ("FIN", 0, 0), ("GS", 0, 0), ("C", 1, 0, 0),
    ("W", ("far", 1, 1)), ("FIN", 1, 0), ("C", 1, 0, 1), ("FIN", 1, 1), ("FIN", 1, 3),
    ("W", ("middle", 0), ("middle", 1), ("out", 0), ("sum", 0, 0), ("term", 0, 1), ("term", 0, 0), ("sum", 0, 1), ("term", 1, 1), ("out", 1), ("sum", 1, 1), ("grad", 0, 1), ("term", 1, 0), ("grad", 1, 0), ("grad", 1, 1), ("sum", 1, 0), ("last",), ("grad", 0, 0)),
)


def flip(index, bit):
    return index + bit - 2 * bit * lax.rem(lax.div(index, bit), 2)


def kernel(
    tok, cot, up, down, mask, out, gtok, gup, gdown,
    held, held_t, raw, uall, dall, uall_t, dall_t, act, act_t, gpre, slope,
    term_send, term_recv, near_term, sum_send, sum_recv, base, z_term,
    half_send, half_recv, last_recv, z_send, z_recv,
    grad_own, grad_peer, grad_recv,
    sends, recvs, local,
):
    shared = (tok, cot)
    seq, tp = lax.axis_index("seq"), lax.axis_index("tp")
    place = {
        "core": (flip(seq, 1), tp),
        "z1": (seq, flip(tp, 1)),
        "z3": (flip(seq, 2), flip(tp, 1)),
        "x1": (seq, flip(tp, 8)),
        "x3": (seq, flip(flip(tp, 8), 16)),
        "y1": (seq, flip(tp, 2)),
        "y3": (seq, flip(flip(tp, 2), 4)),
    }

    def remote(src, dst, key, target):
        return pltpu.make_async_remote_copy(
            src_ref=src,
            dst_ref=dst,
            send_sem=sends.at[FAMILIES[family(key)]],
            recv_sem=recvs.at[NUMBER[key]],
            device_id=place[target],
            device_id_type=MESH,
        )

    def rows(slot, j):
        start = slot * ROWS + j * PART
        return pl.ds(start if isinstance(j, int) else pl.multiple_of(start, PART), PART)

    def piece(j):
        return pl.ds(j * PART, PART)

    def columns(level):
        return pl.ds(level * G, G)

    def transfer(key):
        name, rest = key[0], key[1:]
        if name == "weight":
            if rest[0] == 0:
                return remote(uall.at[:, pl.ds(0, G)], uall.at[:, pl.ds(G, G)], key, "core")
            return remote(dall.at[pl.ds(0, G)], dall.at[pl.ds(G, G)], key, "core")
        if name == "grad":
            at = pl.ds(rest[1] * THIRDS, THIRDS)
            return remote(grad_peer.at[rest[0], at], grad_recv.at[rest[0], at], key, "core")
        if name == "last":
            a, j = "xy".index(rest[0]), rest[1]
            return remote(term_recv.at[0, a, rows(0, j)], last_recv.at[a, piece(j)], key, rest[0] + "3")
        if name in ("near", "far", "term", "sum"):
            axis, which, slot, j = rest
            a, at = "xy".index(axis), rows(slot, j)
            if name == "near":
                src = held.at[which, 0, at] if slot else shared[which].at[piece(j)]
                return remote(src, held.at[which, NEAR[axis], at], key, axis + "1")
            if name == "far":
                return remote(held.at[which, NEAR[axis], at], held.at[which, FAR[axis], at], key, axis + "3")
            if name == "term":
                target = axis + ("1" if (which, slot) == (0, 0) else "3")
                return remote(term_send.at[which, a, at], term_recv.at[which, a, at], key, target)
            return remote(sum_send.at[which, a, at], sum_recv.at[which, a, at], key, axis + "1")
        which, j = rest
        if name == "z1":
            return remote(shared[which].at[piece(j)], held.at[which, 1, rows(0, j)], key, "z1")
        if name == "z3":
            return remote(shared[which].at[piece(j)], held.at[which, 1, rows(1, j)], key, "z3")
        onward = "z3" if j < FIRST else "z1"
        if name == "zr":
            return remote(held.at[which, 1, rows(int(j >= FIRST), j)], held.at[which, 0, rows(1, j)], key, onward)
        if name == "half":
            return remote(half_send.at[which, piece(j)], half_recv.at[which, piece(j)], key, onward)
        slot = int(name == "out3")
        return remote(z_send.at[which, rows(slot, j)], z_recv.at[which, rows(slot, j)], key, "z3" if slot else "z1")

    started, landed, copied, sent = set(), set(), set(), set()

    def send(*keys):
        for key in keys:
            started.add(key)
            transfer(key).start()

    def need(*keys):
        for key in keys:
            if key not in landed:
                landed.add(key)
                transfer(key).wait_recv()

    own = [
        pltpu.make_async_copy(shared[which], held.at[which, 0, pl.ds(0, ROWS)], local.at[which])
        for which in range(2)
    ]
    loads = [pltpu.make_async_copy(ref, raw.at[which], local.at[2 + which]) for which, ref in enumerate((up, down))]
    for copy in loads + own:
        copy.start()

    barrier = pltpu.get_barrier_semaphore()
    for target in place.values():
        pl.semaphore_signal(barrier, inc=1, device_id=target, device_id_type=MESH)
    pl.semaphore_wait(barrier, len(place))

    def scale_up(k, carry):
        factor = mask[0, k].astype(F32)
        uall[pl.ds(pl.multiple_of(k * G, G), G), pl.ds(0, G)] = (raw[0, k].astype(F32) * factor).astype(BF16)
        return carry

    def scale_down(k, carry):
        factor = mask[0, k].astype(F32)
        dall[pl.ds(0, G), pl.ds(pl.multiple_of(k * G, G), G)] = (raw[1, k].astype(F32) * factor).astype(BF16)
        return carry

    def wide(which, at):
        return jnp.concatenate([held[which, level, at] for level in range(LEVELS)], axis=1)

    def tile(slot, t):
        return pl.ds(slot * ROWS + t * TILE, TILE)

    def own_z(which, j):
        send(("z1", which, j), ("z3", which, j))

    def own_xy(which, j):
        send(("near", "x", which, 0, j), ("near", "y", which, 0, j))

    def relay_z(which, j):
        need(("z1" if j < FIRST else "z3", which, j))
        send(("zr", which, j))

    def other(which, j):
        need(("zr", which, j))
        send(("near", "x", which, 1, j), ("near", "y", which, 1, j))

    def relay_xy(which, slot, j):
        for axis in "xy":
            need(("near", axis, which, slot, j))
            send(("far", axis, which, slot, j))

    def mask_up():
        loads[0].wait()
        lax.fori_loop(0, LEVELS, scale_up, 0)
        send(("weight", 0))

    def mask_down():
        loads[1].wait()
        lax.fori_loop(0, LEVELS, scale_down, 0)
        send(("weight", 1))

    def turn_weights():
        need(("weight", 0), ("weight", 1))

        def body(k, carry):
            at = pl.ds(pl.multiple_of(k * G, G), G)
            dall_t[at, :] = dall[:, at].T
            uall_t[:, at] = uall[at, :].T
            return carry

        lax.fori_loop(0, LEVELS, body, 0)

    def turn_held(slot):
        def body(k, carry):
            at = pl.ds(pl.multiple_of(k * G, G), G)
            held_t[at, pl.ds(slot * ROWS, ROWS)] = held[0, k, pl.ds(slot * ROWS, ROWS)].T
            return carry

        lax.fori_loop(0, LEVELS, body, 0)

    def turn_act(slot, t):
        act_t[:, tile(slot, t)] = act[tile(slot, t), :].T

    def inputs(which, slot, t):
        if slot == 0 and ("own", which) not in copied:
            copied.add(("own", which))
            own[which].wait()
        for j in range(t * PER_TILE, (t + 1) * PER_TILE):
            need(("z3" if slot else "z1", which, j))
            for axis in "xy":
                need(("far", axis, which, slot, j))

    def forward(slot, t):
        inputs(0, slot, t)
        need(("weight", 0), ("weight", 1))
        at = tile(slot, t)
        pre = jnp.dot(wide(0, at), uall[...], preferred_element_type=F32)
        square = pre * pre
        tanh = jnp.tanh(SCALE * pre * (1.0 + CUBE * square))
        cdf = 0.5 + 0.5 * tanh
        act[at, :] = (pre * cdf).astype(BF16)
        slope[at, :] = cdf + (0.5 * SCALE) * pre * (1.0 - tanh * tanh) * (1.0 + (3.0 * CUBE) * square)

    def backward(slot, t):
        inputs(1, slot, t)
        at = tile(slot, t)
        gact = jnp.dot(wide(1, at), dall_t[...], preferred_element_type=F32)
        gpre[at, :] = (gact * slope[at, :]).astype(BF16)

    def product(which, slot, t, level):
        if which:
            return jnp.dot(gpre[tile(slot, t), :], uall_t[:, columns(level)], preferred_element_type=F32)
        return jnp.dot(act[tile(slot, t), :], dall[:, columns(level)], preferred_element_type=F32)

    def far_terms(which, slot, t):
        for a, axis in enumerate("xy"):
            term_send[which, a, tile(slot, t)] = product(which, slot, t, FAR[axis]).astype(BF16)

    def near_terms(which, slot, t):
        at = tile(slot, t)
        for a, axis in enumerate("xy"):
            near_term[which, a, at] = product(which, slot, t, NEAR[axis])
        z_term[which, at] = product(which, slot, t, 1)
        base[which, at] = product(which, slot, t, 0)

    def send_term(which, slot, j):
        send(("term", "x", which, slot, j), ("term", "y", which, slot, j))

    def hand_on(j):
        for axis in "xy":
            need(("term", axis, 0, 0, j))
            send(("last", axis, j))

    def join(which, slot, j):
        at = rows(slot, j)
        for a, axis in enumerate("xy"):
            total = near_term[which, a, at]
            if (which, slot) != (0, 0):
                need(("term", axis, which, slot, j))
                total = total + term_recv[which, a, at].astype(F32)
            sum_send[which, a, at] = total.astype(BF16)
            send(("sum", axis, which, slot, j))

    def collect(which, slot, j):
        at = rows(slot, j)
        need(("sum", "x", which, slot, j), ("sum", "y", which, slot, j))
        total = base[which, at] + sum_recv[which, 0, at].astype(F32) + sum_recv[which, 1, at].astype(F32)
        if slot == 0:
            base[which, at] = total
        else:
            half_send[which, piece(j)] = total.astype(BF16)
            send(("half", which, j))

    def plain(which, slot, j):
        z_send[which, rows(slot, j)] = z_term[which, rows(slot, j)].astype(BF16)
        send(("out3" if slot else "out1", which, j))

    def pass_on(which, j):
        slot = int(j >= FIRST)
        at = rows(slot, j)
        need(("half", which, j))
        z_send[which, at] = (z_term[which, at] + half_recv[which, piece(j)].astype(F32)).astype(BF16)
        send(("out3" if slot else "out1", which, j))

    def finish(which, j):
        need(("out1", which, j), ("out3", which, j))
        total = base[which, rows(0, j)] + z_recv[which, rows(0, j)].astype(F32) + z_recv[which, rows(1, j)].astype(F32)
        if which == 0:
            need(("last", "x", j), ("last", "y", j))
            total = total + last_recv[0, piece(j)].astype(F32) + last_recv[1, piece(j)].astype(F32)
        (gtok if which else out)[piece(j), :] = total.astype(BF16)

    def grads(which, third):
        def body(k, carry):
            at = pl.ds(pl.multiple_of(k * G, G), G)
            if which:
                both = jnp.dot(act_t[...], held[1, k], preferred_element_type=F32)
                grad_own[1, k] = both[:G]
                grad_peer[1, k] = both[G:]
            else:
                both = jnp.dot(held_t[at, :], gpre[...], preferred_element_type=F32)
                grad_own[0, k] = both[:, :G]
                grad_peer[0, k] = both[:, G:]
            return carry

        lax.fori_loop(third * THIRDS, (third + 1) * THIRDS, body, 0)
        send(("grad", which, third))

    def write_grad(which, k):
        return pltpu.make_async_copy(grad_own.at[which, k], (gdown if which else gup).at[k], local.at[4 + which * LEVELS + k])

    def grads_sum(which, third):
        need(("grad", which, third))

        def body(k, carry):
            grad_own[which, k] = (grad_own[which, k] + grad_recv[which, k]) * mask[0, k].astype(F32)
            write_grad(which, k).start()
            return carry

        lax.fori_loop(third * THIRDS, (third + 1) * THIRDS, body, 0)

    def finish_sends(*names):
        for name in names:
            sent.add(name)
            if name[0] in ("weight", "grad"):
                transfer(name).wait_send()
            else:
                pltpu.make_async_remote_copy(
                    src_ref=held.at[0, 0],
                    dst_ref=held.at[0, 0],
                    send_sem=sends.at[FAMILIES[name]],
                    recv_sem=recvs.at[0],
                    device_id=place["z1"],
                    device_id_type=MESH,
                ).wait_send()

    steps = {
        "W": finish_sends,
        "oz": own_z, "ox": own_xy, "rz": relay_z, "ot": other, "rx": relay_xy, "su": mask_up, "sd": mask_down,
        "tw": turn_weights, "th": turn_held, "ta": turn_act, "F": forward, "B": backward, "TF": far_terms,
        "TN": near_terms, "S": send_term, "RL": hand_on, "J": join, "C": collect, "Z": plain, "PO": pass_on,
        "FIN": finish, "G": grads, "GS": grads_sum,
    }
    for step in ORDER:
        steps[step[0]](*step[1:])

    assert started == landed == set(NUMBER)
    for which in range(2):
        for k in range(LEVELS):
            write_grad(which, k).wait()
    assert sent == set(FAMILIES)


def hand_out(*refs):
    sources, results, sems = refs[:4], refs[4:8], refs[8]
    copies = []
    for src, dst in zip(sources, results):
        if len(src.shape) == 2:
            pairs = [(src, dst)]
        else:
            pairs = [(src.at[pl.ds(k, 2)], dst.at[pl.ds(k, 2)]) for k in range(0, LEVELS, 2)]
        for a, b in pairs:
            copies.append(pltpu.make_async_copy(a, b, sems.at[len(copies)]))
    for copy in copies:
        copy.start()
    for copy in copies:
        copy.wait()


def shards(tokens, up_weight, down_weight, block_mask, cotangent):
    anywhere = pl.BlockSpec(memory_space=pl.ANY)
    vmem = pl.BlockSpec(memory_space=pltpu.VMEM)
    both = 2 * ROWS
    result = (
        jax.ShapeDtypeStruct((ROWS, G), BF16),
        jax.ShapeDtypeStruct((ROWS, G), BF16),
        jax.ShapeDtypeStruct((LEVELS, G, G), F32),
        jax.ShapeDtypeStruct((LEVELS, G, G), F32),
    )
    operands = [pltpu.with_memory_space_constraint(a, pltpu.HBM) for a in (tokens, cotangent, up_weight[0], down_weight[0])]
    worked = pl.pallas_call(
        kernel,
        out_shape=tuple(pltpu.VMEM(a.shape, a.dtype) for a in result),
        in_specs=[anywhere, anywhere, anywhere, anywhere, pl.BlockSpec(memory_space=pltpu.SMEM)],
        out_specs=(vmem, vmem, anywhere, anywhere),
        scratch_shapes=[
            pltpu.VMEM((2, LEVELS, both, G), BF16),
            pltpu.VMEM((WIDE, both), BF16),
            pltpu.VMEM((2, LEVELS, G, G), BF16),
            pltpu.VMEM((WIDE, 2 * G), BF16),
            pltpu.VMEM((2 * G, WIDE), BF16),
            pltpu.VMEM((2 * G, WIDE), BF16),
            pltpu.VMEM((WIDE, 2 * G), BF16),
            pltpu.VMEM((both, 2 * G), BF16),
            pltpu.VMEM((2 * G, both), BF16),
            pltpu.VMEM((both, 2 * G), BF16),
            pltpu.VMEM((both, 2 * G), F32),
            pltpu.VMEM((2, 2, both, G), BF16),
            pltpu.VMEM((2, 2, both, G), BF16),
            pltpu.VMEM((2, 2, both, G), F32),
            pltpu.VMEM((2, 2, both, G), BF16),
            pltpu.VMEM((2, 2, both, G), BF16),
            pltpu.VMEM((2, both, G), F32),
            pltpu.VMEM((2, both, G), F32),
            pltpu.VMEM((2, ROWS, G), BF16),
            pltpu.VMEM((2, ROWS, G), BF16),
            pltpu.VMEM((2, ROWS, G), BF16),
            pltpu.VMEM((2, both, G), BF16),
            pltpu.VMEM((2, both, G), BF16),
            pltpu.VMEM((2, LEVELS, G, G), F32),
            pltpu.VMEM((2, LEVELS, G, G), F32),
            pltpu.VMEM((2, LEVELS, G, G), F32),
            pltpu.SemaphoreType.DMA((len(FAMILIES),)),
            pltpu.SemaphoreType.DMA((COPIES,)),
            pltpu.SemaphoreType.DMA((4 + 2 * LEVELS,)),
        ],
        compiler_params=pltpu.CompilerParams(
            collective_id=0, has_side_effects=True, vmem_limit_bytes=58 * 1024 * 1024
        ),
    )(*operands, block_mask)
    worked = [pltpu.with_memory_space_constraint(a, pltpu.VMEM) for a in worked]
    output, grad_tokens, grad_up, grad_down = pl.pallas_call(
        hand_out,
        out_shape=result,
        in_specs=[anywhere] * 4,
        out_specs=(anywhere,) * 4,
        scratch_shapes=[pltpu.SemaphoreType.DMA((8,))],
        compiler_params=pltpu.CompilerParams(vmem_limit_bytes=1024 * 1024),
    )(*worked)
    return output, grad_tokens, grad_up[None], grad_down[None]


def solution(mesh):
    placed = (
        P("seq", "tp"),
        P(("seq", "tp"), None, None, None),
        P(("seq", "tp"), None, None, None),
        P(("seq", "tp"), None),
        P("seq", "tp"),
    )
    return jax.shard_map(
        shards,
        mesh=mesh,
        in_specs=placed,
        out_specs=(
            P("seq", "tp"),
            P("seq", "tp"),
            P(("seq", "tp"), None, None, None),
            P(("seq", "tp"), None, None, None),
        ),
        check_vma=False,
    )
```

```python
import functools
import math

import jax
import jax.numpy as jnp
from jax import lax
from jax.experimental import pallas as pl
from jax.experimental.pallas import tpu as pltpu
from jax.sharding import PartitionSpec as P

MESH = pl.DeviceIdType.MESH
F32 = jnp.float32
BF16 = jnp.bfloat16
ROWS = 512
PART = 256
PIECES = ROWS // PART
FIRST = PIECES // 2
TILE = 256
PER_TILE = TILE // PART
THIRDS = 3
G = 256
LEVELS = 6
WIDE = LEVELS * G
NEAR = {"x": 4, "y": 2}
FAR = {"x": 5, "y": 3}
SCALE = math.sqrt(2.0 / math.pi)
CUBE = 0.044715


def numbering():
    keys = []
    for which in range(2):
        keys += [(name, which, j) for name in ("z1", "z3", "zr", "out1", "out3", "half") for j in range(PIECES)]
        keys += [
            (name, axis, which, slot, j)
            for name in ("near", "far", "term", "sum")
            for axis in "xy"
            for slot in range(2)
            for j in range(PIECES)
        ]
        keys += [("weight", which)] + [("grad", which, k) for k in range(LEVELS // THIRDS)]
    return {key: n for n, key in enumerate(keys)}


def family(key):
    name = key[0]
    if name in ("weight", "grad"):
        return key
    if name in ("near", "far", "term", "sum"):
        return name, key[2], key[3]
    return {"z1": "z", "z3": "z", "zr": "middle", "half": "middle", "out1": "out", "out3": "out"}[name], key[1]


NUMBER = numbering()
COPIES = len(NUMBER)
FAMILIES = {name: n for n, name in enumerate(dict.fromkeys(family(key) for key in NUMBER))}

ORDER = (
    ("oz", 0, 0), ("ox", 1, 1), ("su",), ("sd",), ("ox", 0, 0), ("oz", 0, 1), ("rz", 0, 0), ("rx", 1, 0, 1),
    ("ox", 0, 1), ("oz", 1, 0), ("rx", 0, 0, 0), ("rz", 0, 1), ("ox", 1, 0), ("rx", 0, 0, 1), ("ot", 0, 0),
    ("rz", 1, 0), ("tw",), ("rx", 1, 0, 0), ("oz", 1, 1), ("ot", 0, 1), ("rx", 0, 1, 0), ("ot", 1, 0), ("F", 0, 1),
    ("F", 0, 0), ("rx", 0, 1, 1), ("th", 0), ("rz", 1, 1), ("rx", 1, 1, 0), ("F", 1, 0), ("TN", 0, 1, 0),
    ("TF", 0, 1, 0), ("S", 0, 1, 0), ("TF", 0, 0, 0), ("B", 0, 1), ("TN", 0, 0, 1), ("ot", 1, 1), ("F", 1, 1),
    ("TF", 0, 1, 1), ("S", 0, 1, 1), ("TN", 1, 0, 1), ("ta", 0, 1), ("ta", 0, 0), ("B", 0, 0), ("ta", 1, 1),
    ("Z", 1, 0, 1), ("B", 1, 0), ("TN", 0, 1, 1), ("rx", 1, 1, 1), ("TN", 1, 1, 0), ("J", 0, 1, 0), ("th", 1),
    ("TF", 1, 1, 0), ("TN", 0, 0, 0), ("ta", 1, 0), ("Z", 0, 1, 0), ("Z", 0, 0, 1), ("J", 0, 1, 1), ("S", 1, 1, 0),
    ("B", 1, 1), ("TF", 1, 1, 1), ("S", 1, 1, 1), ("C", 0, 1, 0), ("W", ("weight", 0)), ("J", 1, 1, 0),
    ("W", ("weight", 1)), ("TF", 1, 0, 0), ("TF", 0, 0, 1), ("W", ("z", 0)), ("C", 0, 1, 1), ("S", 0, 0, 0),
    ("G", 0, 1), ("W", ("near", 0, 0)), ("TN", 1, 1, 1), ("J", 1, 1, 1), ("Z", 1, 1, 0), ("PO", 0, 0),
    ("W", ("near", 1, 0)), ("S", 1, 0, 0), ("W", ("far", 0, 0)), ("G", 1, 1), ("C", 1, 1, 0), ("J", 0, 0, 0),
    ("TF", 1, 0, 1), ("W", ("far", 1, 0)), ("S", 0, 0, 1), ("W", ("z", 1)), ("G", 0, 0), ("W", ("near", 0, 1)),
    ("TN", 1, 0, 0), ("J", 1, 0, 0), ("C", 1, 1, 1), ("S", 1, 0, 1), ("G", 1, 0), ("W", ("far", 0, 1)), ("PO", 0, 1),
    ("GS", 1, 1), ("J", 0, 0, 1), ("GS", 0, 1), ("PO", 1, 0), ("PO", 1, 1), ("J", 1, 0, 1), ("C", 1, 0, 0),
    ("FIN", 1, 0), ("GS", 0, 0), ("C", 0, 0, 0), ("W", ("near", 1, 1)), ("GS", 1, 0), ("C", 0, 0, 1), ("FIN", 0, 1),
    ("W", ("term", 0, 1)), ("FIN", 0, 0), ("C", 1, 0, 1), ("FIN", 1, 1),
    ("W", ("middle", 0), ("middle", 1), ("far", 1, 1), ("out", 1), ("sum", 0, 1), ("out", 0), ("term", 1, 1), ("sum", 1, 1), ("term", 0, 0), ("grad", 0, 1), ("term", 1, 0), ("grad", 1, 1), ("sum", 0, 0), ("grad", 0, 0), ("sum", 1, 0), ("grad", 1, 0)),
)


def flip(index, bit):
    return index + bit - 2 * bit * lax.rem(lax.div(index, bit), 2)


def kernel(
    tok, cot, up, down, mask, out, gtok, gup, gdown,
    held, held_t, raw, uall, dall, uall_t, dall_t, act, act_t, gpre, slope,
    term_send, term_recv, near_term, sum_send, sum_recv, base, z_term,
    half_send, half_recv, z_send, z_recv,
    grad_own, grad_peer, grad_recv,
    sends, recvs, local,
):
    shared = (tok, cot)
    seq, tp = lax.axis_index("seq"), lax.axis_index("tp")
    place = {
        "core": (flip(seq, 1), tp),
        "z1": (seq, flip(tp, 1)),
        "z3": (flip(seq, 2), flip(tp, 1)),
        "x1": (seq, flip(tp, 8)),
        "x3": (seq, flip(flip(tp, 8), 16)),
        "y1": (seq, flip(tp, 2)),
        "y3": (seq, flip(flip(tp, 2), 4)),
    }

    def remote(src, dst, key, target):
        return pltpu.make_async_remote_copy(
            src_ref=src,
            dst_ref=dst,
            send_sem=sends.at[FAMILIES[family(key)]],
            recv_sem=recvs.at[NUMBER[key]],
            device_id=place[target],
            device_id_type=MESH,
        )

    def rows(slot, j):
        start = slot * ROWS + j * PART
        return pl.ds(start if isinstance(j, int) else pl.multiple_of(start, PART), PART)

    def piece(j):
        return pl.ds(j * PART, PART)

    def columns(level):
        return pl.ds(level * G, G)

    def transfer(key):
        name, rest = key[0], key[1:]
        if name == "weight":
            if rest[0] == 0:
                return remote(uall.at[:, pl.ds(0, G)], uall.at[:, pl.ds(G, G)], key, "core")
            return remote(dall.at[pl.ds(0, G)], dall.at[pl.ds(G, G)], key, "core")
        if name == "grad":
            at = pl.ds(rest[1] * THIRDS, THIRDS)
            return remote(grad_peer.at[rest[0], at], grad_recv.at[rest[0], at], key, "core")
        if name in ("near", "far", "term", "sum"):
            axis, which, slot, j = rest
            a, at = "xy".index(axis), rows(slot, j)
            if name == "near":
                src = held.at[which, 0, at] if slot else shared[which].at[piece(j)]
                return remote(src, held.at[which, NEAR[axis], at], key, axis + "1")
            if name == "far":
                return remote(held.at[which, NEAR[axis], at], held.at[which, FAR[axis], at], key, axis + "3")
            if name == "term":
                return remote(term_send.at[which, a, at], term_recv.at[which, a, at], key, axis + "3")
            return remote(sum_send.at[which, a, at], sum_recv.at[which, a, at], key, axis + "1")
        which, j = rest
        if name == "z1":
            return remote(shared[which].at[piece(j)], held.at[which, 1, rows(0, j)], key, "z1")
        if name == "z3":
            return remote(shared[which].at[piece(j)], held.at[which, 1, rows(1, j)], key, "z3")
        onward = "z3" if j < FIRST else "z1"
        if name == "zr":
            return remote(held.at[which, 1, rows(int(j >= FIRST), j)], held.at[which, 0, rows(1, j)], key, onward)
        if name == "half":
            return remote(half_send.at[which, piece(j)], half_recv.at[which, piece(j)], key, onward)
        slot = int(name == "out3")
        return remote(z_send.at[which, rows(slot, j)], z_recv.at[which, rows(slot, j)], key, "z3" if slot else "z1")

    started, landed, copied, sent = set(), set(), set(), set()

    def send(*keys):
        for key in keys:
            started.add(key)
            transfer(key).start()

    def need(*keys):
        for key in keys:
            if key not in landed:
                landed.add(key)
                transfer(key).wait_recv()

    own = [
        pltpu.make_async_copy(shared[which], held.at[which, 0, pl.ds(0, ROWS)], local.at[which])
        for which in range(2)
    ]
    loads = [pltpu.make_async_copy(ref, raw.at[which], local.at[2 + which]) for which, ref in enumerate((up, down))]
    for copy in loads + own:
        copy.start()

    barrier = pltpu.get_barrier_semaphore()
    for target in place.values():
        pl.semaphore_signal(barrier, inc=1, device_id=target, device_id_type=MESH)
    pl.semaphore_wait(barrier, len(place))

    def scale_up(k, carry):
        factor = mask[0, k].astype(F32)
        uall[pl.ds(pl.multiple_of(k * G, G), G), pl.ds(0, G)] = (raw[0, k].astype(F32) * factor).astype(BF16)
        return carry

    def scale_down(k, carry):
        factor = mask[0, k].astype(F32)
        dall[pl.ds(0, G), pl.ds(pl.multiple_of(k * G, G), G)] = (raw[1, k].astype(F32) * factor).astype(BF16)
        return carry

    def wide(which, at):
        return jnp.concatenate([held[which, level, at] for level in range(LEVELS)], axis=1)

    def tile(slot, t):
        return pl.ds(slot * ROWS + t * TILE, TILE)

    def own_z(which, j):
        send(("z1", which, j), ("z3", which, j))

    def own_xy(which, j):
        send(("near", "x", which, 0, j), ("near", "y", which, 0, j))

    def relay_z(which, j):
        need(("z1" if j < FIRST else "z3", which, j))
        send(("zr", which, j))

    def other(which, j):
        need(("zr", which, j))
        send(("near", "x", which, 1, j), ("near", "y", which, 1, j))

    def relay_xy(which, slot, j):
        for axis in "xy":
            need(("near", axis, which, slot, j))
            send(("far", axis, which, slot, j))

    def mask_up():
        loads[0].wait()
        lax.fori_loop(0, LEVELS, scale_up, 0)
        send(("weight", 0))

    def mask_down():
        loads[1].wait()
        lax.fori_loop(0, LEVELS, scale_down, 0)
        send(("weight", 1))

    def turn_weights():
        need(("weight", 0), ("weight", 1))

        def body(k, carry):
            at = pl.ds(pl.multiple_of(k * G, G), G)
            dall_t[at, :] = dall[:, at].T
            uall_t[:, at] = uall[at, :].T
            return carry

        lax.fori_loop(0, LEVELS, body, 0)

    def turn_held(slot):
        def body(k, carry):
            at = pl.ds(pl.multiple_of(k * G, G), G)
            held_t[at, pl.ds(slot * ROWS, ROWS)] = held[0, k, pl.ds(slot * ROWS, ROWS)].T
            return carry

        lax.fori_loop(0, LEVELS, body, 0)

    def turn_act(slot, t):
        act_t[:, tile(slot, t)] = act[tile(slot, t), :].T

    def inputs(which, slot, t):
        if slot == 0 and ("own", which) not in copied:
            copied.add(("own", which))
            own[which].wait()
        for j in range(t * PER_TILE, (t + 1) * PER_TILE):
            need(("z3" if slot else "z1", which, j))
            for axis in "xy":
                need(("far", axis, which, slot, j))

    def forward(slot, t):
        inputs(0, slot, t)
        need(("weight", 0), ("weight", 1))
        at = tile(slot, t)
        pre = jnp.dot(wide(0, at), uall[...], preferred_element_type=F32)
        square = pre * pre
        tanh = jnp.tanh(SCALE * pre * (1.0 + CUBE * square))
        cdf = 0.5 + 0.5 * tanh
        act[at, :] = (pre * cdf).astype(BF16)
        slope[at, :] = cdf + (0.5 * SCALE) * pre * (1.0 - tanh * tanh) * (1.0 + (3.0 * CUBE) * square)

    def backward(slot, t):
        inputs(1, slot, t)
        at = tile(slot, t)
        gact = jnp.dot(wide(1, at), dall_t[...], preferred_element_type=F32)
        gpre[at, :] = (gact * slope[at, :]).astype(BF16)

    def product(which, slot, t, level):
        if which:
            return jnp.dot(gpre[tile(slot, t), :], uall_t[:, columns(level)], preferred_element_type=F32)
        return jnp.dot(act[tile(slot, t), :], dall[:, columns(level)], preferred_element_type=F32)

    def far_terms(which, slot, t):
        for a, axis in enumerate("xy"):
            term_send[which, a, tile(slot, t)] = product(which, slot, t, FAR[axis]).astype(BF16)

    def near_terms(which, slot, t):
        at = tile(slot, t)
        for a, axis in enumerate("xy"):
            near_term[which, a, at] = product(which, slot, t, NEAR[axis])
        z_term[which, at] = product(which, slot, t, 1)
        base[which, at] = product(which, slot, t, 0)

    def send_term(which, slot, j):
        send(("term", "x", which, slot, j), ("term", "y", which, slot, j))

    def join(which, slot, j):
        at = rows(slot, j)
        for a, axis in enumerate("xy"):
            need(("term", axis, which, slot, j))
            total = near_term[which, a, at] + term_recv[which, a, at].astype(F32)
            sum_send[which, a, at] = total.astype(BF16)
            send(("sum", axis, which, slot, j))

    def collect(which, slot, j):
        at = rows(slot, j)
        need(("sum", "x", which, slot, j), ("sum", "y", which, slot, j))
        total = base[which, at] + sum_recv[which, 0, at].astype(F32) + sum_recv[which, 1, at].astype(F32)
        if slot == 0:
            base[which, at] = total
        else:
            half_send[which, piece(j)] = total.astype(BF16)
            send(("half", which, j))

    def plain(which, slot, j):
        z_send[which, rows(slot, j)] = z_term[which, rows(slot, j)].astype(BF16)
        send(("out3" if slot else "out1", which, j))

    def pass_on(which, j):
        slot = int(j >= FIRST)
        at = rows(slot, j)
        need(("half", which, j))
        z_send[which, at] = (z_term[which, at] + half_recv[which, piece(j)].astype(F32)).astype(BF16)
        send(("out3" if slot else "out1", which, j))

    def finish(which, j):
        need(("out1", which, j), ("out3", which, j))
        total = base[which, rows(0, j)] + z_recv[which, rows(0, j)].astype(F32) + z_recv[which, rows(1, j)].astype(F32)
        (gtok if which else out)[piece(j), :] = total.astype(BF16)

    def grads(which, third):
        def body(k, carry):
            at = pl.ds(pl.multiple_of(k * G, G), G)
            if which:
                both = jnp.dot(act_t[...], held[1, k], preferred_element_type=F32)
                grad_own[1, k] = both[:G]
                grad_peer[1, k] = both[G:]
            else:
                both = jnp.dot(held_t[at, :], gpre[...], preferred_element_type=F32)
                grad_own[0, k] = both[:, :G]
                grad_peer[0, k] = both[:, G:]
            return carry

        lax.fori_loop(third * THIRDS, (third + 1) * THIRDS, body, 0)
        send(("grad", which, third))

    def write_grad(which, k):
        return pltpu.make_async_copy(grad_own.at[which, k], (gdown if which else gup).at[k], local.at[4 + which * LEVELS + k])

    def grads_sum(which, third):
        need(("grad", which, third))

        def body(k, carry):
            grad_own[which, k] = (grad_own[which, k] + grad_recv[which, k]) * mask[0, k].astype(F32)
            write_grad(which, k).start()
            return carry

        lax.fori_loop(third * THIRDS, (third + 1) * THIRDS, body, 0)

    def finish_sends(*names):
        for name in names:
            sent.add(name)
            if name[0] in ("weight", "grad"):
                transfer(name).wait_send()
            else:
                pltpu.make_async_remote_copy(
                    src_ref=held.at[0, 0],
                    dst_ref=held.at[0, 0],
                    send_sem=sends.at[FAMILIES[name]],
                    recv_sem=recvs.at[0],
                    device_id=place["z1"],
                    device_id_type=MESH,
                ).wait_send()

    steps = {
        "W": finish_sends,
        "oz": own_z, "ox": own_xy, "rz": relay_z, "ot": other, "rx": relay_xy, "su": mask_up, "sd": mask_down,
        "tw": turn_weights, "th": turn_held, "ta": turn_act, "F": forward, "B": backward, "TF": far_terms,
        "TN": near_terms, "S": send_term, "J": join, "C": collect, "Z": plain, "PO": pass_on,
        "FIN": finish, "G": grads, "GS": grads_sum,
    }
    for step in ORDER:
        steps[step[0]](*step[1:])

    assert started == landed == set(NUMBER)
    for which in range(2):
        for k in range(LEVELS):
            write_grad(which, k).wait()
    assert sent == set(FAMILIES)


def hand_out(*refs):
    sources, results, sems = refs[:4], refs[4:8], refs[8]
    copies = []
    for src, dst in zip(sources, results):
        if len(src.shape) == 2:
            pairs = [(src, dst)]
        else:
            pairs = [(src.at[pl.ds(k, 2)], dst.at[pl.ds(k, 2)]) for k in range(0, LEVELS, 2)]
        for a, b in pairs:
            copies.append(pltpu.make_async_copy(a, b, sems.at[len(copies)]))
    for copy in copies:
        copy.start()
    for copy in copies:
        copy.wait()


def shards(tokens, up_weight, down_weight, block_mask, cotangent):
    anywhere = pl.BlockSpec(memory_space=pl.ANY)
    vmem = pl.BlockSpec(memory_space=pltpu.VMEM)
    both = 2 * ROWS
    result = (
        jax.ShapeDtypeStruct((ROWS, G), BF16),
        jax.ShapeDtypeStruct((ROWS, G), BF16),
        jax.ShapeDtypeStruct((LEVELS, G, G), F32),
        jax.ShapeDtypeStruct((LEVELS, G, G), F32),
    )
    operands = [pltpu.with_memory_space_constraint(a, pltpu.HBM) for a in (tokens, cotangent, up_weight[0], down_weight[0])]
    worked = pl.pallas_call(
        kernel,
        out_shape=tuple(pltpu.VMEM(a.shape, a.dtype) for a in result),
        in_specs=[anywhere, anywhere, anywhere, anywhere, pl.BlockSpec(memory_space=pltpu.SMEM)],
        out_specs=(vmem, vmem, anywhere, anywhere),
        scratch_shapes=[
            pltpu.VMEM((2, LEVELS, both, G), BF16),
            pltpu.VMEM((WIDE, both), BF16),
            pltpu.VMEM((2, LEVELS, G, G), BF16),
            pltpu.VMEM((WIDE, 2 * G), BF16),
            pltpu.VMEM((2 * G, WIDE), BF16),
            pltpu.VMEM((2 * G, WIDE), BF16),
            pltpu.VMEM((WIDE, 2 * G), BF16),
            pltpu.VMEM((both, 2 * G), BF16),
            pltpu.VMEM((2 * G, both), BF16),
            pltpu.VMEM((both, 2 * G), BF16),
            pltpu.VMEM((both, 2 * G), F32),
            pltpu.VMEM((2, 2, both, G), BF16),
            pltpu.VMEM((2, 2, both, G), BF16),
            pltpu.VMEM((2, 2, both, G), F32),
            pltpu.VMEM((2, 2, both, G), BF16),
            pltpu.VMEM((2, 2, both, G), BF16),
            pltpu.VMEM((2, both, G), F32),
            pltpu.VMEM((2, both, G), F32),
            pltpu.VMEM((2, ROWS, G), BF16),
            pltpu.VMEM((2, ROWS, G), BF16),
            pltpu.VMEM((2, both, G), BF16),
            pltpu.VMEM((2, both, G), BF16),
            pltpu.VMEM((2, LEVELS, G, G), F32),
            pltpu.VMEM((2, LEVELS, G, G), F32),
            pltpu.VMEM((2, LEVELS, G, G), F32),
            pltpu.SemaphoreType.DMA((len(FAMILIES),)),
            pltpu.SemaphoreType.DMA((COPIES,)),
            pltpu.SemaphoreType.DMA((4 + 2 * LEVELS,)),
        ],
        compiler_params=pltpu.CompilerParams(
            collective_id=0, has_side_effects=True, vmem_limit_bytes=58 * 1024 * 1024
        ),
    )(*operands, block_mask)
    worked = [pltpu.with_memory_space_constraint(a, pltpu.VMEM) for a in worked]
    output, grad_tokens, grad_up, grad_down = pl.pallas_call(
        hand_out,
        out_shape=result,
        in_specs=[anywhere] * 4,
        out_specs=(anywhere,) * 4,
        scratch_shapes=[pltpu.SemaphoreType.DMA((8,))],
        compiler_params=pltpu.CompilerParams(vmem_limit_bytes=1024 * 1024),
    )(*worked)
    return output, grad_tokens, grad_up[None], grad_down[None]


def solution(mesh):
    placed = (
        P("seq", "tp"),
        P(("seq", "tp"), None, None, None),
        P(("seq", "tp"), None, None, None),
        P(("seq", "tp"), None),
        P("seq", "tp"),
    )
    return jax.shard_map(
        shards,
        mesh=mesh,
        in_specs=placed,
        out_specs=(
            P("seq", "tp"),
            P("seq", "tp"),
            P(("seq", "tp"), None, None, None),
            P(("seq", "tp"), None, None, None),
        ),
        check_vma=False,
    )
```

```python
import functools
import math

import jax
import jax.numpy as jnp
from jax import lax
from jax.experimental import pallas as pl
from jax.experimental.pallas import tpu as pltpu
from jax.sharding import PartitionSpec as P

MESH = pl.DeviceIdType.MESH
F32 = jnp.float32
BF16 = jnp.bfloat16
ROWS = 512
PART = 128
PIECES = ROWS // PART
FIRST = PIECES // 2
TILE = 256
PER_TILE = TILE // PART
THIRDS = 3
G = 256
LEVELS = 6
WIDE = LEVELS * G
NEAR = {"x": 4, "y": 2}
FAR = {"x": 5, "y": 3}
SCALE = math.sqrt(2.0 / math.pi)
CUBE = 0.044715


def numbering():
    keys = []
    for which in range(2):
        keys += [(name, which, j) for name in ("z1", "z3", "zr", "out1", "out3", "half") for j in range(PIECES)]
        keys += [
            (name, axis, which, slot, j)
            for name in ("near", "far", "term", "sum")
            for axis in "xy"
            for slot in range(2)
            for j in range(PIECES)
        ]
        keys += [("weight", which)] + [("grad", which, k) for k in range(LEVELS // THIRDS)]
    keys += [("last", axis, j) for axis in "xy" for j in PASSED]
    return {key: n for n, key in enumerate(keys)}


def passed(which, slot, j):
    return which == 0 and slot == 0 and j in PASSED


def family(key):
    name = key[0]
    if name in ("weight", "grad"):
        return key
    if name in ("near", "far", "term", "sum"):
        return name, key[2], key[3]
    if name == "last":
        return name, key[2]
    return {"z1": "z", "z3": "z", "zr": "middle", "half": "middle", "out1": "out", "out3": "out"}[name], key[1]


PASSED = (2, 3)
NUMBER = numbering()
COPIES = len(NUMBER)
FAMILIES = {name: n for n, name in enumerate(dict.fromkeys(family(key) for key in NUMBER))}

ORDER = (
    ("oz", 1, 1), ("ox", 0, 2), ("ox", 0, 0), ("ox", 0, 3), ("oz", 0, 2), ("su",), ("oz", 0, 1), ("sd",),
    ("rz", 1, 1), ("ox", 1, 3), ("ox", 0, 1), ("oz", 0, 3), ("rx", 0, 0, 2), ("rx", 0, 0, 0), ("rz", 0, 2),
    ("ox", 1, 2), ("oz", 0, 0), ("rx", 0, 0, 3), ("Fn", 0, 1), ("ox", 1, 1), ("oz", 1, 3), ("rz", 0, 1),
    ("ot", 1, 1), ("rx", 1, 0, 3), ("ox", 1, 0), ("rz", 0, 3), ("rx", 0, 0, 1), ("tw",), ("oz", 1, 2), ("ot", 0, 2),
    ("rz", 0, 0), ("rx", 1, 0, 2), ("F", 0, 1), ("TF", 0, 0, 1), ("rx", 1, 0, 1), ("oz", 1, 0), ("rz", 1, 3),
    ("ot", 0, 3), ("ot", 0, 1), ("TN", 0, 0, 1), ("rx", 1, 1, 1), ("Fn", 0, 0), ("F", 0, 0), ("rz", 1, 2),
    ("rx", 1, 0, 0), ("rx", 0, 1, 2), ("ot", 0, 0), ("th", 0), ("rx", 0, 1, 3), ("ot", 1, 3), ("rz", 1, 0),
    ("Bn", 0, 1), ("ta", 0, 1), ("B", 0, 1), ("ot", 1, 2), ("rx", 0, 1, 1), ("Fn", 1, 1), ("rx", 0, 1, 0),
    ("TF", 1, 0, 1), ("J", 0, 0, 3), ("Fn", 1, 0), ("Bn", 0, 0), ("ot", 1, 0), ("rx", 1, 1, 3), ("TN", 1, 0, 1),
    ("J", 0, 0, 2), ("TF", 0, 0, 0), ("rx", 1, 1, 2), ("F", 1, 1), ("TF", 0, 1, 1), ("Z", 1, 0, 3), ("TN", 0, 1, 1),
    ("Z", 0, 0, 3), ("S", 0, 1, 3), ("Z", 1, 0, 2), ("F", 1, 0), ("ta", 1, 0), ("rx", 1, 1, 0), ("Bn", 1, 1),
    ("TF", 0, 1, 0), ("TN", 0, 1, 0), ("S", 0, 0, 3), ("S", 0, 1, 2), ("ta", 0, 0), ("Bn", 1, 0),
    ("W", ("weight", 0)), ("Z", 0, 0, 2), ("S", 0, 1, 1), ("W", ("weight", 1)), ("S", 0, 0, 2), ("th", 1),
    ("B", 1, 1), ("W", ("near", 0, 0)), ("J", 0, 1, 3), ("S", 0, 1, 0), ("B", 1, 0), ("TF", 1, 1, 0), ("Z", 0, 1, 0),
    ("S", 1, 1, 1), ("W", ("z", 0)), ("B", 0, 0), ("TN", 1, 1, 0), ("TF", 1, 1, 1), ("S", 1, 1, 2), ("J", 0, 1, 2),
    ("ta", 1, 1), ("Z", 1, 1, 0), ("Z", 1, 1, 1), ("W", ("near", 1, 0)), ("J", 0, 1, 1), ("S", 1, 1, 0),
    ("W", ("far", 0, 0)), ("G", 1, 1), ("C", 0, 1, 3), ("J", 0, 1, 0), ("S", 1, 1, 3), ("TN", 1, 1, 1),
    ("Z", 0, 1, 1), ("TF", 1, 0, 0), ("J", 1, 1, 1), ("S", 0, 0, 0), ("W", ("z", 1)), ("C", 0, 1, 2), ("C", 0, 1, 1),
    ("S", 0, 0, 1), ("J", 1, 1, 2), ("G", 0, 1), ("J", 1, 1, 0), ("PO", 0, 3), ("S", 1, 0, 0), ("C", 0, 1, 0),
    ("W", ("far", 1, 0)), ("TN", 0, 0, 0), ("J", 1, 1, 3), ("W", ("near", 0, 1)), ("S", 1, 0, 3), ("PO", 0, 1),
    ("G", 0, 0), ("J", 0, 0, 0), ("C", 1, 1, 2), ("C", 1, 1, 1), ("J", 0, 0, 1), ("S", 1, 0, 2), ("C", 0, 0, 3),
    ("S", 1, 0, 1), ("TN", 1, 0, 0), ("W", ("far", 0, 1)), ("PO", 0, 2), ("J", 1, 0, 0), ("C", 1, 1, 3),
    ("C", 1, 1, 0), ("C", 0, 0, 2), ("W", ("near", 1, 1)), ("RL", 2), ("J", 1, 0, 3), ("PO", 0, 0), ("G", 1, 0),
    ("PO", 1, 2), ("PO", 1, 1), ("J", 1, 0, 2), ("RL", 3), ("GS", 0, 0), ("C", 0, 0, 1), ("PO", 1, 3), ("PO", 1, 0),
    ("J", 1, 0, 1), ("C", 0, 0, 0), ("FIN", 0, 2), ("W", ("far", 1, 1)), ("C", 1, 0, 0), ("GS", 1, 1), ("FIN", 0, 1),
    ("GS", 0, 1), ("C", 1, 0, 2), ("FIN", 0, 0), ("FIN", 1, 2), ("C", 1, 0, 3), ("FIN", 0, 3), ("GS", 1, 0),
    ("FIN", 1, 3), ("FIN", 1, 0), ("C", 1, 0, 1), ("FIN", 1, 1),
    ("W", ("middle", 1), ("middle", 0), ("sum", 0, 0), ("out", 1), ("out", 0), ("term", 0, 1), ("term", 0, 0), ("sum", 0, 1), ("term", 1, 1), ("grad", 1, 1), ("sum", 1, 1), ("grad", 0, 1), ("term", 1, 0), ("grad", 0, 0), ("sum", 1, 0), ("last",), ("grad", 1, 0)),
)


def flip(index, bit):
    return index + bit - 2 * bit * lax.rem(lax.div(index, bit), 2)


def kernel(
    tok, cot, up, down, mask, out, gtok, gup, gdown,
    held, held_t, raw, uall, dall, uall_t, dall_t, act, act_t, gpre, slope, gact,
    term_send, term_recv, near_term, sum_send, sum_recv, base, z_term,
    half_send, half_recv, last_recv, z_send, z_recv,
    grad_own, grad_peer, grad_recv,
    sends, recvs, local,
):
    shared = (tok, cot)
    seq, tp = lax.axis_index("seq"), lax.axis_index("tp")
    place = {
        "core": (flip(seq, 1), tp),
        "z1": (seq, flip(tp, 1)),
        "z3": (flip(seq, 2), flip(tp, 1)),
        "x1": (seq, flip(tp, 8)),
        "x3": (seq, flip(flip(tp, 8), 16)),
        "y1": (seq, flip(tp, 2)),
        "y3": (seq, flip(flip(tp, 2), 4)),
    }

    def remote(src, dst, key, target):
        return pltpu.make_async_remote_copy(
            src_ref=src,
            dst_ref=dst,
            send_sem=sends.at[FAMILIES[family(key)]],
            recv_sem=recvs.at[NUMBER[key]],
            device_id=place[target],
            device_id_type=MESH,
        )

    def rows(slot, j):
        start = slot * ROWS + j * PART
        return pl.ds(start if isinstance(j, int) else pl.multiple_of(start, PART), PART)

    def piece(j):
        return pl.ds(j * PART, PART)

    def columns(level):
        return pl.ds(level * G, G)

    def transfer(key):
        name, rest = key[0], key[1:]
        if name == "weight":
            if rest[0] == 0:
                return remote(uall.at[:, pl.ds(0, G)], uall.at[:, pl.ds(G, G)], key, "core")
            return remote(dall.at[pl.ds(0, G)], dall.at[pl.ds(G, G)], key, "core")
        if name == "grad":
            at = pl.ds(rest[1] * THIRDS, THIRDS)
            return remote(grad_peer.at[rest[0], at], grad_recv.at[rest[0], at], key, "core")
        if name == "last":
            a, j = "xy".index(rest[0]), rest[1]
            return remote(term_recv.at[0, a, rows(0, j)], last_recv.at[a, piece(j)], key, rest[0] + "3")
        if name in ("near", "far", "term", "sum"):
            axis, which, slot, j = rest
            a, at = "xy".index(axis), rows(slot, j)
            if name == "near":
                src = held.at[which, 0, at] if slot else shared[which].at[piece(j)]
                return remote(src, held.at[which, NEAR[axis], at], key, axis + "1")
            if name == "far":
                return remote(held.at[which, NEAR[axis], at], held.at[which, FAR[axis], at], key, axis + "3")
            if name == "term":
                target = axis + ("1" if passed(which, slot, j) else "3")
                return remote(term_send.at[which, a, at], term_recv.at[which, a, at], key, target)
            return remote(sum_send.at[which, a, at], sum_recv.at[which, a, at], key, axis + "1")
        which, j = rest
        if name == "z1":
            return remote(shared[which].at[piece(j)], held.at[which, 1, rows(0, j)], key, "z1")
        if name == "z3":
            return remote(shared[which].at[piece(j)], held.at[which, 1, rows(1, j)], key, "z3")
        onward = "z3" if j < FIRST else "z1"
        if name == "zr":
            return remote(held.at[which, 1, rows(int(j >= FIRST), j)], held.at[which, 0, rows(1, j)], key, onward)
        if name == "half":
            return remote(half_send.at[which, piece(j)], half_recv.at[which, piece(j)], key, onward)
        slot = int(name == "out3")
        return remote(z_send.at[which, rows(slot, j)], z_recv.at[which, rows(slot, j)], key, "z3" if slot else "z1")

    started, landed, copied, sent = set(), set(), set(), set()

    def send(*keys):
        for key in keys:
            started.add(key)
            transfer(key).start()

    def need(*keys):
        for key in keys:
            if key not in landed:
                landed.add(key)
                transfer(key).wait_recv()

    own = [
        pltpu.make_async_copy(shared[which], held.at[which, 0, pl.ds(0, ROWS)], local.at[which])
        for which in range(2)
    ]
    loads = [pltpu.make_async_copy(ref, raw.at[which], local.at[2 + which]) for which, ref in enumerate((up, down))]
    for copy in loads + own:
        copy.start()

    barrier = pltpu.get_barrier_semaphore()
    for target in place.values():
        pl.semaphore_signal(barrier, inc=1, device_id=target, device_id_type=MESH)
    pl.semaphore_wait(barrier, len(place))

    def scale_up(k, carry):
        factor = mask[0, k].astype(F32)
        uall[pl.ds(pl.multiple_of(k * G, G), G), pl.ds(0, G)] = (raw[0, k].astype(F32) * factor).astype(BF16)
        return carry

    def scale_down(k, carry):
        factor = mask[0, k].astype(F32)
        dall[pl.ds(0, G), pl.ds(pl.multiple_of(k * G, G), G)] = (raw[1, k].astype(F32) * factor).astype(BF16)
        return carry

    def tile(slot, t):
        return pl.ds(slot * ROWS + t * TILE, TILE)

    def own_z(which, j):
        send(("z1", which, j), ("z3", which, j))

    def own_xy(which, j):
        send(("near", "x", which, 0, j), ("near", "y", which, 0, j))

    def relay_z(which, j):
        need(("z1" if j < FIRST else "z3", which, j))
        send(("zr", which, j))

    def other(which, j):
        need(("zr", which, j))
        send(("near", "x", which, 1, j), ("near", "y", which, 1, j))

    def relay_xy(which, slot, j):
        for axis in "xy":
            need(("near", axis, which, slot, j))
            send(("far", axis, which, slot, j))

    def mask_up():
        loads[0].wait()
        lax.fori_loop(0, LEVELS, scale_up, 0)
        send(("weight", 0))

    def mask_down():
        loads[1].wait()
        lax.fori_loop(0, LEVELS, scale_down, 0)
        send(("weight", 1))

    def turn_weights():
        need(("weight", 0), ("weight", 1))

        def body(k, carry):
            at = pl.ds(pl.multiple_of(k * G, G), G)
            dall_t[at, :] = dall[:, at].T
            uall_t[:, at] = uall[at, :].T
            return carry

        lax.fori_loop(0, LEVELS, body, 0)

    def turn_held(slot):
        def body(k, carry):
            at = pl.ds(pl.multiple_of(k * G, G), G)
            held_t[at, pl.ds(slot * ROWS, ROWS)] = held[0, k, pl.ds(slot * ROWS, ROWS)].T
            return carry

        lax.fori_loop(0, LEVELS, body, 0)

    def turn_act(slot, t):
        act_t[:, tile(slot, t)] = act[tile(slot, t), :].T

    def near_inputs(which, slot, t):
        if slot == 0 and ("own", which) not in copied:
            copied.add(("own", which))
            own[which].wait()
        for j in range(t * PER_TILE, (t + 1) * PER_TILE):
            need(("z3" if slot else "z1", which, j))

    def far_inputs(which, slot, t):
        for j in range(t * PER_TILE, (t + 1) * PER_TILE):
            for axis in "xy":
                need(("far", axis, which, slot, j))

    def partial(which, at, weights):
        early = jnp.concatenate([held[which, level, at] for level in (0, 1, 2)], axis=1)
        total = jnp.dot(early, weights[pl.ds(0, 3 * G), :], preferred_element_type=F32)
        return total + jnp.dot(held[which, 4, at], weights[pl.ds(4 * G, G), :], preferred_element_type=F32)

    def rest(which, at, weights):
        total = jnp.dot(held[which, 3, at], weights[pl.ds(3 * G, G), :], preferred_element_type=F32)
        return total + jnp.dot(held[which, 5, at], weights[pl.ds(5 * G, G), :], preferred_element_type=F32)

    def forward_near(slot, t):
        near_inputs(0, slot, t)
        need(("weight", 0))
        slope[tile(slot, t), :] = partial(0, tile(slot, t), uall)

    def backward_near(slot, t):
        near_inputs(1, slot, t)
        gact[tile(slot, t), :] = partial(1, tile(slot, t), dall_t)

    def forward(slot, t):
        far_inputs(0, slot, t)
        at = tile(slot, t)
        pre = slope[at, :] + rest(0, at, uall)
        square = pre * pre
        tanh = jnp.tanh(SCALE * pre * (1.0 + CUBE * square))
        cdf = 0.5 + 0.5 * tanh
        act[at, :] = (pre * cdf).astype(BF16)
        slope[at, :] = cdf + (0.5 * SCALE) * pre * (1.0 - tanh * tanh) * (1.0 + (3.0 * CUBE) * square)

    def backward(slot, t):
        far_inputs(1, slot, t)
        at = tile(slot, t)
        gpre[at, :] = ((gact[at, :] + rest(1, at, dall_t)) * slope[at, :]).astype(BF16)

    def product(which, slot, t, level):
        if which:
            return jnp.dot(gpre[tile(slot, t), :], uall_t[:, columns(level)], preferred_element_type=F32)
        return jnp.dot(act[tile(slot, t), :], dall[:, columns(level)], preferred_element_type=F32)

    def far_terms(which, slot, t):
        need(("weight", 1))
        for a, axis in enumerate("xy"):
            term_send[which, a, tile(slot, t)] = product(which, slot, t, FAR[axis]).astype(BF16)

    def near_terms(which, slot, t):
        at = tile(slot, t)
        for a, axis in enumerate("xy"):
            near_term[which, a, at] = product(which, slot, t, NEAR[axis])
        z_term[which, at] = product(which, slot, t, 1)
        base[which, at] = product(which, slot, t, 0)

    def send_term(which, slot, j):
        send(("term", "x", which, slot, j), ("term", "y", which, slot, j))

    def hand_on(j):
        for axis in "xy":
            need(("term", axis, 0, 0, j))
            send(("last", axis, j))

    def join(which, slot, j):
        at = rows(slot, j)
        for a, axis in enumerate("xy"):
            total = near_term[which, a, at]
            if not passed(which, slot, j):
                need(("term", axis, which, slot, j))
                total = total + term_recv[which, a, at].astype(F32)
            sum_send[which, a, at] = total.astype(BF16)
            send(("sum", axis, which, slot, j))

    def collect(which, slot, j):
        at = rows(slot, j)
        need(("sum", "x", which, slot, j), ("sum", "y", which, slot, j))
        total = base[which, at] + sum_recv[which, 0, at].astype(F32) + sum_recv[which, 1, at].astype(F32)
        if slot == 0:
            base[which, at] = total
        else:
            half_send[which, piece(j)] = total.astype(BF16)
            send(("half", which, j))

    def plain(which, slot, j):
        z_send[which, rows(slot, j)] = z_term[which, rows(slot, j)].astype(BF16)
        send(("out3" if slot else "out1", which, j))

    def pass_on(which, j):
        slot = int(j >= FIRST)
        at = rows(slot, j)
        need(("half", which, j))
        z_send[which, at] = (z_term[which, at] + half_recv[which, piece(j)].astype(F32)).astype(BF16)
        send(("out3" if slot else "out1", which, j))

    def finish(which, j):
        need(("out1", which, j), ("out3", which, j))
        total = base[which, rows(0, j)] + z_recv[which, rows(0, j)].astype(F32) + z_recv[which, rows(1, j)].astype(F32)
        if passed(which, 0, j):
            need(("last", "x", j), ("last", "y", j))
            total = total + last_recv[0, piece(j)].astype(F32) + last_recv[1, piece(j)].astype(F32)
        (gtok if which else out)[piece(j), :] = total.astype(BF16)

    def grads(which, third):
        def body(k, carry):
            at = pl.ds(pl.multiple_of(k * G, G), G)
            if which:
                both = jnp.dot(act_t[...], held[1, k], preferred_element_type=F32)
                grad_own[1, k] = both[:G]
                grad_peer[1, k] = both[G:]
            else:
                both = jnp.dot(held_t[at, :], gpre[...], preferred_element_type=F32)
                grad_own[0, k] = both[:, :G]
                grad_peer[0, k] = both[:, G:]
            return carry

        lax.fori_loop(third * THIRDS, (third + 1) * THIRDS, body, 0)
        send(("grad", which, third))

    def write_grad(which, k):
        return pltpu.make_async_copy(grad_own.at[which, k], (gdown if which else gup).at[k], local.at[4 + which * LEVELS + k])

    def grads_sum(which, third):
        need(("grad", which, third))

        def body(k, carry):
            grad_own[which, k] = (grad_own[which, k] + grad_recv[which, k]) * mask[0, k].astype(F32)
            write_grad(which, k).start()
            return carry

        lax.fori_loop(third * THIRDS, (third + 1) * THIRDS, body, 0)

    def finish_sends(*names):
        for name in names:
            sent.update([(name[0], j) for j in PASSED] if name[0] == "last" else [name])
            if name[0] in ("weight", "grad"):
                transfer(name).wait_send()
            elif name[0] == "last":
                for j in PASSED:
                    span = pl.ds(0, 2 * PART)
                    pltpu.make_async_remote_copy(
                        src_ref=held.at[0, 0, span],
                        dst_ref=held.at[0, 0, span],
                        send_sem=sends.at[FAMILIES["last", j]],
                        recv_sem=recvs.at[0],
                        device_id=place["z1"],
                        device_id_type=MESH,
                    ).wait_send()
            else:
                pltpu.make_async_remote_copy(
                    src_ref=held.at[0, 0],
                    dst_ref=held.at[0, 0],
                    send_sem=sends.at[FAMILIES[name]],
                    recv_sem=recvs.at[0],
                    device_id=place["z1"],
                    device_id_type=MESH,
                ).wait_send()

    steps = {
        "W": finish_sends,
        "oz": own_z, "ox": own_xy, "rz": relay_z, "ot": other, "rx": relay_xy, "su": mask_up, "sd": mask_down,
        "tw": turn_weights, "th": turn_held, "ta": turn_act, "F": forward, "B": backward, "Fn": forward_near, "Bn": backward_near, "TF": far_terms,
        "TN": near_terms, "S": send_term, "RL": hand_on, "J": join, "C": collect, "Z": plain, "PO": pass_on,
        "FIN": finish, "G": grads, "GS": grads_sum,
    }
    for step in ORDER:
        steps[step[0]](*step[1:])

    assert started == landed == set(NUMBER)
    for which in range(2):
        for k in range(LEVELS):
            write_grad(which, k).wait()
    assert sent == set(FAMILIES)


def hand_out(*refs):
    sources, results, sems = refs[:4], refs[4:8], refs[8]
    copies = []
    for src, dst in zip(sources, results):
        if len(src.shape) == 2:
            pairs = [(src, dst)]
        else:
            pairs = [(src.at[pl.ds(k, 2)], dst.at[pl.ds(k, 2)]) for k in range(0, LEVELS, 2)]
        for a, b in pairs:
            copies.append(pltpu.make_async_copy(a, b, sems.at[len(copies)]))
    for copy in copies:
        copy.start()
    for copy in copies:
        copy.wait()


def shards(tokens, up_weight, down_weight, block_mask, cotangent):
    anywhere = pl.BlockSpec(memory_space=pl.ANY)
    vmem = pl.BlockSpec(memory_space=pltpu.VMEM)
    both = 2 * ROWS
    result = (
        jax.ShapeDtypeStruct((ROWS, G), BF16),
        jax.ShapeDtypeStruct((ROWS, G), BF16),
        jax.ShapeDtypeStruct((LEVELS, G, G), F32),
        jax.ShapeDtypeStruct((LEVELS, G, G), F32),
    )
    operands = [pltpu.with_memory_space_constraint(a, pltpu.HBM) for a in (tokens, cotangent, up_weight[0], down_weight[0])]
    worked = pl.pallas_call(
        kernel,
        out_shape=tuple(pltpu.VMEM(a.shape, a.dtype) for a in result),
        in_specs=[anywhere, anywhere, anywhere, anywhere, pl.BlockSpec(memory_space=pltpu.SMEM)],
        out_specs=(vmem, vmem, anywhere, anywhere),
        scratch_shapes=[
            pltpu.VMEM((2, LEVELS, both, G), BF16),
            pltpu.VMEM((WIDE, both), BF16),
            pltpu.VMEM((2, LEVELS, G, G), BF16),
            pltpu.VMEM((WIDE, 2 * G), BF16),
            pltpu.VMEM((2 * G, WIDE), BF16),
            pltpu.VMEM((2 * G, WIDE), BF16),
            pltpu.VMEM((WIDE, 2 * G), BF16),
            pltpu.VMEM((both, 2 * G), BF16),
            pltpu.VMEM((2 * G, both), BF16),
            pltpu.VMEM((both, 2 * G), BF16),
            pltpu.VMEM((both, 2 * G), F32),
            pltpu.VMEM((both, 2 * G), F32),
            pltpu.VMEM((2, 2, both, G), BF16),
            pltpu.VMEM((2, 2, both, G), BF16),
            pltpu.VMEM((2, 2, both, G), F32),
            pltpu.VMEM((2, 2, both, G), BF16),
            pltpu.VMEM((2, 2, both, G), BF16),
            pltpu.VMEM((2, both, G), F32),
            pltpu.VMEM((2, both, G), F32),
            pltpu.VMEM((2, ROWS, G), BF16),
            pltpu.VMEM((2, ROWS, G), BF16),
            pltpu.VMEM((2, ROWS, G), BF16),
            pltpu.VMEM((2, both, G), BF16),
            pltpu.VMEM((2, both, G), BF16),
            pltpu.VMEM((2, LEVELS, G, G), F32),
            pltpu.VMEM((2, LEVELS, G, G), F32),
            pltpu.VMEM((2, LEVELS, G, G), F32),
            pltpu.SemaphoreType.DMA((len(FAMILIES),)),
            pltpu.SemaphoreType.DMA((COPIES,)),
            pltpu.SemaphoreType.DMA((4 + 2 * LEVELS,)),
        ],
        compiler_params=pltpu.CompilerParams(
            collective_id=0, has_side_effects=True, vmem_limit_bytes=58 * 1024 * 1024
        ),
    )(*operands, block_mask)
    worked = [pltpu.with_memory_space_constraint(a, pltpu.VMEM) for a in worked]
    output, grad_tokens, grad_up, grad_down = pl.pallas_call(
        hand_out,
        out_shape=result,
        in_specs=[anywhere] * 4,
        out_specs=(anywhere,) * 4,
        scratch_shapes=[pltpu.SemaphoreType.DMA((8,))],
        compiler_params=pltpu.CompilerParams(vmem_limit_bytes=1024 * 1024),
    )(*worked)
    return output, grad_tokens, grad_up[None], grad_down[None]


def solution(mesh):
    placed = (
        P("seq", "tp"),
        P(("seq", "tp"), None, None, None),
        P(("seq", "tp"), None, None, None),
        P(("seq", "tp"), None),
        P("seq", "tp"),
    )
    return jax.shard_map(
        shards,
        mesh=mesh,
        in_specs=placed,
        out_specs=(
            P("seq", "tp"),
            P("seq", "tp"),
            P(("seq", "tp"), None, None, None),
            P(("seq", "tp"), None, None, None),
        ),
        check_vma=False,
    )
```

```python
import functools
import math

import jax
import jax.numpy as jnp
from jax import lax
from jax.experimental import pallas as pl
from jax.experimental.pallas import tpu as pltpu
from jax.sharding import PartitionSpec as P

MESH = pl.DeviceIdType.MESH
F32 = jnp.float32
BF16 = jnp.bfloat16
ROWS = 512
PART = 128
PIECES = ROWS // PART
FIRST = PIECES // 2
TILE = 256
PER_TILE = TILE // PART
THIRDS = 2
G = 256
LEVELS = 6
WIDE = LEVELS * G
NEAR = {"x": 4, "y": 2}
FAR = {"x": 5, "y": 3}
SCALE = math.sqrt(2.0 / math.pi)
CUBE = 0.044715


def numbering():
    keys = []
    for which in range(2):
        keys += [(name, which, j) for name in ("z1", "z3", "zr", "out1", "out3", "half") for j in range(PIECES)]
        keys += [
            (name, axis, which, slot, j)
            for name in ("near", "far", "term", "sum")
            for axis in "xy"
            for slot in range(2)
            for j in range(PIECES)
        ]
        keys += [("weight", which)] + [("grad", which, k) for k in range(LEVELS // THIRDS)]
    keys += [("last", axis, j) for axis in "xy" for j in PASSED]
    return {key: n for n, key in enumerate(keys)}


def passed(which, slot, j):
    return which == 0 and slot == 0 and j in PASSED


def family(key):
    name = key[0]
    if name in ("weight", "grad"):
        return key
    if name in ("near", "far", "term", "sum"):
        return name, key[2], key[3]
    if name == "last":
        return name, key[2]
    return {"z1": "z", "z3": "z", "zr": "middle", "half": "middle", "out1": "out", "out3": "out"}[name], key[1]


PASSED = (2, 3)
NUMBER = numbering()
COPIES = len(NUMBER)
FAMILIES = {name: n for n, name in enumerate(dict.fromkeys(family(key) for key in NUMBER))}

ORDER = (
    ("oz", 0, 2), ("ox", 0, 3), ("oz", 0, 3), ("ox", 1, 3), ("su",), ("oz", 0, 0), ("ox", 0, 0), ("oz", 1, 2),
    ("ox", 0, 2), ("rz", 0, 2), ("ox", 0, 1), ("rx", 0, 0, 3), ("oz", 0, 1), ("rx", 1, 0, 3), ("rx", 0, 0, 0),
    ("rz", 0, 3), ("ox", 1, 2), ("rz", 0, 0), ("sd",), ("rx", 0, 0, 2), ("oz", 1, 3), ("ot", 0, 2), ("Fn", 0, 1),
    ("rz", 0, 1), ("ot", 0, 0), ("rx", 0, 0, 1), ("Fn", 0, 0), ("rx", 1, 0, 2), ("rz", 1, 2), ("ot", 0, 3),
    ("oz", 1, 1), ("F", 0, 1), ("rx", 0, 1, 2), ("ot", 0, 1), ("oz", 1, 0), ("ox", 1, 0), ("rx", 0, 1, 0),
    ("F", 0, 0), ("rx", 0, 1, 3), ("ta", 0, 1), ("ta", 0, 0), ("Fn", 1, 1), ("ot", 1, 2), ("rz", 1, 3), ("ox", 1, 1),
    ("TF", 0, 0, 1), ("TF", 0, 0, 0), ("rx", 0, 1, 1), ("rz", 1, 0), ("TN", 0, 0, 1), ("J", 0, 0, 2), ("Z", 0, 0, 3),
    ("rx", 1, 0, 0), ("rz", 1, 1), ("S", 0, 0, 1), ("tw",), ("F", 1, 1), ("TF", 0, 1, 1), ("S", 0, 1, 2),
    ("ot", 1, 0), ("ot", 1, 3), ("TN", 0, 1, 1), ("Fn", 1, 0), ("rx", 1, 0, 1), ("ot", 1, 1), ("F", 1, 0),
    ("TF", 0, 1, 0), ("S", 0, 1, 3), ("th", 0), ("rx", 1, 1, 2), ("S", 0, 0, 3), ("TN", 0, 1, 0), ("ta", 1, 1),
    ("Bn", 0, 1), ("Z", 0, 1, 0), ("S", 0, 1, 1), ("TN", 0, 0, 0), ("S", 0, 0, 2), ("Bn", 0, 0), ("J", 0, 1, 2),
    ("rx", 1, 1, 1), ("th", 1), ("rx", 1, 1, 0), ("B", 0, 0), ("W", ("weight", 0)), ("Z", 0, 1, 1), ("Bn", 1, 0),
    ("B", 0, 1), ("J", 0, 1, 1), ("rx", 1, 1, 3), ("Bn", 1, 1), ("W", ("near", 0, 0)), ("J", 0, 1, 3),
    ("Z", 0, 0, 2), ("W", ("z", 0)), ("J", 0, 0, 1), ("TF", 1, 0, 1), ("S", 0, 1, 0), ("ta", 1, 0), ("C", 0, 1, 2),
    ("J", 0, 0, 3), ("W", ("weight", 1)), ("B", 1, 0), ("TF", 1, 1, 0), ("S", 1, 1, 1), ("TN", 1, 0, 1),
    ("Z", 1, 0, 3), ("B", 1, 1), ("TF", 1, 1, 1), ("W", ("far", 0, 0)), ("S", 1, 1, 3), ("G", 1, 0), ("J", 0, 1, 0),
    ("S", 1, 1, 2), ("C", 0, 1, 1), ("TN", 1, 1, 0), ("J", 1, 1, 1), ("Z", 1, 1, 0), ("W", ("near", 0, 1)),
    ("S", 1, 1, 0), ("W", ("z", 1)), ("G", 1, 2), ("TN", 1, 1, 1), ("J", 1, 1, 3), ("C", 0, 1, 3), ("S", 0, 0, 0),
    ("Z", 1, 1, 1), ("G", 0, 0), ("J", 1, 1, 2), ("Z", 1, 0, 2), ("S", 1, 0, 3), ("W", ("near", 1, 0)),
    ("C", 0, 1, 0), ("PO", 0, 1), ("TF", 1, 0, 0), ("W", ("far", 0, 1)), ("J", 1, 1, 0), ("S", 1, 0, 0),
    ("C", 1, 1, 1), ("PO", 0, 2), ("G", 1, 1), ("C", 0, 0, 3), ("C", 1, 1, 3), ("J", 0, 0, 0), ("S", 1, 0, 2),
    ("G", 0, 1), ("TN", 1, 0, 0), ("J", 1, 0, 3), ("C", 1, 1, 2), ("S", 1, 0, 1), ("C", 1, 1, 0), ("J", 1, 0, 0),
    ("W", ("far", 1, 0)), ("PO", 0, 0), ("W", ("near", 1, 1)), ("G", 0, 2), ("PO", 1, 3), ("RL", 2), ("GS", 1, 0),
    ("J", 1, 0, 2), ("PO", 1, 1), ("RL", 3), ("PO", 0, 3), ("J", 1, 0, 1), ("C", 1, 0, 3), ("PO", 1, 0),
    ("C", 0, 0, 2), ("GS", 0, 0), ("PO", 1, 2), ("C", 0, 0, 1), ("C", 0, 0, 0), ("FIN", 0, 0), ("FIN", 1, 3),
    ("FIN", 0, 1), ("GS", 1, 1), ("FIN", 0, 2), ("GS", 0, 2), ("GS", 0, 1), ("GS", 1, 2), ("W", ("far", 1, 1)),
    ("C", 1, 0, 0), ("FIN", 0, 3), ("C", 1, 0, 1), ("FIN", 1, 1), ("FIN", 1, 0), ("C", 1, 0, 2),
    ("W", ("term", 0, 1)), ("FIN", 1, 2),
    ("W", ("middle", 0), ("middle", 1), ("sum", 0, 0), ("out", 0), ("term", 0, 0), ("sum", 0, 1), ("term", 1, 1), ("out", 1), ("grad", 1, 0), ("sum", 1, 1), ("grad", 1, 2), ("grad", 0, 0), ("term", 1, 0), ("grad", 1, 1), ("grad", 0, 1), ("sum", 1, 0), ("grad", 0, 2), ("last",)),
)


def flip(index, bit):
    return index + bit - 2 * bit * lax.rem(lax.div(index, bit), 2)


def kernel(
    tok, cot, up, down, mask, out, gtok, gup, gdown,
    held, held_t, raw, uall, dall, uall_t, dall_t, act, act_t, gpre, slope, gact,
    term_send, term_recv, near_term, sum_send, sum_recv, base, z_term,
    half_send, half_recv, last_recv, z_send, z_recv,
    grad_own, grad_peer, grad_recv,
    sends, recvs, local,
):
    shared = (tok, cot)
    seq, tp = lax.axis_index("seq"), lax.axis_index("tp")
    place = {
        "core": (flip(seq, 1), tp),
        "z1": (seq, flip(tp, 1)),
        "z3": (flip(seq, 2), flip(tp, 1)),
        "x1": (seq, flip(tp, 8)),
        "x3": (seq, flip(flip(tp, 8), 16)),
        "y1": (seq, flip(tp, 2)),
        "y3": (seq, flip(flip(tp, 2), 4)),
    }

    def remote(src, dst, key, target):
        return pltpu.make_async_remote_copy(
            src_ref=src,
            dst_ref=dst,
            send_sem=sends.at[FAMILIES[family(key)]],
            recv_sem=recvs.at[NUMBER[key]],
            device_id=place[target],
            device_id_type=MESH,
        )

    def rows(slot, j):
        start = slot * ROWS + j * PART
        return pl.ds(start if isinstance(j, int) else pl.multiple_of(start, PART), PART)

    def piece(j):
        return pl.ds(j * PART, PART)

    def columns(level):
        return pl.ds(level * G, G)

    def transfer(key):
        name, rest = key[0], key[1:]
        if name == "weight":
            if rest[0] == 0:
                return remote(uall.at[:, pl.ds(0, G)], uall.at[:, pl.ds(G, G)], key, "core")
            return remote(dall.at[pl.ds(0, G)], dall.at[pl.ds(G, G)], key, "core")
        if name == "grad":
            at = pl.ds(rest[1] * THIRDS, THIRDS)
            return remote(grad_peer.at[rest[0], at], grad_recv.at[rest[0], at], key, "core")
        if name == "last":
            a, j = "xy".index(rest[0]), rest[1]
            return remote(term_recv.at[0, a, rows(0, j)], last_recv.at[a, piece(j)], key, rest[0] + "3")
        if name in ("near", "far", "term", "sum"):
            axis, which, slot, j = rest
            a, at = "xy".index(axis), rows(slot, j)
            if name == "near":
                src = held.at[which, 0, at] if slot else shared[which].at[piece(j)]
                return remote(src, held.at[which, NEAR[axis], at], key, axis + "1")
            if name == "far":
                return remote(held.at[which, NEAR[axis], at], held.at[which, FAR[axis], at], key, axis + "3")
            if name == "term":
                target = axis + ("1" if passed(which, slot, j) else "3")
                return remote(term_send.at[which, a, at], term_recv.at[which, a, at], key, target)
            return remote(sum_send.at[which, a, at], sum_recv.at[which, a, at], key, axis + "1")
        which, j = rest
        if name == "z1":
            return remote(shared[which].at[piece(j)], held.at[which, 1, rows(0, j)], key, "z1")
        if name == "z3":
            return remote(shared[which].at[piece(j)], held.at[which, 1, rows(1, j)], key, "z3")
        onward = "z3" if j < FIRST else "z1"
        if name == "zr":
            return remote(held.at[which, 1, rows(int(j >= FIRST), j)], held.at[which, 0, rows(1, j)], key, onward)
        if name == "half":
            return remote(half_send.at[which, piece(j)], half_recv.at[which, piece(j)], key, onward)
        slot = int(name == "out3")
        return remote(z_send.at[which, rows(slot, j)], z_recv.at[which, rows(slot, j)], key, "z3" if slot else "z1")

    started, landed, copied, sent = set(), set(), set(), set()

    def send(*keys):
        for key in keys:
            started.add(key)
            transfer(key).start()

    def need(*keys):
        for key in keys:
            if key not in landed:
                landed.add(key)
                transfer(key).wait_recv()

    own = [
        pltpu.make_async_copy(shared[which], held.at[which, 0, pl.ds(0, ROWS)], local.at[which])
        for which in range(2)
    ]
    loads = [pltpu.make_async_copy(ref, raw.at[which], local.at[2 + which]) for which, ref in enumerate((up, down))]
    for copy in loads + own:
        copy.start()

    barrier = pltpu.get_barrier_semaphore()
    for target in place.values():
        pl.semaphore_signal(barrier, inc=1, device_id=target, device_id_type=MESH)
    pl.semaphore_wait(barrier, len(place))

    def scale_up(k, carry):
        factor = mask[0, k].astype(F32)
        uall[pl.ds(pl.multiple_of(k * G, G), G), pl.ds(0, G)] = (raw[0, k].astype(F32) * factor).astype(BF16)
        return carry

    def scale_down(k, carry):
        factor = mask[0, k].astype(F32)
        dall[pl.ds(0, G), pl.ds(pl.multiple_of(k * G, G), G)] = (raw[1, k].astype(F32) * factor).astype(BF16)
        return carry

    def tile(slot, t):
        return pl.ds(slot * ROWS + t * TILE, TILE)

    def own_z(which, j):
        send(("z1", which, j), ("z3", which, j))

    def own_xy(which, j):
        send(("near", "x", which, 0, j), ("near", "y", which, 0, j))

    def relay_z(which, j):
        need(("z1" if j < FIRST else "z3", which, j))
        send(("zr", which, j))

    def other(which, j):
        need(("zr", which, j))
        send(("near", "x", which, 1, j), ("near", "y", which, 1, j))

    def relay_xy(which, slot, j):
        for axis in "xy":
            need(("near", axis, which, slot, j))
            send(("far", axis, which, slot, j))

    def mask_up():
        loads[0].wait()
        lax.fori_loop(0, LEVELS, scale_up, 0)
        send(("weight", 0))

    def mask_down():
        loads[1].wait()
        lax.fori_loop(0, LEVELS, scale_down, 0)
        send(("weight", 1))

    def turn_weights():
        need(("weight", 0), ("weight", 1))

        def body(k, carry):
            at = pl.ds(pl.multiple_of(k * G, G), G)
            dall_t[at, :] = dall[:, at].T
            uall_t[:, at] = uall[at, :].T
            return carry

        lax.fori_loop(0, LEVELS, body, 0)

    def turn_held(slot):
        def body(k, carry):
            at = pl.ds(pl.multiple_of(k * G, G), G)
            held_t[at, pl.ds(slot * ROWS, ROWS)] = held[0, k, pl.ds(slot * ROWS, ROWS)].T
            return carry

        lax.fori_loop(0, LEVELS, body, 0)

    def turn_act(slot, t):
        act_t[:, tile(slot, t)] = act[tile(slot, t), :].T

    def near_inputs(which, slot, t):
        if slot == 0 and ("own", which) not in copied:
            copied.add(("own", which))
            own[which].wait()
        for j in range(t * PER_TILE, (t + 1) * PER_TILE):
            need(("z3" if slot else "z1", which, j))

    def far_inputs(which, slot, t):
        for j in range(t * PER_TILE, (t + 1) * PER_TILE):
            for axis in "xy":
                need(("far", axis, which, slot, j))

    def partial(which, at, weights):
        early = jnp.concatenate([held[which, level, at] for level in (0, 1, 2)], axis=1)
        total = jnp.dot(early, weights[pl.ds(0, 3 * G), :], preferred_element_type=F32)
        return total + jnp.dot(held[which, 4, at], weights[pl.ds(4 * G, G), :], preferred_element_type=F32)

    def rest(which, at, weights):
        total = jnp.dot(held[which, 3, at], weights[pl.ds(3 * G, G), :], preferred_element_type=F32)
        return total + jnp.dot(held[which, 5, at], weights[pl.ds(5 * G, G), :], preferred_element_type=F32)

    def forward_near(slot, t):
        near_inputs(0, slot, t)
        need(("weight", 0))
        slope[tile(slot, t), :] = partial(0, tile(slot, t), uall)

    def backward_near(slot, t):
        near_inputs(1, slot, t)
        gact[tile(slot, t), :] = partial(1, tile(slot, t), dall_t)

    def forward(slot, t):
        far_inputs(0, slot, t)
        at = tile(slot, t)
        pre = slope[at, :] + rest(0, at, uall)
        square = pre * pre
        tanh = jnp.tanh(SCALE * pre * (1.0 + CUBE * square))
        cdf = 0.5 + 0.5 * tanh
        act[at, :] = (pre * cdf).astype(BF16)
        slope[at, :] = cdf + (0.5 * SCALE) * pre * (1.0 - tanh * tanh) * (1.0 + (3.0 * CUBE) * square)

    def backward(slot, t):
        far_inputs(1, slot, t)
        at = tile(slot, t)
        gpre[at, :] = ((gact[at, :] + rest(1, at, dall_t)) * slope[at, :]).astype(BF16)

    def product(which, slot, t, level):
        if which:
            return jnp.dot(gpre[tile(slot, t), :], uall_t[:, columns(level)], preferred_element_type=F32)
        return jnp.dot(act[tile(slot, t), :], dall[:, columns(level)], preferred_element_type=F32)

    def far_terms(which, slot, t):
        need(("weight", 1))
        for a, axis in enumerate("xy"):
            term_send[which, a, tile(slot, t)] = product(which, slot, t, FAR[axis]).astype(BF16)

    def near_terms(which, slot, t):
        at = tile(slot, t)
        for a, axis in enumerate("xy"):
            near_term[which, a, at] = product(which, slot, t, NEAR[axis])
        z_term[which, at] = product(which, slot, t, 1)
        base[which, at] = product(which, slot, t, 0)

    def send_term(which, slot, j):
        send(("term", "x", which, slot, j), ("term", "y", which, slot, j))

    def hand_on(j):
        for axis in "xy":
            need(("term", axis, 0, 0, j))
            send(("last", axis, j))

    def join(which, slot, j):
        at = rows(slot, j)
        for a, axis in enumerate("xy"):
            total = near_term[which, a, at]
            if not passed(which, slot, j):
                need(("term", axis, which, slot, j))
                total = total + term_recv[which, a, at].astype(F32)
            sum_send[which, a, at] = total.astype(BF16)
            send(("sum", axis, which, slot, j))

    def collect(which, slot, j):
        at = rows(slot, j)
        need(("sum", "x", which, slot, j), ("sum", "y", which, slot, j))
        total = base[which, at] + sum_recv[which, 0, at].astype(F32) + sum_recv[which, 1, at].astype(F32)
        if slot == 0:
            base[which, at] = total
        else:
            half_send[which, piece(j)] = total.astype(BF16)
            send(("half", which, j))

    def plain(which, slot, j):
        z_send[which, rows(slot, j)] = z_term[which, rows(slot, j)].astype(BF16)
        send(("out3" if slot else "out1", which, j))

    def pass_on(which, j):
        slot = int(j >= FIRST)
        at = rows(slot, j)
        need(("half", which, j))
        z_send[which, at] = (z_term[which, at] + half_recv[which, piece(j)].astype(F32)).astype(BF16)
        send(("out3" if slot else "out1", which, j))

    def finish(which, j):
        need(("out1", which, j), ("out3", which, j))
        total = base[which, rows(0, j)] + z_recv[which, rows(0, j)].astype(F32) + z_recv[which, rows(1, j)].astype(F32)
        if passed(which, 0, j):
            need(("last", "x", j), ("last", "y", j))
            total = total + last_recv[0, piece(j)].astype(F32) + last_recv[1, piece(j)].astype(F32)
        (gtok if which else out)[piece(j), :] = total.astype(BF16)

    def grads(which, third):
        def body(k, carry):
            at = pl.ds(pl.multiple_of(k * G, G), G)
            if which:
                both = jnp.dot(act_t[...], held[1, k], preferred_element_type=F32)
                grad_own[1, k] = both[:G]
                grad_peer[1, k] = both[G:].astype(BF16)
            else:
                both = jnp.dot(held_t[at, :], gpre[...], preferred_element_type=F32)
                grad_own[0, k] = both[:, :G]
                grad_peer[0, k] = both[:, G:].astype(BF16)
            return carry

        lax.fori_loop(third * THIRDS, (third + 1) * THIRDS, body, 0)
        send(("grad", which, third))

    def write_grad(which, k):
        return pltpu.make_async_copy(grad_own.at[which, k], (gdown if which else gup).at[k], local.at[4 + which * LEVELS + k])

    def grads_sum(which, third):
        need(("grad", which, third))

        def body(k, carry):
            grad_own[which, k] = (grad_own[which, k] + grad_recv[which, k].astype(F32)) * mask[0, k].astype(F32)
            write_grad(which, k).start()
            return carry

        lax.fori_loop(third * THIRDS, (third + 1) * THIRDS, body, 0)

    def finish_sends(*names):
        for name in names:
            sent.update([(name[0], j) for j in PASSED] if name[0] == "last" else [name])
            if name[0] in ("weight", "grad"):
                transfer(name).wait_send()
            elif name[0] == "last":
                for j in PASSED:
                    span = pl.ds(0, 2 * PART)
                    pltpu.make_async_remote_copy(
                        src_ref=held.at[0, 0, span],
                        dst_ref=held.at[0, 0, span],
                        send_sem=sends.at[FAMILIES["last", j]],
                        recv_sem=recvs.at[0],
                        device_id=place["z1"],
                        device_id_type=MESH,
                    ).wait_send()
            else:
                pltpu.make_async_remote_copy(
                    src_ref=held.at[0, 0],
                    dst_ref=held.at[0, 0],
                    send_sem=sends.at[FAMILIES[name]],
                    recv_sem=recvs.at[0],
                    device_id=place["z1"],
                    device_id_type=MESH,
                ).wait_send()

    steps = {
        "W": finish_sends,
        "oz": own_z, "ox": own_xy, "rz": relay_z, "ot": other, "rx": relay_xy, "su": mask_up, "sd": mask_down,
        "tw": turn_weights, "th": turn_held, "ta": turn_act, "F": forward, "B": backward, "Fn": forward_near, "Bn": backward_near, "TF": far_terms,
        "TN": near_terms, "S": send_term, "RL": hand_on, "J": join, "C": collect, "Z": plain, "PO": pass_on,
        "FIN": finish, "G": grads, "GS": grads_sum,
    }
    for step in ORDER:
        steps[step[0]](*step[1:])

    assert started == landed == set(NUMBER)
    for which in range(2):
        for k in range(LEVELS):
            write_grad(which, k).wait()
    assert sent == set(FAMILIES)


def hand_out(*refs):
    sources, results, sems = refs[:4], refs[4:8], refs[8]
    copies = []
    for src, dst in zip(sources, results):
        if len(src.shape) == 2:
            pairs = [(src, dst)]
        else:
            pairs = [(src.at[pl.ds(k, 2)], dst.at[pl.ds(k, 2)]) for k in range(0, LEVELS, 2)]
        for a, b in pairs:
            copies.append(pltpu.make_async_copy(a, b, sems.at[len(copies)]))
    for copy in copies:
        copy.start()
    for copy in copies:
        copy.wait()


def shards(tokens, up_weight, down_weight, block_mask, cotangent):
    anywhere = pl.BlockSpec(memory_space=pl.ANY)
    vmem = pl.BlockSpec(memory_space=pltpu.VMEM)
    both = 2 * ROWS
    result = (
        jax.ShapeDtypeStruct((ROWS, G), BF16),
        jax.ShapeDtypeStruct((ROWS, G), BF16),
        jax.ShapeDtypeStruct((LEVELS, G, G), F32),
        jax.ShapeDtypeStruct((LEVELS, G, G), F32),
    )
    operands = [pltpu.with_memory_space_constraint(a, pltpu.HBM) for a in (tokens, cotangent, up_weight[0], down_weight[0])]
    worked = pl.pallas_call(
        kernel,
        out_shape=tuple(pltpu.VMEM(a.shape, a.dtype) for a in result),
        in_specs=[anywhere, anywhere, anywhere, anywhere, pl.BlockSpec(memory_space=pltpu.SMEM)],
        out_specs=(vmem, vmem, anywhere, anywhere),
        scratch_shapes=[
            pltpu.VMEM((2, LEVELS, both, G), BF16),
            pltpu.VMEM((WIDE, both), BF16),
            pltpu.VMEM((2, LEVELS, G, G), BF16),
            pltpu.VMEM((WIDE, 2 * G), BF16),
            pltpu.VMEM((2 * G, WIDE), BF16),
            pltpu.VMEM((2 * G, WIDE), BF16),
            pltpu.VMEM((WIDE, 2 * G), BF16),
            pltpu.VMEM((both, 2 * G), BF16),
            pltpu.VMEM((2 * G, both), BF16),
            pltpu.VMEM((both, 2 * G), BF16),
            pltpu.VMEM((both, 2 * G), F32),
            pltpu.VMEM((both, 2 * G), F32),
            pltpu.VMEM((2, 2, both, G), BF16),
            pltpu.VMEM((2, 2, both, G), BF16),
            pltpu.VMEM((2, 2, both, G), F32),
            pltpu.VMEM((2, 2, both, G), BF16),
            pltpu.VMEM((2, 2, both, G), BF16),
            pltpu.VMEM((2, both, G), F32),
            pltpu.VMEM((2, both, G), F32),
            pltpu.VMEM((2, ROWS, G), BF16),
            pltpu.VMEM((2, ROWS, G), BF16),
            pltpu.VMEM((2, ROWS, G), BF16),
            pltpu.VMEM((2, both, G), BF16),
            pltpu.VMEM((2, both, G), BF16),
            pltpu.VMEM((2, LEVELS, G, G), F32),
            pltpu.VMEM((2, LEVELS, G, G), BF16),
            pltpu.VMEM((2, LEVELS, G, G), BF16),
            pltpu.SemaphoreType.DMA((len(FAMILIES),)),
            pltpu.SemaphoreType.DMA((COPIES,)),
            pltpu.SemaphoreType.DMA((4 + 2 * LEVELS,)),
        ],
        compiler_params=pltpu.CompilerParams(
            collective_id=0, has_side_effects=True, vmem_limit_bytes=58 * 1024 * 1024
        ),
    )(*operands, block_mask)
    worked = [pltpu.with_memory_space_constraint(a, pltpu.VMEM) for a in worked]
    output, grad_tokens, grad_up, grad_down = pl.pallas_call(
        hand_out,
        out_shape=result,
        in_specs=[anywhere] * 4,
        out_specs=(anywhere,) * 4,
        scratch_shapes=[pltpu.SemaphoreType.DMA((8,))],
        compiler_params=pltpu.CompilerParams(vmem_limit_bytes=1024 * 1024),
    )(*worked)
    return output, grad_tokens, grad_up[None], grad_down[None]


def solution(mesh):
    placed = (
        P("seq", "tp"),
        P(("seq", "tp"), None, None, None),
        P(("seq", "tp"), None, None, None),
        P(("seq", "tp"), None),
        P("seq", "tp"),
    )
    return jax.shard_map(
        shards,
        mesh=mesh,
        in_specs=placed,
        out_specs=(
            P("seq", "tp"),
            P("seq", "tp"),
            P(("seq", "tp"), None, None, None),
            P(("seq", "tp"), None, None, None),
        ),
        check_vma=False,
    )
```

```python
import collections
import math

import jax
import jax.numpy as jnp
from jax import lax
from jax.experimental import pallas as pl
from jax.experimental.pallas import tpu as pltpu
from jax.sharding import PartitionSpec as P

MESH = pl.DeviceIdType.MESH
F32 = jnp.float32
BF16 = jnp.bfloat16
ROWS = 512
PART = 128
PIECES = ROWS // PART
FIRST = PIECES // 2
TILE = 256
PER_TILE = TILE // PART
THIRDS = 3
G = 256
LEVELS = 6
WIDE = LEVELS * G
NEAR = {"x": 4, "y": 2}
FAR = {"x": 5, "y": 3}
SCALE = math.sqrt(2.0 / math.pi)
CUBE = 0.044715


def numbering():
    keys = []
    for which in range(2):
        keys += [(name, which, j) for name in ("z1", "z3", "zr", "out1", "out3", "half") for j in range(PIECES)]
        keys += [
            (name, axis, which, slot, j)
            for name in ("near", "far", "term", "sum")
            for axis in "xy"
            for slot in range(2)
            for j in range(PIECES)
        ]
        keys += [("weight", which)] + [("grad", which, k) for k in range(LEVELS // THIRDS)]
    keys += [("last", axis, j) for axis in "xy" for j in PASSED]
    moved = [(axis, level, which, j) for axis in "xy" for level in "nf" for which, j in MOVED]
    keys += [("hop", *rest) for rest in moved] + [("land", *rest) for rest in moved]
    keys = [k for k in keys if not (k[0] in ("near", "far") and k[3] == 1 and (k[2], k[4]) in MOVED)]
    return {key: n for n, key in enumerate(keys)}


def passed(which, slot, j):
    return which == 0 and slot == 0 and j in PASSED


def family(key):
    name = key[0]
    if name in ("weight", "grad"):
        return key
    if name in ("near", "far", "term", "sum"):
        return name, key[2], key[3]
    if name in ("last", "hop", "land"):
        return (name,)
    return {"z1": "z", "z3": "z", "zr": "middle", "half": "middle", "out1": "out", "out3": "out"}[name], key[1]


PASSED = (2, 3)
MOVED = ((1, 0), (1, 2))
NUMBER = numbering()
COPIES = len(NUMBER)
SIZES = collections.Counter(family(key) for key in NUMBER)
FAMILIES = {name: n for n, name in enumerate(SIZES)}

ORDER = (
    ("oz", 0, 3), ("ox", 0, 3), ("ox", 1, 0), ("oz", 0, 2), ("oz", 0, 1), ("su",), ("oz", 1, 1), ("ox", 1, 2),
    ("ox", 0, 2), ("sd",), ("ox", 0, 1), ("rx", 0, 0, 3), ("ox", 0, 0), ("oz", 0, 0), ("rx", 1, 0, 0), ("ox", 1, 3),
    ("rz", 0, 3), ("rz", 0, 2), ("rx", 1, 0, 2), ("rz", 0, 1), ("oz", 1, 3), ("ox", 1, 1), ("h1", "x", "n", 1, 2),
    ("rx", 0, 0, 2), ("Fn", 0, 1), ("rz", 0, 0), ("rz", 1, 1), ("rx", 0, 0, 1), ("oz", 1, 2), ("h1", "y", "f", 1, 0),
    ("tw",), ("ot", 0, 3), ("h1", "y", "f", 1, 2), ("h1", "x", "f", 1, 2), ("rx", 0, 0, 0), ("F", 0, 1),
    ("rz", 1, 3), ("ot", 0, 2), ("rx", 1, 0, 3), ("h1", "x", "n", 1, 0), ("ot", 0, 1), ("h1", "x", "f", 1, 0),
    ("Fn", 0, 0), ("rx", 1, 0, 1), ("h1", "y", "n", 1, 2), ("h1", "y", "n", 1, 0), ("ot", 0, 0), ("TF", 0, 0, 1),
    ("oz", 1, 0), ("rx", 0, 1, 3), ("TN", 0, 0, 1), ("F", 0, 0), ("TF", 0, 0, 0), ("rx", 0, 1, 2), ("rz", 1, 2),
    ("ot", 1, 1), ("Bn", 0, 1), ("h2", "x", "n", 1, 2), ("B", 0, 1), ("TF", 1, 0, 1), ("rx", 0, 1, 1),
    ("TN", 0, 0, 0), ("ot", 1, 3), ("S", 0, 0, 2), ("TN", 1, 0, 1), ("S", 1, 0, 2), ("h2", "y", "f", 1, 2),
    ("Fn", 1, 1), ("ta", 0, 1), ("J", 0, 0, 2), ("rx", 0, 1, 0), ("F", 1, 1), ("TF", 0, 1, 1), ("S", 0, 1, 2),
    ("h2", "y", "f", 1, 0), ("S", 0, 0, 3), ("rx", 1, 1, 1), ("h2", "x", "n", 1, 0), ("J", 0, 0, 3), ("Fn", 1, 0),
    ("TN", 0, 1, 1), ("S", 0, 1, 3), ("rz", 1, 0), ("Bn", 0, 0), ("ta", 0, 0), ("W", ("weight", 0)),
    ("h2", "x", "f", 1, 0), ("h2", "x", "f", 1, 2), ("B", 0, 0), ("h2", "y", "n", 1, 0), ("W", ("weight", 1)),
    ("TF", 1, 0, 0), ("rx", 1, 1, 3), ("F", 1, 0), ("W", ("near", 0, 0)), ("J", 1, 0, 2), ("W", ("z", 0)),
    ("h2", "y", "n", 1, 2), ("Z", 0, 0, 2), ("TF", 0, 1, 0), ("ta", 1, 0), ("ot", 1, 2), ("S", 0, 1, 0),
    ("Z", 0, 0, 3), ("J", 0, 1, 2), ("W", ("near", 1, 0)), ("Z", 1, 0, 3), ("ta", 1, 1), ("ot", 1, 0),
    ("TN", 0, 1, 0), ("th", 0), ("Z", 0, 1, 0), ("Bn", 1, 0), ("Z", 1, 0, 2), ("B", 1, 0), ("TF", 1, 1, 0),
    ("S", 1, 1, 1), ("TN", 1, 1, 0), ("J", 0, 1, 3), ("W", ("far", 0, 0)), ("S", 1, 1, 0), ("Bn", 1, 1), ("B", 1, 1),
    ("TF", 1, 1, 1), ("J", 0, 1, 0), ("S", 1, 1, 3), ("Z", 1, 1, 1), ("S", 0, 1, 1), ("S", 1, 1, 2),
    ("W", ("far", 1, 0)), ("S", 0, 0, 1), ("Z", 1, 1, 0), ("W", ("hop",)), ("TN", 1, 1, 1), ("W", ("near", 0, 1)),
    ("S", 1, 0, 3), ("J", 1, 1, 1), ("W", ("z", 1)), ("G", 1, 1), ("J", 1, 1, 0), ("C", 0, 1, 0), ("S", 0, 0, 0),
    ("J", 1, 1, 3), ("Z", 0, 1, 1), ("G", 1, 0), ("C", 0, 1, 2), ("C", 1, 1, 1), ("J", 0, 1, 1), ("C", 0, 1, 3),
    ("J", 1, 1, 2), ("th", 1), ("S", 1, 0, 0), ("S", 1, 0, 1), ("C", 1, 1, 0), ("C", 1, 1, 3), ("G", 0, 1),
    ("PO", 0, 2), ("J", 0, 0, 1), ("PO", 0, 0), ("TN", 1, 0, 0), ("W", ("far", 0, 1)), ("J", 1, 0, 3),
    ("C", 0, 1, 1), ("RL", 2), ("C", 1, 1, 2), ("J", 0, 0, 0), ("PO", 1, 1), ("PO", 0, 3), ("G", 0, 0), ("PO", 1, 3),
    ("J", 1, 0, 1), ("PO", 1, 0), ("C", 1, 0, 2), ("RL", 3), ("PO", 0, 1), ("J", 1, 0, 0), ("PO", 1, 2),
    ("GS", 1, 0), ("GS", 0, 1), ("C", 0, 0, 2), ("GS", 1, 1), ("W", ("far", 1, 1)), ("C", 0, 0, 1), ("C", 0, 0, 0),
    ("C", 1, 0, 3), ("W", ("land",)), ("FIN", 0, 2), ("FIN", 0, 0), ("C", 0, 0, 3), ("FIN", 1, 3), ("C", 1, 0, 1),
    ("FIN", 1, 1), ("FIN", 0, 3), ("GS", 0, 0), ("FIN", 1, 2), ("C", 1, 0, 0), ("W", ("near", 1, 1)), ("FIN", 1, 0),
    ("FIN", 0, 1),
    ("W", ("middle", 0), ("middle", 1), ("term", 0, 0), ("term", 1, 0), ("sum", 0, 0), ("term", 0, 1), ("sum", 1, 0), ("out", 0), ("sum", 0, 1), ("out", 1), ("term", 1, 1), ("sum", 1, 1), ("grad", 1, 1), ("grad", 1, 0), ("grad", 0, 1), ("last",), ("grad", 0, 0)),
)


def flip(index, bit):
    return index + bit - 2 * bit * lax.rem(lax.div(index, bit), 2)


def kernel(
    tok, cot, up, down, mask, out, gtok, gup, gdown,
    held, held_t, raw, uall, dall, uall_t, dall_t, act, act_t, gpre, slope, gact,
    term_send, term_recv, near_term, sum_send, sum_recv, base, z_term,
    half_send, half_recv, last_recv, hops, z_send, z_recv,
    grad_own, grad_peer, grad_recv,
    sends, recvs, local,
):
    shared = (tok, cot)
    seq, tp = lax.axis_index("seq"), lax.axis_index("tp")
    place = {
        "core": (flip(seq, 1), tp),
        "z1": (seq, flip(tp, 1)),
        "z3": (flip(seq, 2), flip(tp, 1)),
        "x1": (seq, flip(tp, 8)),
        "x3": (seq, flip(flip(tp, 8), 16)),
        "y1": (seq, flip(tp, 2)),
        "y3": (seq, flip(flip(tp, 2), 4)),
    }

    def remote(src, dst, key, target):
        return pltpu.make_async_remote_copy(
            src_ref=src,
            dst_ref=dst,
            send_sem=sends.at[FAMILIES[family(key)]],
            recv_sem=recvs.at[NUMBER[key]],
            device_id=place[target],
            device_id_type=MESH,
        )

    def rows(slot, j):
        start = slot * ROWS + j * PART
        return pl.ds(start if isinstance(j, int) else pl.multiple_of(start, PART), PART)

    def piece(j):
        return pl.ds(j * PART, PART)

    def columns(level):
        return pl.ds(level * G, G)

    def transfer(key):
        name, rest = key[0], key[1:]
        if name == "weight":
            if rest[0] == 0:
                return remote(uall.at[:, pl.ds(0, G)], uall.at[:, pl.ds(G, G)], key, "core")
            return remote(dall.at[pl.ds(0, G)], dall.at[pl.ds(G, G)], key, "core")
        if name == "grad":
            at = pl.ds(rest[1] * THIRDS, THIRDS)
            return remote(grad_peer.at[rest[0], at], grad_recv.at[rest[0], at], key, "core")
        if name == "last":
            a, j = "xy".index(rest[0]), rest[1]
            return remote(term_recv.at[0, a, rows(0, j)], last_recv.at[a, piece(j)], key, rest[0] + "3")
        if name in ("hop", "land"):
            axis, level, which, j = rest
            n, group = "nf".index(level), (NEAR if level == "n" else FAR)[axis]
            room = hops.at[n, "xy".index(axis), pl.ds(MOVED.index((which, j)) * PART, PART)]
            if name == "hop":
                return remote(held.at[which, group, rows(0, j)], room, key, ("z1", "z3")[n])
            return remote(room, held.at[which, group, rows(1, j)], key, ("z3", "z1")[n])
        if name in ("near", "far", "term", "sum"):
            axis, which, slot, j = rest
            a, at = "xy".index(axis), rows(slot, j)
            if name == "near":
                src = held.at[which, 0, at] if slot else shared[which].at[piece(j)]
                return remote(src, held.at[which, NEAR[axis], at], key, axis + "1")
            if name == "far":
                return remote(held.at[which, NEAR[axis], at], held.at[which, FAR[axis], at], key, axis + "3")
            if name == "term":
                target = axis + ("1" if passed(which, slot, j) else "3")
                return remote(term_send.at[which, a, at], term_recv.at[which, a, at], key, target)
            return remote(sum_send.at[which, a, at], sum_recv.at[which, a, at], key, axis + "1")
        which, j = rest
        if name == "z1":
            return remote(shared[which].at[piece(j)], held.at[which, 1, rows(0, j)], key, "z1")
        if name == "z3":
            return remote(shared[which].at[piece(j)], held.at[which, 1, rows(1, j)], key, "z3")
        onward = "z3" if j < FIRST else "z1"
        if name == "zr":
            return remote(held.at[which, 1, rows(int(j >= FIRST), j)], held.at[which, 0, rows(1, j)], key, onward)
        if name == "half":
            return remote(half_send.at[which, piece(j)], half_recv.at[which, piece(j)], key, onward)
        slot = int(name == "out3")
        return remote(z_send.at[which, rows(slot, j)], z_recv.at[which, rows(slot, j)], key, "z3" if slot else "z1")

    started, landed, copied, sent = set(), set(), set(), set()

    def send(*keys):
        for key in keys:
            started.add(key)
            transfer(key).start()

    def need(*keys):
        for key in keys:
            if key not in landed:
                landed.add(key)
                transfer(key).wait_recv()

    own = [
        pltpu.make_async_copy(shared[which], held.at[which, 0, pl.ds(0, ROWS)], local.at[which])
        for which in range(2)
    ]
    loads = [pltpu.make_async_copy(ref, raw.at[which], local.at[2 + which]) for which, ref in enumerate((up, down))]
    for copy in loads + own:
        copy.start()

    barrier = pltpu.get_barrier_semaphore()
    for target in place.values():
        pl.semaphore_signal(barrier, inc=1, device_id=target, device_id_type=MESH)
    pl.semaphore_wait(barrier, len(place))

    def scale_up(k, carry):
        factor = mask[0, k].astype(F32)
        uall[pl.ds(pl.multiple_of(k * G, G), G), pl.ds(0, G)] = (raw[0, k].astype(F32) * factor).astype(BF16)
        return carry

    def scale_down(k, carry):
        factor = mask[0, k].astype(F32)
        dall[pl.ds(0, G), pl.ds(pl.multiple_of(k * G, G), G)] = (raw[1, k].astype(F32) * factor).astype(BF16)
        return carry

    def tile(slot, t):
        return pl.ds(slot * ROWS + t * TILE, TILE)

    def own_z(which, j):
        send(("z1", which, j), ("z3", which, j))

    def own_xy(which, j):
        send(("near", "x", which, 0, j), ("near", "y", which, 0, j))

    def relay_z(which, j):
        need(("z1" if j < FIRST else "z3", which, j))
        send(("zr", which, j))

    def other(which, j):
        need(("zr", which, j))
        if (which, j) not in MOVED:
            send(("near", "x", which, 1, j), ("near", "y", which, 1, j))

    def relay_xy(which, slot, j):
        for axis in "xy":
            need(("near", axis, which, slot, j))
            send(("far", axis, which, slot, j))

    def hop(axis, level, which, j):
        need(("near" if level == "n" else "far", axis, which, 0, j))
        send(("hop", axis, level, which, j))

    def land(axis, level, which, j):
        need(("hop", axis, level, which, j))
        send(("land", axis, level, which, j))

    def mask_up():
        loads[0].wait()
        lax.fori_loop(0, LEVELS, scale_up, 0)
        send(("weight", 0))

    def mask_down():
        loads[1].wait()
        lax.fori_loop(0, LEVELS, scale_down, 0)
        send(("weight", 1))

    def turn_weights():
        need(("weight", 0), ("weight", 1))

        def body(k, carry):
            at = pl.ds(pl.multiple_of(k * G, G), G)
            dall_t[at, :] = dall[:, at].T
            uall_t[:, at] = uall[at, :].T
            return carry

        lax.fori_loop(0, LEVELS, body, 0)

    def turn_held(slot):
        def body(k, carry):
            at = pl.ds(pl.multiple_of(k * G, G), G)
            held_t[at, pl.ds(slot * ROWS, ROWS)] = held[0, k, pl.ds(slot * ROWS, ROWS)].T
            return carry

        lax.fori_loop(0, LEVELS, body, 0)

    def turn_act(slot, t):
        act_t[:, tile(slot, t)] = act[tile(slot, t), :].T

    def near_inputs(which, slot, t):
        if slot == 0 and ("own", which) not in copied:
            copied.add(("own", which))
            own[which].wait()
        for j in range(t * PER_TILE, (t + 1) * PER_TILE):
            need(("z3" if slot else "z1", which, j))
            if slot and (which, j) in MOVED:
                need(("land", "x", "n", which, j), ("land", "y", "n", which, j))

    def far_inputs(which, slot, t):
        for j in range(t * PER_TILE, (t + 1) * PER_TILE):
            for axis in "xy":
                need(("land", axis, "f", which, j) if slot and (which, j) in MOVED else ("far", axis, which, slot, j))

    def partial(which, at, weights):
        early = jnp.concatenate([held[which, level, at] for level in (0, 1, 2)], axis=1)
        total = jnp.dot(early, weights[pl.ds(0, 3 * G), :], preferred_element_type=F32)
        return total + jnp.dot(held[which, 4, at], weights[pl.ds(4 * G, G), :], preferred_element_type=F32)

    def rest(which, at, weights):
        total = jnp.dot(held[which, 3, at], weights[pl.ds(3 * G, G), :], preferred_element_type=F32)
        return total + jnp.dot(held[which, 5, at], weights[pl.ds(5 * G, G), :], preferred_element_type=F32)

    def forward_near(slot, t):
        near_inputs(0, slot, t)
        need(("weight", 0))
        slope[tile(slot, t), :] = partial(0, tile(slot, t), uall)

    def backward_near(slot, t):
        near_inputs(1, slot, t)
        gact[tile(slot, t), :] = partial(1, tile(slot, t), dall_t)

    def forward(slot, t):
        far_inputs(0, slot, t)
        at = tile(slot, t)
        pre = slope[at, :] + rest(0, at, uall)
        square = pre * pre
        tanh = jnp.tanh(SCALE * pre * (1.0 + CUBE * square))
        cdf = 0.5 + 0.5 * tanh
        act[at, :] = (pre * cdf).astype(BF16)
        slope[at, :] = cdf + (0.5 * SCALE) * pre * (1.0 - tanh * tanh) * (1.0 + (3.0 * CUBE) * square)

    def backward(slot, t):
        far_inputs(1, slot, t)
        at = tile(slot, t)
        gpre[at, :] = ((gact[at, :] + rest(1, at, dall_t)) * slope[at, :]).astype(BF16)

    def product(which, slot, t, level):
        if which:
            return jnp.dot(gpre[tile(slot, t), :], uall_t[:, columns(level)], preferred_element_type=F32)
        return jnp.dot(act[tile(slot, t), :], dall[:, columns(level)], preferred_element_type=F32)

    def far_terms(which, slot, t):
        need(("weight", 1))
        for a, axis in enumerate("xy"):
            term_send[which, a, tile(slot, t)] = product(which, slot, t, FAR[axis]).astype(BF16)

    def near_terms(which, slot, t):
        at = tile(slot, t)
        for a, axis in enumerate("xy"):
            near_term[which, a, at] = product(which, slot, t, NEAR[axis])
        z_term[which, at] = product(which, slot, t, 1)
        base[which, at] = product(which, slot, t, 0)

    def send_term(which, slot, j):
        send(("term", "x", which, slot, j), ("term", "y", which, slot, j))

    def hand_on(j):
        for axis in "xy":
            need(("term", axis, 0, 0, j))
            send(("last", axis, j))

    def join(which, slot, j):
        at = rows(slot, j)
        for a, axis in enumerate("xy"):
            total = near_term[which, a, at]
            if not passed(which, slot, j):
                need(("term", axis, which, slot, j))
                total = total + term_recv[which, a, at].astype(F32)
            sum_send[which, a, at] = total.astype(BF16)
            send(("sum", axis, which, slot, j))

    def collect(which, slot, j):
        at = rows(slot, j)
        need(("sum", "x", which, slot, j), ("sum", "y", which, slot, j))
        total = base[which, at] + sum_recv[which, 0, at].astype(F32) + sum_recv[which, 1, at].astype(F32)
        if slot == 0:
            base[which, at] = total
        else:
            half_send[which, piece(j)] = total.astype(BF16)
            send(("half", which, j))

    def plain(which, slot, j):
        z_send[which, rows(slot, j)] = z_term[which, rows(slot, j)].astype(BF16)
        send(("out3" if slot else "out1", which, j))

    def pass_on(which, j):
        slot = int(j >= FIRST)
        at = rows(slot, j)
        need(("half", which, j))
        z_send[which, at] = (z_term[which, at] + half_recv[which, piece(j)].astype(F32)).astype(BF16)
        send(("out3" if slot else "out1", which, j))

    def finish(which, j):
        need(("out1", which, j), ("out3", which, j))
        total = base[which, rows(0, j)] + z_recv[which, rows(0, j)].astype(F32) + z_recv[which, rows(1, j)].astype(F32)
        if passed(which, 0, j):
            need(("last", "x", j), ("last", "y", j))
            total = total + last_recv[0, piece(j)].astype(F32) + last_recv[1, piece(j)].astype(F32)
        (gtok if which else out)[piece(j), :] = total.astype(BF16)

    def grads(which, third):
        def body(k, carry):
            at = pl.ds(pl.multiple_of(k * G, G), G)
            if which:
                both = jnp.dot(act_t[...], held[1, k], preferred_element_type=F32)
                grad_own[1, k] = both[:G]
                grad_peer[1, k] = both[G:]
            else:
                both = jnp.dot(held_t[at, :], gpre[...], preferred_element_type=F32)
                grad_own[0, k] = both[:, :G]
                grad_peer[0, k] = both[:, G:]
            return carry

        lax.fori_loop(third * THIRDS, (third + 1) * THIRDS, body, 0)
        send(("grad", which, third))

    def write_grad(which, k):
        return pltpu.make_async_copy(grad_own.at[which, k], (gdown if which else gup).at[k], local.at[4 + which * LEVELS + k])

    def grads_sum(which, third):
        need(("grad", which, third))

        def body(k, carry):
            grad_own[which, k] = (grad_own[which, k] + grad_recv[which, k]) * mask[0, k].astype(F32)
            write_grad(which, k).start()
            return carry

        lax.fori_loop(third * THIRDS, (third + 1) * THIRDS, body, 0)

    def finish_sends(*names):
        for name in names:
            sent.add(name)
            if name[0] in ("weight", "grad"):
                transfer(name).wait_send()
            else:
                span = pl.ds(0, SIZES[name] * PART)
                pltpu.make_async_remote_copy(
                    src_ref=held.at[0, 0, span],
                    dst_ref=held.at[0, 0, span],
                    send_sem=sends.at[FAMILIES[name]],
                    recv_sem=recvs.at[0],
                    device_id=place["z1"],
                    device_id_type=MESH,
                ).wait_send()

    steps = {
        "W": finish_sends,
        "oz": own_z, "ox": own_xy, "rz": relay_z, "ot": other, "rx": relay_xy, "su": mask_up, "sd": mask_down,
        "tw": turn_weights, "th": turn_held, "ta": turn_act, "F": forward, "B": backward, "h1": hop, "h2": land, "Fn": forward_near, "Bn": backward_near, "TF": far_terms,
        "TN": near_terms, "S": send_term, "RL": hand_on, "J": join, "C": collect, "Z": plain, "PO": pass_on,
        "FIN": finish, "G": grads, "GS": grads_sum,
    }
    for step in ORDER:
        steps[step[0]](*step[1:])

    assert started == landed == set(NUMBER)
    for which in range(2):
        for k in range(LEVELS):
            write_grad(which, k).wait()
    assert sent == set(FAMILIES)


def hand_out(*refs):
    sources, results, sems = refs[:4], refs[4:8], refs[8]
    copies = []
    for src, dst in zip(sources, results):
        if len(src.shape) == 2:
            pairs = [(src, dst)]
        else:
            pairs = [(src.at[pl.ds(k, 2)], dst.at[pl.ds(k, 2)]) for k in range(0, LEVELS, 2)]
        for a, b in pairs:
            copies.append(pltpu.make_async_copy(a, b, sems.at[len(copies)]))
    for copy in copies:
        copy.start()
    for copy in copies:
        copy.wait()


def shards(tokens, up_weight, down_weight, block_mask, cotangent):
    anywhere = pl.BlockSpec(memory_space=pl.ANY)
    vmem = pl.BlockSpec(memory_space=pltpu.VMEM)
    both = 2 * ROWS
    result = (
        jax.ShapeDtypeStruct((ROWS, G), BF16),
        jax.ShapeDtypeStruct((ROWS, G), BF16),
        jax.ShapeDtypeStruct((LEVELS, G, G), F32),
        jax.ShapeDtypeStruct((LEVELS, G, G), F32),
    )
    operands = [pltpu.with_memory_space_constraint(a, pltpu.HBM) for a in (tokens, cotangent, up_weight[0], down_weight[0])]
    worked = pl.pallas_call(
        kernel,
        out_shape=tuple(pltpu.VMEM(a.shape, a.dtype) for a in result),
        in_specs=[anywhere, anywhere, anywhere, anywhere, pl.BlockSpec(memory_space=pltpu.SMEM)],
        out_specs=(vmem, vmem, anywhere, anywhere),
        scratch_shapes=[
            pltpu.VMEM((2, LEVELS, both, G), BF16),
            pltpu.VMEM((WIDE, both), BF16),
            pltpu.VMEM((2, LEVELS, G, G), BF16),
            pltpu.VMEM((WIDE, 2 * G), BF16),
            pltpu.VMEM((2 * G, WIDE), BF16),
            pltpu.VMEM((2 * G, WIDE), BF16),
            pltpu.VMEM((WIDE, 2 * G), BF16),
            pltpu.VMEM((both, 2 * G), BF16),
            pltpu.VMEM((2 * G, both), BF16),
            pltpu.VMEM((both, 2 * G), BF16),
            pltpu.VMEM((both, 2 * G), F32),
            pltpu.VMEM((both, 2 * G), F32),
            pltpu.VMEM((2, 2, both, G), BF16),
            pltpu.VMEM((2, 2, both, G), BF16),
            pltpu.VMEM((2, 2, both, G), F32),
            pltpu.VMEM((2, 2, both, G), BF16),
            pltpu.VMEM((2, 2, both, G), BF16),
            pltpu.VMEM((2, both, G), F32),
            pltpu.VMEM((2, both, G), F32),
            pltpu.VMEM((2, ROWS, G), BF16),
            pltpu.VMEM((2, ROWS, G), BF16),
            pltpu.VMEM((2, ROWS, G), BF16),
            pltpu.VMEM((2, 2, len(MOVED) * PART, G), BF16),
            pltpu.VMEM((2, both, G), BF16),
            pltpu.VMEM((2, both, G), BF16),
            pltpu.VMEM((2, LEVELS, G, G), F32),
            pltpu.VMEM((2, LEVELS, G, G), F32),
            pltpu.VMEM((2, LEVELS, G, G), F32),
            pltpu.SemaphoreType.DMA((len(FAMILIES),)),
            pltpu.SemaphoreType.DMA((COPIES,)),
            pltpu.SemaphoreType.DMA((4 + 2 * LEVELS,)),
        ],
        compiler_params=pltpu.CompilerParams(
            collective_id=0, has_side_effects=True, vmem_limit_bytes=58 * 1024 * 1024
        ),
    )(*operands, block_mask)
    worked = [pltpu.with_memory_space_constraint(a, pltpu.VMEM) for a in worked]
    output, grad_tokens, grad_up, grad_down = pl.pallas_call(
        hand_out,
        out_shape=result,
        in_specs=[anywhere] * 4,
        out_specs=(anywhere,) * 4,
        scratch_shapes=[pltpu.SemaphoreType.DMA((8,))],
        compiler_params=pltpu.CompilerParams(vmem_limit_bytes=1024 * 1024),
    )(*worked)
    return output, grad_tokens, grad_up[None], grad_down[None]


def solution(mesh):
    placed = (
        P("seq", "tp"),
        P(("seq", "tp"), None, None, None),
        P(("seq", "tp"), None, None, None),
        P(("seq", "tp"), None),
        P("seq", "tp"),
    )
    return jax.shard_map(
        shards,
        mesh=mesh,
        in_specs=placed,
        out_specs=(
            P("seq", "tp"),
            P("seq", "tp"),
            P(("seq", "tp"), None, None, None),
            P(("seq", "tp"), None, None, None),
        ),
        check_vma=False,
    )
```

```python
import collections
import math

import jax
import jax.numpy as jnp
from jax import lax
from jax.experimental import pallas as pl
from jax.experimental.pallas import tpu as pltpu
from jax.sharding import PartitionSpec as P

MESH = pl.DeviceIdType.MESH
F32 = jnp.float32
BF16 = jnp.bfloat16
ROWS = 512
PART = 128
PIECES = ROWS // PART
FIRST = PIECES // 2
TILE = 256
PER_TILE = TILE // PART
THIRDS = 3
G = 256
LEVELS = 6
WIDE = LEVELS * G
LEVEL = (0, 1, 2, 4, 3, 5)
NEAR = {"x": 3, "y": 2}
FAR = {"x": 5, "y": 4}
SCALE = math.sqrt(2.0 / math.pi)
CUBE = 0.044715


def numbering():
    keys = []
    for which in range(2):
        keys += [(name, which, j) for name in ("z1", "z3", "zr", "out1", "out3", "half") for j in range(PIECES)]
        keys += [
            (name, axis, which, slot, j)
            for name in ("near", "far", "term", "sum")
            for axis in "xy"
            for slot in range(2)
            for j in range(PIECES)
        ]
        keys += [("weight", which)] + [("grad", which, k) for k in range(LEVELS // THIRDS)]
    keys += [("last", axis, j) for axis in "xy" for j in PASSED]
    moved = [(axis, level, which, j) for axis in "xy" for level in "nf" for which, j in MOVED]
    keys += [("hop", *rest) for rest in moved] + [("land", *rest) for rest in moved]
    keys = [k for k in keys if not (k[0] in ("near", "far") and k[3] == 1 and (k[2], k[4]) in MOVED)]
    return {key: n for n, key in enumerate(keys)}


def passed(which, slot, j):
    return which == 0 and slot == 0 and j in PASSED


def family(key):
    name = key[0]
    if name in ("weight", "grad"):
        return key
    if name in ("near", "far", "term", "sum"):
        return name, key[2], key[3]
    if name in ("last", "hop", "land"):
        return (name,)
    return {"z1": "z", "z3": "z", "zr": "middle", "half": "middle", "out1": "out", "out3": "out"}[name], key[1]


def arrival(key):
    name = key[0]
    if name in ("near", "far", "term", "sum"):
        return name, *key[2:]
    if name in ("out1", "out3"):
        return "out", *key[1:]
    if name in ("last", "land"):
        return name, *key[2:]
    return key


PASSED = (2, 3)
MOVED = ((1, 0), (1, 2))
NUMBER = numbering()
ARRIVALS = collections.Counter(arrival(key) for key in NUMBER)
LANDINGS = {name: n for n, name in enumerate(ARRIVALS)}
SIZES = collections.Counter(family(key) for key in NUMBER)
FAMILIES = {name: n for n, name in enumerate(SIZES)}

S_OX, S_OZ, S_RZ, S_OT, S_RX, S_H1, S_H2, S_SU, S_SD, S_TW, S_TH, S_TA, S_FN, S_F, \
    S_BN, S_B, S_TF, S_TN, S_S, S_RL, S_J, S_C, S_Z, S_PO, S_FIN, S_G, S_GS, S_W = range(28)
X, Y, NR, FR = "x", "y", "n", "f"
ORDER = (
    (S_OZ, 0, 3), (S_OX, 0, 3), (S_OX, 1, 0), (S_OZ, 0, 2), (S_OZ, 0, 1), (S_SU,), (S_OZ, 1, 1), (S_OX, 1, 2),
    (S_OX, 0, 2), (S_SD,), (S_OX, 0, 1), (S_RX, 0, 0, 3), (S_OX, 0, 0), (S_OZ, 0, 0), (S_RX, 1, 0, 0), (S_OX, 1, 3),
    (S_RZ, 0, 3), (S_RZ, 0, 2), (S_RX, 1, 0, 2), (S_RZ, 0, 1), (S_OZ, 1, 3), (S_OX, 1, 1), (S_H1, X, NR, 1, 2),
    (S_RX, 0, 0, 2), (S_FN, 0, 1), (S_RZ, 0, 0), (S_RZ, 1, 1), (S_RX, 0, 0, 1), (S_OZ, 1, 2), (S_H1, Y, FR, 1, 0),
    (S_TW,), (S_OT, 0, 3), (S_H1, Y, FR, 1, 2), (S_H1, X, FR, 1, 2), (S_RX, 0, 0, 0), (S_F, 0, 1), (S_RZ, 1, 3),
    (S_OT, 0, 2), (S_RX, 1, 0, 3), (S_H1, X, NR, 1, 0), (S_OT, 0, 1), (S_H1, X, FR, 1, 0), (S_FN, 0, 0),
    (S_RX, 1, 0, 1), (S_H1, Y, NR, 1, 2), (S_H1, Y, NR, 1, 0), (S_OT, 0, 0), (S_TF, 0, 0, 1), (S_OZ, 1, 0),
    (S_RX, 0, 1, 3), (S_TN, 0, 0, 1), (S_F, 0, 0), (S_TF, 0, 0, 0), (S_RX, 0, 1, 2), (S_RZ, 1, 2), (S_OT, 1, 1),
    (S_BN, 0, 1), (S_H2, X, NR, 1, 2), (S_B, 0, 1), (S_TF, 1, 0, 1), (S_RX, 0, 1, 1), (S_TN, 0, 0, 0), (S_OT, 1, 3),
    (S_S, 0, 0, 2), (S_TN, 1, 0, 1), (S_S, 1, 0, 2), (S_H2, Y, FR, 1, 2), (S_FN, 1, 1), (S_TA, 0, 1), (S_J, 0, 0, 2),
    (S_RX, 0, 1, 0), (S_F, 1, 1), (S_TF, 0, 1, 1), (S_S, 0, 1, 2), (S_H2, Y, FR, 1, 0), (S_S, 0, 0, 3),
    (S_RX, 1, 1, 1), (S_H2, X, NR, 1, 0), (S_J, 0, 0, 3), (S_FN, 1, 0), (S_TN, 0, 1, 1), (S_S, 0, 1, 3),
    (S_RZ, 1, 0), (S_BN, 0, 0), (S_TA, 0, 0), (S_W, 11), (S_H2, X, FR, 1, 0), (S_H2, X, FR, 1, 2), (S_B, 0, 0),
    (S_H2, Y, NR, 1, 0), (S_W, 25), (S_TF, 1, 0, 0), (S_RX, 1, 1, 3), (S_F, 1, 0), (S_W, 3), (S_J, 1, 0, 2),
    (S_W, 0), (S_H2, Y, NR, 1, 2), (S_Z, 0, 0, 2), (S_TF, 0, 1, 0), (S_TA, 1, 0), (S_OT, 1, 2), (S_S, 0, 1, 0),
    (S_Z, 0, 0, 3), (S_J, 0, 1, 2), (S_W, 17), (S_Z, 1, 0, 3), (S_TA, 1, 1), (S_OT, 1, 0), (S_TN, 0, 1, 0),
    (S_TH, 0), (S_Z, 0, 1, 0), (S_BN, 1, 0), (S_Z, 1, 0, 2), (S_B, 1, 0), (S_TF, 1, 1, 0), (S_S, 1, 1, 1),
    (S_TN, 1, 1, 0), (S_J, 0, 1, 3), (S_W, 5), (S_S, 1, 1, 0), (S_BN, 1, 1), (S_B, 1, 1), (S_TF, 1, 1, 1),
    (S_J, 0, 1, 0), (S_S, 1, 1, 3), (S_Z, 1, 1, 1), (S_S, 0, 1, 1), (S_S, 1, 1, 2), (S_W, 19), (S_S, 0, 0, 1),
    (S_Z, 1, 1, 0), (S_W, 29), (S_TN, 1, 1, 1), (S_W, 4), (S_S, 1, 0, 3), (S_J, 1, 1, 1), (S_W, 14), (S_G, 1, 1),
    (S_J, 1, 1, 0), (S_C, 0, 1, 0), (S_S, 0, 0, 0), (S_J, 1, 1, 3), (S_Z, 0, 1, 1), (S_G, 1, 0), (S_C, 0, 1, 2),
    (S_C, 1, 1, 1), (S_J, 0, 1, 1), (S_C, 0, 1, 3), (S_J, 1, 1, 2), (S_TH, 1), (S_S, 1, 0, 0), (S_S, 1, 0, 1),
    (S_C, 1, 1, 0), (S_C, 1, 1, 3), (S_G, 0, 1), (S_PO, 0, 2), (S_J, 0, 0, 1), (S_PO, 0, 0), (S_TN, 1, 0, 0),
    (S_W, 6), (S_J, 1, 0, 3), (S_C, 0, 1, 1), (S_RL, 2), (S_C, 1, 1, 2), (S_J, 0, 0, 0), (S_PO, 1, 1), (S_PO, 0, 3),
    (S_G, 0, 0), (S_PO, 1, 3), (S_J, 1, 0, 1), (S_PO, 1, 0), (S_C, 1, 0, 2), (S_RL, 3), (S_PO, 0, 1), (S_J, 1, 0, 0),
    (S_PO, 1, 2), (S_GS, 1, 0), (S_GS, 0, 1), (S_C, 0, 0, 2), (S_GS, 1, 1), (S_W, 20), (S_C, 0, 0, 1),
    (S_C, 0, 0, 0), (S_C, 1, 0, 3), (S_W, 30), (S_FIN, 0, 2), (S_FIN, 0, 0), (S_C, 0, 0, 3), (S_FIN, 1, 3),
    (S_C, 1, 0, 1), (S_FIN, 1, 1), (S_FIN, 0, 3), (S_GS, 0, 0), (S_FIN, 1, 2), (S_C, 1, 0, 0), (S_W, 18),
    (S_FIN, 1, 0), (S_FIN, 0, 1), (S_W, 1, 15, 7, 21, 9, 8, 23, 2, 10, 16, 22, 24, 27, 26, 13, 28, 12),
)


def flip(index, bit):
    return index + bit - 2 * bit * lax.rem(lax.div(index, bit), 2)


def kernel(
    tok, cot, up, down, mask, out, gtok, gup, gdown,
    held, held_t, raw, uall, dall, uall_t, dall_t, act, act_t, gpre, slope, gact,
    term_send, term_recv, near_term, sum_send, sum_recv, base, z_term,
    half_send, half_recv, last_recv, hops, z_send, z_recv,
    grad_own, grad_peer, grad_recv,
    sends, recvs, local,
):
    shared = (tok, cot)
    seq, tp = lax.axis_index("seq"), lax.axis_index("tp")
    place = {
        "core": (flip(seq, 1), tp),
        "z1": (seq, flip(tp, 1)),
        "z3": (flip(seq, 2), flip(tp, 1)),
        "x1": (seq, flip(tp, 8)),
        "x3": (seq, flip(flip(tp, 8), 16)),
        "y1": (seq, flip(tp, 2)),
        "y3": (seq, flip(flip(tp, 2), 4)),
    }

    def remote(src, dst, key, target):
        return pltpu.make_async_remote_copy(
            src_ref=src,
            dst_ref=dst,
            send_sem=sends.at[FAMILIES[family(key)]],
            recv_sem=recvs.at[LANDINGS[arrival(key)]],
            device_id=place[target],
            device_id_type=MESH,
        )

    def rows(slot, j):
        start = slot * ROWS + j * PART
        return pl.ds(start if isinstance(j, int) else pl.multiple_of(start, PART), PART)

    def piece(j):
        return pl.ds(j * PART, PART)

    def columns(level):
        return pl.ds(level * G, G)

    def transfer(key):
        name, rest = key[0], key[1:]
        if name == "weight":
            if rest[0] == 0:
                return remote(uall.at[:, pl.ds(0, G)], uall.at[:, pl.ds(G, G)], key, "core")
            return remote(dall.at[pl.ds(0, G)], dall.at[pl.ds(G, G)], key, "core")
        if name == "grad":
            at = pl.ds(rest[1] * THIRDS, THIRDS)
            return remote(grad_peer.at[rest[0], at], grad_recv.at[rest[0], at], key, "core")
        if name == "last":
            a, j = "xy".index(rest[0]), rest[1]
            return remote(term_recv.at[0, a, rows(0, j)], last_recv.at[a, piece(j)], key, rest[0] + "3")
        if name in ("hop", "land"):
            axis, level, which, j = rest
            n, group = "nf".index(level), (NEAR if level == "n" else FAR)[axis]
            room = hops.at[n, "xy".index(axis), pl.ds(MOVED.index((which, j)) * PART, PART)]
            if name == "hop":
                return remote(held.at[which, group, rows(0, j)], room, key, ("z1", "z3")[n])
            return remote(room, held.at[which, group, rows(1, j)], key, ("z3", "z1")[n])
        if name in ("near", "far", "term", "sum"):
            axis, which, slot, j = rest
            a, at = "xy".index(axis), rows(slot, j)
            if name == "near":
                src = held.at[which, 0, at] if slot else shared[which].at[piece(j)]
                return remote(src, held.at[which, NEAR[axis], at], key, axis + "1")
            if name == "far":
                return remote(held.at[which, NEAR[axis], at], held.at[which, FAR[axis], at], key, axis + "3")
            if name == "term":
                target = axis + ("1" if passed(which, slot, j) else "3")
                return remote(term_send.at[which, a, at], term_recv.at[which, a, at], key, target)
            return remote(sum_send.at[which, a, at], sum_recv.at[which, a, at], key, axis + "1")
        which, j = rest
        if name == "z1":
            return remote(shared[which].at[piece(j)], held.at[which, 1, rows(0, j)], key, "z1")
        if name == "z3":
            return remote(shared[which].at[piece(j)], held.at[which, 1, rows(1, j)], key, "z3")
        onward = "z3" if j < FIRST else "z1"
        if name == "zr":
            return remote(held.at[which, 1, rows(int(j >= FIRST), j)], held.at[which, 0, rows(1, j)], key, onward)
        if name == "half":
            return remote(half_send.at[which, piece(j)], half_recv.at[which, piece(j)], key, onward)
        slot = int(name == "out3")
        return remote(z_send.at[which, rows(slot, j)], z_recv.at[which, rows(slot, j)], key, "z3" if slot else "z1")

    def together(pieces, sent_by, landed_by):
        span = held.at[0, 0, pl.ds(0, pieces * PART)]
        return pltpu.make_async_remote_copy(
            src_ref=span,
            dst_ref=span,
            send_sem=sends.at[sent_by],
            recv_sem=recvs.at[landed_by],
            device_id=place["z1"],
            device_id_type=MESH,
        )

    started, landed, copied, sent = set(), set(), set(), set()

    def send(*keys):
        for key in keys:
            started.add(key)
            transfer(key).start()

    def need(*keys):
        for key in keys:
            name = arrival(key)
            if name in landed:
                continue
            landed.add(name)
            if name[0] in ("weight", "grad"):
                transfer(key).wait_recv()
            else:
                together(ARRIVALS[name], 0, LANDINGS[name]).wait_recv()

    own = [
        pltpu.make_async_copy(shared[which], held.at[which, 0, pl.ds(0, ROWS)], local.at[which])
        for which in range(2)
    ]
    loads = [pltpu.make_async_copy(ref, raw.at[which], local.at[2 + which]) for which, ref in enumerate((up, down))]
    barrier = pltpu.get_barrier_semaphore()
    for target in place.values():
        pl.semaphore_signal(barrier, inc=1, device_id=target, device_id_type=MESH)
    for copy in loads + own:
        copy.start()
    pl.semaphore_wait(barrier, len(place))

    def tile(slot, t):
        return pl.ds(slot * ROWS + t * TILE, TILE)

    def own_z(which, j):
        send(("z1", which, j), ("z3", which, j))

    def own_xy(which, j):
        send(("near", "x", which, 0, j), ("near", "y", which, 0, j))

    def relay_z(which, j):
        need(("z1" if j < FIRST else "z3", which, j))
        send(("zr", which, j))

    def other(which, j):
        need(("zr", which, j))
        if (which, j) not in MOVED:
            send(("near", "x", which, 1, j), ("near", "y", which, 1, j))

    def relay_xy(which, slot, j):
        for axis in "xy":
            need(("near", axis, which, slot, j))
            send(("far", axis, which, slot, j))

    def hop(axis, level, which, j):
        need(("near" if level == "n" else "far", axis, which, 0, j))
        send(("hop", axis, level, which, j))

    def land(axis, level, which, j):
        need(("hop", axis, level, which, j))
        send(("land", axis, level, which, j))

    def mask_up():
        loads[0].wait()
        for k, level in enumerate(LEVEL):
            uall[pl.ds(k * G, G), pl.ds(0, G)] = (raw[0, level].astype(F32) * mask[0, level].astype(F32)).astype(BF16)
        send(("weight", 0))

    def mask_down():
        loads[1].wait()
        for k, level in enumerate(LEVEL):
            dall[pl.ds(0, G), pl.ds(k * G, G)] = (raw[1, level].astype(F32) * mask[0, level].astype(F32)).astype(BF16)
        send(("weight", 1))

    def turn_weights():
        need(("weight", 0), ("weight", 1))

        def body(k, carry):
            at = pl.ds(pl.multiple_of(k * G, G), G)
            dall_t[at, :] = dall[:, at].T
            uall_t[:, at] = uall[at, :].T
            return carry

        lax.fori_loop(0, LEVELS, body, 0)

    def turn_held(slot):
        def body(k, carry):
            at = pl.ds(pl.multiple_of(k * G, G), G)
            held_t[at, pl.ds(slot * ROWS, ROWS)] = held[0, k, pl.ds(slot * ROWS, ROWS)].T
            return carry

        lax.fori_loop(0, LEVELS, body, 0)

    def turn_act(slot, t):
        act_t[:, tile(slot, t)] = act[tile(slot, t), :].T

    def near_inputs(which, slot, t):
        if slot == 0 and ("own", which) not in copied:
            copied.add(("own", which))
            own[which].wait()
        for j in range(t * PER_TILE, (t + 1) * PER_TILE):
            need(("z3" if slot else "z1", which, j))
            if slot and (which, j) in MOVED:
                need(("land", "x", "n", which, j), ("land", "y", "n", which, j))

    def far_inputs(which, slot, t):
        for j in range(t * PER_TILE, (t + 1) * PER_TILE):
            for axis in "xy":
                need(("land", axis, "f", which, j) if slot and (which, j) in MOVED else ("far", axis, which, slot, j))

    def partial(which, at, weights):
        early = jnp.concatenate([held[which, k, at] for k in range(4)], axis=1)
        return jnp.dot(early, weights[pl.ds(0, 4 * G), :], preferred_element_type=F32)

    def rest(which, at, weights):
        late = jnp.concatenate([held[which, k, at] for k in (4, 5)], axis=1)
        return jnp.dot(late, weights[pl.ds(4 * G, 2 * G), :], preferred_element_type=F32)

    def forward_near(slot, t):
        near_inputs(0, slot, t)
        need(("weight", 0))
        slope[tile(slot, t), :] = partial(0, tile(slot, t), uall)

    def backward_near(slot, t):
        near_inputs(1, slot, t)
        gact[tile(slot, t), :] = partial(1, tile(slot, t), dall_t)

    def forward(slot, t):
        far_inputs(0, slot, t)
        at = tile(slot, t)
        pre = slope[at, :] + rest(0, at, uall)
        square = pre * pre
        tanh = jnp.tanh(SCALE * pre * (1.0 + CUBE * square))
        cdf = 0.5 + 0.5 * tanh
        act[at, :] = (pre * cdf).astype(BF16)
        slope[at, :] = cdf + (0.5 * SCALE) * pre * (1.0 - tanh * tanh) * (1.0 + (3.0 * CUBE) * square)

    def backward(slot, t):
        far_inputs(1, slot, t)
        at = tile(slot, t)
        gpre[at, :] = ((gact[at, :] + rest(1, at, dall_t)) * slope[at, :]).astype(BF16)

    def product(which, slot, t, level):
        if which:
            return jnp.dot(gpre[tile(slot, t), :], uall_t[:, columns(level)], preferred_element_type=F32)
        return jnp.dot(act[tile(slot, t), :], dall[:, columns(level)], preferred_element_type=F32)

    def far_terms(which, slot, t):
        need(("weight", 1))
        for a, axis in enumerate("xy"):
            term_send[which, a, tile(slot, t)] = product(which, slot, t, FAR[axis]).astype(BF16)

    def near_terms(which, slot, t):
        at = tile(slot, t)
        for a, axis in enumerate("xy"):
            near_term[which, a, at] = product(which, slot, t, NEAR[axis])
        z_term[which, at] = product(which, slot, t, 1)
        base[which, at] = product(which, slot, t, 0)

    def send_term(which, slot, j):
        send(("term", "x", which, slot, j), ("term", "y", which, slot, j))

    def hand_on(j):
        for axis in "xy":
            need(("term", axis, 0, 0, j))
            send(("last", axis, j))

    def join(which, slot, j):
        at = rows(slot, j)
        for a, axis in enumerate("xy"):
            total = near_term[which, a, at]
            if not passed(which, slot, j):
                need(("term", axis, which, slot, j))
                total = total + term_recv[which, a, at].astype(F32)
            sum_send[which, a, at] = total.astype(BF16)
            send(("sum", axis, which, slot, j))

    def collect(which, slot, j):
        at = rows(slot, j)
        need(("sum", "x", which, slot, j), ("sum", "y", which, slot, j))
        total = base[which, at] + sum_recv[which, 0, at].astype(F32) + sum_recv[which, 1, at].astype(F32)
        if slot == 0:
            base[which, at] = total
        else:
            half_send[which, piece(j)] = total.astype(BF16)
            send(("half", which, j))

    def plain(which, slot, j):
        z_send[which, rows(slot, j)] = z_term[which, rows(slot, j)].astype(BF16)
        send(("out3" if slot else "out1", which, j))

    def pass_on(which, j):
        slot = int(j >= FIRST)
        at = rows(slot, j)
        need(("half", which, j))
        z_send[which, at] = (z_term[which, at] + half_recv[which, piece(j)].astype(F32)).astype(BF16)
        send(("out3" if slot else "out1", which, j))

    def finish(which, j):
        need(("out1", which, j), ("out3", which, j))
        total = base[which, rows(0, j)] + z_recv[which, rows(0, j)].astype(F32) + z_recv[which, rows(1, j)].astype(F32)
        if passed(which, 0, j):
            need(("last", "x", j), ("last", "y", j))
            total = total + last_recv[0, piece(j)].astype(F32) + last_recv[1, piece(j)].astype(F32)
        (gtok if which else out)[piece(j), :] = total.astype(BF16)

    def grads(which, third):
        def body(k, carry):
            at = pl.ds(pl.multiple_of(k * G, G), G)
            if which:
                both = jnp.dot(act_t[...], held[1, k], preferred_element_type=F32)
                grad_own[1, k] = both[:G]
                grad_peer[1, k] = both[G:]
            else:
                both = jnp.dot(held_t[at, :], gpre[...], preferred_element_type=F32)
                grad_own[0, k] = both[:, :G]
                grad_peer[0, k] = both[:, G:]
            return carry

        lax.fori_loop(third * THIRDS, (third + 1) * THIRDS, body, 0)
        send(("grad", which, third))

    def write_grad(which, k):
        return pltpu.make_async_copy(grad_own.at[which, k], (gdown if which else gup).at[LEVEL[k]], local.at[4 + which * LEVELS + k])

    def grads_sum(which, third):
        need(("grad", which, third))

        for k in range(third * THIRDS, (third + 1) * THIRDS):
            total = grad_own[which, k] + grad_recv[which, k]
            grad_own[which, k] = total * mask[0, LEVEL[k]].astype(F32)
            write_grad(which, k).start()

    def finish_sends(*numbers):
        for name in (tuple(SIZES)[n] for n in numbers):
            sent.add(name)
            if name[0] in ("weight", "grad"):
                transfer(name).wait_send()
            else:
                together(SIZES[name], FAMILIES[name], 0).wait_send()

    steps = (
        own_xy, own_z, relay_z, other, relay_xy, hop, land, mask_up, mask_down, turn_weights, turn_held, turn_act,
        forward_near, forward, backward_near, backward, far_terms, near_terms, send_term, hand_on, join, collect,
        plain, pass_on, finish, grads, grads_sum, finish_sends,
    )
    for step in ORDER:
        steps[step[0]](*step[1:])

    assert started == set(NUMBER) and landed == set(ARRIVALS)
    for which in range(2):
        for k in range(LEVELS):
            write_grad(which, k).wait()
    assert sent == set(FAMILIES)


def hand_out(*refs):
    sources, results, sems = refs[:4], refs[4:8], refs[8]
    copies = []
    for src, dst in zip(sources, results):
        if len(src.shape) == 2:
            pairs = [(src, dst)]
        else:
            pairs = [(src.at[pl.ds(k, 2)], dst.at[pl.ds(k, 2)]) for k in range(0, LEVELS, 2)]
        for a, b in pairs:
            copies.append(pltpu.make_async_copy(a, b, sems.at[len(copies)]))
    for copy in copies:
        copy.start()
    for copy in copies:
        copy.wait()


def shards(tokens, up_weight, down_weight, block_mask, cotangent):
    anywhere = pl.BlockSpec(memory_space=pl.ANY)
    vmem = pl.BlockSpec(memory_space=pltpu.VMEM)
    both = 2 * ROWS
    result = (
        jax.ShapeDtypeStruct((ROWS, G), BF16),
        jax.ShapeDtypeStruct((ROWS, G), BF16),
        jax.ShapeDtypeStruct((LEVELS, G, G), F32),
        jax.ShapeDtypeStruct((LEVELS, G, G), F32),
    )
    operands = [pltpu.with_memory_space_constraint(a, pltpu.HBM) for a in (tokens, cotangent, up_weight[0], down_weight[0])]
    worked = pl.pallas_call(
        kernel,
        out_shape=tuple(pltpu.VMEM(a.shape, a.dtype) for a in result),
        in_specs=[anywhere, anywhere, anywhere, anywhere, pl.BlockSpec(memory_space=pltpu.SMEM)],
        out_specs=(vmem, vmem, anywhere, anywhere),
        scratch_shapes=[
            pltpu.VMEM((2, LEVELS, both, G), BF16),
            pltpu.VMEM((WIDE, both), BF16),
            pltpu.VMEM((2, LEVELS, G, G), BF16),
            pltpu.VMEM((WIDE, 2 * G), BF16),
            pltpu.VMEM((2 * G, WIDE), BF16),
            pltpu.VMEM((2 * G, WIDE), BF16),
            pltpu.VMEM((WIDE, 2 * G), BF16),
            pltpu.VMEM((both, 2 * G), BF16),
            pltpu.VMEM((2 * G, both), BF16),
            pltpu.VMEM((both, 2 * G), BF16),
            pltpu.VMEM((both, 2 * G), F32),
            pltpu.VMEM((both, 2 * G), F32),
            pltpu.VMEM((2, 2, both, G), BF16),
            pltpu.VMEM((2, 2, both, G), BF16),
            pltpu.VMEM((2, 2, both, G), F32),
            pltpu.VMEM((2, 2, both, G), BF16),
            pltpu.VMEM((2, 2, both, G), BF16),
            pltpu.VMEM((2, both, G), F32),
            pltpu.VMEM((2, both, G), F32),
            pltpu.VMEM((2, ROWS, G), BF16),
            pltpu.VMEM((2, ROWS, G), BF16),
            pltpu.VMEM((2, ROWS, G), BF16),
            pltpu.VMEM((2, 2, len(MOVED) * PART, G), BF16),
            pltpu.VMEM((2, both, G), BF16),
            pltpu.VMEM((2, both, G), BF16),
            pltpu.VMEM((2, LEVELS, G, G), F32),
            pltpu.VMEM((2, LEVELS, G, G), F32),
            pltpu.VMEM((2, LEVELS, G, G), F32),
            pltpu.SemaphoreType.DMA((len(FAMILIES),)),
            pltpu.SemaphoreType.DMA((len(LANDINGS),)),
            pltpu.SemaphoreType.DMA((4 + 2 * LEVELS,)),
        ],
        compiler_params=pltpu.CompilerParams(
            collective_id=0, has_side_effects=True, vmem_limit_bytes=58 * 1024 * 1024
        ),
    )(*operands, block_mask)
    worked = [pltpu.with_memory_space_constraint(a, pltpu.VMEM) for a in worked]
    output, grad_tokens, grad_up, grad_down = pl.pallas_call(
        hand_out,
        out_shape=result,
        in_specs=[anywhere] * 4,
        out_specs=(anywhere,) * 4,
        scratch_shapes=[pltpu.SemaphoreType.DMA((8,))],
        compiler_params=pltpu.CompilerParams(vmem_limit_bytes=1024 * 1024),
    )(*worked)
    return output, grad_tokens, grad_up[None], grad_down[None]


def solution(mesh):
    placed = (
        P("seq", "tp"),
        P(("seq", "tp"), None, None, None),
        P(("seq", "tp"), None, None, None),
        P(("seq", "tp"), None),
        P("seq", "tp"),
    )
    return jax.shard_map(
        shards,
        mesh=mesh,
        in_specs=placed,
        out_specs=(
            P("seq", "tp"),
            P("seq", "tp"),
            P(("seq", "tp"), None, None, None),
            P(("seq", "tp"), None, None, None),
        ),
        check_vma=False,
    )
```

```python
import collections
import math

import jax
import jax.numpy as jnp
from jax import lax
from jax.experimental import pallas as pl
from jax.experimental.pallas import tpu as pltpu
from jax.sharding import PartitionSpec as P

MESH = pl.DeviceIdType.MESH
F32 = jnp.float32
BF16 = jnp.bfloat16
ROWS = 512
PART = 128
PIECES = ROWS // PART
FIRST = PIECES // 2
TILE = 256
PER_TILE = TILE // PART
THIRDS = 3
G = 256
LEVELS = 6
WIDE = LEVELS * G
LEVEL = (0, 1, 2, 4, 3, 5)
NEAR = {"x": 3, "y": 2}
FAR = {"x": 5, "y": 4}
SCALE = math.sqrt(2.0 / math.pi)
CUBE = 0.044715


def numbering():
    keys = []
    for which in range(2):
        keys += [(name, which, j) for name in ("z1", "z3", "zr", "out1", "out3", "half") for j in range(PIECES)]
        keys += [
            (name, axis, which, slot, j)
            for name in ("near", "far", "term", "sum")
            for axis in "xy"
            for slot in range(2)
            for j in range(PIECES)
        ]
        keys += [("weight", which)] + [("grad", which, k) for k in range(LEVELS // THIRDS)]
    keys += [("last", axis, j) for axis in "xy" for j in PASSED]
    moved = [(axis, level, which, j) for axis in "xy" for level in "nf" for which, j in MOVED]
    keys += [("hop", *rest) for rest in moved] + [("land", *rest) for rest in moved]
    keys = [k for k in keys if not (k[0] in ("near", "far") and k[3] == 1 and (k[2], k[4]) in MOVED)]
    return {key: n for n, key in enumerate(keys)}


def passed(which, slot, j):
    return which == 0 and slot == 0 and j in PASSED


def family(key):
    name = key[0]
    if name in ("weight", "grad"):
        return key
    if name in ("near", "far", "term", "sum"):
        return name, key[2], key[3]
    if name in ("last", "hop", "land"):
        return (name,)
    return {"z1": "z", "z3": "z", "zr": "middle", "half": "middle", "out1": "out", "out3": "out"}[name], key[1]


def arrival(key):
    name = key[0]
    if name in ("near", "far", "term", "sum"):
        return name, *key[2:]
    if name in ("out1", "out3"):
        return "out", *key[1:]
    if name in ("last", "land"):
        return name, *key[2:]
    return key


PASSED = (2, 3)
MOVED = ((1, 0), (1, 2))
NUMBER = numbering()
ARRIVALS = collections.Counter(arrival(key) for key in NUMBER)
LANDINGS = {name: n for n, name in enumerate(ARRIVALS)}
SIZES = collections.Counter(family(key) for key in NUMBER)
FAMILIES = {name: n for n, name in enumerate(SIZES)}

S_OX, S_OZ, S_RZ, S_OT, S_RX, S_H1, S_H2, S_SU, S_SD, S_TW, S_TH, S_TA, S_FN, S_F, \
    S_BN, S_B, S_TF, S_TN, S_S, S_RL, S_J, S_C, S_Z, S_PO, S_FIN, S_G, S_GS, S_W = range(28)
X, Y, NR, FR = "x", "y", "n", "f"
ORDER = (
    (S_OX, 0, 3), (S_OZ, 0, 2), (S_OX, 1, 0), (S_OZ, 0, 3), (S_SU,), (S_SD,), (S_OX, 1, 2), (S_OZ, 0, 0),
    (S_RX, 0, 0, 3), (S_OX, 0, 2), (S_OZ, 0, 1), (S_OX, 0, 1), (S_RX, 1, 0, 0), (S_OX, 0, 0), (S_RZ, 0, 3),
    (S_OZ, 1, 1), (S_OX, 1, 3), (S_RZ, 0, 2), (S_OZ, 1, 3), (S_RX, 1, 0, 2), (S_H1, Y, NR, 1, 2), (S_RZ, 0, 0),
    (S_OX, 1, 1), (S_RX, 0, 0, 2), (S_RZ, 0, 1), (S_OZ, 1, 2), (S_H1, X, NR, 1, 0), (S_FN, 0, 1),
    (S_H1, Y, FR, 1, 0), (S_RX, 0, 0, 1), (S_OT, 0, 3), (S_TW,), (S_RX, 0, 0, 0), (S_FN, 0, 0), (S_RX, 1, 0, 3),
    (S_OT, 0, 2), (S_F, 0, 1), (S_RZ, 1, 1), (S_OT, 0, 0), (S_RZ, 1, 3), (S_RX, 1, 0, 1), (S_TF, 0, 0, 1),
    (S_TN, 0, 0, 1), (S_H1, X, FR, 1, 0), (S_OT, 0, 1), (S_H1, X, FR, 1, 2), (S_J, 0, 0, 2), (S_RX, 0, 1, 3),
    (S_OZ, 1, 0), (S_H1, Y, FR, 1, 2), (S_J, 0, 0, 3), (S_F, 0, 0), (S_RX, 0, 1, 2), (S_FN, 1, 1), (S_TF, 0, 0, 0),
    (S_BN, 0, 1), (S_RZ, 1, 2), (S_H1, Y, NR, 1, 0), (S_RX, 0, 1, 0), (S_B, 0, 1), (S_TF, 1, 0, 1), (S_TN, 0, 0, 0),
    (S_OT, 1, 1), (S_RX, 0, 1, 1), (S_H1, X, NR, 1, 2), (S_S, 0, 0, 2), (S_H2, Y, FR, 1, 0), (S_FN, 1, 0),
    (S_S, 1, 0, 2), (S_H2, X, FR, 1, 0), (S_OT, 1, 3), (S_F, 1, 1), (S_TF, 0, 1, 1), (S_S, 0, 1, 3), (S_TA, 0, 0),
    (S_H2, X, NR, 1, 0), (S_TN, 1, 0, 1), (S_BN, 0, 0), (S_B, 0, 0), (S_RZ, 1, 0), (S_S, 0, 1, 2), (S_F, 1, 0),
    (S_OT, 1, 2), (S_TF, 0, 1, 0), (S_W, 11), (S_H2, Y, NR, 1, 0), (S_W, 25), (S_TA, 0, 1), (S_H2, Y, FR, 1, 2),
    (S_TN, 0, 1, 0), (S_TN, 0, 1, 1), (S_RX, 1, 1, 1), (S_W, 0), (S_H2, X, FR, 1, 2), (S_S, 0, 1, 0),
    (S_H2, X, NR, 1, 2), (S_W, 3), (S_J, 0, 1, 3), (S_J, 1, 0, 2), (S_Z, 0, 0, 3), (S_H2, Y, NR, 1, 2),
    (S_S, 0, 0, 3), (S_TH, 1), (S_TF, 1, 0, 0), (S_TA, 1, 0), (S_J, 0, 1, 2), (S_W, 17), (S_OT, 1, 0),
    (S_RX, 1, 1, 3), (S_Z, 1, 0, 3), (S_Z, 0, 1, 1), (S_BN, 1, 0), (S_B, 1, 0), (S_TF, 1, 1, 0), (S_S, 1, 1, 1),
    (S_S, 1, 1, 0), (S_TN, 1, 1, 0), (S_W, 5), (S_C, 0, 1, 3), (S_Z, 1, 1, 1), (S_J, 0, 1, 0), (S_TA, 1, 1),
    (S_Z, 1, 0, 2), (S_S, 0, 1, 1), (S_Z, 0, 1, 0), (S_Z, 0, 0, 2), (S_W, 19), (S_Z, 1, 1, 0), (S_BN, 1, 1),
    (S_B, 1, 1), (S_G, 1, 1), (S_W, 4), (S_J, 1, 1, 1), (S_TF, 1, 1, 1), (S_S, 1, 1, 3), (S_S, 1, 1, 2), (S_W, 14),
    (S_S, 0, 0, 1), (S_S, 0, 0, 0), (S_S, 1, 0, 3), (S_J, 1, 1, 0), (S_TN, 1, 1, 1), (S_C, 0, 1, 2), (S_S, 1, 0, 0),
    (S_C, 0, 1, 0), (S_J, 0, 1, 1), (S_G, 1, 0), (S_C, 1, 1, 1), (S_J, 1, 1, 3), (S_TH, 0), (S_J, 1, 1, 2),
    (S_C, 1, 1, 0), (S_W, 6), (S_PO, 0, 0), (S_W, 29), (S_G, 0, 1), (S_J, 0, 0, 1), (S_C, 0, 1, 1), (S_C, 1, 1, 3),
    (S_PO, 0, 2), (S_S, 1, 0, 1), (S_J, 0, 0, 0), (S_PO, 0, 3), (S_TN, 1, 0, 0), (S_C, 1, 1, 2), (S_C, 0, 0, 2),
    (S_PO, 1, 1), (S_J, 1, 0, 3), (S_G, 0, 0), (S_RL, 3), (S_J, 1, 0, 0), (S_PO, 1, 3), (S_PO, 1, 0), (S_C, 0, 0, 3),
    (S_RL, 2), (S_J, 1, 0, 1), (S_C, 1, 0, 2), (S_PO, 0, 1), (S_GS, 0, 1), (S_PO, 1, 2), (S_GS, 1, 1), (S_GS, 1, 0),
    (S_C, 1, 0, 3), (S_FIN, 1, 3), (S_C, 1, 0, 0), (S_FIN, 1, 0), (S_FIN, 0, 3), (S_W, 30), (S_C, 0, 0, 1),
    (S_C, 0, 0, 0), (S_FIN, 0, 0), (S_GS, 0, 0), (S_FIN, 0, 2), (S_C, 1, 0, 1), (S_W, 18), (S_FIN, 1, 1), (S_W, 20),
    (S_FIN, 1, 2), (S_FIN, 0, 1), (S_W, 1, 15, 9, 7, 21, 8, 10, 23, 2, 16, 22, 27, 24, 26, 13, 12, 28),
)


def flip(index, bit):
    return index + bit - 2 * bit * lax.rem(lax.div(index, bit), 2)


def kernel(
    tok, cot, up, down, mask, out, gtok, gup, gdown,
    held, held_t, raw, uall, dall, uall_t, dall_t, act, act_t, gpre, slope, gact,
    term_send, term_recv, near_term, sum_send, sum_recv, base, z_term,
    half_send, half_recv, last_recv, hops, z_send, z_recv,
    grad_own, grad_peer, grad_recv,
    sends, recvs, local,
):
    shared = (tok, cot)
    seq, tp = lax.axis_index("seq"), lax.axis_index("tp")
    place = {
        "core": (flip(seq, 1), tp),
        "z1": (seq, flip(tp, 1)),
        "z3": (flip(seq, 2), flip(tp, 1)),
        "x1": (seq, flip(tp, 8)),
        "x3": (seq, flip(flip(tp, 8), 16)),
        "y1": (seq, flip(tp, 2)),
        "y3": (seq, flip(flip(tp, 2), 4)),
    }

    def remote(src, dst, key, target):
        return pltpu.make_async_remote_copy(
            src_ref=src,
            dst_ref=dst,
            send_sem=sends.at[FAMILIES[family(key)]],
            recv_sem=recvs.at[LANDINGS[arrival(key)]],
            device_id=place[target],
            device_id_type=MESH,
        )

    def rows(slot, j):
        start = slot * ROWS + j * PART
        return pl.ds(start if isinstance(j, int) else pl.multiple_of(start, PART), PART)

    def piece(j):
        return pl.ds(j * PART, PART)

    def columns(level):
        return pl.ds(level * G, G)

    def transfer(key):
        name, rest = key[0], key[1:]
        if name == "weight":
            if rest[0] == 0:
                return remote(uall.at[:, pl.ds(0, G)], uall.at[:, pl.ds(G, G)], key, "core")
            return remote(dall.at[pl.ds(0, G)], dall.at[pl.ds(G, G)], key, "core")
        if name == "grad":
            at = pl.ds(rest[1] * THIRDS, THIRDS)
            return remote(grad_peer.at[rest[0], at], grad_recv.at[rest[0], at], key, "core")
        if name == "last":
            a, j = "xy".index(rest[0]), rest[1]
            return remote(term_recv.at[0, a, rows(0, j)], last_recv.at[a, piece(j)], key, rest[0] + "3")
        if name in ("hop", "land"):
            axis, level, which, j = rest
            n, group = "nf".index(level), (NEAR if level == "n" else FAR)[axis]
            room = hops.at[n, "xy".index(axis), pl.ds(MOVED.index((which, j)) * PART, PART)]
            if name == "hop":
                return remote(held.at[which, group, rows(0, j)], room, key, ("z1", "z3")[n])
            return remote(room, held.at[which, group, rows(1, j)], key, ("z3", "z1")[n])
        if name in ("near", "far", "term", "sum"):
            axis, which, slot, j = rest
            a, at = "xy".index(axis), rows(slot, j)
            if name == "near":
                src = held.at[which, 0, at] if slot else shared[which].at[piece(j)]
                return remote(src, held.at[which, NEAR[axis], at], key, axis + "1")
            if name == "far":
                return remote(held.at[which, NEAR[axis], at], held.at[which, FAR[axis], at], key, axis + "3")
            if name == "term":
                target = axis + ("1" if passed(which, slot, j) else "3")
                return remote(term_send.at[which, a, at], term_recv.at[which, a, at], key, target)
            return remote(sum_send.at[which, a, at], sum_recv.at[which, a, at], key, axis + "1")
        which, j = rest
        if name == "z1":
            return remote(shared[which].at[piece(j)], held.at[which, 1, rows(0, j)], key, "z1")
        if name == "z3":
            return remote(shared[which].at[piece(j)], held.at[which, 1, rows(1, j)], key, "z3")
        onward = "z3" if j < FIRST else "z1"
        if name == "zr":
            return remote(held.at[which, 1, rows(int(j >= FIRST), j)], held.at[which, 0, rows(1, j)], key, onward)
        if name == "half":
            return remote(half_send.at[which, piece(j)], half_recv.at[which, piece(j)], key, onward)
        slot = int(name == "out3")
        return remote(z_send.at[which, rows(slot, j)], z_recv.at[which, rows(slot, j)], key, "z3" if slot else "z1")

    def together(pieces, sent_by, landed_by):
        span = held.at[0, 0, pl.ds(0, pieces * PART)]
        return pltpu.make_async_remote_copy(
            src_ref=span,
            dst_ref=span,
            send_sem=sends.at[sent_by],
            recv_sem=recvs.at[landed_by],
            device_id=place["z1"],
            device_id_type=MESH,
        )

    started, landed, copied, sent = set(), set(), set(), set()

    def send(*keys):
        for key in keys:
            started.add(key)
            transfer(key).start()

    def need(*keys):
        for key in keys:
            name = arrival(key)
            if name in landed:
                continue
            landed.add(name)
            if name[0] in ("weight", "grad"):
                transfer(key).wait_recv()
            else:
                together(ARRIVALS[name], 0, LANDINGS[name]).wait_recv()

    own = [
        pltpu.make_async_copy(shared[which], held.at[which, 0, pl.ds(0, ROWS)], local.at[which])
        for which in range(2)
    ]
    loads = [pltpu.make_async_copy(ref, raw.at[which], local.at[2 + which]) for which, ref in enumerate((up, down))]
    barrier = pltpu.get_barrier_semaphore()
    for target in place.values():
        pl.semaphore_signal(barrier, inc=1, device_id=target, device_id_type=MESH)
    for copy in loads + own:
        copy.start()
    pl.semaphore_wait(barrier, len(place))

    def tile(slot, t):
        return pl.ds(slot * ROWS + t * TILE, TILE)

    def own_z(which, j):
        send(("z1", which, j), ("z3", which, j))

    def own_xy(which, j):
        send(("near", "x", which, 0, j), ("near", "y", which, 0, j))

    def relay_z(which, j):
        need(("z1" if j < FIRST else "z3", which, j))
        send(("zr", which, j))

    def other(which, j):
        need(("zr", which, j))
        if (which, j) not in MOVED:
            send(("near", "x", which, 1, j), ("near", "y", which, 1, j))

    def relay_xy(which, slot, j):
        for axis in "xy":
            need(("near", axis, which, slot, j))
            send(("far", axis, which, slot, j))

    def hop(axis, level, which, j):
        need(("near" if level == "n" else "far", axis, which, 0, j))
        send(("hop", axis, level, which, j))

    def land(axis, level, which, j):
        need(("hop", axis, level, which, j))
        send(("land", axis, level, which, j))

    def mask_up():
        loads[0].wait()
        for k, level in enumerate(LEVEL):
            uall[pl.ds(k * G, G), pl.ds(0, G)] = (raw[0, level].astype(F32) * mask[0, level].astype(F32)).astype(BF16)
        send(("weight", 0))

    def mask_down():
        loads[1].wait()
        for k, level in enumerate(LEVEL):
            dall[pl.ds(0, G), pl.ds(k * G, G)] = (raw[1, level].astype(F32) * mask[0, level].astype(F32)).astype(BF16)
        send(("weight", 1))

    def turn_weights():
        need(("weight", 0), ("weight", 1))

        def body(k, carry):
            at = pl.ds(pl.multiple_of(k * G, G), G)
            dall_t[at, :] = dall[:, at].T
            uall_t[:, at] = uall[at, :].T
            return carry

        lax.fori_loop(0, LEVELS, body, 0)

    def turn_held(slot):
        def body(k, carry):
            at = pl.ds(pl.multiple_of(k * G, G), G)
            held_t[at, pl.ds(slot * ROWS, ROWS)] = held[0, k, pl.ds(slot * ROWS, ROWS)].T
            return carry

        lax.fori_loop(0, LEVELS, body, 0)

    def turn_act(slot, t):
        act_t[:, tile(slot, t)] = act[tile(slot, t), :].T

    def near_inputs(which, slot, t):
        if slot == 0 and ("own", which) not in copied:
            copied.add(("own", which))
            own[which].wait()
        for j in range(t * PER_TILE, (t + 1) * PER_TILE):
            need(("z3" if slot else "z1", which, j))
            if slot and (which, j) in MOVED:
                need(("land", "x", "n", which, j), ("land", "y", "n", which, j))

    def far_inputs(which, slot, t):
        for j in range(t * PER_TILE, (t + 1) * PER_TILE):
            for axis in "xy":
                need(("land", axis, "f", which, j) if slot and (which, j) in MOVED else ("far", axis, which, slot, j))

    def partial(which, at, weights):
        early = jnp.concatenate([held[which, k, at] for k in range(4)], axis=1)
        return jnp.dot(early, weights[pl.ds(0, 4 * G), :], preferred_element_type=F32)

    def rest(which, at, weights):
        late = jnp.concatenate([held[which, k, at] for k in (4, 5)], axis=1)
        return jnp.dot(late, weights[pl.ds(4 * G, 2 * G), :], preferred_element_type=F32)

    def forward_near(slot, t):
        near_inputs(0, slot, t)
        need(("weight", 0))
        slope[tile(slot, t), :] = partial(0, tile(slot, t), uall)

    def backward_near(slot, t):
        near_inputs(1, slot, t)
        gact[tile(slot, t), :] = partial(1, tile(slot, t), dall_t)

    def forward(slot, t):
        far_inputs(0, slot, t)
        at = tile(slot, t)
        pre = slope[at, :] + rest(0, at, uall)
        square = pre * pre
        tanh = jnp.tanh(SCALE * pre * (1.0 + CUBE * square))
        cdf = 0.5 + 0.5 * tanh
        act[at, :] = (pre * cdf).astype(BF16)
        slope[at, :] = cdf + (0.5 * SCALE) * pre * (1.0 - tanh * tanh) * (1.0 + (3.0 * CUBE) * square)

    def backward(slot, t):
        far_inputs(1, slot, t)
        at = tile(slot, t)
        gpre[at, :] = ((gact[at, :] + rest(1, at, dall_t)) * slope[at, :]).astype(BF16)

    def product(which, slot, t, level):
        if which:
            return jnp.dot(gpre[tile(slot, t), :], uall_t[:, columns(level)], preferred_element_type=F32)
        return jnp.dot(act[tile(slot, t), :], dall[:, columns(level)], preferred_element_type=F32)

    def far_terms(which, slot, t):
        need(("weight", 1))
        for a, axis in enumerate("xy"):
            term_send[which, a, tile(slot, t)] = product(which, slot, t, FAR[axis]).astype(BF16)

    def near_terms(which, slot, t):
        at = tile(slot, t)
        for a, axis in enumerate("xy"):
            near_term[which, a, at] = product(which, slot, t, NEAR[axis])
        z_term[which, at] = product(which, slot, t, 1)
        base[which, at] = product(which, slot, t, 0)

    def send_term(which, slot, j):
        send(("term", "x", which, slot, j), ("term", "y", which, slot, j))

    def hand_on(j):
        for axis in "xy":
            need(("term", axis, 0, 0, j))
            send(("last", axis, j))

    def join(which, slot, j):
        at = rows(slot, j)
        for a, axis in enumerate("xy"):
            total = near_term[which, a, at]
            if not passed(which, slot, j):
                need(("term", axis, which, slot, j))
                total = total + term_recv[which, a, at].astype(F32)
            sum_send[which, a, at] = total.astype(BF16)
            send(("sum", axis, which, slot, j))

    def collect(which, slot, j):
        at = rows(slot, j)
        need(("sum", "x", which, slot, j), ("sum", "y", which, slot, j))
        total = base[which, at] + sum_recv[which, 0, at].astype(F32) + sum_recv[which, 1, at].astype(F32)
        if slot == 0:
            base[which, at] = total
        else:
            half_send[which, piece(j)] = total.astype(BF16)
            send(("half", which, j))

    def plain(which, slot, j):
        z_send[which, rows(slot, j)] = z_term[which, rows(slot, j)].astype(BF16)
        send(("out3" if slot else "out1", which, j))

    def pass_on(which, j):
        slot = int(j >= FIRST)
        at = rows(slot, j)
        need(("half", which, j))
        z_send[which, at] = (z_term[which, at] + half_recv[which, piece(j)].astype(F32)).astype(BF16)
        send(("out3" if slot else "out1", which, j))

    def finish(which, j):
        need(("out1", which, j), ("out3", which, j))
        total = base[which, rows(0, j)] + z_recv[which, rows(0, j)].astype(F32) + z_recv[which, rows(1, j)].astype(F32)
        if passed(which, 0, j):
            need(("last", "x", j), ("last", "y", j))
            total = total + last_recv[0, piece(j)].astype(F32) + last_recv[1, piece(j)].astype(F32)
        (gtok if which else out)[piece(j), :] = total.astype(BF16)

    def grads(which, third):
        def body(k, carry):
            at = pl.ds(pl.multiple_of(k * G, G), G)
            if which:
                both = jnp.dot(act_t[...], held[1, k], preferred_element_type=F32)
                grad_own[1, k] = both[:G]
                grad_peer[1, k] = both[G:]
            else:
                both = jnp.dot(held_t[at, :], gpre[...], preferred_element_type=F32)
                grad_own[0, k] = both[:, :G]
                grad_peer[0, k] = both[:, G:]
            return carry

        lax.fori_loop(third * THIRDS, (third + 1) * THIRDS, body, 0)
        send(("grad", which, third))

    def write_grad(which, k):
        return pltpu.make_async_copy(grad_own.at[which, k], (gdown if which else gup).at[LEVEL[k]], local.at[4 + which * LEVELS + k])

    def grads_sum(which, third):
        need(("grad", which, third))

        for k in range(third * THIRDS, (third + 1) * THIRDS):
            total = grad_own[which, k] + grad_recv[which, k]
            grad_own[which, k] = total * mask[0, LEVEL[k]].astype(F32)
            write_grad(which, k).start()

    def finish_sends(*numbers):
        for name in (tuple(SIZES)[n] for n in numbers):
            sent.add(name)
            if name[0] in ("weight", "grad"):
                transfer(name).wait_send()
            else:
                together(SIZES[name], FAMILIES[name], 0).wait_send()

    steps = (
        own_xy, own_z, relay_z, other, relay_xy, hop, land, mask_up, mask_down, turn_weights, turn_held, turn_act,
        forward_near, forward, backward_near, backward, far_terms, near_terms, send_term, hand_on, join, collect,
        plain, pass_on, finish, grads, grads_sum, finish_sends,
    )
    for step in ORDER:
        steps[step[0]](*step[1:])

    assert started == set(NUMBER) and landed == set(ARRIVALS)
    for which in range(2):
        for k in range(LEVELS):
            write_grad(which, k).wait()
    assert sent == set(FAMILIES)


def hand_out(*refs):
    sources, results, sems = refs[:4], refs[4:8], refs[8]
    copies = []
    for src, dst in zip(sources, results):
        if len(src.shape) == 2:
            pairs = [(src, dst)]
        else:
            pairs = [(src.at[pl.ds(k, 2)], dst.at[pl.ds(k, 2)]) for k in range(0, LEVELS, 2)]
        for a, b in pairs:
            copies.append(pltpu.make_async_copy(a, b, sems.at[len(copies)]))
    for copy in copies:
        copy.start()
    for copy in copies:
        copy.wait()


def shards(tokens, up_weight, down_weight, block_mask, cotangent):
    anywhere = pl.BlockSpec(memory_space=pl.ANY)
    vmem = pl.BlockSpec(memory_space=pltpu.VMEM)
    both = 2 * ROWS
    result = (
        jax.ShapeDtypeStruct((ROWS, G), BF16),
        jax.ShapeDtypeStruct((ROWS, G), BF16),
        jax.ShapeDtypeStruct((LEVELS, G, G), F32),
        jax.ShapeDtypeStruct((LEVELS, G, G), F32),
    )
    operands = [pltpu.with_memory_space_constraint(a, pltpu.HBM) for a in (tokens, cotangent, up_weight[0], down_weight[0])]
    worked = pl.pallas_call(
        kernel,
        out_shape=tuple(pltpu.VMEM(a.shape, a.dtype) for a in result),
        in_specs=[anywhere, anywhere, anywhere, anywhere, pl.BlockSpec(memory_space=pltpu.SMEM)],
        out_specs=(vmem, vmem, anywhere, anywhere),
        scratch_shapes=[
            pltpu.VMEM((2, LEVELS, both, G), BF16),
            pltpu.VMEM((WIDE, both), BF16),
            pltpu.VMEM((2, LEVELS, G, G), BF16),
            pltpu.VMEM((WIDE, 2 * G), BF16),
            pltpu.VMEM((2 * G, WIDE), BF16),
            pltpu.VMEM((2 * G, WIDE), BF16),
            pltpu.VMEM((WIDE, 2 * G), BF16),
            pltpu.VMEM((both, 2 * G), BF16),
            pltpu.VMEM((2 * G, both), BF16),
            pltpu.VMEM((both, 2 * G), BF16),
            pltpu.VMEM((both, 2 * G), F32),
            pltpu.VMEM((both, 2 * G), F32),
            pltpu.VMEM((2, 2, both, G), BF16),
            pltpu.VMEM((2, 2, both, G), BF16),
            pltpu.VMEM((2, 2, both, G), F32),
            pltpu.VMEM((2, 2, both, G), BF16),
            pltpu.VMEM((2, 2, both, G), BF16),
            pltpu.VMEM((2, both, G), F32),
            pltpu.VMEM((2, both, G), F32),
            pltpu.VMEM((2, ROWS, G), BF16),
            pltpu.VMEM((2, ROWS, G), BF16),
            pltpu.VMEM((2, ROWS, G), BF16),
            pltpu.VMEM((2, 2, len(MOVED) * PART, G), BF16),
            pltpu.VMEM((2, both, G), BF16),
            pltpu.VMEM((2, both, G), BF16),
            pltpu.VMEM((2, LEVELS, G, G), F32),
            pltpu.VMEM((2, LEVELS, G, G), F32),
            pltpu.VMEM((2, LEVELS, G, G), F32),
            pltpu.SemaphoreType.DMA((len(FAMILIES),)),
            pltpu.SemaphoreType.DMA((len(LANDINGS),)),
            pltpu.SemaphoreType.DMA((4 + 2 * LEVELS,)),
        ],
        compiler_params=pltpu.CompilerParams(
            collective_id=0, has_side_effects=True, vmem_limit_bytes=58 * 1024 * 1024
        ),
    )(*operands, block_mask)
    worked = [pltpu.with_memory_space_constraint(a, pltpu.VMEM) for a in worked]
    output, grad_tokens, grad_up, grad_down = pl.pallas_call(
        hand_out,
        out_shape=result,
        in_specs=[anywhere] * 4,
        out_specs=(anywhere,) * 4,
        scratch_shapes=[pltpu.SemaphoreType.DMA((8,))],
        compiler_params=pltpu.CompilerParams(vmem_limit_bytes=1024 * 1024),
    )(*worked)
    return output, grad_tokens, grad_up[None], grad_down[None]


def solution(mesh):
    placed = (
        P("seq", "tp"),
        P(("seq", "tp"), None, None, None),
        P(("seq", "tp"), None, None, None),
        P(("seq", "tp"), None),
        P("seq", "tp"),
    )
    return jax.shard_map(
        shards,
        mesh=mesh,
        in_specs=placed,
        out_specs=(
            P("seq", "tp"),
            P("seq", "tp"),
            P(("seq", "tp"), None, None, None),
            P(("seq", "tp"), None, None, None),
        ),
        check_vma=False,
    )
```

```python
import collections
import math

import jax
import jax.numpy as jnp
from jax import lax
from jax.experimental import pallas as pl
from jax.experimental.pallas import tpu as pltpu
from jax.sharding import PartitionSpec as P

MESH = pl.DeviceIdType.MESH
F32 = jnp.float32
BF16 = jnp.bfloat16
ROWS = 512
PART = 128
PIECES = ROWS // PART
FIRST = PIECES // 2
TILE = 256
PER_TILE = TILE // PART
THIRDS = 3
G = 256
LEVELS = 6
WIDE = LEVELS * G
LEVEL = (0, 1, 2, 4, 3, 5)
NEAR = {"x": 3, "y": 2}
FAR = {"x": 5, "y": 4}
SCALE = math.sqrt(2.0 / math.pi)
CUBE = 0.044715


def numbering():
    keys = []
    for which in range(2):
        keys += [(name, which, j) for name in ("z1", "z3", "zr", "out1", "out3", "half") for j in range(PIECES)]
        keys += [
            (name, axis, which, slot, j)
            for name in ("near", "far", "term", "sum")
            for axis in "xy"
            for slot in range(2)
            for j in range(PIECES)
        ]
        keys += [("weight", which)] + [("grad", which, k) for k in range(LEVELS // THIRDS)]
    keys += [("last", axis, j) for axis in "xy" for j in PASSED]
    moved = [(axis, level, which, j) for axis in "xy" for level in "nf" for which, j in MOVED]
    keys += [("hop", *rest) for rest in moved] + [("land", *rest) for rest in moved]
    keys = [k for k in keys if not (k[0] in ("near", "far") and k[3] == 1 and (k[2], k[4]) in MOVED)]
    return {key: n for n, key in enumerate(keys)}


def passed(which, slot, j):
    return which == 0 and slot == 0 and j in PASSED


def family(key):
    name = key[0]
    if name in ("weight", "grad"):
        return key
    if name in ("near", "far", "term", "sum"):
        return name, key[2], key[3]
    if name in ("last", "hop", "land"):
        return (name,)
    return {"z1": "z", "z3": "z", "zr": "middle", "half": "middle", "out1": "out", "out3": "out"}[name], key[1]


def arrival(key):
    name = key[0]
    if name in ("near", "far", "term", "sum"):
        return name, *key[2:]
    if name in ("out1", "out3"):
        return "out", *key[1:]
    if name in ("last", "land"):
        return name, *key[2:]
    return key


PASSED = (2, 3)
MOVED = ((1, 0), (1, 2))
NUMBER = numbering()
ARRIVALS = collections.Counter(arrival(key) for key in NUMBER)
LANDINGS = {name: n for n, name in enumerate(ARRIVALS)}
SIZES = collections.Counter(family(key) for key in NUMBER)
FAMILIES = {name: n for n, name in enumerate(SIZES)}

S_OX, S_OZ, S_RZ, S_OT, S_RX, S_H1, S_H2, S_SU, S_SD, S_TW, S_TH, S_TA, S_FN, S_F, \
    S_BN, S_B, S_TF, S_TN, S_S, S_RL, S_J, S_C, S_Z, S_PO, S_FIN, S_G, S_GS, S_W = range(28)
X, Y, NR, FR = "x", "y", "n", "f"
ORDER = (
    (S_OZ, 0, 3), (S_OX, 0, 3), (S_OX, 1, 0), (S_OZ, 0, 2), (S_OZ, 0, 1), (S_SU,), (S_OZ, 1, 1), (S_OX, 1, 2),
    (S_OX, 0, 2), (S_SD,), (S_OX, 0, 1), (S_RX, 0, 0, 3), (S_OX, 0, 0), (S_OZ, 0, 0), (S_RX, 1, 0, 0), (S_OX, 1, 3),
    (S_RZ, 0, 3), (S_RZ, 0, 2), (S_RX, 1, 0, 2), (S_RZ, 0, 1), (S_OZ, 1, 3), (S_OX, 1, 1), (S_H1, X, NR, 1, 2),
    (S_RX, 0, 0, 2), (S_FN, 0, 1), (S_RZ, 0, 0), (S_RZ, 1, 1), (S_RX, 0, 0, 1), (S_OZ, 1, 2), (S_H1, Y, FR, 1, 0),
    (S_TW,), (S_OT, 0, 3), (S_H1, Y, FR, 1, 2), (S_H1, X, FR, 1, 2), (S_RX, 0, 0, 0), (S_F, 0, 1), (S_RZ, 1, 3),
    (S_OT, 0, 2), (S_RX, 1, 0, 3), (S_H1, X, NR, 1, 0), (S_OT, 0, 1), (S_H1, X, FR, 1, 0), (S_FN, 0, 0),
    (S_RX, 1, 0, 1), (S_H1, Y, NR, 1, 2), (S_H1, Y, NR, 1, 0), (S_OT, 0, 0), (S_TF, 0, 0, 1), (S_OZ, 1, 0),
    (S_RX, 0, 1, 3), (S_TN, 0, 0, 1), (S_F, 0, 0), (S_TF, 0, 0, 0), (S_RX, 0, 1, 2), (S_RZ, 1, 2), (S_OT, 1, 1),
    (S_BN, 0, 1), (S_H2, X, NR, 1, 2), (S_B, 0, 1), (S_TF, 1, 0, 1), (S_RX, 0, 1, 1), (S_TN, 0, 0, 0), (S_OT, 1, 3),
    (S_S, 0, 0, 2), (S_TN, 1, 0, 1), (S_S, 1, 0, 2), (S_H2, Y, FR, 1, 2), (S_FN, 1, 1), (S_TA, 0, 1), (S_J, 0, 0, 2),
    (S_RX, 0, 1, 0), (S_F, 1, 1), (S_TF, 0, 1, 1), (S_S, 0, 1, 2), (S_H2, Y, FR, 1, 0), (S_S, 0, 0, 3),
    (S_RX, 1, 1, 1), (S_H2, X, NR, 1, 0), (S_J, 0, 0, 3), (S_FN, 1, 0), (S_TN, 0, 1, 1), (S_S, 0, 1, 3),
    (S_RZ, 1, 0), (S_BN, 0, 0), (S_TA, 0, 0), (S_W, 11), (S_H2, X, FR, 1, 0), (S_H2, X, FR, 1, 2), (S_B, 0, 0),
    (S_H2, Y, NR, 1, 0), (S_W, 25), (S_TF, 1, 0, 0), (S_RX, 1, 1, 3), (S_F, 1, 0), (S_W, 3), (S_J, 1, 0, 2),
    (S_W, 0), (S_H2, Y, NR, 1, 2), (S_Z, 0, 0, 2), (S_TF, 0, 1, 0), (S_TA, 1, 0), (S_OT, 1, 2), (S_S, 0, 1, 0),
    (S_Z, 0, 0, 3), (S_J, 0, 1, 2), (S_W, 17), (S_Z, 1, 0, 3), (S_TA, 1, 1), (S_OT, 1, 0), (S_TN, 0, 1, 0),
    (S_TH, 0), (S_Z, 0, 1, 0), (S_BN, 1, 0), (S_Z, 1, 0, 2), (S_B, 1, 0), (S_TF, 1, 1, 0), (S_S, 1, 1, 1),
    (S_TN, 1, 1, 0), (S_J, 0, 1, 3), (S_W, 5), (S_S, 1, 1, 0), (S_BN, 1, 1), (S_B, 1, 1), (S_TF, 1, 1, 1),
    (S_J, 0, 1, 0), (S_S, 1, 1, 3), (S_Z, 1, 1, 1), (S_S, 0, 1, 1), (S_S, 1, 1, 2), (S_W, 19), (S_S, 0, 0, 1),
    (S_Z, 1, 1, 0), (S_W, 29), (S_TN, 1, 1, 1), (S_W, 4), (S_S, 1, 0, 3), (S_J, 1, 1, 1), (S_W, 14), (S_G, 1, 1),
    (S_J, 1, 1, 0), (S_C, 0, 1, 0), (S_S, 0, 0, 0), (S_J, 1, 1, 3), (S_Z, 0, 1, 1), (S_G, 1, 0), (S_C, 0, 1, 2),
    (S_C, 1, 1, 1), (S_J, 0, 1, 1), (S_C, 0, 1, 3), (S_J, 1, 1, 2), (S_TH, 1), (S_S, 1, 0, 0), (S_S, 1, 0, 1),
    (S_C, 1, 1, 0), (S_C, 1, 1, 3), (S_G, 0, 1), (S_PO, 0, 2), (S_J, 0, 0, 1), (S_PO, 0, 0), (S_TN, 1, 0, 0),
    (S_W, 6), (S_J, 1, 0, 3), (S_C, 0, 1, 1), (S_RL, 2), (S_C, 1, 1, 2), (S_J, 0, 0, 0), (S_PO, 1, 1), (S_PO, 0, 3),
    (S_G, 0, 0), (S_PO, 1, 3), (S_J, 1, 0, 1), (S_PO, 1, 0), (S_C, 1, 0, 2), (S_RL, 3), (S_PO, 0, 1), (S_J, 1, 0, 0),
    (S_PO, 1, 2), (S_GS, 1, 0), (S_GS, 0, 1), (S_C, 0, 0, 2), (S_GS, 1, 1), (S_W, 20), (S_C, 0, 0, 1),
    (S_C, 0, 0, 0), (S_C, 1, 0, 3), (S_W, 30), (S_FIN, 0, 2), (S_FIN, 0, 0), (S_C, 0, 0, 3), (S_FIN, 1, 3),
    (S_C, 1, 0, 1), (S_FIN, 1, 1), (S_FIN, 0, 3), (S_GS, 0, 0), (S_FIN, 1, 2), (S_C, 1, 0, 0), (S_W, 18),
    (S_FIN, 1, 0), (S_FIN, 0, 1), (S_W, 1, 15, 7, 21, 9, 8, 23, 2, 10, 16, 22, 24, 27, 26, 13, 28, 12),
)


def flip(index, bit):
    return index + bit - 2 * bit * lax.rem(lax.div(index, bit), 2)


def kernel(
    tok, cot, up, down, present, out, gtok, gup, gdown,
    mask, held, held_t, raw, uall, dall, uall_t, dall_t, act, act_t, gpre, slope, gact,
    term_send, term_recv, near_term, sum_send, sum_recv, base, z_term,
    half_send, half_recv, last_recv, hops, z_send, z_recv,
    grad_own, grad_peer, grad_recv,
    sends, recvs, local,
):
    shared = (tok, cot)
    seq, tp = lax.axis_index("seq"), lax.axis_index("tp")
    place = {
        "core": (flip(seq, 1), tp),
        "z1": (seq, flip(tp, 1)),
        "z3": (flip(seq, 2), flip(tp, 1)),
        "x1": (seq, flip(tp, 8)),
        "x3": (seq, flip(flip(tp, 8), 16)),
        "y1": (seq, flip(tp, 2)),
        "y3": (seq, flip(flip(tp, 2), 4)),
    }

    def remote(src, dst, key, target):
        return pltpu.make_async_remote_copy(
            src_ref=src,
            dst_ref=dst,
            send_sem=sends.at[FAMILIES[family(key)]],
            recv_sem=recvs.at[LANDINGS[arrival(key)]],
            device_id=place[target],
            device_id_type=MESH,
        )

    def rows(slot, j):
        start = slot * ROWS + j * PART
        return pl.ds(start if isinstance(j, int) else pl.multiple_of(start, PART), PART)

    def piece(j):
        return pl.ds(j * PART, PART)

    def columns(level):
        return pl.ds(level * G, G)

    def transfer(key):
        name, rest = key[0], key[1:]
        if name == "weight":
            if rest[0] == 0:
                return remote(uall.at[:, pl.ds(0, G)], uall.at[:, pl.ds(G, G)], key, "core")
            return remote(dall.at[pl.ds(0, G)], dall.at[pl.ds(G, G)], key, "core")
        if name == "grad":
            at = pl.ds(rest[1] * THIRDS, THIRDS)
            return remote(grad_peer.at[rest[0], at], grad_recv.at[rest[0], at], key, "core")
        if name == "last":
            a, j = "xy".index(rest[0]), rest[1]
            return remote(term_recv.at[0, a, rows(0, j)], last_recv.at[a, piece(j)], key, rest[0] + "3")
        if name in ("hop", "land"):
            axis, level, which, j = rest
            n, group = "nf".index(level), (NEAR if level == "n" else FAR)[axis]
            room = hops.at[n, "xy".index(axis), pl.ds(MOVED.index((which, j)) * PART, PART)]
            if name == "hop":
                return remote(held.at[which, group, rows(0, j)], room, key, ("z1", "z3")[n])
            return remote(room, held.at[which, group, rows(1, j)], key, ("z3", "z1")[n])
        if name in ("near", "far", "term", "sum"):
            axis, which, slot, j = rest
            a, at = "xy".index(axis), rows(slot, j)
            if name == "near":
                src = held.at[which, 0, at] if slot else shared[which].at[piece(j)]
                return remote(src, held.at[which, NEAR[axis], at], key, axis + "1")
            if name == "far":
                return remote(held.at[which, NEAR[axis], at], held.at[which, FAR[axis], at], key, axis + "3")
            if name == "term":
                target = axis + ("1" if passed(which, slot, j) else "3")
                return remote(term_send.at[which, a, at], term_recv.at[which, a, at], key, target)
            return remote(sum_send.at[which, a, at], sum_recv.at[which, a, at], key, axis + "1")
        which, j = rest
        if name == "z1":
            return remote(shared[which].at[piece(j)], held.at[which, 1, rows(0, j)], key, "z1")
        if name == "z3":
            return remote(shared[which].at[piece(j)], held.at[which, 1, rows(1, j)], key, "z3")
        onward = "z3" if j < FIRST else "z1"
        if name == "zr":
            return remote(held.at[which, 1, rows(int(j >= FIRST), j)], held.at[which, 0, rows(1, j)], key, onward)
        if name == "half":
            return remote(half_send.at[which, piece(j)], half_recv.at[which, piece(j)], key, onward)
        slot = int(name == "out3")
        return remote(z_send.at[which, rows(slot, j)], z_recv.at[which, rows(slot, j)], key, "z3" if slot else "z1")

    def together(pieces, sent_by, landed_by):
        span = held.at[0, 0, pl.ds(0, pieces * PART)]
        return pltpu.make_async_remote_copy(
            src_ref=span,
            dst_ref=span,
            send_sem=sends.at[sent_by],
            recv_sem=recvs.at[landed_by],
            device_id=place["z1"],
            device_id_type=MESH,
        )

    started, landed, copied, sent = set(), set(), set(), set()

    def send(*keys):
        for key in keys:
            started.add(key)
            transfer(key).start()

    def need(*keys):
        for key in keys:
            name = arrival(key)
            if name in landed:
                continue
            landed.add(name)
            if name[0] in ("weight", "grad"):
                transfer(key).wait_recv()
            else:
                together(ARRIVALS[name], 0, LANDINGS[name]).wait_recv()

    own = [
        pltpu.make_async_copy(shared[which], held.at[which, 0, pl.ds(0, ROWS)], local.at[which])
        for which in range(2)
    ]
    loads = [pltpu.make_async_copy(ref, raw.at[which], local.at[2 + which]) for which, ref in enumerate((up, down))]
    mask_load = pltpu.make_async_copy(present, mask, local.at[4 + 2 * LEVELS])
    barrier = pltpu.get_barrier_semaphore()
    for target in place.values():
        pl.semaphore_signal(barrier, inc=1, device_id=target, device_id_type=MESH)
    mask_load.start()
    for copy in loads + own:
        copy.start()
    pl.semaphore_wait(barrier, len(place))

    def tile(slot, t):
        return pl.ds(slot * ROWS + t * TILE, TILE)

    def own_z(which, j):
        send(("z1", which, j), ("z3", which, j))

    def own_xy(which, j):
        send(("near", "x", which, 0, j), ("near", "y", which, 0, j))

    def relay_z(which, j):
        need(("z1" if j < FIRST else "z3", which, j))
        send(("zr", which, j))

    def other(which, j):
        need(("zr", which, j))
        if (which, j) not in MOVED:
            send(("near", "x", which, 1, j), ("near", "y", which, 1, j))

    def relay_xy(which, slot, j):
        for axis in "xy":
            need(("near", axis, which, slot, j))
            send(("far", axis, which, slot, j))

    def hop(axis, level, which, j):
        need(("near" if level == "n" else "far", axis, which, 0, j))
        send(("hop", axis, level, which, j))

    def land(axis, level, which, j):
        need(("hop", axis, level, which, j))
        send(("land", axis, level, which, j))

    def mask_loaded():
        if "mask" not in copied:
            copied.add("mask")
            mask_load.wait()

    def mask_up():
        mask_loaded()
        loads[0].wait()
        for k, level in enumerate(LEVEL):
            uall[pl.ds(k * G, G), pl.ds(0, G)] = (raw[0, level].astype(F32) * mask[0, level].astype(F32)).astype(BF16)
        send(("weight", 0))

    def mask_down():
        mask_loaded()
        loads[1].wait()
        for k, level in enumerate(LEVEL):
            dall[pl.ds(0, G), pl.ds(k * G, G)] = (raw[1, level].astype(F32) * mask[0, level].astype(F32)).astype(BF16)
        send(("weight", 1))

    def turn_weights():
        need(("weight", 0), ("weight", 1))

        def body(k, carry):
            at = pl.ds(pl.multiple_of(k * G, G), G)
            dall_t[at, :] = dall[:, at].T
            uall_t[:, at] = uall[at, :].T
            return carry

        lax.fori_loop(0, LEVELS, body, 0)

    def turn_held(slot):
        def body(k, carry):
            at = pl.ds(pl.multiple_of(k * G, G), G)
            held_t[at, pl.ds(slot * ROWS, ROWS)] = held[0, k, pl.ds(slot * ROWS, ROWS)].T
            return carry

        lax.fori_loop(0, LEVELS, body, 0)

    def turn_act(slot, t):
        act_t[:, tile(slot, t)] = act[tile(slot, t), :].T

    def near_inputs(which, slot, t):
        if slot == 0 and ("own", which) not in copied:
            copied.add(("own", which))
            own[which].wait()
        for j in range(t * PER_TILE, (t + 1) * PER_TILE):
            need(("z3" if slot else "z1", which, j))
            if slot and (which, j) in MOVED:
                need(("land", "x", "n", which, j), ("land", "y", "n", which, j))

    def far_inputs(which, slot, t):
        for j in range(t * PER_TILE, (t + 1) * PER_TILE):
            for axis in "xy":
                need(("land", axis, "f", which, j) if slot and (which, j) in MOVED else ("far", axis, which, slot, j))

    def partial(which, at, weights):
        early = jnp.concatenate([held[which, k, at] for k in range(4)], axis=1)
        return jnp.dot(early, weights[pl.ds(0, 4 * G), :], preferred_element_type=F32)

    def rest(which, at, weights):
        late = jnp.concatenate([held[which, k, at] for k in (4, 5)], axis=1)
        return jnp.dot(late, weights[pl.ds(4 * G, 2 * G), :], preferred_element_type=F32)

    def forward_near(slot, t):
        near_inputs(0, slot, t)
        need(("weight", 0))
        slope[tile(slot, t), :] = partial(0, tile(slot, t), uall)

    def backward_near(slot, t):
        near_inputs(1, slot, t)
        gact[tile(slot, t), :] = partial(1, tile(slot, t), dall_t)

    def forward(slot, t):
        far_inputs(0, slot, t)
        at = tile(slot, t)
        pre = slope[at, :] + rest(0, at, uall)
        square = pre * pre
        tanh = jnp.tanh(SCALE * pre * (1.0 + CUBE * square))
        cdf = 0.5 + 0.5 * tanh
        act[at, :] = (pre * cdf).astype(BF16)
        slope[at, :] = cdf + (0.5 * SCALE) * pre * (1.0 - tanh * tanh) * (1.0 + (3.0 * CUBE) * square)

    def backward(slot, t):
        far_inputs(1, slot, t)
        at = tile(slot, t)
        gpre[at, :] = ((gact[at, :] + rest(1, at, dall_t)) * slope[at, :]).astype(BF16)

    def product(which, slot, t, level):
        if which:
            return jnp.dot(gpre[tile(slot, t), :], uall_t[:, columns(level)], preferred_element_type=F32)
        return jnp.dot(act[tile(slot, t), :], dall[:, columns(level)], preferred_element_type=F32)

    def far_terms(which, slot, t):
        need(("weight", 1))
        for a, axis in enumerate("xy"):
            term_send[which, a, tile(slot, t)] = product(which, slot, t, FAR[axis]).astype(BF16)

    def near_terms(which, slot, t):
        at = tile(slot, t)
        for a, axis in enumerate("xy"):
            near_term[which, a, at] = product(which, slot, t, NEAR[axis])
        z_term[which, at] = product(which, slot, t, 1)
        base[which, at] = product(which, slot, t, 0)

    def send_term(which, slot, j):
        send(("term", "x", which, slot, j), ("term", "y", which, slot, j))

    def hand_on(j):
        for axis in "xy":
            need(("term", axis, 0, 0, j))
            send(("last", axis, j))

    def join(which, slot, j):
        at = rows(slot, j)
        for a, axis in enumerate("xy"):
            total = near_term[which, a, at]
            if not passed(which, slot, j):
                need(("term", axis, which, slot, j))
                total = total + term_recv[which, a, at].astype(F32)
            sum_send[which, a, at] = total.astype(BF16)
            send(("sum", axis, which, slot, j))

    def collect(which, slot, j):
        at = rows(slot, j)
        need(("sum", "x", which, slot, j), ("sum", "y", which, slot, j))
        total = base[which, at] + sum_recv[which, 0, at].astype(F32) + sum_recv[which, 1, at].astype(F32)
        if slot == 0:
            base[which, at] = total
        else:
            half_send[which, piece(j)] = total.astype(BF16)
            send(("half", which, j))

    def plain(which, slot, j):
        z_send[which, rows(slot, j)] = z_term[which, rows(slot, j)].astype(BF16)
        send(("out3" if slot else "out1", which, j))

    def pass_on(which, j):
        slot = int(j >= FIRST)
        at = rows(slot, j)
        need(("half", which, j))
        z_send[which, at] = (z_term[which, at] + half_recv[which, piece(j)].astype(F32)).astype(BF16)
        send(("out3" if slot else "out1", which, j))

    def finish(which, j):
        need(("out1", which, j), ("out3", which, j))
        total = base[which, rows(0, j)] + z_recv[which, rows(0, j)].astype(F32) + z_recv[which, rows(1, j)].astype(F32)
        if passed(which, 0, j):
            need(("last", "x", j), ("last", "y", j))
            total = total + last_recv[0, piece(j)].astype(F32) + last_recv[1, piece(j)].astype(F32)
        (gtok if which else out)[piece(j), :] = total.astype(BF16)

    def grads(which, third):
        def body(k, carry):
            at = pl.ds(pl.multiple_of(k * G, G), G)
            if which:
                both = jnp.dot(act_t[...], held[1, k], preferred_element_type=F32)
                grad_own[1, k] = both[:G]
                grad_peer[1, k] = both[G:]
            else:
                both = jnp.dot(held_t[at, :], gpre[...], preferred_element_type=F32)
                grad_own[0, k] = both[:, :G]
                grad_peer[0, k] = both[:, G:]
            return carry

        lax.fori_loop(third * THIRDS, (third + 1) * THIRDS, body, 0)
        send(("grad", which, third))

    def write_grad(which, k):
        return pltpu.make_async_copy(grad_own.at[which, k], (gdown if which else gup).at[LEVEL[k]], local.at[4 + which * LEVELS + k])

    def grads_sum(which, third):
        need(("grad", which, third))

        for k in range(third * THIRDS, (third + 1) * THIRDS):
            total = grad_own[which, k] + grad_recv[which, k]
            grad_own[which, k] = total * mask[0, LEVEL[k]].astype(F32)
            write_grad(which, k).start()

    def finish_sends(*numbers):
        for name in (tuple(SIZES)[n] for n in numbers):
            sent.add(name)
            if name[0] in ("weight", "grad"):
                transfer(name).wait_send()
            else:
                together(SIZES[name], FAMILIES[name], 0).wait_send()

    steps = (
        own_xy, own_z, relay_z, other, relay_xy, hop, land, mask_up, mask_down, turn_weights, turn_held, turn_act,
        forward_near, forward, backward_near, backward, far_terms, near_terms, send_term, hand_on, join, collect,
        plain, pass_on, finish, grads, grads_sum, finish_sends,
    )
    for step in ORDER:
        steps[step[0]](*step[1:])

    assert started == set(NUMBER) and landed == set(ARRIVALS)
    for which in range(2):
        for k in range(LEVELS):
            write_grad(which, k).wait()
    assert sent == set(FAMILIES)


def hand_out(*refs):
    sources, results, sems = refs[:4], refs[4:8], refs[8]
    copies = []
    for src, dst in zip(sources, results):
        if len(src.shape) == 2:
            pairs = [(src, dst)]
        else:
            pairs = [(src.at[pl.ds(k, 2)], dst.at[pl.ds(k, 2)]) for k in range(0, LEVELS, 2)]
        for a, b in pairs:
            copies.append(pltpu.make_async_copy(a, b, sems.at[len(copies)]))
    for copy in copies:
        copy.start()
    for copy in copies:
        copy.wait()


def shards(tokens, up_weight, down_weight, block_mask, cotangent):
    anywhere = pl.BlockSpec(memory_space=pl.ANY)
    vmem = pl.BlockSpec(memory_space=pltpu.VMEM)
    both = 2 * ROWS
    result = (
        jax.ShapeDtypeStruct((ROWS, G), BF16),
        jax.ShapeDtypeStruct((ROWS, G), BF16),
        jax.ShapeDtypeStruct((LEVELS, G, G), F32),
        jax.ShapeDtypeStruct((LEVELS, G, G), F32),
    )
    operands = [pltpu.with_memory_space_constraint(a, pltpu.HBM) for a in (tokens, cotangent, up_weight[0], down_weight[0], block_mask)]
    worked = pl.pallas_call(
        kernel,
        out_shape=tuple(pltpu.VMEM(a.shape, a.dtype) for a in result),
        in_specs=[anywhere] * 5,
        out_specs=(vmem, vmem, anywhere, anywhere),
        scratch_shapes=[
            pltpu.SMEM((1, LEVELS), jnp.int32),
            pltpu.VMEM((2, LEVELS, both, G), BF16),
            pltpu.VMEM((WIDE, both), BF16),
            pltpu.VMEM((2, LEVELS, G, G), BF16),
            pltpu.VMEM((WIDE, 2 * G), BF16),
            pltpu.VMEM((2 * G, WIDE), BF16),
            pltpu.VMEM((2 * G, WIDE), BF16),
            pltpu.VMEM((WIDE, 2 * G), BF16),
            pltpu.VMEM((both, 2 * G), BF16),
            pltpu.VMEM((2 * G, both), BF16),
            pltpu.VMEM((both, 2 * G), BF16),
            pltpu.VMEM((both, 2 * G), F32),
            pltpu.VMEM((both, 2 * G), F32),
            pltpu.VMEM((2, 2, both, G), BF16),
            pltpu.VMEM((2, 2, both, G), BF16),
            pltpu.VMEM((2, 2, both, G), F32),
            pltpu.VMEM((2, 2, both, G), BF16),
            pltpu.VMEM((2, 2, both, G), BF16),
            pltpu.VMEM((2, both, G), F32),
            pltpu.VMEM((2, both, G), F32),
            pltpu.VMEM((2, ROWS, G), BF16),
            pltpu.VMEM((2, ROWS, G), BF16),
            pltpu.VMEM((2, ROWS, G), BF16),
            pltpu.VMEM((2, 2, len(MOVED) * PART, G), BF16),
            pltpu.VMEM((2, both, G), BF16),
            pltpu.VMEM((2, both, G), BF16),
            pltpu.VMEM((2, LEVELS, G, G), F32),
            pltpu.VMEM((2, LEVELS, G, G), F32),
            pltpu.VMEM((2, LEVELS, G, G), F32),
            pltpu.SemaphoreType.DMA((len(FAMILIES),)),
            pltpu.SemaphoreType.DMA((len(LANDINGS),)),
            pltpu.SemaphoreType.DMA((5 + 2 * LEVELS,)),
        ],
        compiler_params=pltpu.CompilerParams(
            collective_id=0, has_side_effects=True, vmem_limit_bytes=58 * 1024 * 1024
        ),
    )(*operands)
    worked = [pltpu.with_memory_space_constraint(a, pltpu.VMEM) for a in worked]
    output, grad_tokens, grad_up, grad_down = pl.pallas_call(
        hand_out,
        out_shape=result,
        in_specs=[anywhere] * 4,
        out_specs=(anywhere,) * 4,
        scratch_shapes=[pltpu.SemaphoreType.DMA((8,))],
        compiler_params=pltpu.CompilerParams(vmem_limit_bytes=1024 * 1024),
    )(*worked)
    return output, grad_tokens, grad_up[None], grad_down[None]


def solution(mesh):
    placed = (
        P("seq", "tp"),
        P(("seq", "tp"), None, None, None),
        P(("seq", "tp"), None, None, None),
        P(("seq", "tp"), None),
        P("seq", "tp"),
    )
    return jax.shard_map(
        shards,
        mesh=mesh,
        in_specs=placed,
        out_specs=(
            P("seq", "tp"),
            P("seq", "tp"),
            P(("seq", "tp"), None, None, None),
            P(("seq", "tp"), None, None, None),
        ),
        check_vma=False,
    )
```

```python
import collections
import math

import jax
import jax.numpy as jnp
from jax import lax
from jax.experimental import pallas as pl
from jax.experimental.pallas import tpu as pltpu
from jax.sharding import PartitionSpec as P

MESH = pl.DeviceIdType.MESH
F32 = jnp.float32
BF16 = jnp.bfloat16
ROWS = 512
PART = 128
PIECES = ROWS // PART
FIRST = PIECES // 2
TILE = 256
PER_TILE = TILE // PART
THIRDS = 3
G = 256
LEVELS = 6
WIDE = LEVELS * G
LEVEL = (0, 1, 2, 4, 3, 5)
NEAR = {"x": 3, "y": 2}
FAR = {"x": 5, "y": 4}
SCALE = math.sqrt(2.0 / math.pi)
CUBE = 0.044715


def numbering():
    keys = []
    for which in range(2):
        keys += [(name, which, j) for name in ("z1", "z3", "zr", "out1", "out3", "half") for j in range(PIECES)]
        keys += [
            (name, axis, which, slot, j)
            for name in ("near", "far", "term", "sum")
            for axis in "xy"
            for slot in range(2)
            for j in range(PIECES)
        ]
        keys += [("weight", which)] + [("grad", which, k) for k in range(LEVELS // THIRDS)]
    keys += [("last", axis, j) for axis in "xy" for j in PASSED]
    moved = [(axis, level, which, j) for axis in "xy" for level in "nf" for which, j in MOVED]
    keys += [("hop", *rest) for rest in moved] + [("land", *rest) for rest in moved]
    keys = [k for k in keys if not (k[0] in ("near", "far") and k[3] == 1 and (k[2], k[4]) in MOVED)]
    return {key: n for n, key in enumerate(keys)}


def passed(which, slot, j):
    return which == 0 and slot == 0 and j in PASSED


def family(key):
    name = key[0]
    if name in ("weight", "grad"):
        return key
    if name in ("near", "far", "term", "sum"):
        return name, key[2], key[3]
    if name in ("last", "hop", "land"):
        return (name,)
    return {"z1": "z", "z3": "z", "zr": "middle", "half": "middle", "out1": "out", "out3": "out"}[name], key[1]


def arrival(key):
    name = key[0]
    if name in ("near", "far", "term", "sum"):
        return name, *key[2:]
    if name in ("out1", "out3"):
        return "out", *key[1:]
    if name in ("last", "land"):
        return name, *key[2:]
    return key


PASSED = (2, 3)
MOVED = ((1, 0), (1, 2))
NUMBER = numbering()
ARRIVALS = collections.Counter(arrival(key) for key in NUMBER)
LANDINGS = {name: n for n, name in enumerate(ARRIVALS)}
SIZES = collections.Counter(family(key) for key in NUMBER)
FAMILIES = {name: n for n, name in enumerate(SIZES)}

S_OX, S_OZ, S_RZ, S_OT, S_RX, S_H1, S_H2, S_SU, S_SD, S_TW, S_TH, S_TA, S_FN, S_F, \
    S_BN, S_B, S_TF, S_TN, S_S, S_RL, S_J, S_C, S_Z, S_PO, S_FIN, S_G, S_GS, S_W = range(28)
X, Y, NR, FR = "x", "y", "n", "f"
ORDER = (
    (S_OZ, 0, 3), (S_OX, 0, 3), (S_OX, 1, 0), (S_OZ, 0, 2), (S_OZ, 0, 1), (S_SU,), (S_OZ, 1, 1), (S_OX, 1, 2),
    (S_OX, 0, 2), (S_SD,), (S_OX, 0, 1), (S_RX, 0, 0, 3), (S_OX, 0, 0), (S_OZ, 0, 0), (S_RX, 1, 0, 0), (S_OX, 1, 3),
    (S_RZ, 0, 3), (S_RZ, 0, 2), (S_RX, 1, 0, 2), (S_RZ, 0, 1), (S_OZ, 1, 3), (S_OX, 1, 1), (S_H1, X, NR, 1, 2),
    (S_RX, 0, 0, 2), (S_FN, 0, 1), (S_RZ, 0, 0), (S_RZ, 1, 1), (S_RX, 0, 0, 1), (S_OZ, 1, 2), (S_H1, Y, FR, 1, 0),
    (S_TW,), (S_OT, 0, 3), (S_H1, Y, FR, 1, 2), (S_H1, X, FR, 1, 2), (S_RX, 0, 0, 0), (S_F, 0, 1), (S_RZ, 1, 3),
    (S_OT, 0, 2), (S_RX, 1, 0, 3), (S_H1, X, NR, 1, 0), (S_OT, 0, 1), (S_H1, X, FR, 1, 0), (S_FN, 0, 0),
    (S_RX, 1, 0, 1), (S_H1, Y, NR, 1, 2), (S_H1, Y, NR, 1, 0), (S_OT, 0, 0), (S_TF, 0, 0, 1), (S_OZ, 1, 0),
    (S_RX, 0, 1, 3), (S_TN, 0, 0, 1), (S_F, 0, 0), (S_TF, 0, 0, 0), (S_RX, 0, 1, 2), (S_RZ, 1, 2), (S_OT, 1, 1),
    (S_BN, 0, 1), (S_H2, X, NR, 1, 2), (S_B, 0, 1), (S_TF, 1, 0, 1), (S_RX, 0, 1, 1), (S_TN, 0, 0, 0), (S_OT, 1, 3),
    (S_S, 0, 0, 2), (S_TN, 1, 0, 1), (S_S, 1, 0, 2), (S_H2, Y, FR, 1, 2), (S_FN, 1, 1), (S_TA, 0, 1), (S_J, 0, 0, 2),
    (S_RX, 0, 1, 0), (S_F, 1, 1), (S_TF, 0, 1, 1), (S_S, 0, 1, 2), (S_H2, Y, FR, 1, 0), (S_S, 0, 0, 3),
    (S_RX, 1, 1, 1), (S_H2, X, NR, 1, 0), (S_J, 0, 0, 3), (S_FN, 1, 0), (S_TN, 0, 1, 1), (S_S, 0, 1, 3),
    (S_RZ, 1, 0), (S_BN, 0, 0), (S_TA, 0, 0), (S_W, 11), (S_H2, X, FR, 1, 0), (S_H2, X, FR, 1, 2), (S_B, 0, 0),
    (S_H2, Y, NR, 1, 0), (S_W, 25), (S_TF, 1, 0, 0), (S_RX, 1, 1, 3), (S_F, 1, 0), (S_W, 3), (S_J, 1, 0, 2),
    (S_W, 0), (S_H2, Y, NR, 1, 2), (S_Z, 0, 0, 2), (S_TF, 0, 1, 0), (S_TA, 1, 0), (S_OT, 1, 2), (S_S, 0, 1, 0),
    (S_Z, 0, 0, 3), (S_J, 0, 1, 2), (S_W, 17), (S_Z, 1, 0, 3), (S_TA, 1, 1), (S_OT, 1, 0), (S_TN, 0, 1, 0),
    (S_TH, 0), (S_Z, 0, 1, 0), (S_BN, 1, 0), (S_Z, 1, 0, 2), (S_B, 1, 0), (S_TF, 1, 1, 0), (S_S, 1, 1, 1),
    (S_TN, 1, 1, 0), (S_J, 0, 1, 3), (S_W, 5), (S_S, 1, 1, 0), (S_BN, 1, 1), (S_B, 1, 1), (S_TF, 1, 1, 1),
    (S_J, 0, 1, 0), (S_S, 1, 1, 3), (S_Z, 1, 1, 1), (S_S, 0, 1, 1), (S_S, 1, 1, 2), (S_W, 19), (S_S, 0, 0, 1),
    (S_Z, 1, 1, 0), (S_W, 29), (S_TN, 1, 1, 1), (S_W, 4), (S_S, 1, 0, 3), (S_J, 1, 1, 1), (S_W, 14), (S_G, 1, 1),
    (S_J, 1, 1, 0), (S_C, 0, 1, 0), (S_S, 0, 0, 0), (S_J, 1, 1, 3), (S_Z, 0, 1, 1), (S_G, 1, 0), (S_C, 0, 1, 2),
    (S_C, 1, 1, 1), (S_J, 0, 1, 1), (S_C, 0, 1, 3), (S_J, 1, 1, 2), (S_TH, 1), (S_S, 1, 0, 0), (S_S, 1, 0, 1),
    (S_C, 1, 1, 0), (S_C, 1, 1, 3), (S_G, 0, 1), (S_PO, 0, 2), (S_J, 0, 0, 1), (S_PO, 0, 0), (S_TN, 1, 0, 0),
    (S_W, 6), (S_J, 1, 0, 3), (S_C, 0, 1, 1), (S_RL, 2), (S_C, 1, 1, 2), (S_J, 0, 0, 0), (S_PO, 1, 1), (S_PO, 0, 3),
    (S_G, 0, 0), (S_PO, 1, 3), (S_J, 1, 0, 1), (S_PO, 1, 0), (S_C, 1, 0, 2), (S_RL, 3), (S_PO, 0, 1), (S_J, 1, 0, 0),
    (S_PO, 1, 2), (S_GS, 1, 0), (S_GS, 0, 1), (S_C, 0, 0, 2), (S_GS, 1, 1), (S_W, 20), (S_C, 0, 0, 1),
    (S_C, 0, 0, 0), (S_C, 1, 0, 3), (S_W, 30), (S_FIN, 0, 2), (S_FIN, 0, 0), (S_C, 0, 0, 3), (S_FIN, 1, 3),
    (S_C, 1, 0, 1), (S_FIN, 1, 1), (S_FIN, 0, 3), (S_GS, 0, 0), (S_FIN, 1, 2), (S_C, 1, 0, 0), (S_W, 18),
    (S_FIN, 1, 0), (S_FIN, 0, 1), (S_W, 1, 15, 7, 21, 9, 8, 23, 2, 10, 16, 22, 24, 27, 26, 13, 28, 12),
)


def flip(index, bit):
    return index + bit - 2 * bit * lax.rem(lax.div(index, bit), 2)


def kernel(
    tok, cot, up, down, present, out, gtok, gup, gdown,
    mask, held, held_t, raw, uall, dall, uall_t, dall_t, act, act_t, gpre, slope, gact,
    term_send, term_recv, near_term, sum_send, sum_recv, base, z_term,
    half_send, half_recv, last_recv, hops, z_send, z_recv, final,
    grad_own, grad_peer, grad_recv,
    sends, recvs, local,
):
    shared = (tok, cot)
    seq, tp = lax.axis_index("seq"), lax.axis_index("tp")
    place = {
        "core": (flip(seq, 1), tp),
        "z1": (seq, flip(tp, 1)),
        "z3": (flip(seq, 2), flip(tp, 1)),
        "x1": (seq, flip(tp, 8)),
        "x3": (seq, flip(flip(tp, 8), 16)),
        "y1": (seq, flip(tp, 2)),
        "y3": (seq, flip(flip(tp, 2), 4)),
    }

    def remote(src, dst, key, target):
        return pltpu.make_async_remote_copy(
            src_ref=src,
            dst_ref=dst,
            send_sem=sends.at[FAMILIES[family(key)]],
            recv_sem=recvs.at[LANDINGS[arrival(key)]],
            device_id=place[target],
            device_id_type=MESH,
        )

    def rows(slot, j):
        start = slot * ROWS + j * PART
        return pl.ds(start if isinstance(j, int) else pl.multiple_of(start, PART), PART)

    def piece(j):
        return pl.ds(j * PART, PART)

    def columns(level):
        return pl.ds(level * G, G)

    def transfer(key):
        name, rest = key[0], key[1:]
        if name == "weight":
            if rest[0] == 0:
                return remote(uall.at[:, pl.ds(0, G)], uall.at[:, pl.ds(G, G)], key, "core")
            return remote(dall.at[pl.ds(0, G)], dall.at[pl.ds(G, G)], key, "core")
        if name == "grad":
            at = pl.ds(rest[1] * THIRDS, THIRDS)
            return remote(grad_peer.at[rest[0], at], grad_recv.at[rest[0], at], key, "core")
        if name == "last":
            a, j = "xy".index(rest[0]), rest[1]
            return remote(term_recv.at[0, a, rows(0, j)], last_recv.at[a, piece(j)], key, rest[0] + "3")
        if name in ("hop", "land"):
            axis, level, which, j = rest
            n, group = "nf".index(level), (NEAR if level == "n" else FAR)[axis]
            room = hops.at[n, "xy".index(axis), pl.ds(MOVED.index((which, j)) * PART, PART)]
            if name == "hop":
                return remote(held.at[which, group, rows(0, j)], room, key, ("z1", "z3")[n])
            return remote(room, held.at[which, group, rows(1, j)], key, ("z3", "z1")[n])
        if name in ("near", "far", "term", "sum"):
            axis, which, slot, j = rest
            a, at = "xy".index(axis), rows(slot, j)
            if name == "near":
                src = held.at[which, 0, at] if slot else shared[which].at[piece(j)]
                return remote(src, held.at[which, NEAR[axis], at], key, axis + "1")
            if name == "far":
                return remote(held.at[which, NEAR[axis], at], held.at[which, FAR[axis], at], key, axis + "3")
            if name == "term":
                target = axis + ("1" if passed(which, slot, j) else "3")
                return remote(term_send.at[which, a, at], term_recv.at[which, a, at], key, target)
            return remote(sum_send.at[which, a, at], sum_recv.at[which, a, at], key, axis + "1")
        which, j = rest
        if name == "z1":
            return remote(shared[which].at[piece(j)], held.at[which, 1, rows(0, j)], key, "z1")
        if name == "z3":
            return remote(shared[which].at[piece(j)], held.at[which, 1, rows(1, j)], key, "z3")
        onward = "z3" if j < FIRST else "z1"
        if name == "zr":
            return remote(held.at[which, 1, rows(int(j >= FIRST), j)], held.at[which, 0, rows(1, j)], key, onward)
        if name == "half":
            return remote(half_send.at[which, piece(j)], half_recv.at[which, piece(j)], key, onward)
        slot = int(name == "out3")
        return remote(z_send.at[which, rows(slot, j)], z_recv.at[which, rows(slot, j)], key, "z3" if slot else "z1")

    def together(pieces, sent_by, landed_by):
        span = held.at[0, 0, pl.ds(0, pieces * PART)]
        return pltpu.make_async_remote_copy(
            src_ref=span,
            dst_ref=span,
            send_sem=sends.at[sent_by],
            recv_sem=recvs.at[landed_by],
            device_id=place["z1"],
            device_id_type=MESH,
        )

    started, landed, copied, sent = set(), set(), set(), set()

    def send(*keys):
        for key in keys:
            started.add(key)
            transfer(key).start()

    def need(*keys):
        for key in keys:
            name = arrival(key)
            if name in landed:
                continue
            landed.add(name)
            if name[0] in ("weight", "grad"):
                transfer(key).wait_recv()
            else:
                together(ARRIVALS[name], 0, LANDINGS[name]).wait_recv()

    own = [
        pltpu.make_async_copy(shared[which], held.at[which, 0, pl.ds(0, ROWS)], local.at[which])
        for which in range(2)
    ]
    loads = [pltpu.make_async_copy(ref, raw.at[which], local.at[2 + which]) for which, ref in enumerate((up, down))]
    mask_load = pltpu.make_async_copy(present, mask, local.at[4 + 2 * LEVELS])
    barrier = pltpu.get_barrier_semaphore()
    for target in place.values():
        pl.semaphore_signal(barrier, inc=1, device_id=target, device_id_type=MESH)
    mask_load.start()
    for copy in loads + own:
        copy.start()
    pl.semaphore_wait(barrier, len(place))

    def tile(slot, t):
        return pl.ds(slot * ROWS + t * TILE, TILE)

    def own_z(which, j):
        send(("z1", which, j), ("z3", which, j))

    def own_xy(which, j):
        send(("near", "x", which, 0, j), ("near", "y", which, 0, j))

    def relay_z(which, j):
        need(("z1" if j < FIRST else "z3", which, j))
        send(("zr", which, j))

    def other(which, j):
        need(("zr", which, j))
        if (which, j) not in MOVED:
            send(("near", "x", which, 1, j), ("near", "y", which, 1, j))

    def relay_xy(which, slot, j):
        for axis in "xy":
            need(("near", axis, which, slot, j))
            send(("far", axis, which, slot, j))

    def hop(axis, level, which, j):
        need(("near" if level == "n" else "far", axis, which, 0, j))
        send(("hop", axis, level, which, j))

    def land(axis, level, which, j):
        need(("hop", axis, level, which, j))
        send(("land", axis, level, which, j))

    def mask_loaded():
        if "mask" not in copied:
            copied.add("mask")
            mask_load.wait()

    def mask_up():
        mask_loaded()
        loads[0].wait()
        for k, level in enumerate(LEVEL):
            uall[pl.ds(k * G, G), pl.ds(0, G)] = (raw[0, level].astype(F32) * mask[0, level].astype(F32)).astype(BF16)
        send(("weight", 0))

    def mask_down():
        mask_loaded()
        loads[1].wait()
        for k, level in enumerate(LEVEL):
            dall[pl.ds(0, G), pl.ds(k * G, G)] = (raw[1, level].astype(F32) * mask[0, level].astype(F32)).astype(BF16)
        send(("weight", 1))

    def turn_weights():
        need(("weight", 0), ("weight", 1))

        def body(k, carry):
            at = pl.ds(pl.multiple_of(k * G, G), G)
            dall_t[at, :] = dall[:, at].T
            uall_t[:, at] = uall[at, :].T
            return carry

        lax.fori_loop(0, LEVELS, body, 0)

    def turn_held(slot):
        def body(k, carry):
            at = pl.ds(pl.multiple_of(k * G, G), G)
            held_t[at, pl.ds(slot * ROWS, ROWS)] = held[0, k, pl.ds(slot * ROWS, ROWS)].T
            return carry

        lax.fori_loop(0, LEVELS, body, 0)

    def turn_act(slot, t):
        act_t[:, tile(slot, t)] = act[tile(slot, t), :].T

    def near_inputs(which, slot, t):
        if slot == 0 and ("own", which) not in copied:
            copied.add(("own", which))
            own[which].wait()
        for j in range(t * PER_TILE, (t + 1) * PER_TILE):
            need(("z3" if slot else "z1", which, j))
            if slot and (which, j) in MOVED:
                need(("land", "x", "n", which, j), ("land", "y", "n", which, j))

    def far_inputs(which, slot, t):
        for j in range(t * PER_TILE, (t + 1) * PER_TILE):
            for axis in "xy":
                need(("land", axis, "f", which, j) if slot and (which, j) in MOVED else ("far", axis, which, slot, j))

    def partial(which, at, weights):
        early = jnp.concatenate([held[which, k, at] for k in range(4)], axis=1)
        return jnp.dot(early, weights[pl.ds(0, 4 * G), :], preferred_element_type=F32)

    def rest(which, at, weights):
        late = jnp.concatenate([held[which, k, at] for k in (4, 5)], axis=1)
        return jnp.dot(late, weights[pl.ds(4 * G, 2 * G), :], preferred_element_type=F32)

    def forward_near(slot, t):
        near_inputs(0, slot, t)
        need(("weight", 0))
        slope[tile(slot, t), :] = partial(0, tile(slot, t), uall)

    def backward_near(slot, t):
        near_inputs(1, slot, t)
        gact[tile(slot, t), :] = partial(1, tile(slot, t), dall_t)

    def forward(slot, t):
        far_inputs(0, slot, t)
        at = tile(slot, t)
        pre = slope[at, :] + rest(0, at, uall)
        square = pre * pre
        tanh = jnp.tanh(SCALE * pre * (1.0 + CUBE * square))
        cdf = 0.5 + 0.5 * tanh
        act[at, :] = (pre * cdf).astype(BF16)
        slope[at, :] = cdf + (0.5 * SCALE) * pre * (1.0 - tanh * tanh) * (1.0 + (3.0 * CUBE) * square)

    def backward(slot, t):
        far_inputs(1, slot, t)
        at = tile(slot, t)
        gpre[at, :] = ((gact[at, :] + rest(1, at, dall_t)) * slope[at, :]).astype(BF16)

    def product(which, slot, t, level):
        if which:
            return jnp.dot(gpre[tile(slot, t), :], uall_t[:, columns(level)], preferred_element_type=F32)
        return jnp.dot(act[tile(slot, t), :], dall[:, columns(level)], preferred_element_type=F32)

    def far_terms(which, slot, t):
        need(("weight", 1))
        for a, axis in enumerate("xy"):
            term_send[which, a, tile(slot, t)] = product(which, slot, t, FAR[axis]).astype(BF16)

    def near_terms(which, slot, t):
        at = tile(slot, t)
        for a, axis in enumerate("xy"):
            near_term[which, a, at] = product(which, slot, t, NEAR[axis])
        z_term[which, at] = product(which, slot, t, 1)
        base[which, at] = product(which, slot, t, 0)

    def send_term(which, slot, j):
        send(("term", "x", which, slot, j), ("term", "y", which, slot, j))

    def hand_on(j):
        for axis in "xy":
            need(("term", axis, 0, 0, j))
            send(("last", axis, j))

    def join(which, slot, j):
        at = rows(slot, j)
        for a, axis in enumerate("xy"):
            total = near_term[which, a, at]
            if not passed(which, slot, j):
                need(("term", axis, which, slot, j))
                total = total + term_recv[which, a, at].astype(F32)
            sum_send[which, a, at] = total.astype(BF16)
            send(("sum", axis, which, slot, j))

    def collect(which, slot, j):
        at = rows(slot, j)
        need(("sum", "x", which, slot, j), ("sum", "y", which, slot, j))
        total = base[which, at] + sum_recv[which, 0, at].astype(F32) + sum_recv[which, 1, at].astype(F32)
        if slot == 0:
            base[which, at] = total
        else:
            half_send[which, piece(j)] = total.astype(BF16)
            send(("half", which, j))

    def plain(which, slot, j):
        z_send[which, rows(slot, j)] = z_term[which, rows(slot, j)].astype(BF16)
        send(("out3" if slot else "out1", which, j))

    def pass_on(which, j):
        slot = int(j >= FIRST)
        at = rows(slot, j)
        need(("half", which, j))
        z_send[which, at] = (z_term[which, at] + half_recv[which, piece(j)].astype(F32)).astype(BF16)
        send(("out3" if slot else "out1", which, j))

    def finish(which, j):
        need(("out1", which, j), ("out3", which, j))
        total = base[which, rows(0, j)] + z_recv[which, rows(0, j)].astype(F32) + z_recv[which, rows(1, j)].astype(F32)
        if passed(which, 0, j):
            need(("last", "x", j), ("last", "y", j))
            total = total + last_recv[0, piece(j)].astype(F32) + last_recv[1, piece(j)].astype(F32)
        final[which, piece(j)] = total.astype(BF16)
        write_final(which, j).start()

    def write_final(which, j):
        number = 5 + 2 * LEVELS + which * PIECES + j
        return pltpu.make_async_copy(final.at[which, piece(j)], (gtok if which else out).at[piece(j)], local.at[number])

    def grads(which, third):
        def body(k, carry):
            at = pl.ds(pl.multiple_of(k * G, G), G)
            if which:
                both = jnp.dot(act_t[...], held[1, k], preferred_element_type=F32)
                grad_own[1, k] = both[:G]
                grad_peer[1, k] = both[G:]
            else:
                both = jnp.dot(held_t[at, :], gpre[...], preferred_element_type=F32)
                grad_own[0, k] = both[:, :G]
                grad_peer[0, k] = both[:, G:]
            return carry

        lax.fori_loop(third * THIRDS, (third + 1) * THIRDS, body, 0)
        send(("grad", which, third))

    def write_grad(which, k):
        return pltpu.make_async_copy(grad_own.at[which, k], (gdown if which else gup).at[LEVEL[k]], local.at[4 + which * LEVELS + k])

    def grads_sum(which, third):
        need(("grad", which, third))

        for k in range(third * THIRDS, (third + 1) * THIRDS):
            total = grad_own[which, k] + grad_recv[which, k]
            grad_own[which, k] = total * mask[0, LEVEL[k]].astype(F32)
            write_grad(which, k).start()

    def finish_sends(*numbers):
        for name in (tuple(SIZES)[n] for n in numbers):
            sent.add(name)
            if name[0] in ("weight", "grad"):
                transfer(name).wait_send()
            else:
                together(SIZES[name], FAMILIES[name], 0).wait_send()

    steps = (
        own_xy, own_z, relay_z, other, relay_xy, hop, land, mask_up, mask_down, turn_weights, turn_held, turn_act,
        forward_near, forward, backward_near, backward, far_terms, near_terms, send_term, hand_on, join, collect,
        plain, pass_on, finish, grads, grads_sum, finish_sends,
    )
    for step in ORDER:
        steps[step[0]](*step[1:])

    assert started == set(NUMBER) and landed == set(ARRIVALS)
    for which in range(2):
        for k in range(LEVELS):
            write_grad(which, k).wait()
        for j in range(PIECES):
            write_final(which, j).wait()
    assert sent == set(FAMILIES)


def hand_out(*refs):
    sources, results, sems = refs[:4], refs[4:8], refs[8]
    copies = []
    for src, dst in zip(sources, results):
        if len(src.shape) == 2:
            pairs = [(src, dst)]
        else:
            pairs = [(src.at[pl.ds(k, 2)], dst.at[pl.ds(k, 2)]) for k in range(0, LEVELS, 2)]
        for a, b in pairs:
            copies.append(pltpu.make_async_copy(a, b, sems.at[len(copies)]))
    for copy in copies:
        copy.start()
    for copy in copies:
        copy.wait()


def shards(tokens, up_weight, down_weight, block_mask, cotangent):
    anywhere = pl.BlockSpec(memory_space=pl.ANY)
    both = 2 * ROWS
    result = (
        jax.ShapeDtypeStruct((ROWS, G), BF16),
        jax.ShapeDtypeStruct((ROWS, G), BF16),
        jax.ShapeDtypeStruct((LEVELS, G, G), F32),
        jax.ShapeDtypeStruct((LEVELS, G, G), F32),
    )
    operands = [pltpu.with_memory_space_constraint(a, pltpu.HBM) for a in (tokens, cotangent, up_weight[0], down_weight[0], block_mask)]
    worked = pl.pallas_call(
        kernel,
        out_shape=tuple(pltpu.VMEM(a.shape, a.dtype) for a in result),
        in_specs=[anywhere] * 5,
        out_specs=[anywhere] * 4,
        scratch_shapes=[
            pltpu.SMEM((1, LEVELS), jnp.int32),
            pltpu.VMEM((2, LEVELS, both, G), BF16),
            pltpu.VMEM((WIDE, both), BF16),
            pltpu.VMEM((2, LEVELS, G, G), BF16),
            pltpu.VMEM((WIDE, 2 * G), BF16),
            pltpu.VMEM((2 * G, WIDE), BF16),
            pltpu.VMEM((2 * G, WIDE), BF16),
            pltpu.VMEM((WIDE, 2 * G), BF16),
            pltpu.VMEM((both, 2 * G), BF16),
            pltpu.VMEM((2 * G, both), BF16),
            pltpu.VMEM((both, 2 * G), BF16),
            pltpu.VMEM((both, 2 * G), F32),
            pltpu.VMEM((both, 2 * G), F32),
            pltpu.VMEM((2, 2, both, G), BF16),
            pltpu.VMEM((2, 2, both, G), BF16),
            pltpu.VMEM((2, 2, both, G), F32),
            pltpu.VMEM((2, 2, both, G), BF16),
            pltpu.VMEM((2, 2, both, G), BF16),
            pltpu.VMEM((2, both, G), F32),
            pltpu.VMEM((2, both, G), F32),
            pltpu.VMEM((2, ROWS, G), BF16),
            pltpu.VMEM((2, ROWS, G), BF16),
            pltpu.VMEM((2, ROWS, G), BF16),
            pltpu.VMEM((2, 2, len(MOVED) * PART, G), BF16),
            pltpu.VMEM((2, both, G), BF16),
            pltpu.VMEM((2, both, G), BF16),
            pltpu.VMEM((2, ROWS, G), BF16),
            pltpu.VMEM((2, LEVELS, G, G), F32),
            pltpu.VMEM((2, LEVELS, G, G), F32),
            pltpu.VMEM((2, LEVELS, G, G), F32),
            pltpu.SemaphoreType.DMA((len(FAMILIES),)),
            pltpu.SemaphoreType.DMA((len(LANDINGS),)),
            pltpu.SemaphoreType.DMA((5 + 2 * LEVELS + 2 * PIECES,)),
        ],
        compiler_params=pltpu.CompilerParams(
            collective_id=0, has_side_effects=True, vmem_limit_bytes=58 * 1024 * 1024
        ),
    )(*operands)
    worked = [pltpu.with_memory_space_constraint(a, pltpu.VMEM) for a in worked]
    output, grad_tokens, grad_up, grad_down = pl.pallas_call(
        hand_out,
        out_shape=result,
        in_specs=[anywhere] * 4,
        out_specs=(anywhere,) * 4,
        scratch_shapes=[pltpu.SemaphoreType.DMA((8,))],
        compiler_params=pltpu.CompilerParams(vmem_limit_bytes=1024 * 1024),
    )(*worked)
    return output, grad_tokens, grad_up[None], grad_down[None]


def solution(mesh):
    placed = (
        P("seq", "tp"),
        P(("seq", "tp"), None, None, None),
        P(("seq", "tp"), None, None, None),
        P(("seq", "tp"), None),
        P("seq", "tp"),
    )
    return jax.shard_map(
        shards,
        mesh=mesh,
        in_specs=placed,
        out_specs=(
            P("seq", "tp"),
            P("seq", "tp"),
            P(("seq", "tp"), None, None, None),
            P(("seq", "tp"), None, None, None),
        ),
        check_vma=False,
    )
```

```python
import collections
import math

import jax
import jax.numpy as jnp
from jax import lax
from jax.experimental import pallas as pl
from jax.experimental.pallas import tpu as pltpu
from jax.sharding import PartitionSpec as P

MESH = pl.DeviceIdType.MESH
F32 = jnp.float32
BF16 = jnp.bfloat16
ROWS = 512
PART = 128
PIECES = ROWS // PART
FIRST = PIECES // 2
TILE = 256
PER_TILE = TILE // PART
THIRDS = 3
G = 256
LEVELS = 6
WIDE = LEVELS * G
LEVEL = (0, 1, 2, 4, 3, 5)
NEAR = {"x": 3, "y": 2}
FAR = {"x": 5, "y": 4}
SCALE = math.sqrt(2.0 / math.pi)
CUBE = 0.044715


def numbering():
    keys = []
    for which in range(2):
        keys += [(name, which, j) for name in ("z1", "z3", "zr", "out1", "out3", "half") for j in range(PIECES)]
        keys += [
            (name, axis, which, slot, j)
            for name in ("near", "far", "term", "sum")
            for axis in "xy"
            for slot in range(2)
            for j in range(PIECES)
        ]
        keys += [("weight", which)] + [("grad", which, k) for k in range(LEVELS // THIRDS)]
    keys += [("last", axis, j) for axis in "xy" for j in PASSED]
    moved = [(axis, level, which, j) for axis in "xy" for level in "nf" for which, j in MOVED]
    keys += [("hop", *rest) for rest in moved] + [("land", *rest) for rest in moved]
    keys = [k for k in keys if not (k[0] in ("near", "far") and k[3] == 1 and (k[2], k[4]) in MOVED)]
    return {key: n for n, key in enumerate(keys)}


def passed(which, slot, j):
    return which == 0 and slot == 0 and j in PASSED


def family(key):
    name = key[0]
    if name in ("weight", "grad"):
        return key
    if name in ("near", "far", "term", "sum"):
        return name, key[2], key[3]
    if name in ("last", "hop", "land"):
        return (name,)
    return {"z1": "z", "z3": "z", "zr": "middle", "half": "middle", "out1": "out", "out3": "out"}[name], key[1]


def arrival(key):
    name = key[0]
    if name in ("near", "far", "term", "sum"):
        return name, *key[2:]
    if name in ("out1", "out3"):
        return "out", *key[1:]
    if name in ("last", "land"):
        return name, *key[2:]
    return key


PASSED = (2, 3)
MOVED = ((1, 0), (1, 2))
NUMBER = numbering()
ARRIVALS = collections.Counter(arrival(key) for key in NUMBER)
LANDINGS = {name: n for n, name in enumerate(ARRIVALS)}
SIZES = collections.Counter(family(key) for key in NUMBER)
FAMILIES = {name: n for n, name in enumerate(SIZES)}

S_OX, S_OZ, S_RZ, S_OT, S_RX, S_H1, S_H2, S_SU, S_SD, S_TW, S_TH, S_TA, S_FN, S_F, \
    S_BN, S_B, S_TF, S_TN, S_S, S_RL, S_J, S_C, S_Z, S_PO, S_FIN, S_G, S_GS, S_W = range(28)
X, Y, NR, FR = "x", "y", "n", "f"
ORDER = (
    (S_OZ, 0, 3), (S_OX, 0, 3), (S_OX, 1, 0), (S_OZ, 0, 2), (S_OZ, 0, 1), (S_SU,), (S_OZ, 1, 1), (S_OX, 1, 2),
    (S_OX, 0, 2), (S_SD,), (S_OX, 0, 1), (S_RX, 0, 0, 3), (S_OX, 0, 0), (S_OZ, 0, 0), (S_RX, 1, 0, 0), (S_OX, 1, 3),
    (S_RZ, 0, 3), (S_RZ, 0, 2), (S_RX, 1, 0, 2), (S_RZ, 0, 1), (S_OZ, 1, 3), (S_OX, 1, 1), (S_H1, X, NR, 1, 2),
    (S_RX, 0, 0, 2), (S_FN, 0, 1), (S_RZ, 0, 0), (S_RZ, 1, 1), (S_RX, 0, 0, 1), (S_OZ, 1, 2), (S_H1, Y, FR, 1, 0),
    (S_TW,), (S_OT, 0, 3), (S_H1, Y, FR, 1, 2), (S_H1, X, FR, 1, 2), (S_RX, 0, 0, 0), (S_F, 0, 1), (S_RZ, 1, 3),
    (S_OT, 0, 2), (S_RX, 1, 0, 3), (S_H1, X, NR, 1, 0), (S_OT, 0, 1), (S_H1, X, FR, 1, 0), (S_FN, 0, 0),
    (S_RX, 1, 0, 1), (S_H1, Y, NR, 1, 2), (S_H1, Y, NR, 1, 0), (S_OT, 0, 0), (S_TF, 0, 0, 1), (S_OZ, 1, 0),
    (S_RX, 0, 1, 3), (S_TN, 0, 0, 1), (S_F, 0, 0), (S_TF, 0, 0, 0), (S_RX, 0, 1, 2), (S_RZ, 1, 2), (S_OT, 1, 1),
    (S_BN, 0, 1), (S_H2, X, NR, 1, 2), (S_B, 0, 1), (S_TF, 1, 0, 1), (S_RX, 0, 1, 1), (S_TN, 0, 0, 0), (S_OT, 1, 3),
    (S_S, 0, 0, 2), (S_TN, 1, 0, 1), (S_S, 1, 0, 2), (S_H2, Y, FR, 1, 2), (S_FN, 1, 1), (S_TA, 0, 1), (S_J, 0, 0, 2),
    (S_RX, 0, 1, 0), (S_F, 1, 1), (S_TF, 0, 1, 1), (S_S, 0, 1, 2), (S_H2, Y, FR, 1, 0), (S_S, 0, 0, 3),
    (S_RX, 1, 1, 1), (S_H2, X, NR, 1, 0), (S_J, 0, 0, 3), (S_FN, 1, 0), (S_TN, 0, 1, 1), (S_S, 0, 1, 3),
    (S_RZ, 1, 0), (S_BN, 0, 0), (S_TA, 0, 0), (S_W, 11), (S_H2, X, FR, 1, 0), (S_H2, X, FR, 1, 2), (S_B, 0, 0),
    (S_H2, Y, NR, 1, 0), (S_W, 25), (S_TF, 1, 0, 0), (S_RX, 1, 1, 3), (S_F, 1, 0), (S_W, 3), (S_J, 1, 0, 2),
    (S_W, 0), (S_H2, Y, NR, 1, 2), (S_Z, 0, 0, 2), (S_TF, 0, 1, 0), (S_TA, 1, 0), (S_OT, 1, 2), (S_S, 0, 1, 0),
    (S_Z, 0, 0, 3), (S_J, 0, 1, 2), (S_W, 17), (S_Z, 1, 0, 3), (S_TA, 1, 1), (S_OT, 1, 0), (S_TN, 0, 1, 0),
    (S_TH, 0), (S_Z, 0, 1, 0), (S_BN, 1, 0), (S_Z, 1, 0, 2), (S_B, 1, 0), (S_TF, 1, 1, 0), (S_S, 1, 1, 1),
    (S_TN, 1, 1, 0), (S_J, 0, 1, 3), (S_W, 5), (S_S, 1, 1, 0), (S_BN, 1, 1), (S_B, 1, 1), (S_TF, 1, 1, 1),
    (S_J, 0, 1, 0), (S_S, 1, 1, 3), (S_Z, 1, 1, 1), (S_S, 0, 1, 1), (S_S, 1, 1, 2), (S_W, 19), (S_S, 0, 0, 1),
    (S_Z, 1, 1, 0), (S_W, 29), (S_TN, 1, 1, 1), (S_W, 4), (S_S, 1, 0, 3), (S_J, 1, 1, 1), (S_W, 14), (S_G, 1, 1),
    (S_J, 1, 1, 0), (S_C, 0, 1, 0), (S_S, 0, 0, 0), (S_J, 1, 1, 3), (S_Z, 0, 1, 1), (S_G, 1, 0), (S_C, 0, 1, 2),
    (S_C, 1, 1, 1), (S_J, 0, 1, 1), (S_C, 0, 1, 3), (S_J, 1, 1, 2), (S_TH, 1), (S_S, 1, 0, 0), (S_S, 1, 0, 1),
    (S_C, 1, 1, 0), (S_C, 1, 1, 3), (S_G, 0, 1), (S_PO, 0, 2), (S_J, 0, 0, 1), (S_PO, 0, 0), (S_TN, 1, 0, 0),
    (S_W, 6), (S_J, 1, 0, 3), (S_C, 0, 1, 1), (S_RL, 2), (S_C, 1, 1, 2), (S_J, 0, 0, 0), (S_PO, 1, 1), (S_PO, 0, 3),
    (S_G, 0, 0), (S_PO, 1, 3), (S_J, 1, 0, 1), (S_PO, 1, 0), (S_C, 1, 0, 2), (S_RL, 3), (S_PO, 0, 1), (S_J, 1, 0, 0),
    (S_PO, 1, 2), (S_GS, 1, 0), (S_GS, 0, 1), (S_C, 0, 0, 2), (S_GS, 1, 1), (S_W, 20), (S_C, 0, 0, 1),
    (S_C, 0, 0, 0), (S_C, 1, 0, 3), (S_W, 30), (S_FIN, 0, 2), (S_FIN, 0, 0), (S_C, 0, 0, 3), (S_FIN, 1, 3),
    (S_C, 1, 0, 1), (S_FIN, 1, 1), (S_FIN, 0, 3), (S_GS, 0, 0), (S_FIN, 1, 2), (S_C, 1, 0, 0), (S_W, 18),
    (S_FIN, 1, 0), (S_FIN, 0, 1), (S_W, 1, 15, 7, 21, 9, 8, 23, 2, 10, 16, 22, 24, 27, 26, 13, 28, 12),
)


def flip(index, bit):
    return index + bit - 2 * bit * lax.rem(lax.div(index, bit), 2)


def kernel(
    tok, cot, up, down, present, out, gtok, gup, gdown,
    mask, held, held_t, raw, uall, dall, uall_t, dall_t, act, act_t, gpre, slope, gact,
    term_send, term_recv, near_term, sum_send, sum_recv, base, z_term,
    half_send, half_recv, last_recv, hops, z_send, z_recv,
    grad_own, grad_peer, grad_recv,
    sends, recvs, local,
):
    shared = (tok, cot)
    seq, tp = lax.axis_index("seq"), lax.axis_index("tp")
    core = lax.rem(seq, 2)
    place = {
        "core": (flip(seq, 1), tp),
        "z1": (seq, flip(tp, 1)),
        "z3": (flip(seq, 2), flip(tp, 1)),
        "x1": (seq, flip(tp, 8)),
        "x3": (seq, flip(flip(tp, 8), 16)),
        "y1": (seq, flip(tp, 2)),
        "y3": (seq, flip(flip(tp, 2), 4)),
    }

    def remote(src, dst, key, target):
        return pltpu.make_async_remote_copy(
            src_ref=src,
            dst_ref=dst,
            send_sem=sends.at[FAMILIES[family(key)]],
            recv_sem=recvs.at[LANDINGS[arrival(key)]],
            device_id=place[target],
            device_id_type=MESH,
        )

    def rows(slot, j):
        start = slot * ROWS + j * PART
        return pl.ds(start if isinstance(j, int) else pl.multiple_of(start, PART), PART)

    def piece(j):
        return pl.ds(j * PART, PART)

    def columns(level):
        return pl.ds(level * G, G)

    def transfer(key):
        name, rest = key[0], key[1:]
        if name == "weight":
            if rest[0] == 0:
                return remote(uall.at[:, pl.ds(0, G)], uall.at[:, pl.ds(G, G)], key, "core")
            return remote(dall.at[pl.ds(0, G)], dall.at[pl.ds(G, G)], key, "core")
        if name == "grad":
            at = pl.ds(rest[1] * THIRDS, THIRDS)
            return remote(grad_peer.at[rest[0], at], grad_recv.at[rest[0], at], key, "core")
        if name == "last":
            a, j = "xy".index(rest[0]), rest[1]
            return remote(term_recv.at[0, a, rows(0, j)], last_recv.at[a, piece(j)], key, rest[0] + "3")
        if name in ("hop", "land"):
            axis, level, which, j = rest
            n, group = "nf".index(level), (NEAR if level == "n" else FAR)[axis]
            room = hops.at[n, "xy".index(axis), pl.ds(MOVED.index((which, j)) * PART, PART)]
            if name == "hop":
                return remote(held.at[which, group, rows(0, j)], room, key, ("z1", "z3")[n])
            return remote(room, held.at[which, group, rows(1, j)], key, ("z3", "z1")[n])
        if name in ("near", "far", "term", "sum"):
            axis, which, slot, j = rest
            a, at = "xy".index(axis), rows(slot, j)
            if name == "near":
                src = held.at[which, 0, at] if slot else shared[which].at[piece(j)]
                return remote(src, held.at[which, NEAR[axis], at], key, axis + "1")
            if name == "far":
                return remote(held.at[which, NEAR[axis], at], held.at[which, FAR[axis], at], key, axis + "3")
            if name == "term":
                target = axis + ("1" if passed(which, slot, j) else "3")
                return remote(term_send.at[which, a, at], term_recv.at[which, a, at], key, target)
            return remote(sum_send.at[which, a, at], sum_recv.at[which, a, at], key, axis + "1")
        which, j = rest
        if name == "z1":
            return remote(shared[which].at[piece(j)], held.at[which, 1, rows(0, j)], key, "z1")
        if name == "z3":
            return remote(shared[which].at[piece(j)], held.at[which, 1, rows(1, j)], key, "z3")
        onward = "z3" if j < FIRST else "z1"
        if name == "zr":
            return remote(held.at[which, 1, rows(int(j >= FIRST), j)], held.at[which, 0, rows(1, j)], key, onward)
        if name == "half":
            return remote(half_send.at[which, piece(j)], half_recv.at[which, piece(j)], key, onward)
        slot = int(name == "out3")
        return remote(z_send.at[which, rows(slot, j)], z_recv.at[which, rows(slot, j)], key, "z3" if slot else "z1")

    def together(pieces, sent_by, landed_by):
        span = held.at[0, 0, pl.ds(0, pieces * PART)]
        return pltpu.make_async_remote_copy(
            src_ref=span,
            dst_ref=span,
            send_sem=sends.at[sent_by],
            recv_sem=recvs.at[landed_by],
            device_id=place["z1"],
            device_id_type=MESH,
        )

    started, landed, copied, sent = set(), set(), set(), set()

    def send(*keys):
        for key in keys:
            started.add(key)
            transfer(key).start()

    def need(*keys):
        for key in keys:
            name = arrival(key)
            if name in landed:
                continue
            landed.add(name)
            if name[0] in ("weight", "grad"):
                transfer(key).wait_recv()
            else:
                together(ARRIVALS[name], 0, LANDINGS[name]).wait_recv()

    own = [
        pltpu.make_async_copy(shared[which], held.at[which, 0, pl.ds(0, ROWS)], local.at[which])
        for which in range(2)
    ]
    loads = [pltpu.make_async_copy(ref, raw.at[which], local.at[2 + which]) for which, ref in enumerate((up, down))]
    mask_load = pltpu.make_async_copy(present, mask, local.at[4 + 2 * LEVELS])
    barrier = pltpu.get_barrier_semaphore()
    for target in place.values():
        pl.semaphore_signal(barrier, inc=1, device_id=target, device_id_type=MESH)
    mask_load.start()
    for copy in loads + own:
        copy.start()
    pl.semaphore_wait(barrier, len(place))

    def tile(slot, t):
        return pl.ds(slot * ROWS + t * TILE, TILE)

    def own_z(which, j):
        send(("z1", which, j), ("z3", which, j))

    def own_xy(which, j):
        send(("near", "x", which, 0, j), ("near", "y", which, 0, j))

    def relay_z(which, j):
        need(("z1" if j < FIRST else "z3", which, j))
        send(("zr", which, j))

    def other(which, j):
        need(("zr", which, j))
        if (which, j) not in MOVED:
            send(("near", "x", which, 1, j), ("near", "y", which, 1, j))

    def relay_xy(which, slot, j):
        for axis in "xy":
            need(("near", axis, which, slot, j))
            send(("far", axis, which, slot, j))

    def hop(axis, level, which, j):
        need(("near" if level == "n" else "far", axis, which, 0, j))
        send(("hop", axis, level, which, j))

    def land(axis, level, which, j):
        need(("hop", axis, level, which, j))
        send(("land", axis, level, which, j))

    def mask_up(late=True):
        @pl.when(core == (0 if late else 1))
        def _():
            mask_load.wait()
            loads[0].wait()
            for k, level in enumerate(LEVEL):
                uall[pl.ds(k * G, G), pl.ds(0, G)] = (raw[0, level].astype(F32) * mask[0, level].astype(F32)).astype(BF16)
            send(("weight", 0))

    def mask_down(late=True):
        @pl.when(core == (0 if late else 1))
        def _():
            loads[1].wait()
            for k, level in enumerate(LEVEL):
                dall[pl.ds(0, G), pl.ds(k * G, G)] = (raw[1, level].astype(F32) * mask[0, level].astype(F32)).astype(BF16)
            send(("weight", 1))

    def turn_weights():
        need(("weight", 0), ("weight", 1))

        def body(k, carry):
            at = pl.ds(pl.multiple_of(k * G, G), G)
            dall_t[at, :] = dall[:, at].T
            uall_t[:, at] = uall[at, :].T
            return carry

        lax.fori_loop(0, LEVELS, body, 0)

    def turn_held(slot):
        def body(k, carry):
            at = pl.ds(pl.multiple_of(k * G, G), G)
            held_t[at, pl.ds(slot * ROWS, ROWS)] = held[0, k, pl.ds(slot * ROWS, ROWS)].T
            return carry

        lax.fori_loop(0, LEVELS, body, 0)

    def turn_act(slot, t):
        act_t[:, tile(slot, t)] = act[tile(slot, t), :].T

    def near_inputs(which, slot, t):
        if slot == 0 and ("own", which) not in copied:
            copied.add(("own", which))
            own[which].wait()
        for j in range(t * PER_TILE, (t + 1) * PER_TILE):
            need(("z3" if slot else "z1", which, j))
            if slot and (which, j) in MOVED:
                need(("land", "x", "n", which, j), ("land", "y", "n", which, j))

    def far_inputs(which, slot, t):
        for j in range(t * PER_TILE, (t + 1) * PER_TILE):
            for axis in "xy":
                need(("land", axis, "f", which, j) if slot and (which, j) in MOVED else ("far", axis, which, slot, j))

    def partial(which, at, weights):
        early = jnp.concatenate([held[which, k, at] for k in range(4)], axis=1)
        return jnp.dot(early, weights[pl.ds(0, 4 * G), :], preferred_element_type=F32)

    def rest(which, at, weights):
        late = jnp.concatenate([held[which, k, at] for k in (4, 5)], axis=1)
        return jnp.dot(late, weights[pl.ds(4 * G, 2 * G), :], preferred_element_type=F32)

    def forward_near(slot, t):
        near_inputs(0, slot, t)
        need(("weight", 0))
        slope[tile(slot, t), :] = partial(0, tile(slot, t), uall)

    def backward_near(slot, t):
        near_inputs(1, slot, t)
        gact[tile(slot, t), :] = partial(1, tile(slot, t), dall_t)

    def forward(slot, t):
        far_inputs(0, slot, t)
        at = tile(slot, t)
        pre = slope[at, :] + rest(0, at, uall)
        square = pre * pre
        tanh = jnp.tanh(SCALE * pre * (1.0 + CUBE * square))
        cdf = 0.5 + 0.5 * tanh
        act[at, :] = (pre * cdf).astype(BF16)
        slope[at, :] = cdf + (0.5 * SCALE) * pre * (1.0 - tanh * tanh) * (1.0 + (3.0 * CUBE) * square)

    def backward(slot, t):
        far_inputs(1, slot, t)
        at = tile(slot, t)
        gpre[at, :] = ((gact[at, :] + rest(1, at, dall_t)) * slope[at, :]).astype(BF16)

    def product(which, slot, t, level):
        if which:
            return jnp.dot(gpre[tile(slot, t), :], uall_t[:, columns(level)], preferred_element_type=F32)
        return jnp.dot(act[tile(slot, t), :], dall[:, columns(level)], preferred_element_type=F32)

    def far_terms(which, slot, t):
        need(("weight", 1))
        for a, axis in enumerate("xy"):
            term_send[which, a, tile(slot, t)] = product(which, slot, t, FAR[axis]).astype(BF16)

    def near_terms(which, slot, t):
        at = tile(slot, t)
        for a, axis in enumerate("xy"):
            near_term[which, a, at] = product(which, slot, t, NEAR[axis])
        z_term[which, at] = product(which, slot, t, 1)
        base[which, at] = product(which, slot, t, 0)

    def send_term(which, slot, j):
        send(("term", "x", which, slot, j), ("term", "y", which, slot, j))

    def hand_on(j):
        for axis in "xy":
            need(("term", axis, 0, 0, j))
            send(("last", axis, j))

    def join(which, slot, j):
        at = rows(slot, j)
        for a, axis in enumerate("xy"):
            total = near_term[which, a, at]
            if not passed(which, slot, j):
                need(("term", axis, which, slot, j))
                total = total + term_recv[which, a, at].astype(F32)
            sum_send[which, a, at] = total.astype(BF16)
            send(("sum", axis, which, slot, j))

    def collect(which, slot, j):
        at = rows(slot, j)
        need(("sum", "x", which, slot, j), ("sum", "y", which, slot, j))
        total = base[which, at] + sum_recv[which, 0, at].astype(F32) + sum_recv[which, 1, at].astype(F32)
        if slot == 0:
            base[which, at] = total
        else:
            half_send[which, piece(j)] = total.astype(BF16)
            send(("half", which, j))

    def plain(which, slot, j):
        z_send[which, rows(slot, j)] = z_term[which, rows(slot, j)].astype(BF16)
        send(("out3" if slot else "out1", which, j))

    def pass_on(which, j):
        slot = int(j >= FIRST)
        at = rows(slot, j)
        need(("half", which, j))
        z_send[which, at] = (z_term[which, at] + half_recv[which, piece(j)].astype(F32)).astype(BF16)
        send(("out3" if slot else "out1", which, j))

    def finish(which, j):
        need(("out1", which, j), ("out3", which, j))
        total = base[which, rows(0, j)] + z_recv[which, rows(0, j)].astype(F32) + z_recv[which, rows(1, j)].astype(F32)
        if passed(which, 0, j):
            need(("last", "x", j), ("last", "y", j))
            total = total + last_recv[0, piece(j)].astype(F32) + last_recv[1, piece(j)].astype(F32)
        (gtok if which else out)[piece(j), :] = total.astype(BF16)

    def grads(which, third):
        def body(k, carry):
            at = pl.ds(pl.multiple_of(k * G, G), G)
            if which:
                both = jnp.dot(act_t[...], held[1, k], preferred_element_type=F32)
                grad_own[1, k] = both[:G]
                grad_peer[1, k] = both[G:]
            else:
                both = jnp.dot(held_t[at, :], gpre[...], preferred_element_type=F32)
                grad_own[0, k] = both[:, :G]
                grad_peer[0, k] = both[:, G:]
            return carry

        lax.fori_loop(third * THIRDS, (third + 1) * THIRDS, body, 0)
        send(("grad", which, third))

    def write_grad(which, k):
        return pltpu.make_async_copy(grad_own.at[which, k], (gdown if which else gup).at[LEVEL[k]], local.at[4 + which * LEVELS + k])

    def grads_sum(which, third):
        need(("grad", which, third))

        for k in range(third * THIRDS, (third + 1) * THIRDS):
            total = grad_own[which, k] + grad_recv[which, k]
            grad_own[which, k] = total * mask[0, LEVEL[k]].astype(F32)
            write_grad(which, k).start()

    def finish_sends(*numbers):
        for name in (tuple(SIZES)[n] for n in numbers):
            sent.add(name)
            if name[0] in ("weight", "grad"):
                transfer(name).wait_send()
            else:
                together(SIZES[name], FAMILIES[name], 0).wait_send()

    steps = (
        own_xy, own_z, relay_z, other, relay_xy, hop, land, mask_up, mask_down, turn_weights, turn_held, turn_act,
        forward_near, forward, backward_near, backward, far_terms, near_terms, send_term, hand_on, join, collect,
        plain, pass_on, finish, grads, grads_sum, finish_sends,
    )
    mask_up(late=False)
    mask_down(late=False)
    for step in ORDER:
        steps[step[0]](*step[1:])

    assert started == set(NUMBER) and landed == set(ARRIVALS)
    for which in range(2):
        for k in range(LEVELS):
            write_grad(which, k).wait()
    assert sent == set(FAMILIES)


def hand_out(*refs):
    sources, results, sems = refs[:4], refs[4:8], refs[8]
    copies = []
    for src, dst in zip(sources, results):
        if len(src.shape) == 2:
            pairs = [(src, dst)]
        else:
            pairs = [(src.at[pl.ds(k, 2)], dst.at[pl.ds(k, 2)]) for k in range(0, LEVELS, 2)]
        for a, b in pairs:
            copies.append(pltpu.make_async_copy(a, b, sems.at[len(copies)]))
    for copy in copies:
        copy.start()
    for copy in copies:
        copy.wait()


def shards(tokens, up_weight, down_weight, block_mask, cotangent):
    anywhere = pl.BlockSpec(memory_space=pl.ANY)
    vmem = pl.BlockSpec(memory_space=pltpu.VMEM)
    both = 2 * ROWS
    result = (
        jax.ShapeDtypeStruct((ROWS, G), BF16),
        jax.ShapeDtypeStruct((ROWS, G), BF16),
        jax.ShapeDtypeStruct((LEVELS, G, G), F32),
        jax.ShapeDtypeStruct((LEVELS, G, G), F32),
    )
    operands = [pltpu.with_memory_space_constraint(a, pltpu.HBM) for a in (tokens, cotangent, up_weight[0], down_weight[0], block_mask)]
    worked = pl.pallas_call(
        kernel,
        out_shape=tuple(pltpu.VMEM(a.shape, a.dtype) for a in result),
        in_specs=[anywhere] * 5,
        out_specs=(vmem, vmem, anywhere, anywhere),
        scratch_shapes=[
            pltpu.SMEM((1, LEVELS), jnp.int32),
            pltpu.VMEM((2, LEVELS, both, G), BF16),
            pltpu.VMEM((WIDE, both), BF16),
            pltpu.VMEM((2, LEVELS, G, G), BF16),
            pltpu.VMEM((WIDE, 2 * G), BF16),
            pltpu.VMEM((2 * G, WIDE), BF16),
            pltpu.VMEM((2 * G, WIDE), BF16),
            pltpu.VMEM((WIDE, 2 * G), BF16),
            pltpu.VMEM((both, 2 * G), BF16),
            pltpu.VMEM((2 * G, both), BF16),
            pltpu.VMEM((both, 2 * G), BF16),
            pltpu.VMEM((both, 2 * G), F32),
            pltpu.VMEM((both, 2 * G), F32),
            pltpu.VMEM((2, 2, both, G), BF16),
            pltpu.VMEM((2, 2, both, G), BF16),
            pltpu.VMEM((2, 2, both, G), F32),
            pltpu.VMEM((2, 2, both, G), BF16),
            pltpu.VMEM((2, 2, both, G), BF16),
            pltpu.VMEM((2, both, G), F32),
            pltpu.VMEM((2, both, G), F32),
            pltpu.VMEM((2, ROWS, G), BF16),
            pltpu.VMEM((2, ROWS, G), BF16),
            pltpu.VMEM((2, ROWS, G), BF16),
            pltpu.VMEM((2, 2, len(MOVED) * PART, G), BF16),
            pltpu.VMEM((2, both, G), BF16),
            pltpu.VMEM((2, both, G), BF16),
            pltpu.VMEM((2, LEVELS, G, G), F32),
            pltpu.VMEM((2, LEVELS, G, G), F32),
            pltpu.VMEM((2, LEVELS, G, G), F32),
            pltpu.SemaphoreType.DMA((len(FAMILIES),)),
            pltpu.SemaphoreType.DMA((len(LANDINGS),)),
            pltpu.SemaphoreType.DMA((5 + 2 * LEVELS,)),
        ],
        compiler_params=pltpu.CompilerParams(
            collective_id=0, has_side_effects=True, vmem_limit_bytes=58 * 1024 * 1024
        ),
    )(*operands)
    worked = [pltpu.with_memory_space_constraint(a, pltpu.VMEM) for a in worked]
    output, grad_tokens, grad_up, grad_down = pl.pallas_call(
        hand_out,
        out_shape=result,
        in_specs=[anywhere] * 4,
        out_specs=(anywhere,) * 4,
        scratch_shapes=[pltpu.SemaphoreType.DMA((8,))],
        compiler_params=pltpu.CompilerParams(vmem_limit_bytes=1024 * 1024),
    )(*worked)
    return output, grad_tokens, grad_up[None], grad_down[None]


def solution(mesh):
    placed = (
        P("seq", "tp"),
        P(("seq", "tp"), None, None, None),
        P(("seq", "tp"), None, None, None),
        P(("seq", "tp"), None),
        P("seq", "tp"),
    )
    return jax.shard_map(
        shards,
        mesh=mesh,
        in_specs=placed,
        out_specs=(
            P("seq", "tp"),
            P("seq", "tp"),
            P(("seq", "tp"), None, None, None),
            P(("seq", "tp"), None, None, None),
        ),
        check_vma=False,
    )
```

```python
import collections
import math

import jax
import jax.numpy as jnp
from jax import lax
from jax.experimental import pallas as pl
from jax.experimental.pallas import tpu as pltpu
from jax.sharding import PartitionSpec as P

MESH = pl.DeviceIdType.MESH
F32 = jnp.float32
BF16 = jnp.bfloat16
ROWS = 512
PART = 128
PIECES = ROWS // PART
FIRST = PIECES // 2
TILE = 256
PER_TILE = TILE // PART
THIRDS = 3
G = 256
LEVELS = 6
WIDE = LEVELS * G
LEVEL = (0, 1, 2, 4, 3, 5)
NEAR = {"x": 3, "y": 2}
FAR = {"x": 5, "y": 4}
SCALE = math.sqrt(2.0 / math.pi)
CUBE = 0.044715


def numbering():
    keys = []
    for which in range(2):
        keys += [(name, which, j) for name in ("z1", "z3", "zr", "out1", "out3", "half") for j in range(PIECES)]
        keys += [
            (name, axis, which, slot, j)
            for name in ("near", "far", "term", "sum")
            for axis in "xy"
            for slot in range(2)
            for j in range(PIECES)
        ]
        keys += [("weight", which)] + [("grad", which, k) for k in range(LEVELS // THIRDS)]
    keys += [("last", axis, j) for axis in "xy" for j in PASSED]
    moved = [(axis, level, which, j) for axis in "xy" for level in "nf" for which, j in MOVED]
    keys += [("hop", *rest) for rest in moved] + [("land", *rest) for rest in moved]
    keys = [k for k in keys if not (k[0] in ("near", "far") and k[3] == 1 and (k[2], k[4]) in MOVED)]
    return {key: n for n, key in enumerate(keys)}


def passed(which, slot, j):
    return which == 0 and slot == 0 and j in PASSED


def family(key):
    name = key[0]
    if name in ("weight", "grad"):
        return key
    if name in ("near", "far", "term", "sum"):
        return name, key[2], key[3]
    if name in ("last", "hop", "land"):
        return (name,)
    return {"z1": "z", "z3": "z", "zr": "middle", "half": "middle", "out1": "out", "out3": "out"}[name], key[1]


def arrival(key):
    name = key[0]
    if name in ("near", "far", "term", "sum"):
        return name, *key[2:]
    if name in ("out1", "out3"):
        return "out", *key[1:]
    if name in ("last", "land"):
        return name, *key[2:]
    return key


PASSED = (2, 3)
MOVED = ((1, 0), (1, 2))
NUMBER = numbering()
ARRIVALS = collections.Counter(arrival(key) for key in NUMBER)
LANDINGS = {name: n for n, name in enumerate(ARRIVALS)}
SIZES = collections.Counter(family(key) for key in NUMBER)
FAMILIES = {name: n for n, name in enumerate(SIZES)}

S_OX, S_OZ, S_RZ, S_OT, S_RX, S_H1, S_H2, S_SU, S_SD, S_TW, S_TH, S_TA, S_FN, S_F, \
    S_BN, S_B, S_TF, S_TN, S_S, S_RL, S_J, S_C, S_Z, S_PO, S_FIN, S_G, S_GS, S_W = range(28)
X, Y, NR, FR = "x", "y", "n", "f"
ORDER = (
    (S_OZ, 0, 3), (S_OX, 0, 3), (S_OX, 1, 0), (S_OZ, 0, 2), (S_OZ, 0, 1), (S_SU,), (S_OZ, 1, 1), (S_OX, 1, 2),
    (S_OX, 0, 2), (S_SD,), (S_OX, 0, 1), (S_RX, 0, 0, 3), (S_OX, 0, 0), (S_OZ, 0, 0), (S_RX, 1, 0, 0), (S_OX, 1, 3),
    (S_RZ, 0, 3), (S_RZ, 0, 2), (S_RX, 1, 0, 2), (S_RZ, 0, 1), (S_OZ, 1, 3), (S_OX, 1, 1), (S_H1, X, NR, 1, 2),
    (S_RX, 0, 0, 2), (S_FN, 0, 1), (S_RZ, 0, 0), (S_RZ, 1, 1), (S_RX, 0, 0, 1), (S_OZ, 1, 2), (S_H1, Y, FR, 1, 0),
    (S_TW,), (S_OT, 0, 3), (S_H1, Y, FR, 1, 2), (S_H1, X, FR, 1, 2), (S_RX, 0, 0, 0), (S_F, 0, 1), (S_RZ, 1, 3),
    (S_OT, 0, 2), (S_RX, 1, 0, 3), (S_H1, X, NR, 1, 0), (S_OT, 0, 1), (S_H1, X, FR, 1, 0), (S_FN, 0, 0),
    (S_RX, 1, 0, 1), (S_H1, Y, NR, 1, 2), (S_H1, Y, NR, 1, 0), (S_OT, 0, 0), (S_TF, 0, 0, 1), (S_OZ, 1, 0),
    (S_RX, 0, 1, 3), (S_TN, 0, 0, 1), (S_F, 0, 0), (S_TF, 0, 0, 0), (S_RX, 0, 1, 2), (S_RZ, 1, 2), (S_OT, 1, 1),
    (S_BN, 0, 1), (S_H2, X, NR, 1, 2), (S_B, 0, 1), (S_TF, 1, 0, 1), (S_RX, 0, 1, 1), (S_TN, 0, 0, 0), (S_OT, 1, 3),
    (S_S, 0, 0, 2), (S_TN, 1, 0, 1), (S_S, 1, 0, 2), (S_H2, Y, FR, 1, 2), (S_FN, 1, 1), (S_TA, 0, 1), (S_J, 0, 0, 2),
    (S_RX, 0, 1, 0), (S_F, 1, 1), (S_TF, 0, 1, 1), (S_S, 0, 1, 2), (S_H2, Y, FR, 1, 0), (S_S, 0, 0, 3),
    (S_RX, 1, 1, 1), (S_H2, X, NR, 1, 0), (S_J, 0, 0, 3), (S_FN, 1, 0), (S_TN, 0, 1, 1), (S_S, 0, 1, 3),
    (S_RZ, 1, 0), (S_BN, 0, 0), (S_TA, 0, 0), (S_W, 11), (S_H2, X, FR, 1, 0), (S_H2, X, FR, 1, 2), (S_B, 0, 0),
    (S_H2, Y, NR, 1, 0), (S_W, 25), (S_TF, 1, 0, 0), (S_RX, 1, 1, 3), (S_F, 1, 0), (S_W, 3), (S_J, 1, 0, 2),
    (S_W, 0), (S_H2, Y, NR, 1, 2), (S_Z, 0, 0, 2), (S_TF, 0, 1, 0), (S_TA, 1, 0), (S_OT, 1, 2), (S_S, 0, 1, 0),
    (S_Z, 0, 0, 3), (S_J, 0, 1, 2), (S_W, 17), (S_Z, 1, 0, 3), (S_TA, 1, 1), (S_OT, 1, 0), (S_TN, 0, 1, 0),
    (S_TH, 0), (S_Z, 0, 1, 0), (S_BN, 1, 0), (S_Z, 1, 0, 2), (S_B, 1, 0), (S_TF, 1, 1, 0), (S_S, 1, 1, 1),
    (S_TN, 1, 1, 0), (S_J, 0, 1, 3), (S_W, 5), (S_S, 1, 1, 0), (S_BN, 1, 1), (S_B, 1, 1), (S_TF, 1, 1, 1),
    (S_J, 0, 1, 0), (S_S, 1, 1, 3), (S_Z, 1, 1, 1), (S_S, 0, 1, 1), (S_S, 1, 1, 2), (S_W, 19), (S_S, 0, 0, 1),
    (S_Z, 1, 1, 0), (S_W, 29), (S_TN, 1, 1, 1), (S_W, 4), (S_S, 1, 0, 3), (S_J, 1, 1, 1), (S_W, 14), (S_G, 1, 1),
    (S_J, 1, 1, 0), (S_C, 0, 1, 0), (S_S, 0, 0, 0), (S_J, 1, 1, 3), (S_Z, 0, 1, 1), (S_G, 1, 0), (S_C, 0, 1, 2),
    (S_C, 1, 1, 1), (S_J, 0, 1, 1), (S_C, 0, 1, 3), (S_J, 1, 1, 2), (S_TH, 1), (S_S, 1, 0, 0), (S_S, 1, 0, 1),
    (S_C, 1, 1, 0), (S_C, 1, 1, 3), (S_G, 0, 1), (S_PO, 0, 2), (S_J, 0, 0, 1), (S_PO, 0, 0), (S_TN, 1, 0, 0),
    (S_W, 6), (S_J, 1, 0, 3), (S_C, 0, 1, 1), (S_RL, 2), (S_C, 1, 1, 2), (S_J, 0, 0, 0), (S_PO, 1, 1), (S_PO, 0, 3),
    (S_G, 0, 0), (S_PO, 1, 3), (S_J, 1, 0, 1), (S_PO, 1, 0), (S_C, 1, 0, 2), (S_RL, 3), (S_PO, 0, 1), (S_J, 1, 0, 0),
    (S_PO, 1, 2), (S_GS, 1, 0), (S_GS, 0, 1), (S_C, 0, 0, 2), (S_GS, 1, 1), (S_W, 20), (S_C, 0, 0, 1),
    (S_C, 0, 0, 0), (S_C, 1, 0, 3), (S_W, 30), (S_FIN, 0, 2), (S_FIN, 0, 0), (S_C, 0, 0, 3), (S_FIN, 1, 3),
    (S_C, 1, 0, 1), (S_FIN, 1, 1), (S_FIN, 0, 3), (S_GS, 0, 0), (S_FIN, 1, 2), (S_C, 1, 0, 0), (S_W, 18),
    (S_FIN, 1, 0), (S_FIN, 0, 1), (S_W, 1, 15, 7, 21, 9, 8, 23, 2, 10, 16, 22, 24, 27, 26, 13, 28, 12),
)


def flip(index, bit):
    return index + bit - 2 * bit * lax.rem(lax.div(index, bit), 2)


def dot_nt(a, b):
    return lax.dot_general(a, b, (((1,), (1,)), ((), ())), preferred_element_type=F32)


def kernel(
    tok, cot, up, down, present, out, gtok, gup, gdown,
    mask, held, held_t, raw, uall, dall, act, act_t, gpre, slope, gact,
    term_send, term_recv, near_term, sum_send, sum_recv, base, z_term,
    half_send, half_recv, last_recv, hops, z_send, z_recv,
    grad_own, grad_peer, grad_recv,
    sends, recvs, local,
):
    shared = (tok, cot)
    seq, tp = lax.axis_index("seq"), lax.axis_index("tp")
    place = {
        "core": (flip(seq, 1), tp),
        "z1": (seq, flip(tp, 1)),
        "z3": (flip(seq, 2), flip(tp, 1)),
        "x1": (seq, flip(tp, 8)),
        "x3": (seq, flip(flip(tp, 8), 16)),
        "y1": (seq, flip(tp, 2)),
        "y3": (seq, flip(flip(tp, 2), 4)),
    }

    def remote(src, dst, key, target):
        return pltpu.make_async_remote_copy(
            src_ref=src,
            dst_ref=dst,
            send_sem=sends.at[FAMILIES[family(key)]],
            recv_sem=recvs.at[LANDINGS[arrival(key)]],
            device_id=place[target],
            device_id_type=MESH,
        )

    def rows(slot, j):
        start = slot * ROWS + j * PART
        return pl.ds(start if isinstance(j, int) else pl.multiple_of(start, PART), PART)

    def piece(j):
        return pl.ds(j * PART, PART)

    def columns(level):
        return pl.ds(level * G, G)

    def transfer(key):
        name, rest = key[0], key[1:]
        if name == "weight":
            if rest[0] == 0:
                return remote(uall.at[:, pl.ds(0, G)], uall.at[:, pl.ds(G, G)], key, "core")
            return remote(dall.at[pl.ds(0, G)], dall.at[pl.ds(G, G)], key, "core")
        if name == "grad":
            at = pl.ds(rest[1] * THIRDS, THIRDS)
            return remote(grad_peer.at[rest[0], at], grad_recv.at[rest[0], at], key, "core")
        if name == "last":
            a, j = "xy".index(rest[0]), rest[1]
            return remote(term_recv.at[0, a, rows(0, j)], last_recv.at[a, piece(j)], key, rest[0] + "3")
        if name in ("hop", "land"):
            axis, level, which, j = rest
            n, group = "nf".index(level), (NEAR if level == "n" else FAR)[axis]
            room = hops.at[n, "xy".index(axis), pl.ds(MOVED.index((which, j)) * PART, PART)]
            if name == "hop":
                return remote(held.at[which, group, rows(0, j)], room, key, ("z1", "z3")[n])
            return remote(room, held.at[which, group, rows(1, j)], key, ("z3", "z1")[n])
        if name in ("near", "far", "term", "sum"):
            axis, which, slot, j = rest
            a, at = "xy".index(axis), rows(slot, j)
            if name == "near":
                src = held.at[which, 0, at] if slot else shared[which].at[piece(j)]
                return remote(src, held.at[which, NEAR[axis], at], key, axis + "1")
            if name == "far":
                return remote(held.at[which, NEAR[axis], at], held.at[which, FAR[axis], at], key, axis + "3")
            if name == "term":
                target = axis + ("1" if passed(which, slot, j) else "3")
                return remote(term_send.at[which, a, at], term_recv.at[which, a, at], key, target)
            return remote(sum_send.at[which, a, at], sum_recv.at[which, a, at], key, axis + "1")
        which, j = rest
        if name == "z1":
            return remote(shared[which].at[piece(j)], held.at[which, 1, rows(0, j)], key, "z1")
        if name == "z3":
            return remote(shared[which].at[piece(j)], held.at[which, 1, rows(1, j)], key, "z3")
        onward = "z3" if j < FIRST else "z1"
        if name == "zr":
            return remote(held.at[which, 1, rows(int(j >= FIRST), j)], held.at[which, 0, rows(1, j)], key, onward)
        if name == "half":
            return remote(half_send.at[which, piece(j)], half_recv.at[which, piece(j)], key, onward)
        slot = int(name == "out3")
        return remote(z_send.at[which, rows(slot, j)], z_recv.at[which, rows(slot, j)], key, "z3" if slot else "z1")

    def together(pieces, sent_by, landed_by):
        span = held.at[0, 0, pl.ds(0, pieces * PART)]
        return pltpu.make_async_remote_copy(
            src_ref=span,
            dst_ref=span,
            send_sem=sends.at[sent_by],
            recv_sem=recvs.at[landed_by],
            device_id=place["z1"],
            device_id_type=MESH,
        )

    started, landed, copied, sent = set(), set(), set(), set()

    def send(*keys):
        for key in keys:
            started.add(key)
            transfer(key).start()

    def need(*keys):
        for key in keys:
            name = arrival(key)
            if name in landed:
                continue
            landed.add(name)
            if name[0] in ("weight", "grad"):
                transfer(key).wait_recv()
            else:
                together(ARRIVALS[name], 0, LANDINGS[name]).wait_recv()

    own = [
        pltpu.make_async_copy(shared[which], held.at[which, 0, pl.ds(0, ROWS)], local.at[which])
        for which in range(2)
    ]
    loads = [pltpu.make_async_copy(ref, raw.at[which], local.at[2 + which]) for which, ref in enumerate((up, down))]
    mask_load = pltpu.make_async_copy(present, mask, local.at[4 + 2 * LEVELS])
    barrier = pltpu.get_barrier_semaphore()
    for target in place.values():
        pl.semaphore_signal(barrier, inc=1, device_id=target, device_id_type=MESH)
    mask_load.start()
    for copy in loads + own:
        copy.start()
    pl.semaphore_wait(barrier, len(place))

    def tile(slot, t):
        return pl.ds(slot * ROWS + t * TILE, TILE)

    def own_z(which, j):
        send(("z1", which, j), ("z3", which, j))

    def own_xy(which, j):
        send(("near", "x", which, 0, j), ("near", "y", which, 0, j))

    def relay_z(which, j):
        need(("z1" if j < FIRST else "z3", which, j))
        send(("zr", which, j))

    def other(which, j):
        need(("zr", which, j))
        if (which, j) not in MOVED:
            send(("near", "x", which, 1, j), ("near", "y", which, 1, j))

    def relay_xy(which, slot, j):
        for axis in "xy":
            need(("near", axis, which, slot, j))
            send(("far", axis, which, slot, j))

    def hop(axis, level, which, j):
        need(("near" if level == "n" else "far", axis, which, 0, j))
        send(("hop", axis, level, which, j))

    def land(axis, level, which, j):
        need(("hop", axis, level, which, j))
        send(("land", axis, level, which, j))

    def mask_loaded():
        if "mask" not in copied:
            copied.add("mask")
            mask_load.wait()

    def mask_up():
        mask_loaded()
        loads[0].wait()
        for k, level in enumerate(LEVEL):
            uall[pl.ds(k * G, G), pl.ds(0, G)] = (raw[0, level].astype(F32) * mask[0, level].astype(F32)).astype(BF16)
        send(("weight", 0))

    def mask_down():
        mask_loaded()
        loads[1].wait()
        for k, level in enumerate(LEVEL):
            dall[pl.ds(0, G), pl.ds(k * G, G)] = (raw[1, level].astype(F32) * mask[0, level].astype(F32)).astype(BF16)
        send(("weight", 1))

    def turn_weights():
        need(("weight", 0), ("weight", 1))

    def turn_held(slot):
        def body(k, carry):
            at = pl.ds(pl.multiple_of(k * G, G), G)
            held_t[at, pl.ds(slot * ROWS, ROWS)] = held[0, k, pl.ds(slot * ROWS, ROWS)].T
            return carry

        lax.fori_loop(0, LEVELS, body, 0)

    def turn_act(slot, t):
        act_t[:, tile(slot, t)] = act[tile(slot, t), :].T

    def near_inputs(which, slot, t):
        if slot == 0 and ("own", which) not in copied:
            copied.add(("own", which))
            own[which].wait()
        for j in range(t * PER_TILE, (t + 1) * PER_TILE):
            need(("z3" if slot else "z1", which, j))
            if slot and (which, j) in MOVED:
                need(("land", "x", "n", which, j), ("land", "y", "n", which, j))

    def far_inputs(which, slot, t):
        for j in range(t * PER_TILE, (t + 1) * PER_TILE):
            for axis in "xy":
                need(("land", axis, "f", which, j) if slot and (which, j) in MOVED else ("far", axis, which, slot, j))

    def share(which, at, places):
        inputs = jnp.concatenate([held[which, k, at] for k in places], axis=1)
        span = pl.ds(places[0] * G, len(places) * G)
        if which:
            return dot_nt(inputs, dall[:, span])
        return jnp.dot(inputs, uall[span, :], preferred_element_type=F32)

    def forward_near(slot, t):
        near_inputs(0, slot, t)
        need(("weight", 0))
        slope[tile(slot, t), :] = share(0, tile(slot, t), (0, 1, 2, 3))

    def backward_near(slot, t):
        near_inputs(1, slot, t)
        gact[tile(slot, t), :] = share(1, tile(slot, t), (0, 1, 2, 3))

    def forward(slot, t):
        far_inputs(0, slot, t)
        at = tile(slot, t)
        pre = slope[at, :] + share(0, at, (4, 5))
        square = pre * pre
        tanh = jnp.tanh(SCALE * pre * (1.0 + CUBE * square))
        cdf = 0.5 + 0.5 * tanh
        act[at, :] = (pre * cdf).astype(BF16)
        slope[at, :] = cdf + (0.5 * SCALE) * pre * (1.0 - tanh * tanh) * (1.0 + (3.0 * CUBE) * square)

    def backward(slot, t):
        far_inputs(1, slot, t)
        at = tile(slot, t)
        gpre[at, :] = ((gact[at, :] + share(1, at, (4, 5))) * slope[at, :]).astype(BF16)

    def product(which, slot, t, level):
        if which:
            return dot_nt(gpre[tile(slot, t), :], uall[columns(level), :])
        return jnp.dot(act[tile(slot, t), :], dall[:, columns(level)], preferred_element_type=F32)

    def far_terms(which, slot, t):
        need(("weight", 1))
        for a, axis in enumerate("xy"):
            term_send[which, a, tile(slot, t)] = product(which, slot, t, FAR[axis]).astype(BF16)

    def near_terms(which, slot, t):
        at = tile(slot, t)
        for a, axis in enumerate("xy"):
            near_term[which, a, at] = product(which, slot, t, NEAR[axis])
        z_term[which, at] = product(which, slot, t, 1)
        base[which, at] = product(which, slot, t, 0)

    def send_term(which, slot, j):
        send(("term", "x", which, slot, j), ("term", "y", which, slot, j))

    def hand_on(j):
        for axis in "xy":
            need(("term", axis, 0, 0, j))
            send(("last", axis, j))

    def join(which, slot, j):
        at = rows(slot, j)
        for a, axis in enumerate("xy"):
            total = near_term[which, a, at]
            if not passed(which, slot, j):
                need(("term", axis, which, slot, j))
                total = total + term_recv[which, a, at].astype(F32)
            sum_send[which, a, at] = total.astype(BF16)
            send(("sum", axis, which, slot, j))

    def collect(which, slot, j):
        at = rows(slot, j)
        need(("sum", "x", which, slot, j), ("sum", "y", which, slot, j))
        total = base[which, at] + sum_recv[which, 0, at].astype(F32) + sum_recv[which, 1, at].astype(F32)
        if slot == 0:
            base[which, at] = total
        else:
            half_send[which, piece(j)] = total.astype(BF16)
            send(("half", which, j))

    def plain(which, slot, j):
        z_send[which, rows(slot, j)] = z_term[which, rows(slot, j)].astype(BF16)
        send(("out3" if slot else "out1", which, j))

    def pass_on(which, j):
        slot = int(j >= FIRST)
        at = rows(slot, j)
        need(("half", which, j))
        z_send[which, at] = (z_term[which, at] + half_recv[which, piece(j)].astype(F32)).astype(BF16)
        send(("out3" if slot else "out1", which, j))

    def finish(which, j):
        need(("out1", which, j), ("out3", which, j))
        total = base[which, rows(0, j)] + z_recv[which, rows(0, j)].astype(F32) + z_recv[which, rows(1, j)].astype(F32)
        if passed(which, 0, j):
            need(("last", "x", j), ("last", "y", j))
            total = total + last_recv[0, piece(j)].astype(F32) + last_recv[1, piece(j)].astype(F32)
        (gtok if which else out)[piece(j), :] = total.astype(BF16)

    def grads(which, third):
        def body(k, carry):
            at = pl.ds(pl.multiple_of(k * G, G), G)
            if which:
                both = jnp.dot(act_t[...], held[1, k], preferred_element_type=F32)
                grad_own[1, k] = both[:G]
                grad_peer[1, k] = both[G:]
            else:
                both = jnp.dot(held_t[at, :], gpre[...], preferred_element_type=F32)
                grad_own[0, k] = both[:, :G]
                grad_peer[0, k] = both[:, G:]
            return carry

        lax.fori_loop(third * THIRDS, (third + 1) * THIRDS, body, 0)
        send(("grad", which, third))

    def write_grad(which, k):
        return pltpu.make_async_copy(grad_own.at[which, k], (gdown if which else gup).at[LEVEL[k]], local.at[4 + which * LEVELS + k])

    def grads_sum(which, third):
        need(("grad", which, third))

        for k in range(third * THIRDS, (third + 1) * THIRDS):
            total = grad_own[which, k] + grad_recv[which, k]
            grad_own[which, k] = total * mask[0, LEVEL[k]].astype(F32)
            write_grad(which, k).start()

    def finish_sends(*numbers):
        for name in (tuple(SIZES)[n] for n in numbers):
            sent.add(name)
            if name[0] in ("weight", "grad"):
                transfer(name).wait_send()
            else:
                together(SIZES[name], FAMILIES[name], 0).wait_send()

    steps = (
        own_xy, own_z, relay_z, other, relay_xy, hop, land, mask_up, mask_down, turn_weights, turn_held, turn_act,
        forward_near, forward, backward_near, backward, far_terms, near_terms, send_term, hand_on, join, collect,
        plain, pass_on, finish, grads, grads_sum, finish_sends,
    )
    for step in ORDER:
        steps[step[0]](*step[1:])

    assert started == set(NUMBER) and landed == set(ARRIVALS)
    for which in range(2):
        for k in range(LEVELS):
            write_grad(which, k).wait()
    assert sent == set(FAMILIES)


def hand_out(*refs):
    sources, results, sems = refs[:4], refs[4:8], refs[8]
    copies = []
    for src, dst in zip(sources, results):
        if len(src.shape) == 2:
            pairs = [(src, dst)]
        else:
            pairs = [(src.at[pl.ds(k, 2)], dst.at[pl.ds(k, 2)]) for k in range(0, LEVELS, 2)]
        for a, b in pairs:
            copies.append(pltpu.make_async_copy(a, b, sems.at[len(copies)]))
    for copy in copies:
        copy.start()
    for copy in copies:
        copy.wait()


def shards(tokens, up_weight, down_weight, block_mask, cotangent):
    anywhere = pl.BlockSpec(memory_space=pl.ANY)
    vmem = pl.BlockSpec(memory_space=pltpu.VMEM)
    both = 2 * ROWS
    result = (
        jax.ShapeDtypeStruct((ROWS, G), BF16),
        jax.ShapeDtypeStruct((ROWS, G), BF16),
        jax.ShapeDtypeStruct((LEVELS, G, G), F32),
        jax.ShapeDtypeStruct((LEVELS, G, G), F32),
    )
    operands = [pltpu.with_memory_space_constraint(a, pltpu.HBM) for a in (tokens, cotangent, up_weight[0], down_weight[0], block_mask)]
    worked = pl.pallas_call(
        kernel,
        out_shape=tuple(pltpu.VMEM(a.shape, a.dtype) for a in result),
        in_specs=[anywhere] * 5,
        out_specs=(vmem, vmem, anywhere, anywhere),
        scratch_shapes=[
            pltpu.SMEM((1, LEVELS), jnp.int32),
            pltpu.VMEM((2, LEVELS, both, G), BF16),
            pltpu.VMEM((WIDE, both), BF16),
            pltpu.VMEM((2, LEVELS, G, G), BF16),
            pltpu.VMEM((WIDE, 2 * G), BF16),
            pltpu.VMEM((2 * G, WIDE), BF16),
            pltpu.VMEM((both, 2 * G), BF16),
            pltpu.VMEM((2 * G, both), BF16),
            pltpu.VMEM((both, 2 * G), BF16),
            pltpu.VMEM((both, 2 * G), F32),
            pltpu.VMEM((both, 2 * G), F32),
            pltpu.VMEM((2, 2, both, G), BF16),
            pltpu.VMEM((2, 2, both, G), BF16),
            pltpu.VMEM((2, 2, both, G), F32),
            pltpu.VMEM((2, 2, both, G), BF16),
            pltpu.VMEM((2, 2, both, G), BF16),
            pltpu.VMEM((2, both, G), F32),
            pltpu.VMEM((2, both, G), F32),
            pltpu.VMEM((2, ROWS, G), BF16),
            pltpu.VMEM((2, ROWS, G), BF16),
            pltpu.VMEM((2, ROWS, G), BF16),
            pltpu.VMEM((2, 2, len(MOVED) * PART, G), BF16),
            pltpu.VMEM((2, both, G), BF16),
            pltpu.VMEM((2, both, G), BF16),
            pltpu.VMEM((2, LEVELS, G, G), F32),
            pltpu.VMEM((2, LEVELS, G, G), F32),
            pltpu.VMEM((2, LEVELS, G, G), F32),
            pltpu.SemaphoreType.DMA((len(FAMILIES),)),
            pltpu.SemaphoreType.DMA((len(LANDINGS),)),
            pltpu.SemaphoreType.DMA((5 + 2 * LEVELS,)),
        ],
        compiler_params=pltpu.CompilerParams(
            collective_id=0, has_side_effects=True, vmem_limit_bytes=58 * 1024 * 1024
        ),
    )(*operands)
    worked = [pltpu.with_memory_space_constraint(a, pltpu.VMEM) for a in worked]
    output, grad_tokens, grad_up, grad_down = pl.pallas_call(
        hand_out,
        out_shape=result,
        in_specs=[anywhere] * 4,
        out_specs=(anywhere,) * 4,
        scratch_shapes=[pltpu.SemaphoreType.DMA((8,))],
        compiler_params=pltpu.CompilerParams(vmem_limit_bytes=1024 * 1024),
    )(*worked)
    return output, grad_tokens, grad_up[None], grad_down[None]


def solution(mesh):
    placed = (
        P("seq", "tp"),
        P(("seq", "tp"), None, None, None),
        P(("seq", "tp"), None, None, None),
        P(("seq", "tp"), None),
        P("seq", "tp"),
    )
    return jax.shard_map(
        shards,
        mesh=mesh,
        in_specs=placed,
        out_specs=(
            P("seq", "tp"),
            P("seq", "tp"),
            P(("seq", "tp"), None, None, None),
            P(("seq", "tp"), None, None, None),
        ),
        check_vma=False,
    )
```

```python
import collections
import math

import jax
import jax.numpy as jnp
from jax import lax
from jax.experimental import pallas as pl
from jax.experimental.pallas import tpu as pltpu
from jax.sharding import PartitionSpec as P

MESH = pl.DeviceIdType.MESH
F32 = jnp.float32
BF16 = jnp.bfloat16
ROWS = 512
PART = 128
PIECES = ROWS // PART
FIRST = PIECES // 2
TILE = 256
PER_TILE = TILE // PART
THIRDS = 3
G = 256
LEVELS = 6
WIDE = LEVELS * G
LEVEL = (0, 1, 2, 4, 3, 5)
NEAR = {"x": 3, "y": 2}
FAR = {"x": 5, "y": 4}
SCALE = math.sqrt(2.0 / math.pi)
CUBE = 0.044715


def numbering():
    keys = []
    for which in range(2):
        keys += [(name, which, j) for name in ("z1", "z3", "zr", "out1", "out3", "half") for j in range(PIECES)]
        keys += [
            (name, axis, which, slot, j)
            for name in ("near", "far", "term", "sum")
            for axis in "xy"
            for slot in range(2)
            for j in range(PIECES)
        ]
        keys += [("weight", which)] + [("grad", which, k) for k in range(LEVELS // THIRDS)]
    keys += [("last", axis, j) for axis in "xy" for j in PASSED]
    moved = [(axis, level, which, j) for axis in "xy" for level in "nf" for which, j in MOVED]
    keys += [("hop", *rest) for rest in moved] + [("land", *rest) for rest in moved]
    keys = [k for k in keys if not (k[0] in ("near", "far") and k[3] == 1 and (k[2], k[4]) in MOVED)]
    return {key: n for n, key in enumerate(keys)}


def passed(which, slot, j):
    return which == 0 and slot == 0 and j in PASSED


def family(key):
    name = key[0]
    if name in ("weight", "grad"):
        return key
    if name in ("near", "far", "term", "sum"):
        return name, key[2], key[3]
    if name in ("last", "hop", "land"):
        return (name,)
    return {"z1": "z", "z3": "z", "zr": "middle", "half": "middle", "out1": "out", "out3": "out"}[name], key[1]


def arrival(key):
    name = key[0]
    if name in ("near", "far", "term", "sum"):
        return name, *key[2:]
    if name in ("out1", "out3"):
        return "out", *key[1:]
    if name in ("last", "land"):
        return name, *key[2:]
    return key


PASSED = (2, 3)
MOVED = ((1, 0), (1, 2))
NUMBER = numbering()
ARRIVALS = collections.Counter(arrival(key) for key in NUMBER)
LANDINGS = {name: n for n, name in enumerate(ARRIVALS)}
SIZES = collections.Counter(family(key) for key in NUMBER)
FAMILIES = {name: n for n, name in enumerate(SIZES)}

S_OX, S_OZ, S_RZ, S_OT, S_RX, S_H1, S_H2, S_SU, S_SD, S_TW, S_TH, S_TA, S_FN, S_F, \
    S_BN, S_B, S_TF, S_TN, S_S, S_RL, S_J, S_C, S_Z, S_PO, S_FIN, S_G, S_GS, S_W = range(28)
X, Y, NR, FR = "x", "y", "n", "f"
ORDER = (
    (S_OZ, 0, 3), (S_OX, 0, 3), (S_OX, 1, 0), (S_OZ, 0, 2), (S_OZ, 0, 1), (S_SU,), (S_OZ, 1, 1), (S_OX, 1, 2),
    (S_OX, 0, 2), (S_SD,), (S_OX, 0, 1), (S_RX, 0, 0, 3), (S_OX, 0, 0), (S_OZ, 0, 0), (S_RX, 1, 0, 0), (S_OX, 1, 3),
    (S_RZ, 0, 3), (S_RZ, 0, 2), (S_RX, 1, 0, 2), (S_RZ, 0, 1), (S_OZ, 1, 3), (S_OX, 1, 1), (S_H1, X, NR, 1, 2),
    (S_RX, 0, 0, 2), (S_FN, 0, 1), (S_RZ, 0, 0), (S_RZ, 1, 1), (S_RX, 0, 0, 1), (S_OZ, 1, 2), (S_H1, Y, FR, 1, 0),
    (S_TW,), (S_OT, 0, 3), (S_H1, Y, FR, 1, 2), (S_H1, X, FR, 1, 2), (S_RX, 0, 0, 0), (S_F, 0, 1), (S_RZ, 1, 3),
    (S_OT, 0, 2), (S_RX, 1, 0, 3), (S_H1, X, NR, 1, 0), (S_OT, 0, 1), (S_H1, X, FR, 1, 0), (S_FN, 0, 0),
    (S_RX, 1, 0, 1), (S_H1, Y, NR, 1, 2), (S_H1, Y, NR, 1, 0), (S_OT, 0, 0), (S_TF, 0, 0, 1), (S_OZ, 1, 0),
    (S_RX, 0, 1, 3), (S_TN, 0, 0, 1), (S_F, 0, 0), (S_TF, 0, 0, 0), (S_RX, 0, 1, 2), (S_RZ, 1, 2), (S_OT, 1, 1),
    (S_BN, 0, 1), (S_H2, X, NR, 1, 2), (S_B, 0, 1), (S_TF, 1, 0, 1), (S_RX, 0, 1, 1), (S_TN, 0, 0, 0), (S_OT, 1, 3),
    (S_S, 0, 0, 2), (S_TN, 1, 0, 1), (S_S, 1, 0, 2), (S_H2, Y, FR, 1, 2), (S_FN, 1, 1), (S_TA, 0, 1), (S_J, 0, 0, 2),
    (S_RX, 0, 1, 0), (S_F, 1, 1), (S_TF, 0, 1, 1), (S_S, 0, 1, 2), (S_H2, Y, FR, 1, 0), (S_S, 0, 0, 3),
    (S_RX, 1, 1, 1), (S_H2, X, NR, 1, 0), (S_J, 0, 0, 3), (S_FN, 1, 0), (S_TN, 0, 1, 1), (S_S, 0, 1, 3),
    (S_RZ, 1, 0), (S_BN, 0, 0), (S_TA, 0, 0), (S_W, 11), (S_H2, X, FR, 1, 0), (S_H2, X, FR, 1, 2), (S_B, 0, 0),
    (S_H2, Y, NR, 1, 0), (S_W, 25), (S_TF, 1, 0, 0), (S_RX, 1, 1, 3), (S_F, 1, 0), (S_W, 3), (S_J, 1, 0, 2),
    (S_W, 0), (S_H2, Y, NR, 1, 2), (S_Z, 0, 0, 2), (S_TF, 0, 1, 0), (S_TA, 1, 0), (S_OT, 1, 2), (S_S, 0, 1, 0),
    (S_Z, 0, 0, 3), (S_J, 0, 1, 2), (S_W, 17), (S_Z, 1, 0, 3), (S_TA, 1, 1), (S_OT, 1, 0), (S_TN, 0, 1, 0),
    (S_TH, 0), (S_Z, 0, 1, 0), (S_BN, 1, 0), (S_Z, 1, 0, 2), (S_B, 1, 0), (S_TF, 1, 1, 0), (S_S, 1, 1, 1),
    (S_TN, 1, 1, 0), (S_J, 0, 1, 3), (S_W, 5), (S_S, 1, 1, 0), (S_BN, 1, 1), (S_B, 1, 1), (S_TF, 1, 1, 1),
    (S_J, 0, 1, 0), (S_S, 1, 1, 3), (S_Z, 1, 1, 1), (S_S, 0, 1, 1), (S_S, 1, 1, 2), (S_W, 19), (S_S, 0, 0, 1),
    (S_Z, 1, 1, 0), (S_W, 29), (S_TN, 1, 1, 1), (S_W, 4), (S_S, 1, 0, 3), (S_J, 1, 1, 1), (S_W, 14), (S_G, 1, 1),
    (S_J, 1, 1, 0), (S_C, 0, 1, 0), (S_S, 0, 0, 0), (S_J, 1, 1, 3), (S_Z, 0, 1, 1), (S_G, 1, 0), (S_C, 0, 1, 2),
    (S_C, 1, 1, 1), (S_J, 0, 1, 1), (S_C, 0, 1, 3), (S_J, 1, 1, 2), (S_TH, 1), (S_S, 1, 0, 0), (S_S, 1, 0, 1),
    (S_C, 1, 1, 0), (S_C, 1, 1, 3), (S_G, 0, 1), (S_PO, 0, 2), (S_J, 0, 0, 1), (S_PO, 0, 0), (S_TN, 1, 0, 0),
    (S_W, 6), (S_J, 1, 0, 3), (S_C, 0, 1, 1), (S_RL, 2), (S_C, 1, 1, 2), (S_J, 0, 0, 0), (S_PO, 1, 1), (S_PO, 0, 3),
    (S_G, 0, 0), (S_PO, 1, 3), (S_J, 1, 0, 1), (S_PO, 1, 0), (S_C, 1, 0, 2), (S_RL, 3), (S_PO, 0, 1), (S_J, 1, 0, 0),
    (S_PO, 1, 2), (S_GS, 1, 0), (S_GS, 0, 1), (S_C, 0, 0, 2), (S_GS, 1, 1), (S_W, 20), (S_C, 0, 0, 1),
    (S_C, 0, 0, 0), (S_C, 1, 0, 3), (S_W, 30), (S_FIN, 0, 2), (S_FIN, 0, 0), (S_C, 0, 0, 3), (S_FIN, 1, 3),
    (S_C, 1, 0, 1), (S_FIN, 1, 1), (S_FIN, 0, 3), (S_GS, 0, 0), (S_FIN, 1, 2), (S_C, 1, 0, 0), (S_W, 18),
    (S_FIN, 1, 0), (S_FIN, 0, 1), (S_W, 1, 15, 7, 21, 9, 8, 23, 2, 10, 16, 22, 24, 27, 26, 13, 28, 12),
)


def flip(index, bit):
    return index + bit - 2 * bit * lax.rem(lax.div(index, bit), 2)


def kernel(
    tok, cot, up, down, present, out, gtok, gup, gdown,
    mask, held, held_t, raw, uall, dall, uall_t, dall_t, act, act_t, gpre, slope, gact,
    term_send, term_recv, near_term, sum_send, sum_recv, base, z_term,
    half_send, half_recv, last_recv, hops, z_send, z_recv,
    grad_own, grad_peer, grad_recv,
    sends, recvs, local,
):
    shared = (tok, cot)
    seq, tp = lax.axis_index("seq"), lax.axis_index("tp")
    place = {
        "core": (flip(seq, 1), tp),
        "z1": (seq, flip(tp, 1)),
        "z3": (flip(seq, 2), flip(tp, 1)),
        "x1": (seq, flip(tp, 8)),
        "x3": (seq, flip(flip(tp, 8), 16)),
        "y1": (seq, flip(tp, 2)),
        "y3": (seq, flip(flip(tp, 2), 4)),
    }

    def remote(src, dst, key, target):
        return pltpu.make_async_remote_copy(
            src_ref=src,
            dst_ref=dst,
            send_sem=sends.at[FAMILIES[family(key)]],
            recv_sem=recvs.at[LANDINGS[arrival(key)]],
            device_id=place[target],
            device_id_type=MESH,
        )

    def rows(slot, j):
        start = slot * ROWS + j * PART
        return pl.ds(start if isinstance(j, int) else pl.multiple_of(start, PART), PART)

    def piece(j):
        return pl.ds(j * PART, PART)

    def columns(level):
        return pl.ds(level * G, G)

    def transfer(key):
        name, rest = key[0], key[1:]
        if name == "weight":
            if rest[0] == 0:
                return remote(uall.at[:, pl.ds(0, G)], uall.at[:, pl.ds(G, G)], key, "core")
            return remote(dall.at[pl.ds(0, G)], dall.at[pl.ds(G, G)], key, "core")
        if name == "grad":
            at = pl.ds(rest[1] * THIRDS, THIRDS)
            return remote(grad_peer.at[rest[0], at], grad_recv.at[rest[0], at], key, "core")
        if name == "last":
            a, j = "xy".index(rest[0]), rest[1]
            return remote(term_recv.at[0, a, rows(0, j)], last_recv.at[a, piece(j)], key, rest[0] + "3")
        if name in ("hop", "land"):
            axis, level, which, j = rest
            n, group = "nf".index(level), (NEAR if level == "n" else FAR)[axis]
            room = hops.at[n, "xy".index(axis), pl.ds(MOVED.index((which, j)) * PART, PART)]
            if name == "hop":
                return remote(held.at[which, group, rows(0, j)], room, key, ("z1", "z3")[n])
            return remote(room, held.at[which, group, rows(1, j)], key, ("z3", "z1")[n])
        if name in ("near", "far", "term", "sum"):
            axis, which, slot, j = rest
            a, at = "xy".index(axis), rows(slot, j)
            if name == "near":
                src = held.at[which, 0, at] if slot else shared[which].at[piece(j)]
                return remote(src, held.at[which, NEAR[axis], at], key, axis + "1")
            if name == "far":
                return remote(held.at[which, NEAR[axis], at], held.at[which, FAR[axis], at], key, axis + "3")
            if name == "term":
                target = axis + ("1" if passed(which, slot, j) else "3")
                return remote(term_send.at[which, a, at], term_recv.at[which, a, at], key, target)
            return remote(sum_send.at[which, a, at], sum_recv.at[which, a, at], key, axis + "1")
        which, j = rest
        if name == "z1":
            return remote(shared[which].at[piece(j)], held.at[which, 1, rows(0, j)], key, "z1")
        if name == "z3":
            return remote(shared[which].at[piece(j)], held.at[which, 1, rows(1, j)], key, "z3")
        onward = "z3" if j < FIRST else "z1"
        if name == "zr":
            return remote(held.at[which, 1, rows(int(j >= FIRST), j)], held.at[which, 0, rows(1, j)], key, onward)
        if name == "half":
            return remote(half_send.at[which, piece(j)], half_recv.at[which, piece(j)], key, onward)
        slot = int(name == "out3")
        return remote(z_send.at[which, rows(slot, j)], z_recv.at[which, rows(slot, j)], key, "z3" if slot else "z1")

    def together(pieces, sent_by, landed_by):
        span = held.at[0, 0, pl.ds(0, pieces * PART)]
        return pltpu.make_async_remote_copy(
            src_ref=span,
            dst_ref=span,
            send_sem=sends.at[sent_by],
            recv_sem=recvs.at[landed_by],
            device_id=place["z1"],
            device_id_type=MESH,
        )

    started, landed, copied, sent = set(), set(), set(), set()

    def send(*keys):
        for key in keys:
            started.add(key)
            transfer(key).start()

    def need(*keys):
        for key in keys:
            name = arrival(key)
            if name in landed:
                continue
            landed.add(name)
            if name[0] in ("weight", "grad"):
                transfer(key).wait_recv()
            else:
                together(ARRIVALS[name], 0, LANDINGS[name]).wait_recv()

    own = [
        pltpu.make_async_copy(shared[which], held.at[which, 0, pl.ds(0, ROWS)], local.at[which])
        for which in range(2)
    ]
    loads = [pltpu.make_async_copy(ref, raw.at[which], local.at[2 + which]) for which, ref in enumerate((up, down))]
    mask_load = pltpu.make_async_copy(present, mask, local.at[4 + 2 * LEVELS])
    barrier = pltpu.get_barrier_semaphore()
    for target in place.values():
        pl.semaphore_signal(barrier, inc=1, device_id=target, device_id_type=MESH)
    mask_load.start()
    for copy in loads + own:
        copy.start()
    pl.semaphore_wait(barrier, len(place))

    def tile(slot, t):
        return pl.ds(slot * ROWS + t * TILE, TILE)

    def own_z(which, j):
        send(("z1", which, j), ("z3", which, j))

    def own_xy(which, j):
        send(("near", "x", which, 0, j), ("near", "y", which, 0, j))

    def relay_z(which, j):
        need(("z1" if j < FIRST else "z3", which, j))
        send(("zr", which, j))

    def other(which, j):
        need(("zr", which, j))
        if (which, j) not in MOVED:
            send(("near", "x", which, 1, j), ("near", "y", which, 1, j))

    def relay_xy(which, slot, j):
        for axis in "xy":
            need(("near", axis, which, slot, j))
            send(("far", axis, which, slot, j))

    def hop(axis, level, which, j):
        need(("near" if level == "n" else "far", axis, which, 0, j))
        send(("hop", axis, level, which, j))

    def land(axis, level, which, j):
        need(("hop", axis, level, which, j))
        send(("land", axis, level, which, j))

    def mask_loaded():
        if "mask" not in copied:
            copied.add("mask")
            mask_load.wait()

    def mask_up():
        mask_loaded()
        loads[0].wait()
        for k, level in enumerate(LEVEL):
            uall[pl.ds(k * G, G), pl.ds(0, G)] = (raw[0, level].astype(F32) * mask[0, level].astype(F32)).astype(BF16)
        send(("weight", 0))

    def mask_down():
        mask_loaded()
        loads[1].wait()
        for k, level in enumerate(LEVEL):
            dall[pl.ds(0, G), pl.ds(k * G, G)] = (raw[1, level].astype(F32) * mask[0, level].astype(F32)).astype(BF16)
        send(("weight", 1))

    def turn_weights():
        need(("weight", 0), ("weight", 1))

        def body(k, carry):
            at = pl.ds(pl.multiple_of(k * G, G), G)
            dall_t[at, :] = dall[:, at].T
            uall_t[:, at] = uall[at, :].T
            return carry

        lax.fori_loop(0, LEVELS, body, 0)

    def turn_held(slot):
        def body(k, carry):
            at = pl.ds(pl.multiple_of(k * G, G), G)
            held_t[at, pl.ds(slot * ROWS, ROWS)] = held[0, k, pl.ds(slot * ROWS, ROWS)].T
            return carry

        lax.fori_loop(0, LEVELS, body, 0)

    def turn_act(slot, t):
        act_t[:, tile(slot, t)] = act[tile(slot, t), :].T

    def near_inputs(which, slot, t):
        if slot == 0 and ("own", which) not in copied:
            copied.add(("own", which))
            own[which].wait()
        for j in range(t * PER_TILE, (t + 1) * PER_TILE):
            need(("z3" if slot else "z1", which, j))
            if slot and (which, j) in MOVED:
                need(("land", "x", "n", which, j), ("land", "y", "n", which, j))

    def far_inputs(which, slot, t):
        for j in range(t * PER_TILE, (t + 1) * PER_TILE):
            for axis in "xy":
                need(("land", axis, "f", which, j) if slot and (which, j) in MOVED else ("far", axis, which, slot, j))

    def partial(which, at, weights):
        early = jnp.concatenate([held[which, k, at] for k in range(4)], axis=1)
        return jnp.dot(early, weights[pl.ds(0, 4 * G), :], preferred_element_type=F32)

    def rest(which, at, weights):
        late = jnp.concatenate([held[which, k, at] for k in (4, 5)], axis=1)
        return jnp.dot(late, weights[pl.ds(4 * G, 2 * G), :], preferred_element_type=F32)

    def forward_near(slot, t):
        near_inputs(0, slot, t)
        need(("weight", 0))
        slope[tile(slot, t), :] = partial(0, tile(slot, t), uall)

    def backward_near(slot, t):
        near_inputs(1, slot, t)
        gact[tile(slot, t), :] = partial(1, tile(slot, t), dall_t)

    def forward(slot, t):
        far_inputs(0, slot, t)
        at = tile(slot, t)
        pre = slope[at, :] + rest(0, at, uall)
        square = pre * pre
        tanh = jnp.tanh(SCALE * pre * (1.0 + CUBE * square))
        cdf = 0.5 + 0.5 * tanh
        act[at, :] = (pre * cdf).astype(BF16)
        slope[at, :] = cdf + (0.5 * SCALE) * pre * (1.0 - tanh * tanh) * (1.0 + (3.0 * CUBE) * square)

    def backward(slot, t):
        far_inputs(1, slot, t)
        at = tile(slot, t)
        gpre[at, :] = ((gact[at, :] + rest(1, at, dall_t)) * slope[at, :]).astype(BF16)

    def product(which, slot, t, level):
        if which:
            return jnp.dot(gpre[tile(slot, t), :], uall_t[:, columns(level)], preferred_element_type=F32)
        return jnp.dot(act[tile(slot, t), :], dall[:, columns(level)], preferred_element_type=F32)

    def far_terms(which, slot, t):
        need(("weight", 1))
        for a, axis in enumerate("xy"):
            term_send[which, a, tile(slot, t)] = product(which, slot, t, FAR[axis]).astype(BF16)

    def near_terms(which, slot, t):
        at = tile(slot, t)
        for a, axis in enumerate("xy"):
            near_term[which, a, at] = product(which, slot, t, NEAR[axis])
        z_term[which, at] = product(which, slot, t, 1)
        base[which, at] = product(which, slot, t, 0)

    def send_term(which, slot, j):
        send(("term", "x", which, slot, j), ("term", "y", which, slot, j))

    def hand_on(j):
        for axis in "xy":
            need(("term", axis, 0, 0, j))
            send(("last", axis, j))

    def join(which, slot, j):
        at = rows(slot, j)
        for a, axis in enumerate("xy"):
            total = near_term[which, a, at]
            if not passed(which, slot, j):
                need(("term", axis, which, slot, j))
                total = total + term_recv[which, a, at].astype(F32)
            sum_send[which, a, at] = total.astype(BF16)
            send(("sum", axis, which, slot, j))

    def collect(which, slot, j):
        at = rows(slot, j)
        need(("sum", "x", which, slot, j), ("sum", "y", which, slot, j))
        total = base[which, at] + sum_recv[which, 0, at].astype(F32) + sum_recv[which, 1, at].astype(F32)
        if slot == 0:
            base[which, at] = total
        else:
            half_send[which, piece(j)] = total.astype(BF16)
            send(("half", which, j))

    def plain(which, slot, j):
        z_send[which, rows(slot, j)] = z_term[which, rows(slot, j)].astype(BF16)
        send(("out3" if slot else "out1", which, j))

    def pass_on(which, j):
        slot = int(j >= FIRST)
        at = rows(slot, j)
        need(("half", which, j))
        z_send[which, at] = (z_term[which, at] + half_recv[which, piece(j)].astype(F32)).astype(BF16)
        send(("out3" if slot else "out1", which, j))

    def finish(which, j):
        need(("out1", which, j), ("out3", which, j))
        total = base[which, rows(0, j)] + z_recv[which, rows(0, j)].astype(F32) + z_recv[which, rows(1, j)].astype(F32)
        if passed(which, 0, j):
            need(("last", "x", j), ("last", "y", j))
            total = total + last_recv[0, piece(j)].astype(F32) + last_recv[1, piece(j)].astype(F32)
        (gtok if which else out)[piece(j), :] = total.astype(BF16)

    def grads(which, third):
        def body(k, carry):
            at = pl.ds(pl.multiple_of(k * G, G), G)
            if which:
                both = jnp.dot(act_t[...], held[1, k], preferred_element_type=F32)
                grad_own[1, k] = both[:G]
                grad_peer[1, k] = both[G:].astype(BF16)
            else:
                both = jnp.dot(held_t[at, :], gpre[...], preferred_element_type=F32)
                grad_own[0, k] = both[:, :G]
                grad_peer[0, k] = both[:, G:].astype(BF16)
            return carry

        lax.fori_loop(third * THIRDS, (third + 1) * THIRDS, body, 0)
        send(("grad", which, third))

    def write_grad(which, k):
        return pltpu.make_async_copy(grad_own.at[which, k], (gdown if which else gup).at[LEVEL[k]], local.at[4 + which * LEVELS + k])

    def grads_sum(which, third):
        need(("grad", which, third))

        for k in range(third * THIRDS, (third + 1) * THIRDS):
            total = grad_own[which, k] + grad_recv[which, k].astype(F32)
            grad_own[which, k] = total * mask[0, LEVEL[k]].astype(F32)
            write_grad(which, k).start()

    def finish_sends(*numbers):
        for name in (tuple(SIZES)[n] for n in numbers):
            sent.add(name)
            if name[0] in ("weight", "grad"):
                transfer(name).wait_send()
            else:
                together(SIZES[name], FAMILIES[name], 0).wait_send()

    steps = (
        own_xy, own_z, relay_z, other, relay_xy, hop, land, mask_up, mask_down, turn_weights, turn_held, turn_act,
        forward_near, forward, backward_near, backward, far_terms, near_terms, send_term, hand_on, join, collect,
        plain, pass_on, finish, grads, grads_sum, finish_sends,
    )
    for step in ORDER:
        steps[step[0]](*step[1:])

    assert started == set(NUMBER) and landed == set(ARRIVALS)
    for which in range(2):
        for k in range(LEVELS):
            write_grad(which, k).wait()
    assert sent == set(FAMILIES)


def hand_out(*refs):
    sources, results, sems = refs[:4], refs[4:8], refs[8]
    copies = []
    for src, dst in zip(sources, results):
        if len(src.shape) == 2:
            pairs = [(src, dst)]
        else:
            pairs = [(src.at[pl.ds(k, 2)], dst.at[pl.ds(k, 2)]) for k in range(0, LEVELS, 2)]
        for a, b in pairs:
            copies.append(pltpu.make_async_copy(a, b, sems.at[len(copies)]))
    for copy in copies:
        copy.start()
    for copy in copies:
        copy.wait()


def shards(tokens, up_weight, down_weight, block_mask, cotangent):
    anywhere = pl.BlockSpec(memory_space=pl.ANY)
    vmem = pl.BlockSpec(memory_space=pltpu.VMEM)
    both = 2 * ROWS
    result = (
        jax.ShapeDtypeStruct((ROWS, G), BF16),
        jax.ShapeDtypeStruct((ROWS, G), BF16),
        jax.ShapeDtypeStruct((LEVELS, G, G), F32),
        jax.ShapeDtypeStruct((LEVELS, G, G), F32),
    )
    operands = [pltpu.with_memory_space_constraint(a, pltpu.HBM) for a in (tokens, cotangent, up_weight[0], down_weight[0], block_mask)]
    worked = pl.pallas_call(
        kernel,
        out_shape=tuple(pltpu.VMEM(a.shape, a.dtype) for a in result),
        in_specs=[anywhere] * 5,
        out_specs=(vmem, vmem, anywhere, anywhere),
        scratch_shapes=[
            pltpu.SMEM((1, LEVELS), jnp.int32),
            pltpu.VMEM((2, LEVELS, both, G), BF16),
            pltpu.VMEM((WIDE, both), BF16),
            pltpu.VMEM((2, LEVELS, G, G), BF16),
            pltpu.VMEM((WIDE, 2 * G), BF16),
            pltpu.VMEM((2 * G, WIDE), BF16),
            pltpu.VMEM((2 * G, WIDE), BF16),
            pltpu.VMEM((WIDE, 2 * G), BF16),
            pltpu.VMEM((both, 2 * G), BF16),
            pltpu.VMEM((2 * G, both), BF16),
            pltpu.VMEM((both, 2 * G), BF16),
            pltpu.VMEM((both, 2 * G), F32),
            pltpu.VMEM((both, 2 * G), F32),
            pltpu.VMEM((2, 2, both, G), BF16),
            pltpu.VMEM((2, 2, both, G), BF16),
            pltpu.VMEM((2, 2, both, G), F32),
            pltpu.VMEM((2, 2, both, G), BF16),
            pltpu.VMEM((2, 2, both, G), BF16),
            pltpu.VMEM((2, both, G), F32),
            pltpu.VMEM((2, both, G), F32),
            pltpu.VMEM((2, ROWS, G), BF16),
            pltpu.VMEM((2, ROWS, G), BF16),
            pltpu.VMEM((2, ROWS, G), BF16),
            pltpu.VMEM((2, 2, len(MOVED) * PART, G), BF16),
            pltpu.VMEM((2, both, G), BF16),
            pltpu.VMEM((2, both, G), BF16),
            pltpu.VMEM((2, LEVELS, G, G), F32),
            pltpu.VMEM((2, LEVELS, G, G), BF16),
            pltpu.VMEM((2, LEVELS, G, G), BF16),
            pltpu.SemaphoreType.DMA((len(FAMILIES),)),
            pltpu.SemaphoreType.DMA((len(LANDINGS),)),
            pltpu.SemaphoreType.DMA((5 + 2 * LEVELS,)),
        ],
        compiler_params=pltpu.CompilerParams(
            collective_id=0, has_side_effects=True, vmem_limit_bytes=58 * 1024 * 1024
        ),
    )(*operands)
    worked = [pltpu.with_memory_space_constraint(a, pltpu.VMEM) for a in worked]
    output, grad_tokens, grad_up, grad_down = pl.pallas_call(
        hand_out,
        out_shape=result,
        in_specs=[anywhere] * 4,
        out_specs=(anywhere,) * 4,
        scratch_shapes=[pltpu.SemaphoreType.DMA((8,))],
        compiler_params=pltpu.CompilerParams(vmem_limit_bytes=1024 * 1024),
    )(*worked)
    return output, grad_tokens, grad_up[None], grad_down[None]


def solution(mesh):
    placed = (
        P("seq", "tp"),
        P(("seq", "tp"), None, None, None),
        P(("seq", "tp"), None, None, None),
        P(("seq", "tp"), None),
        P("seq", "tp"),
    )
    return jax.shard_map(
        shards,
        mesh=mesh,
        in_specs=placed,
        out_specs=(
            P("seq", "tp"),
            P("seq", "tp"),
            P(("seq", "tp"), None, None, None),
            P(("seq", "tp"), None, None, None),
        ),
        check_vma=False,
    )
```
